32 devices in a mesh: dp: 8 (over z, x), head: 4 (over y, core).
Axes of the slice: x: 2, y: 2, z: 4, core: 2. Of those that a mesh axis runs over, the one named last changes fastest.
Arguments:
- clean_latents: float32 [24, 832, 20], P('dp', 'head'), may hold values from -6 to 6
- noise_draw: float32 [24, 832, 20], P('dp', 'head'), may hold values from -6 to 6
- timesteps: float32 [24], P('dp'), may hold values from 0.02 to 0.98
- captions: bfloat16 [24, 256, 768], P('dp'), may hold values from -6 to 6
- cap_len: int32 [24], P('dp'), may hold values from 5 to 256, as said below
- pairing: int32 [24], P('dp'), may hold values from 0 to 23, each once
- adam_step: int32 [1], replicated, may hold values from 2 to 20
- qkv_weight: float32 [2, 768, 2304], P(None, 'dp', 'head'), may hold values from -0.21875 to 0.21875
- out_weight: float32 [2, 768, 768], P(None, 'dp', 'head'), may hold values from -1.25 to 1.25
- up_weight: float32 [2, 768, 3072], P(None, 'dp', 'head'), may hold values from -0.21875 to 0.21875
- down_weight: float32 [2, 768, 3072], P(None, 'dp', 'head'), may hold values from -0.109375 to 0.109375
- ada_weight: float32 [2, 768, 4608], P(None, 'dp', 'head'), may hold values from -0.4375 to 0.4375
- time_weight: float32 [768, 768], P('dp', 'head'), may hold values from -0.21875 to 0.21875
- io_weight: float32 [2, 768, 20], P(None, 'dp', 'head'), may hold values from -0.6 to 0.6
- qkv_moment: float32 [2, 768, 2304], P(None, 'dp', 'head'), may hold values from -0.0012207031 to 0.0012207031
- out_moment: float32 [2, 768, 768], P(None, 'dp', 'head'), may hold values from -0.0012207031 to 0.0012207031
- up_moment: float32 [2, 768, 3072], P(None, 'dp', 'head'), may hold values from -0.0012207031 to 0.0012207031
- down_moment: float32 [2, 768, 3072], P(None, 'dp', 'head'), may hold values from -0.0012207031 to 0.0012207031
- ada_first: float32 [2, 768, 4608], P(None, 'dp', 'head'), may hold values from -0.00015258789 to 0.00015258789
- ada_second: float32 [2, 768, 4608], P(None, 'dp', 'head'), may hold values from 4.575778e-11 to 1.8303112e-10
- time_first: float32 [768, 768], P('dp', 'head'), may hold values from -0.00015258789 to 0.00015258789
- time_second: float32 [768, 768], P('dp', 'head'), may hold values from 4.575778e-11 to 1.8303112e-10
- io_first: float32 [2, 768, 20], P(None, 'dp', 'head'), may hold values from -0.00015258789 to 0.00015258789
- io_second: float32 [2, 768, 20], P(None, 'dp', 'head'), may hold values from 4.575778e-11 to 1.8303112e-10
Outputs:
- total_loss: float32 [], replicated
- grad_norm: float32 [], replicated
- pooled: float32 [24, 768], P('dp')
- qkv_new: float32 [2, 768, 2304], P(None, 'dp', 'head')
- qkv_moment_new: float32 [2, 768, 2304], P(None, 'dp', 'head')
- out_new: float32 [2, 768, 768], P(None, 'dp', 'head')
- out_moment_new: float32 [2, 768, 768], P(None, 'dp', 'head')
- up_new: float32 [2, 768, 3072], P(None, 'dp', 'head')
- up_moment_new: float32 [2, 768, 3072], P(None, 'dp', 'head')
- down_new: float32 [2, 768, 3072], P(None, 'dp', 'head')
- down_moment_new: float32 [2, 768, 3072], P(None, 'dp', 'head')
- ada_new: float32 [2, 768, 4608], P(None, 'dp', 'head')
- ada_first_new: float32 [2, 768, 4608], P(None, 'dp', 'head')
- ada_second_new: float32 [2, 768, 4608], P(None, 'dp', 'head')
- time_new: float32 [768, 768], P('dp', 'head')
- time_first_new: float32 [768, 768], P('dp', 'head')
- time_second_new: float32 [768, 768], P('dp', 'head')
- io_new: float32 [2, 768, 20], P(None, 'dp', 'head')
- io_first_new: float32 [2, 768, 20], P(None, 'dp', 'head')
- io_second_new: float32 [2, 768, 20], P(None, 'dp', 'head')
The draws below stay inside these ranges and needn't reach their ends.
Inputs may be any that keep to these rules, and one draw needn't show every extreme that they name: `cap_len`: some clip's caption has all 256 tokens. `pairing`: every caption index is named by exactly one clip.
All inputs are finite; a program needn't handle non-finite values.
Results may differ from the reference program's by a relative error of at most 0.0045.
The reference program's roundings to bfloat16 on the way count: a program that leaves them out, or rounds other values in their place, can miss the bound.
Values may be sent and summed in bfloat16 or wider, within the bound.
A program may use at most 384 MiB of HBM per device.

```python
import math
import jax
import jax.numpy as jnp
from jax import lax

D = 768
HEADS = 12
HDIM = 64
FF = 3072
C = 20
LEN = 832
CAP = 256
CLIPS_DEV = 3
NS_STEPS = 5
CLIPS = 24


def draw_cap_len(key, part):
    length_key = jax.random.fold_in(key, 11)
    place_key = jax.random.fold_in(key, 12)
    lengths = jax.random.randint(length_key, (CLIPS,), 5, CAP + 1)
    longest = jax.random.randint(place_key, (), 0, CLIPS)
    return jnp.where(jnp.arange(CLIPS) == longest, CAP, lengths).astype(jnp.int32)


def block_scale(own_key, dims, cuts, low, top_value):
    loudness, own = 1.0, jax.random.fold_in(own_key, 6)
    for position, blocks in cuts:
        heights = jnp.exp(jax.random.uniform(jax.random.fold_in(own, position), (blocks,), jnp.float32, low / len(cuts), top_value / len(cuts)))
        loudness = loudness * jnp.repeat(heights, dims[position] // blocks).reshape([-1 if axis == position else 1 for axis in range(len(dims))])
    return loudness


def centred(rng, extent, deviation, bound, shards=(), kind=jnp.bfloat16):
    level = block_scale(rng, extent, shards, -0.22, 0.18) if shards else 1.0
    array = jax.random.normal(rng, extent, jnp.float32) * deviation * level
    return jnp.minimum(jnp.maximum(array, -bound), bound).astype(kind)


def setup_inputs(seed: int = 0) -> dict:
    key_of = jax.random.split(jax.random.key(seed), 25)
    clean_latents = centred(key_of[0], (CLIPS, LEN, C), 1.0, 6.0, ((0, 8), (1, 4)), jnp.float32)
    noise_draw = centred(key_of[1], (CLIPS, LEN, C), 1.0, 6.0, ((0, 8), (1, 4)), jnp.float32)
    timesteps = jnp.clip(0.02 + 0.96000002 * jax.random.uniform(key_of[2], (CLIPS,), jnp.float32) ** block_scale(key_of[2], (CLIPS,), ((0, 8),), -0.2, 0.2), 0.02, 0.98)
    captions = centred(key_of[3], (CLIPS, CAP, D), 1.0, 6.0, ((0, 8),))
    cap_len = draw_cap_len(jax.random.fold_in(key_of[24], 71), 0)
    pairing = jax.random.permutation(key_of[5], CLIPS).astype(jnp.int32)
    adam_step = jax.random.randint(key_of[6], (1,), 2, 21).astype(jnp.int32)
    qkv_weight = centred(key_of[7], (2, D, 3 * D), D ** -0.5, 0.21875, ((1, 8), (2, 4)), jnp.float32)
    out_weight = centred(key_of[8], (2, D, D), (D // 32) ** -0.5, 1.25, ((1, 8), (2, 4)), jnp.float32)
    up_weight = centred(key_of[9], (2, D, FF), D ** -0.5, 0.21875, ((1, 8), (2, 4)), jnp.float32)
    down_weight = centred(key_of[10], (2, D, FF), FF ** -0.5, 0.109375, ((1, 8), (2, 4)), jnp.float32)
    ada_weight = centred(key_of[11], (2, D, 6 * D), (D // 4) ** -0.5, 0.4375, ((1, 8), (2, 4)), jnp.float32)
    time_weight = centred(key_of[12], (D, D), D ** -0.5, 0.21875, ((0, 8), (1, 4)), jnp.float32)
    io_weight = centred(key_of[13], (2, D, C), 0.1, 0.6, ((1, 8), (2, 4)), jnp.float32)
    qkv_moment = centred(key_of[14], (2, D, 3 * D), ((37 * D * D + 2 * D * C) ** -0.5), 0.0012207031, ((1, 8), (2, 4)), jnp.float32)
    out_moment = centred(key_of[15], (2, D, D), ((37 * D * D + 2 * D * C) ** -0.5), 0.0012207031, ((1, 8), (2, 4)), jnp.float32)
    up_moment = centred(key_of[16], (2, D, FF), ((37 * D * D + 2 * D * C) ** -0.5), 0.0012207031, ((1, 8), (2, 4)), jnp.float32)
    down_moment = centred(key_of[17], (2, D, FF), ((37 * D * D + 2 * D * C) ** -0.5), 0.0012207031, ((1, 8), (2, 4)), jnp.float32)
    ada_first = centred(key_of[18], (2, D, 6 * D), (0.11 * (37 * D * D + 2 * D * C) ** -0.5), 0.00015258789, ((1, 8), (2, 4)), jnp.float32)
    ada_second = jnp.clip(jnp.exp(math.log(1.8303111803952277e-10) - 1.3862944 * jax.random.uniform(key_of[19], (2, D, 6 * D), jnp.float32) ** block_scale(key_of[19], (2, D, 6 * D), ((1, 8), (2, 4)), -0.2, 0.2)), 4.575777950988069e-11, 1.8303111803952277e-10)
    time_first = centred(key_of[20], (D, D), (0.11 * (37 * D * D + 2 * D * C) ** -0.5), 0.00015258789, ((0, 8), (1, 4)), jnp.float32)
    time_second = jnp.clip(jnp.exp(math.log(1.8303111803952277e-10) - 1.3862944 * jax.random.uniform(key_of[21], (D, D), jnp.float32) ** block_scale(key_of[21], (D, D), ((0, 8), (1, 4)), -0.2, 0.2)), 4.575777950988069e-11, 1.8303111803952277e-10)
    io_first = centred(key_of[22], (2, D, C), (0.11 * (37 * D * D + 2 * D * C) ** -0.5), 0.00015258789, ((1, 8), (2, 4)), jnp.float32)
    io_second = jnp.clip(jnp.exp(math.log(1.8303111803952277e-10) - 1.3862944 * jax.random.uniform(key_of[23], (2, D, C), jnp.float32) ** block_scale(key_of[23], (2, D, C), ((1, 8), (2, 4)), -0.2, 0.2)), 4.575777950988069e-11, 1.8303111803952277e-10)
    return {"clean_latents": clean_latents, "noise_draw": noise_draw, "timesteps": timesteps, "captions": captions, "cap_len": cap_len, "pairing": pairing, "adam_step": adam_step, "qkv_weight": qkv_weight, "out_weight": out_weight, "up_weight": up_weight, "down_weight": down_weight, "ada_weight": ada_weight, "time_weight": time_weight, "io_weight": io_weight, "qkv_moment": qkv_moment, "out_moment": out_moment, "up_moment": up_moment, "down_moment": down_moment, "ada_first": ada_first, "ada_second": ada_second, "time_first": time_first, "time_second": time_second, "io_first": io_first, "io_second": io_second}


HIGHEST_PRECISION = lax.Precision.HIGHEST
NEWTON_COEFFS = (3.4445, -4.775, 2.0315)
CLIP_NORM = 1.0
MUON_RATE = 0.2
MUON_DECAY = 0.1
MUON_BETA = 0.95
ADAM_RATE = 0.02
ADAM_DECAY = 0.01
ADAM_FIRST = 0.9
ADAM_SECOND = 0.999

@jax.custom_vjp
def low(v):
    return lax.optimization_barrier(v.astype(jnp.bfloat16)).astype(jnp.float32)

@jax.custom_vjp
def low_back(v):
    return v

def low_keep(v):
    return (low(v), None)

def low_pass(kept, grad):
    return (grad,)

def back_keep(v):
    return (v, None)

def back_low(kept, grad):
    return (low(grad),)
low.defvjp(low_keep, low_pass)
low_back.defvjp(back_keep, back_low)

def sigmoid_unit(values):
    return values * jax.nn.sigmoid(values)

def soft_gelu(values):
    return 0.5 * values * (1.0 + jnp.tanh(0.7978845608 * (values + 0.044715 * values * values * values)))

def norm_rows(values):
    centre = values - lax.optimization_barrier(jnp.mean(values, -1, keepdims=True))
    return centre * lax.rsqrt(lax.optimization_barrier(jnp.mean(centre * centre, -1, keepdims=True)) + 1e-06)

def modulate(hidden, shift, stretch):
    return norm_rows(hidden) * (1.0 + stretch) + shift

def time_table(timesteps, width):
    half_width = width // 2
    frequency = jnp.exp(-math.log(10000.0) * jnp.arange(half_width).astype(timesteps.dtype) / half_width)
    angles = 1000.0 * timesteps[:, None] * frequency[None, :]
    return jnp.concatenate([jnp.cos(angles), jnp.sin(angles)], axis=-1)

def mult(form, left, right):
    return jnp.einsum(form, left, right, precision=HIGHEST_PRECISION)

def attend(pieces):
    query, keys, values, key_mask = pieces
    raw_scores = mult('qhe,khe->hqk', query, keys) * query.shape[-1] ** (-0.5)
    scores = jnp.where(key_mask[None, None, :], low_back(raw_scores), -1e+30)
    row_top = lax.optimization_barrier(jnp.max(scores, -1, keepdims=True))
    exponent = jnp.exp(scores - row_top)
    probability = low(exponent / lax.optimization_barrier(jnp.sum(exponent, -1, keepdims=True)))
    return mult('hqk,khe->qhe', probability, values)

def group_pass(params, clean_latents, noise_draw, timesteps, captions, keep_mask):
    qkv_weight, out_weight, up_weight, down_weight, ada_weight, time_weight, io_weight = params
    clip_count, length, channels = clean_latents.shape
    condition = sigmoid_unit(mult('fd,dn->fn', low(time_table(timesteps, D)), low(time_weight)))
    signal = low(sigmoid_unit(condition))
    blended = (1.0 - timesteps)[:, None, None] * clean_latents + timesteps[:, None, None] * noise_draw
    hidden = low_back(mult('flc,dc->fld', low(blended), low(io_weight[0])))

    def split_heads(values):
        return values.reshape(values.shape[0], values.shape[1], HEADS, HDIM)
    for layer_index in range(2):
        modulation = mult('fd,dn->fn', signal, low(ada_weight[layer_index])).reshape(clip_count, 1, 6, D)
        mod_parts = [modulation[:, :, member] for member in range(6)]
        normed = low(modulate(hidden, mod_parts[0], mod_parts[1]))
        weight = low(qkv_weight[layer_index])
        if layer_index == 0:
            projected = low(low_back(mult('fld,dn->fln', normed, weight)))
            query = projected[..., :D]
            keys = projected[..., D:2 * D]
            values = projected[..., 2 * D:]
            key_mask = jnp.ones((clip_count, length), dtype=bool)
        else:
            query = low(low_back(mult('fld,dn->fln', normed, weight[:, :D])))
            pair_kv = low(low_back(mult('ftd,dn->ftn', captions, weight[:, D:])))
            keys = pair_kv[..., :D]
            values = pair_kv[..., D:]
            key_mask = keep_mask
        mixed = lax.map(jax.checkpoint(attend), (split_heads(query), split_heads(keys), split_heads(values), key_mask))
        mixed = low(low_back(mixed.reshape(clip_count, length, D)))
        branch = low_back(mult('fle,de->fld', mixed, low(out_weight[layer_index])))
        hidden = hidden + mod_parts[2] * branch
        normed = low(modulate(hidden, mod_parts[3], mod_parts[4]))
        upper = low_back(mult('fld,dn->fln', normed, low(up_weight[layer_index])))
        active = low(soft_gelu(upper))
        down_out = low_back(mult('fln,dn->fld', active, low(down_weight[layer_index])))
        hidden = hidden + mod_parts[5] * down_out
    final = norm_rows(hidden)
    predicted = low_back(mult('fld,dc->flc', low(final), low(io_weight[1])))
    errors = predicted - (noise_draw - clean_latents)
    return (jnp.sum(lax.optimization_barrier(jnp.mean(errors * errors, -1))), lax.optimization_barrier(jnp.mean(final, axis=1)))

def forward(params, clean_latents, noise_draw, timesteps, captions, keep_mask, pairing, cap_unit):
    groups = clean_latents.shape[0] // CLIPS_DEV

    def grouped(values):
        return values.reshape((groups, CLIPS_DEV) + values.shape[1:])

    def one_group(pieces):
        return group_pass(params, *pieces)
    flows, pooled = lax.map(jax.checkpoint(one_group), (grouped(clean_latents), grouped(noise_draw), grouped(timesteps), grouped(captions), grouped(keep_mask)))
    pooled = pooled.reshape(CLIPS, D)
    unit_rows = pooled * lax.rsqrt(lax.optimization_barrier(jnp.mean(pooled * pooled, -1, keepdims=True)) + 1e-06)
    logits = mult('id,jd->ij', unit_rows, cap_unit) * (2.0 / math.sqrt(D))
    row_top = lax.optimization_barrier(jnp.max(logits, -1, keepdims=True))
    log_total = row_top[:, 0] + jnp.log(lax.optimization_barrier(jnp.sum(jnp.exp(logits - row_top), -1)))
    picked = lax.optimization_barrier(jnp.sum(jnp.where(jnp.arange(CLIPS)[None, :] == pairing[:, None], logits, 0.0), -1))
    return (jnp.sum(flows) + LEN * jnp.sum(log_total - picked), pooled)

def orthogonal(moment):
    coeff_a, coeff_b, coeff_c = NEWTON_COEFFS
    size_frob = jnp.sqrt(lax.optimization_barrier(jnp.sum(moment * moment, axis=(1, 2), keepdims=True)))
    ortho_rows = moment / (size_frob + 1e-07)
    for ns_step in range(NS_STEPS):
        gram_rows = mult('lrc,lkc->lrk', ortho_rows, ortho_rows)
        poly_rows = coeff_b * gram_rows + coeff_c * mult('lrk,lkj->lrj', gram_rows, gram_rows)
        ortho_rows = coeff_a * ortho_rows + mult('lrk,lkc->lrc', poly_rows, ortho_rows)
    return ortho_rows

def muon_update(weight, grad_part, moment, clip_scale):
    moment = MUON_BETA * moment + clip_scale * grad_part
    stretch = 0.2 * math.sqrt(max(weight.shape[1], weight.shape[2]))
    return (weight * (1.0 - MUON_RATE * MUON_DECAY) - MUON_RATE * stretch * orthogonal(moment), moment)

def adam_update(weight, grad_part, first_moment, second_moment, step_count):
    first_moment = ADAM_FIRST * first_moment + (1.0 - ADAM_FIRST) * grad_part
    second_moment = ADAM_SECOND * second_moment + (1.0 - ADAM_SECOND) * grad_part * grad_part
    first_fix = 1.0 - jnp.power(ADAM_FIRST, step_count)
    second_fix = 1.0 - jnp.power(ADAM_SECOND, step_count)
    direction = first_moment / first_fix / (jnp.sqrt(second_moment / second_fix) + 1e-08)
    return (weight - ADAM_RATE * (direction + ADAM_DECAY * weight), first_moment, second_moment)

def reference(clean_latents, noise_draw, timesteps, captions, cap_len, pairing, adam_step, qkv_weight, out_weight, up_weight, down_weight, ada_weight, time_weight, io_weight, qkv_moment, out_moment, up_moment, down_moment, ada_first, ada_second, time_first, time_second, io_first, io_second):
    keep_mask = jnp.arange(CAP)[None, :] < cap_len[:, None]
    caption_values = captions.astype(jnp.float32)
    cap_mean = lax.optimization_barrier(jnp.sum(jnp.where(keep_mask[:, :, None], caption_values, 0.0), 1)) / cap_len[:, None].astype(jnp.float32)
    cap_unit = cap_mean * lax.rsqrt(lax.optimization_barrier(jnp.mean(cap_mean * cap_mean, -1, keepdims=True)) + 1e-06)
    params = (qkv_weight, out_weight, up_weight, down_weight, ada_weight, time_weight, io_weight)

    def loss_of(weights):
        return forward(weights, clean_latents, noise_draw, timesteps, caption_values, keep_mask, pairing, cap_unit)
    total_loss, backward, pooled = jax.vjp(loss_of, params, has_aux=True)
    grads = backward(jnp.ones_like(total_loss))[0]
    square = sum((jnp.sum(grad_part * grad_part) for grad_part in grads))
    grad_norm = jnp.sqrt(square)
    clip_scale = jnp.minimum(1.0, CLIP_NORM / (grad_norm + 1e-06))
    qkv_new, qkv_moment_new = muon_update(qkv_weight, grads[0], qkv_moment, clip_scale)
    out_new, out_moment_new = muon_update(out_weight, grads[1], out_moment, clip_scale)
    up_new, up_moment_new = muon_update(up_weight, grads[2], up_moment, clip_scale)
    down_new, down_moment_new = muon_update(down_weight, grads[3], down_moment, clip_scale)
    step_count = adam_step[0].astype(jnp.float32)
    ada_new, ada_first_new, ada_second_new = adam_update(ada_weight, clip_scale * grads[4], ada_first, ada_second, step_count)
    time_new, time_first_new, time_second_new = adam_update(time_weight, clip_scale * grads[5], time_first, time_second, step_count)
    io_new, io_first_new, io_second_new = adam_update(io_weight, clip_scale * grads[6], io_first, io_second, step_count)
    return (total_loss, grad_norm, pooled, qkv_new, qkv_moment_new, out_new, out_moment_new, up_new, up_moment_new, down_new, down_moment_new, ada_new, ada_first_new, ada_second_new, time_new, time_first_new, time_second_new, io_new, io_first_new, io_second_new)
```

```python
import math

import jax
import jax.numpy as jnp
from jax import lax
from jax.sharding import PartitionSpec as P

D = 768
HEADS = 12
HDIM = 64
CAP = 256
NS_STEPS = 5


HIGHEST_PRECISION = lax.Precision.HIGHEST
NEWTON_COEFFS = (3.4445, -4.775, 2.0315)
CLIP_NORM = 1.0
MUON_RATE = 0.2
MUON_DECAY = 0.1
MUON_BETA = 0.95
ADAM_RATE = 0.02
ADAM_DECAY = 0.01
ADAM_FIRST = 0.9
ADAM_SECOND = 0.999


def to_bf16(values):
    return values.astype(jnp.bfloat16)


def sigmoid_unit(values):
    return values * jax.nn.sigmoid(values)


def double_silu(values):
    return sigmoid_unit(sigmoid_unit(values))


def soft_gelu(values):
    return (
        0.5
        * values
        * (1.0 + jnp.tanh(0.7978845608 * (values + 0.044715 * values * values * values)))
    )


def norm_rows(values):
    centre = values - jnp.mean(values, -1, keepdims=True)
    return centre * lax.rsqrt(jnp.mean(centre * centre, -1, keepdims=True) + 1e-06)


def modulate(hidden, shift, stretch):
    return norm_rows(hidden) * (1.0 + stretch) + shift


def time_table(timesteps, width):
    half_width = width // 2
    frequency = jnp.exp(
        -math.log(10000.0) * jnp.arange(half_width).astype(timesteps.dtype) / half_width
    )
    angles = 1000.0 * timesteps[:, None] * frequency[None, :]
    return jnp.concatenate([jnp.cos(angles), jnp.sin(angles)], axis=-1)


def product(form, left, right):
    return jnp.einsum(form, left, right, preferred_element_type=jnp.float32)


def exact_product(form, left, right):
    return jnp.einsum(form, left, right, precision=HIGHEST_PRECISION)


def to_heads(frames):
    return lax.all_to_all(frames, "head", split_axis=3, concat_axis=1, tiled=True)


def to_frames(heads):
    return lax.all_to_all(heads, "head", split_axis=1, concat_axis=3, tiled=True)


def scores_of(query, keys, key_mask):
    raw_scores = product("qhe,khe->hqk", query, keys) * query.shape[-1] ** (-0.5)
    return jnp.where(key_mask[None, None, :], raw_scores, -1e30)


def attend_forward(pieces):
    query, keys, values, key_mask = pieces
    scores = scores_of(query, keys, key_mask)
    row_top = jnp.max(scores, -1, keepdims=True)
    exponent = jnp.exp(scores - row_top)
    row_total = jnp.sum(exponent, -1, keepdims=True)
    probability = to_bf16(exponent / row_total)
    mixed = product("hqk,khe->qhe", probability, values)
    return (to_bf16(mixed), row_top + jnp.log(row_total))


def attend_backward(pieces):
    query, keys, values, key_mask, log_total, grad_mixed = pieces
    scores = scores_of(query, keys, key_mask)
    probability = jnp.exp(scores - log_total)
    grad_prob = product("qhe,khe->hqk", grad_mixed, values)
    grad_scores = to_bf16(
        probability * (grad_prob - jnp.sum(probability * grad_prob, -1, keepdims=True))
    )
    factor = query.shape[-1] ** (-0.5)
    grad_query = product("hqk,khe->qhe", grad_scores, keys) * factor
    grad_keys = product("hqk,qhe->khe", grad_scores, query) * factor
    grad_values = product("hqk,qhe->khe", to_bf16(probability), grad_mixed)
    return (to_bf16(grad_query), to_bf16(grad_keys), to_bf16(grad_values))


def adam_update(weight, grad_part, first_moment, second_moment, step_count):
    first_moment = ADAM_FIRST * first_moment + (1.0 - ADAM_FIRST) * grad_part
    second_moment = ADAM_SECOND * second_moment + (1.0 - ADAM_SECOND) * grad_part * grad_part
    first_fix = 1.0 - jnp.power(ADAM_FIRST, step_count)
    second_fix = 1.0 - jnp.power(ADAM_SECOND, step_count)
    direction = first_moment / first_fix / (jnp.sqrt(second_moment / second_fix) + 1e-08)
    return (weight - ADAM_RATE * (direction + ADAM_DECAY * weight), first_moment, second_moment)


def body(
    clean_latents,
    noise_draw,
    timesteps,
    captions,
    cap_len,
    pairing,
    adam_step,
    qkv_weight,
    out_weight,
    up_weight,
    down_weight,
    ada_weight,
    time_weight,
    io_weight,
    qkv_moment,
    out_moment,
    up_moment,
    down_moment,
    ada_first,
    ada_second,
    time_first,
    time_second,
    io_first,
    io_second,
):
    data_count = lax.axis_size("dp")
    head_count = lax.axis_size("head")
    clip_count = clean_latents.shape[0]
    frame_rows = clean_latents.shape[1]
    length = frame_rows * head_count
    head_share = D // head_count
    local_heads = head_share // HDIM
    rows_own = qkv_weight.shape[1]
    own_row = lax.axis_index("dp") * rows_own

    def whole_weight(shard):
        layers, rows, cols = shard.shape
        blocks = lax.all_gather(to_bf16(shard), ("head", "dp"), axis=0, tiled=False)
        blocks = blocks.reshape(head_count, data_count, layers, rows, cols)
        return blocks.transpose(2, 1, 3, 0, 4).reshape(layers, D, head_count * cols)

    small = jnp.concatenate(
        [time_weight.reshape(-1), io_weight.reshape(-1), jnp.pad(timesteps, (0, 125))]
    )
    small_all = lax.all_gather(small, ("dp", "head"), axis=0, tiled=False)
    small_all = small_all.reshape(data_count, head_count, -1)
    time_size = time_weight.size
    io_size = io_weight.size
    time_full = to_bf16(
        small_all[:, :, :time_size]
        .reshape(data_count, head_count, rows_own, -1)
        .transpose(0, 2, 1, 3)
        .reshape(D, D)
    )
    io_full = to_bf16(
        small_all[:, :, time_size : time_size + io_size]
        .reshape(data_count, head_count, 2, rows_own, -1)
        .transpose(2, 0, 3, 1, 4)
        .reshape(2, D, -1)
    )
    times_all = small_all[:, 0, time_size + io_size : time_size + io_size + clip_count].reshape(-1)
    gathered = (
        [whole_weight(qkv_weight[layer : layer + 1])[0] for layer in range(2)],
        [whole_weight(out_weight[layer : layer + 1])[0] for layer in range(2)],
    )
    qkv_full, out_full = gathered
    up_full, down_full = [None, None], [None, None]
    for layer in range(2):
        pair = whole_weight(jnp.stack([up_weight[layer], down_weight[layer]]))
        up_full[layer], down_full[layer] = pair[0], pair[1]
    keep_mask = jnp.arange(CAP)[None, :] < cap_len[:, None]
    cap_mean = product("ft,ftd->fd", keep_mask.astype(jnp.bfloat16), captions) / cap_len[
        :, None
    ].astype(jnp.float32)
    cap_unit = cap_mean * lax.rsqrt(jnp.mean(cap_mean * cap_mean, -1, keepdims=True) + 1e-06)
    cap_all = lax.all_gather(cap_unit, "dp", axis=0, tiled=True)
    table_bf = to_bf16(time_table(times_all, D))
    time_hidden = jnp.dot(table_bf, time_full, preferred_element_type=jnp.float32)
    signal_bf = to_bf16(double_silu(time_hidden))
    signal_own = lax.dynamic_slice_in_dim(signal_bf, own_row, rows_own, 1)
    table_own = lax.dynamic_slice_in_dim(table_bf, own_row, rows_own, 1)
    ada_bf = to_bf16(ada_weight)
    mod_part = product("fd,ldn->fln", signal_own, ada_bf)
    mod_own = lax.psum_scatter(mod_part, "dp", scatter_dimension=0, tiled=True)
    mod_all = lax.all_gather(mod_own, "head", axis=2, tiled=True)
    blended = (1.0 - timesteps)[:, None, None] * clean_latents + timesteps[
        :, None, None
    ] * noise_draw
    input_bf = to_bf16(blended)
    hidden = product("flc,dc->fld", input_bf, io_full[0])

    def split_heads(values, rows_count):
        return values.reshape(clip_count, rows_count, local_heads, HDIM)

    def layer_forward(layer_index, hidden):
        modulation = mod_all[:, layer_index].reshape(clip_count, 1, 6, D)
        mod_parts = [modulation[:, :, member] for member in range(6)]
        normed = to_bf16(modulate(hidden, mod_parts[0], mod_parts[1]))
        weight = qkv_full[layer_index]
        in_frames = layer_index == 1
        if layer_index == 0:
            projected = to_bf16(product("fld,dn->fln", normed, weight))
            head_rows = to_heads(projected.reshape(clip_count, frame_rows, 3, D))
            query = split_heads(head_rows[:, :, 0], length)
            keys = split_heads(head_rows[:, :, 1], length)
            values = split_heads(head_rows[:, :, 2], length)
            key_mask = jnp.ones((clip_count, length), dtype=bool)
        else:
            projected = to_bf16(product("fld,dn->fln", normed, weight[:, :D]))
            query = projected.reshape(clip_count, frame_rows, HEADS, HDIM)
            pair_kv = to_bf16(product("ftd,dn->ftn", captions, weight[:, D:]))
            keys = pair_kv[..., :D].reshape(clip_count, CAP, HEADS, HDIM)
            values = pair_kv[..., D:].reshape(clip_count, CAP, HEADS, HDIM)
            key_mask = keep_mask
        mixed, log_total = lax.map(attend_forward, (query, keys, values, key_mask))
        if in_frames:
            mixed_frames = mixed.reshape(clip_count, frame_rows, D)
        else:
            mixed_frames = to_frames(mixed.reshape(clip_count, length, 1, head_share)).reshape(
                clip_count, frame_rows, D
            )
        branch = product("fle,de->fld", mixed_frames, out_full[layer_index])
        middle = hidden + mod_parts[2] * branch
        normed2 = to_bf16(modulate(middle, mod_parts[3], mod_parts[4]))
        upper = product("fld,dn->fln", normed2, up_full[layer_index])
        active = to_bf16(soft_gelu(upper))
        down_out = product("fln,dn->fld", active, down_full[layer_index])
        kept = (
            hidden,
            mod_parts,
            normed,
            query,
            keys,
            values,
            key_mask,
            log_total,
            mixed_frames,
            branch,
            middle,
            normed2,
            upper,
            active,
            down_out,
        )
        return (middle + mod_parts[5] * down_out, kept)

    saved_layers = []
    for layer_index in range(2):
        hidden, kept = layer_forward(layer_index, hidden)
        saved_layers.append(kept)
    final = norm_rows(hidden)
    final_bf = to_bf16(final)
    predicted = product("fld,dc->flc", final_bf, io_full[1])
    errors = predicted - (noise_draw - clean_latents)
    flow_part = jnp.sum(jnp.mean(errors * errors, -1))
    grad_pred = to_bf16(2.0 * errors / errors.shape[-1])
    pool_sum = lax.psum(jnp.sum(final, 1), "head")
    pooled_out = pool_sum / length

    def contrast_of(pool_total):
        pooled = pool_total / length
        unit_rows = pooled * lax.rsqrt(jnp.mean(pooled * pooled, -1, keepdims=True) + 1e-06)
        logits = exact_product("id,jd->ij", unit_rows, cap_all) * (2.0 / math.sqrt(D))
        row_top = jnp.max(logits, -1, keepdims=True)
        log_total = row_top[:, 0] + jnp.log(jnp.sum(jnp.exp(logits - row_top), -1))
        picked = jnp.sum(
            jnp.where(jnp.arange(logits.shape[1])[None, :] == pairing[:, None], logits, 0.0), -1
        )
        return length * jnp.sum(log_total - picked)

    contrast_value, contrast_back = jax.vjp(contrast_of, pool_sum)
    grad_pool = contrast_back(jnp.ones_like(contrast_value))[0]
    loss_part = flow_part + contrast_value / head_count
    grad_final = product("flc,dc->fld", grad_pred, io_full[1]) + grad_pool[:, None, :]
    final_value, final_back = jax.vjp(norm_rows, hidden)
    grad_hidden = final_back(grad_final)[0]
    fin_grad = product("flc,fld->dc", grad_pred, final_bf)
    layer_grads = [None, None]
    ada_grads = [None, None]
    for layer_index in (1, 0):
        layer_kept = saved_layers[layer_index]
        (
            layer_hidden,
            layer_mod_parts,
            layer_normed,
            layer_query,
            layer_keys,
            layer_values,
            layer_key_mask,
            layer_log_total,
            layer_mixed_frames,
            layer_branch,
            layer_middle,
            layer_normed2,
            layer_upper,
            layer_active,
            layer_down_out,
        ) = layer_kept
        layer_in_frames = layer_index == 1
        d_gate2 = jnp.sum(layer_down_out * grad_hidden, axis=1, keepdims=True)
        grad_down = to_bf16(layer_mod_parts[5] * grad_hidden)
        grad_active = product("fld,dn->fln", grad_down, down_full[layer_index])
        gelu_value, gelu_back = jax.vjp(soft_gelu, layer_upper)
        grad_upper = to_bf16(gelu_back(grad_active)[0])
        down_grad = product("fld,fln->dn", grad_down, layer_active)
        up_grad = product("fld,fln->dn", layer_normed2, grad_upper)
        grad_normed2 = product("fln,dn->fld", grad_upper, up_full[layer_index])
        mod_value, mod_back = jax.vjp(
            modulate, layer_middle, layer_mod_parts[3], layer_mod_parts[4]
        )
        grad_middle, d_shift2, d_scale2 = mod_back(grad_normed2)
        grad_middle = grad_middle + grad_hidden
        d_gate1 = jnp.sum(layer_branch * grad_middle, axis=1, keepdims=True)
        grad_branch = to_bf16(layer_mod_parts[2] * grad_middle)
        out_grad = product("fld,fle->de", grad_branch, layer_mixed_frames)
        grad_mixed = to_bf16(product("fld,de->fle", grad_branch, out_full[layer_index]))
        if layer_in_frames:
            grad_heads = grad_mixed.reshape(clip_count, frame_rows, HEADS, HDIM)
        else:
            grad_heads = split_heads(
                to_heads(grad_mixed.reshape(clip_count, frame_rows, 1, D))[:, :, 0], length
            )
        grad_query, grad_keys, grad_values = lax.map(
            attend_backward,
            (layer_query, layer_keys, layer_values, layer_key_mask, layer_log_total, grad_heads),
        )
        layer_weight = qkv_full[layer_index]
        if layer_index == 0:
            stacked = jnp.stack([grad_query, grad_keys, grad_values], 2).reshape(
                clip_count, length, 3, head_share
            )
            grad_proj = to_frames(stacked).reshape(clip_count, frame_rows, 3 * D)
            qkv_grad = product("fld,fln->dn", layer_normed, grad_proj)
            grad_normed = product("fln,dn->fld", grad_proj, layer_weight)
        else:
            grad_proj = grad_query.reshape(clip_count, frame_rows, D)
            query_grad = product("fld,fln->dn", layer_normed, grad_proj)
            key_grad = product("ftd,ftn->dn", captions, grad_keys.reshape(clip_count, CAP, D))
            value_grad = product("ftd,ftn->dn", captions, grad_values.reshape(clip_count, CAP, D))
            qkv_grad = jnp.concatenate([query_grad, key_grad, value_grad], 1)
            grad_normed = product("fln,dn->fld", grad_proj, layer_weight[:, :D])
        first_value, first_back = jax.vjp(
            modulate, layer_hidden, layer_mod_parts[0], layer_mod_parts[1]
        )
        grad_in, d_shift1, d_scale1 = first_back(grad_normed)
        d_mod = jnp.concatenate([d_shift1, d_scale1, d_gate1, d_shift2, d_scale2, d_gate2], -1)[
            :, 0
        ]
        grad_hidden, layer_grads[layer_index], d_mod = (
            grad_in + grad_middle,
            (qkv_grad, out_grad, up_grad, down_grad),
            d_mod,
        )
        ada_grads[layer_index] = d_mod
    in_grad = product("fld,flc->dc", to_bf16(grad_hidden), input_bf)
    d_mod_own = lax.psum_scatter(
        jnp.stack(ada_grads, 1), "head", scatter_dimension=2, tiled=True
    )
    d_mod_all = lax.all_gather(d_mod_own, "dp", axis=0, tiled=True)
    ada_grad = exact_product("fd,fln->ldn", signal_own.astype(jnp.float32), d_mod_all)
    grad_signal = lax.psum(
        exact_product("fln,ldn->fd", d_mod_all, ada_bf.astype(jnp.float32)), "head"
    )
    hidden_own = lax.dynamic_slice_in_dim(time_hidden, own_row, rows_own, 1)
    signal_own_value, signal_back = jax.vjp(double_silu, hidden_own)
    grad_cond = lax.all_gather(signal_back(grad_signal)[0], "dp", axis=1, tiled=True)
    time_cols = time_weight.shape[1]
    time_grad = exact_product(
        "fd,fn->dn",
        table_own.astype(jnp.float32),
        lax.dynamic_slice_in_dim(grad_cond, lax.axis_index("head") * time_cols, time_cols, 1),
    )

    def scatter(parts):
        stacked = jnp.stack(parts)
        layers, rows_all, cols_all = stacked.shape
        blocks = stacked.reshape(
            layers, data_count, rows_all // data_count, head_count, cols_all // head_count
        ).transpose(3, 1, 0, 2, 4)
        blocks = blocks.reshape((head_count * data_count,) + blocks.shape[2:])
        return lax.psum_scatter(blocks, ("head", "dp"), scatter_dimension=0, tiled=True)[0]

    per_layer = [
        (
            scatter([layer_grads[layer][0]])[0],
            scatter([layer_grads[layer][1]])[0],
            scatter([layer_grads[layer][2], layer_grads[layer][3]]),
        )
        for layer in range(2)
    ]
    shards = (
        jnp.stack([per_layer[0][0], per_layer[1][0]]),
        jnp.stack([per_layer[0][1], per_layer[1][1]]),
        jnp.stack([per_layer[0][2][0], per_layer[1][2][0]]),
        jnp.stack([per_layer[0][2][1], per_layer[1][2][1]]),
        ada_grad,
        time_grad[None],
        scatter([in_grad, fin_grad]),
    )
    square = sum((jnp.sum(shard * shard) for shard in shards))
    old_moments = (qkv_moment, out_moment, up_moment, down_moment)
    total_square, total_loss = lax.psum((square, loss_part), ("dp", "head"))
    grad_norm = jnp.sqrt(total_square)
    clip_scale = jnp.minimum(1.0, CLIP_NORM / (grad_norm + 1e-06))
    moments = tuple(
        (MUON_BETA * old_moments[member] + clip_scale * shards[member] for member in range(4))
    )
    coeff_a, coeff_b, coeff_c = NEWTON_COEFFS
    wide = max(moment.shape[2] for moment in moments)
    sent = jnp.concatenate(
        [jnp.pad(moment, ((0, 0), (0, 0), (0, wide - moment.shape[2]))) for moment in moments]
    )
    matrices = sent.shape[0]
    sent = jnp.pad(sent, ((0, data_count - matrices), (0, 0), (0, 0)))
    own_matrix = lax.all_to_all(sent, "dp", split_axis=0, concat_axis=0, tiled=True)
    own_matrix = own_matrix.reshape(D, wide)

    def near_product(form, left, right):
        return jnp.einsum(form, left, right, precision=lax.Precision.HIGH)

    gram = lax.psum(near_product("rc,kc->rk", own_matrix, own_matrix), "head")
    unit = jnp.eye(D, dtype=jnp.float32)
    size_frob = jnp.sqrt(jnp.sum(gram * unit)) + 1e-07
    gram = gram / (size_frob * size_frob)
    factor = None
    for ns_step in range(NS_STEPS):
        poly = coeff_a * unit + coeff_b * gram + coeff_c * near_product("rk,kj->rj", gram, gram)
        factor = poly if factor is None else near_product("rk,kj->rj", poly, factor)
        if ns_step < NS_STEPS - 1:
            gram = near_product("rk,kj->rj", near_product("rk,kj->rj", poly, gram), poly)
    ortho_matrix = near_product("rk,kc->rc", factor, own_matrix) / size_frob
    ortho_back = lax.all_to_all(
        ortho_matrix.reshape(data_count, rows_own, wide),
        "dp",
        split_axis=0,
        concat_axis=0,
        tiled=True,
    )
    ortho_rows = tuple(
        (
            ortho_back[2 * member : 2 * member + 2, :, : moments[member].shape[2]]
            for member in range(4)
        )
    )
    muon_weights = (qkv_weight, out_weight, up_weight, down_weight)
    muon_new = tuple(
        (
            muon_weights[member] * (1.0 - MUON_RATE * MUON_DECAY)
            - MUON_RATE
            * 0.2
            * math.sqrt(max(D, muon_weights[member].shape[2] * head_count))
            * ortho_rows[member]
            for member in range(4)
        )
    )
    step_count = adam_step[0].astype(jnp.float32)
    ada_new, ada_first_new, ada_second_new = adam_update(
        ada_weight, clip_scale * shards[4], ada_first, ada_second, step_count
    )
    time_new, time_first_new, time_second_new = adam_update(
        time_weight, clip_scale * shards[5][0], time_first, time_second, step_count
    )
    io_new, io_first_new, io_second_new = adam_update(
        io_weight, clip_scale * shards[6], io_first, io_second, step_count
    )
    return (
        total_loss,
        grad_norm,
        pooled_out,
        muon_new[0],
        moments[0],
        muon_new[1],
        moments[1],
        muon_new[2],
        moments[2],
        muon_new[3],
        moments[3],
        ada_new,
        ada_first_new,
        ada_second_new,
        time_new,
        time_first_new,
        time_second_new,
        io_new,
        io_first_new,
        io_second_new,
    )


def solution(mesh):
    placed = (
        P("dp", "head", None),
        P("dp", "head", None),
        P("dp"),
        P("dp", None, None),
        P("dp"),
        P("dp"),
        P(),
        P(None, "dp", "head"),
        P(None, "dp", "head"),
        P(None, "dp", "head"),
        P(None, "dp", "head"),
        P(None, "dp", "head"),
        P("dp", "head"),
        P(None, "dp", "head"),
        P(None, "dp", "head"),
        P(None, "dp", "head"),
        P(None, "dp", "head"),
        P(None, "dp", "head"),
        P(None, "dp", "head"),
        P(None, "dp", "head"),
        P("dp", "head"),
        P("dp", "head"),
        P(None, "dp", "head"),
        P(None, "dp", "head"),
    )
    return jax.shard_map(
        body,
        mesh=mesh,
        in_specs=placed,
        out_specs=(
            P(),
            P(),
            P("dp", None),
            P(None, "dp", "head"),
            P(None, "dp", "head"),
            P(None, "dp", "head"),
            P(None, "dp", "head"),
            P(None, "dp", "head"),
            P(None, "dp", "head"),
            P(None, "dp", "head"),
            P(None, "dp", "head"),
            P(None, "dp", "head"),
            P(None, "dp", "head"),
            P(None, "dp", "head"),
            P("dp", "head"),
            P("dp", "head"),
            P("dp", "head"),
            P(None, "dp", "head"),
            P(None, "dp", "head"),
            P(None, "dp", "head"),
        ),
        check_vma=False,
    )
```

```python
import functools
import math

import jax
import jax.numpy as jnp
from jax import lax
from jax.experimental import pallas as pl
from jax.experimental.pallas import tpu as pltpu
from jax.sharding import PartitionSpec as P

D = 768
HEADS = 12
HDIM = 64
CAP = 256
NS_STEPS = 5


HIGHEST_PRECISION = lax.Precision.HIGHEST
NEWTON_COEFFS = (3.4445, -4.775, 2.0315)
CLIP_NORM = 1.0
MUON_RATE = 0.2
MUON_DECAY = 0.1
MUON_BETA = 0.95
ADAM_RATE = 0.02
ADAM_DECAY = 0.01
ADAM_FIRST = 0.9
ADAM_SECOND = 0.999


def to_bf16(values):
    return values.astype(jnp.bfloat16)


def sigmoid_unit(values):
    return values * jax.nn.sigmoid(values)


def double_silu(values):
    return sigmoid_unit(sigmoid_unit(values))


def soft_gelu(values):
    return (
        0.5
        * values
        * (1.0 + jnp.tanh(0.7978845608 * (values + 0.044715 * values * values * values)))
    )


def norm_rows(values):
    centre = values - jnp.mean(values, -1, keepdims=True)
    return centre * lax.rsqrt(jnp.mean(centre * centre, -1, keepdims=True) + 1e-06)


def modulate(hidden, shift, stretch):
    return norm_rows(hidden) * (1.0 + stretch) + shift


def time_table(timesteps, width):
    half_width = width // 2
    frequency = jnp.exp(
        -math.log(10000.0) * jnp.arange(half_width).astype(timesteps.dtype) / half_width
    )
    angles = 1000.0 * timesteps[:, None] * frequency[None, :]
    return jnp.concatenate([jnp.cos(angles), jnp.sin(angles)], axis=-1)


def product(form, left, right):
    return jnp.einsum(form, left, right, preferred_element_type=jnp.float32)


def exact_product(form, left, right):
    return jnp.einsum(form, left, right, precision=HIGHEST_PRECISION)


def adam_update(weight, grad_part, first_moment, second_moment, step_count):
    first_moment = ADAM_FIRST * first_moment + (1.0 - ADAM_FIRST) * grad_part
    second_moment = ADAM_SECOND * second_moment + (1.0 - ADAM_SECOND) * grad_part * grad_part
    first_fix = 1.0 - jnp.power(ADAM_FIRST, step_count)
    second_fix = 1.0 - jnp.power(ADAM_SECOND, step_count)
    direction = first_moment / first_fix / (jnp.sqrt(second_moment / second_fix) + 1e-08)
    return (weight - ADAM_RATE * (direction + ADAM_DECAY * weight), first_moment, second_moment)


MESH = pl.DeviceIdType.MESH
ROWS_A = 64
PIECE_COLS = 256
SLOTS = 4
HALF = 384
WIDE = 256
VMEM_BYTES = 56 * 1024 * 1024


def vmem():
    return pl.BlockSpec(memory_space=pltpu.VMEM)


def anywhere():
    return pl.BlockSpec(memory_space=pl.ANY)


def comm_params(collective_id):
    return pltpu.CompilerParams(
        collective_id=collective_id, has_side_effects=True, vmem_limit_bytes=VMEM_BYTES
    )


def greet(peers):
    barrier = pltpu.get_barrier_semaphore()
    for peer in peers:
        pl.semaphore_signal(barrier, inc=1, device_id=peer, device_id_type=MESH)
    pl.semaphore_wait(barrier, len(peers))


def exchange_kernel(axis, count, swapped, x_ref, out_ref, send_sem, recv_sem):
    me = lax.axis_index(axis)
    peers = [lax.rem(me + shift, count) for shift in range(1, count)]
    greet([{axis: peer} for peer in peers])
    copies = []
    for place, peer in enumerate(peers):
        copy = pltpu.make_async_remote_copy(
            src_ref=x_ref.at[peer] if swapped else x_ref,
            dst_ref=out_ref.at[me],
            send_sem=send_sem.at[place],
            recv_sem=recv_sem.at[place],
            device_id={axis: peer},
            device_id_type=MESH,
        )
        copy.start()
        copies.append(copy)
    out_ref[me] = x_ref[me] if swapped else x_ref[...]
    for copy in copies:
        copy.wait()


def exchange(x, axis, swapped, collective_id):
    count = lax.axis_size(axis)
    block = x.shape[1:] if swapped else x.shape
    return pl.pallas_call(
        functools.partial(exchange_kernel, axis, count, swapped),
        out_shape=jax.ShapeDtypeStruct((count,) + block, x.dtype),
        in_specs=[vmem()],
        out_specs=vmem(),
        scratch_shapes=[
            pltpu.SemaphoreType.DMA((count - 1,)),
            pltpu.SemaphoreType.DMA((count - 1,)),
        ],
        compiler_params=comm_params(collective_id),
        name="swap" if swapped else "spread",
    )(x)


def link_peers(d, h):
    return {
        "core": (d, h ^ 1),
        "y": (d, h ^ 2),
        "x": (d ^ 1, h),
        "zl": (d ^ 2, h),
        "zh": (d ^ 4, h),
    }


def gather_kernel(groups, *refs):
    own_refs, out_refs = refs[:groups], refs[groups : 2 * groups]
    send_sem, recv_sem, core_send, core_recv, local_sem = refs[2 * groups :]
    d = lax.axis_index("dp")
    h = lax.axis_index("head")
    peers = link_peers(d, h)
    greet(list(peers.values()))
    y, c = h // 2, h % 2
    zh, zl, x = d // 4, (d // 2) % 2, d % 2
    every = slice(None)
    pieces = [
        (group, start)
        for group in range(groups)
        for start in range(0, own_refs[group].shape[1], PIECE_COLS)
    ]
    order_a = (("zh", (zh, zl, x)), ("zl", (every, zl, x)), ("x", (every, every, x)),
               ("y", (every, every, every)))
    order_b = (("y", (zh, zl, x)), ("zh", (zh, zl, x)), ("zl", (every, zl, x)),
               ("x", (every, every, x)))

    def columns_of(piece, head):
        group, start = pieces[piece]
        width = own_refs[group].shape[1]
        return pl.ds(pl.multiple_of(head * width + start, 128), PIECE_COLS)

    def own_copy(piece):
        group, start = pieces[piece]
        return pltpu.make_async_copy(
            own_refs[group].at[:, pl.ds(start, PIECE_COLS)],
            out_refs[group].at[zh, zl, x, :, columns_of(piece, h)],
            local_sem.at[piece],
        )

    def hop(piece, step, stream):
        group, start = pieces[piece]
        rows_all = own_refs[group].shape[0]
        rows = pl.ds(0, ROWS_A) if stream == 0 else pl.ds(ROWS_A, rows_all - ROWS_A)
        head = h if stream < 2 else h ^ 2
        peer, index = (order_a if stream == 0 else order_b)[step]
        view = out_refs[group].at[index + (rows, columns_of(piece, head))]
        source = view
        if step == 0:
            source = own_refs[group].at[rows, pl.ds(start, PIECE_COLS)]
        return pltpu.make_async_remote_copy(
            src_ref=source,
            dst_ref=view,
            send_sem=send_sem.at[piece, step, stream],
            recv_sem=recv_sem.at[piece, step, stream],
            device_id=peers[peer],
            device_id_type=MESH,
        )

    def streams(step):
        return range(2) if step == 0 else range(3)

    def across(piece, side):
        group, start = pieces[piece]
        view = out_refs[group].at[:, :, :, :, columns_of(piece, h ^ (2 * side))]
        return pltpu.make_async_remote_copy(
            src_ref=view,
            dst_ref=view,
            send_sem=core_send.at[piece, side],
            recv_sem=core_recv.at[piece, side],
            device_id=peers["core"],
            device_id_type=MESH,
        )

    for piece in range(len(pieces)):
        own_copy(piece).start()
    for turn in range(len(pieces) + 4):
        for step in range(5):
            piece = turn - step
            if not 0 <= piece < len(pieces):
                continue
            if step == 1:
                own_copy(piece).wait()
            if step >= 1:
                for stream in streams(step - 1):
                    hop(piece, step - 1, stream).wait_recv()
            if step < 4:
                for stream in streams(step):
                    hop(piece, step, stream).start()
            else:
                for side in range(2):
                    across(piece, side).start()
    for piece in range(len(pieces)):
        for step in range(4):
            for stream in streams(step):
                hop(piece, step, stream).wait_send()
        for side in range(2):
            across(piece, side).wait()


def gather_whole(owns, collective_id):
    groups = len(owns)
    pieces = sum(own.shape[1] // PIECE_COLS for own in owns)
    wholes = pl.pallas_call(
        functools.partial(gather_kernel, groups),
        out_shape=[
            jax.ShapeDtypeStruct((2, 2, 2, own.shape[0], 4 * own.shape[1]), own.dtype)
            for own in owns
        ],
        in_specs=[anywhere()] * groups,
        out_specs=[anywhere()] * groups,
        scratch_shapes=[
            pltpu.SemaphoreType.DMA((pieces, 4, 3)),
            pltpu.SemaphoreType.DMA((pieces, 4, 3)),
            pltpu.SemaphoreType.DMA((pieces, 2)),
            pltpu.SemaphoreType.DMA((pieces, 2)),
            pltpu.SemaphoreType.DMA((pieces,)),
        ],
        compiler_params=pltpu.CompilerParams(collective_id=collective_id, has_side_effects=True),
        name="gather_weights",
    )(*owns)
    return [whole.reshape(8 * own.shape[0], -1) for whole, own in zip(wholes, owns)]


def gather_general(own):
    rows, columns = own.shape
    blocks = lax.all_gather(own, ("dp", "head"), axis=0, tiled=False)
    blocks = blocks.reshape(-1, lax.axis_size("head"), rows, columns)
    return blocks.transpose(0, 2, 1, 3).reshape(-1, lax.axis_size("head") * columns)


def reduce_kernel(groups, pieces, *refs):
    part_refs = refs[:groups]
    out_ref = refs[groups]
    (own, near, send_a, send_b, got_a, got_b, keep_a, keep_b, own_sem, near_send, near_recv,
     hop_send, hop_recv) = refs[groups + 1 :]
    per_group = 768 // PIECE_COLS
    d = lax.axis_index("dp")
    h = lax.axis_index("head")
    peers = link_peers(d, h)
    greet(list(peers.values()))
    y, c = h // 2, h % 2
    zh, zl, x = d // 4, (d // 2) % 2, d % 2
    order = (("y", "x"), ("x", "zl"), ("zl", "zh"), ("zh", "y"))
    bottom_rows = own.shape[-2] - ROWS_A
    top, bottom = pl.ds(0, ROWS_A), pl.ds(ROWS_A, bottom_rows)
    every = slice(None)

    def columns_of(piece, group, head):
        width = part_refs[group].shape[-1] // 4
        start = head * width + (piece % per_group) * PIECE_COLS
        return pl.ds(pl.multiple_of(start, PIECE_COLS), PIECE_COLS)

    def own_copy(piece, group, side):
        return pltpu.make_async_copy(
            part_refs[group].at[:, :, :, :, columns_of(piece, group, 2 * side + c)],
            own.at[piece % SLOTS, side],
            own_sem.at[piece % SLOTS, side],
        )

    def near_copy(piece, group, side):
        return pltpu.make_async_remote_copy(
            src_ref=part_refs[group].at[:, :, :, :, columns_of(piece, group, 2 * side + 1 - c)],
            dst_ref=near.at[piece % SLOTS, side],
            send_sem=near_send.at[piece % SLOTS, side],
            recv_sem=near_recv.at[piece % SLOTS, side],
            device_id=peers["core"],
            device_id_type=MESH,
        )

    def bring(piece):
        for group in range(groups):

            @pl.when(piece // per_group == group)
            def _():
                for side in range(2):
                    near_copy(piece, group, side).start()
                    own_copy(piece, group, side).start()

    def hop(piece, step, stream):
        slot = piece % SLOTS
        sent, got = (send_a, got_a) if stream == 0 else (send_b, got_b)
        return pltpu.make_async_remote_copy(
            src_ref=sent[step].at[slot],
            dst_ref=got[step].at[slot],
            send_sem=hop_send.at[step, stream, slot],
            recv_sem=hop_recv.at[step, stream, slot],
            device_id=peers[order[step][stream]],
            device_id_type=MESH,
        )

    def first(piece):
        slot = piece % SLOTS
        for side in range(2):
            near_copy(piece, 0, side).wait()
            own_copy(piece, 0, side).wait()

        def total(*index):
            return own[(slot,) + index] + near[(slot,) + index]

        send_a[0][slot] = to_bf16(total(1 - y, every, every, every, top))
        hop(piece, 0, 0).start()
        send_b[0][slot] = to_bf16(total(every, every, every, 1 - x, bottom))
        hop(piece, 0, 1).start()
        keep_a[0][slot] = total(y, every, every, every, top)
        keep_b[0][slot] = total(every, every, every, x, bottom)

    cut_a = (None, (2, x), (1, zl), (0, zh))
    cut_b = (None, (2, zl), (1, zh), (0, y))

    def later(piece, step):
        slot = piece % SLOTS
        for stream in range(2):
            keep, got, sent = (keep_a, got_a, send_a) if stream == 0 else (keep_b, got_b, send_b)
            axis, mine = (cut_a if stream == 0 else cut_b)[step]
            hop(piece, step - 1, stream).wait()

            def total(which):
                index = (slot,) + (every,) * axis + (which,)
                return keep[step - 1][index] + got[step - 1][index].astype(jnp.float32)

            sent[step][slot] = to_bf16(total(1 - mine))
            hop(piece, step, stream).start()
            keep[step][slot] = total(mine)

    def last(piece):
        slot = piece % SLOTS
        for stream in range(2):
            keep, got = (keep_a, got_a) if stream == 0 else (keep_b, got_b)
            hop(piece, 3, stream).wait()
            out_ref[piece, top if stream == 0 else bottom, :] = keep[3][slot] + got[3][
                slot
            ].astype(jnp.float32)

    bring(0)

    @pl.loop(0, pieces + 4)
    def _(turn):
        @pl.when(turn + 1 < pieces)
        def _():
            bring(turn + 1)

        @pl.when(turn < pieces)
        def _():
            first(turn)

        for step in (1, 2, 3):

            @pl.when((turn >= step) & (turn - step < pieces))
            def _():
                later(turn - step, step)

        @pl.when(turn >= 4)
        def _():
            last(turn - 4)


def reduce_whole(parts, collective_id):
    groups = len(parts)
    rows = parts[0].shape[0] // 8
    widths = [part.shape[1] // 4 for part in parts]
    pieces = sum(widths) // PIECE_COLS
    views = [part.reshape(2, 2, 2, rows, part.shape[1]) for part in parts]
    leads = ((2, 2, 2), (2, 2), (2,), ())

    def buffers(count, dtype):
        return [pltpu.VMEM((SLOTS,) + lead + (count, PIECE_COLS), dtype) for lead in leads]

    bottom_rows = rows - ROWS_A
    whole = (SLOTS, 2, 2, 2, 2, rows, PIECE_COLS)
    summed = pl.pallas_call(
        functools.partial(reduce_kernel, groups, pieces),
        out_shape=jax.ShapeDtypeStruct((pieces, rows, PIECE_COLS), jnp.float32),
        in_specs=[anywhere()] * groups,
        out_specs=vmem(),
        scratch_shapes=[
            pltpu.VMEM(whole, jnp.float32),
            pltpu.VMEM(whole, jnp.float32),
            buffers(ROWS_A, jnp.bfloat16),
            buffers(bottom_rows, jnp.bfloat16),
            buffers(ROWS_A, jnp.bfloat16),
            buffers(bottom_rows, jnp.bfloat16),
            buffers(ROWS_A, jnp.float32),
            buffers(bottom_rows, jnp.float32),
            pltpu.SemaphoreType.DMA((SLOTS, 2)),
            pltpu.SemaphoreType.DMA((SLOTS, 2)),
            pltpu.SemaphoreType.DMA((SLOTS, 2)),
            pltpu.SemaphoreType.DMA((4, 2, SLOTS)),
            pltpu.SemaphoreType.DMA((4, 2, SLOTS)),
        ],
        compiler_params=comm_params(collective_id),
        name="reduce_grads",
    )(*views)
    blocks, at = [], 0
    for width in widths:
        count = width // PIECE_COLS
        blocks.append(summed[at : at + count].transpose(1, 0, 2).reshape(rows, width))
        at += count
    return blocks


def reduce_general(part):
    data_count, head_count = lax.axis_size("dp"), lax.axis_size("head")
    blocks = part.reshape(
        data_count, part.shape[0] // data_count, head_count, part.shape[1] // head_count
    ).transpose(0, 2, 1, 3)
    blocks = blocks.reshape((-1,) + blocks.shape[2:])
    return lax.psum_scatter(blocks, ("dp", "head"), scatter_dimension=0, tiled=True)[0]


def send_to(source, target, sems, place, peer):
    return pltpu.make_async_remote_copy(
        src_ref=source,
        dst_ref=target,
        send_sem=sems[0].at[place],
        recv_sem=sems[1].at[place],
        device_id={"head": peer},
        device_id_type=MESH,
    )


def half_mask(pair_half):
    lane = lax.broadcasted_iota(jnp.int32, (1, 128), 1)
    return (lane // 64) == pair_half


def dot_nt(left, right):
    return lax.dot_general(
        left, right, (((1,), (1,)), ((), ())), preferred_element_type=jnp.float32
    )


def dot_nn(left, right):
    return lax.dot_general(
        left, right, (((1,), (0,)), ((), ())), preferred_element_type=jnp.float32
    )


def dot_tn(left, right):
    return lax.dot_general(
        left, right, (((0,), (0,)), ((), ())), preferred_element_type=jnp.float32
    )


def own_exchange(h, pair_in, pair_all, quad_in, quad_all, sems, start_place):
    c = h % 2
    pair = [send_to(pair_in.at[1 - c], pair_all.at[c], sems, start_place, h ^ 1)]
    quad = [
        send_to(quad_in.at[h ^ other], quad_all.at[h], sems, start_place + other, h ^ other)
        for other in (1, 2, 3)
    ]
    return pair, quad


def attend_kernel(pair_in, quad_in, pair_mix, quad_mix, pair_all, quad_all, log_ref,
                  pair_out, quad_out, send_sem, recv_sem):
    h = lax.axis_index("head")
    c = h % 2
    sems = (send_sem, recv_sem)
    greet([{"head": h ^ other} for other in (1, 2, 3)])
    pair_copies, quad_copies = own_exchange(h, pair_in, pair_all, quad_in, quad_all, sems, 0)
    for copy in pair_copies + quad_copies:
        copy.start()
    pair_all[c] = pair_in[c]
    quad_all[h] = quad_in[h]
    tile = quad_in.shape[1]

    def one_pair(packed, starts, head_place, heads, out):
        length = packed.shape[0] * packed.shape[1]

        def cols(start):
            return packed[:, :, start : start + 128].reshape(length, 128)

        keys, values = cols(starts[1]), cols(starts[2])

        for row in range(length // tile):
            per = packed.shape[1] // tile
            query = packed[row // per, (row % per) * tile : (row % per + 1) * tile,
                           starts[0] : starts[0] + 128]
            mixed = jnp.zeros((tile, 128), jnp.float32)
            logs = log_ref[row * tile : (row + 1) * tile, :]
            lane = lax.broadcasted_iota(jnp.int32, (1, 128), 1)
            for half in range(heads):
                mask = half_mask(half)
                scores = dot_nt(jnp.where(mask, query, 0), keys) * 0.125
                top = jnp.max(scores, -1, keepdims=True)
                exponent = jnp.exp(scores - top)
                total = jnp.sum(exponent, -1, keepdims=True)
                probability = to_bf16(exponent / total)
                mixed = mixed + dot_nn(probability, jnp.where(mask, values, 0))
                logs = jnp.where(lane == head_place + half, top + jnp.log(total), logs)
            log_ref[row * tile : (row + 1) * tile, :] = logs
            out(row, to_bf16(mixed))

    log_ref[...] = jnp.zeros_like(log_ref)
    for copy in pair_copies:
        copy.wait()
    for pair in range(3):

        def put(row, value, pair=pair):
            pair_out[row // 2, (row % 2) * tile : (row % 2 + 1) * tile,
                     pair * 128 : pair * 128 + 128] = value

        one_pair(pair_all, (pair * 128, HALF + pair * 128, 2 * HALF + pair * 128),
                 2 * pair, 2, put)
    back = [send_to(pair_out.at[1 - c], pair_mix.at[c], sems, 4, h ^ 1)]
    back[0].start()
    pair_mix[c] = pair_out[c]
    for copy in quad_copies:
        copy.wait()
    for pair in range(2):

        def put(row, value, pair=pair):
            quad_out[row, :, pair * 128 : pair * 128 + 128] = value

        one_pair(quad_all, (pair * 128, WIDE + pair * 128, 2 * WIDE + pair * 128),
                 6 + 2 * pair, 2 - pair, put)
    for other in (1, 2, 3):
        back.append(send_to(quad_out.at[h ^ other], quad_mix.at[h], sems, 4 + other, h ^ other))
        back[-1].start()
    quad_mix[h] = quad_out[h]
    for copy in back:
        copy.wait()


def attend(pair_in, quad_in, collective_id):
    rows, tile = pair_in.shape[1], quad_in.shape[1]
    low = jnp.bfloat16
    return pl.pallas_call(
        attend_kernel,
        out_shape=[
            jax.ShapeDtypeStruct((2, rows, HALF), low),
            jax.ShapeDtypeStruct((4, tile, WIDE), low),
            jax.ShapeDtypeStruct(pair_in.shape, low),
            jax.ShapeDtypeStruct(quad_in.shape, low),
            jax.ShapeDtypeStruct((4 * tile, 128), jnp.float32),
        ],
        in_specs=[vmem()] * 2,
        out_specs=[vmem()] * 5,
        scratch_shapes=[
            pltpu.VMEM((2, rows, HALF), low),
            pltpu.VMEM((4, tile, WIDE), low),
            pltpu.SemaphoreType.DMA((8,)),
            pltpu.SemaphoreType.DMA((8,)),
        ],
        compiler_params=comm_params(collective_id),
        name="attend",
    )(pair_in, quad_in)


def attend_back_kernel(pair_all, quad_all, log_ref, pair_grad_in, quad_grad_in,
                       pair_grad, quad_grad, pair_mixed, quad_mixed, pair_out, quad_out,
                       grad_keys, grad_values, send_sem, recv_sem):
    h = lax.axis_index("head")
    c = h % 2
    sems = (send_sem, recv_sem)
    greet([{"head": h ^ other} for other in (1, 2, 3)])
    pair_copies, quad_copies = own_exchange(
        h, pair_grad_in, pair_mixed, quad_grad_in, quad_mixed, sems, 0
    )
    for copy in pair_copies + quad_copies:
        copy.start()
    pair_mixed[c] = pair_grad_in[c]
    quad_mixed[h] = quad_grad_in[h]
    tile = quad_all.shape[1]
    length = 4 * tile

    def one_pair(packed, grad_mixed, grad_start, starts, head_place, heads, out, wide):
        per = packed.shape[1] // tile

        def cols(start):
            return packed[:, :, start : start + 128].reshape(length, 128)

        keys, values = cols(starts[1]), cols(starts[2])
        grad_keys[...] = jnp.zeros_like(grad_keys)
        grad_values[...] = jnp.zeros_like(grad_values)
        for row in range(4):
            rows = slice((row % per) * tile, (row % per + 1) * tile)
            query = packed[row // per, rows, starts[0] : starts[0] + 128]
            grad_out = grad_mixed[row // per, rows, grad_start : grad_start + 128]
            lane = lax.broadcasted_iota(jnp.int32, (1, 128), 1)
            grad_query = jnp.zeros((tile, 128), jnp.float32)
            for half in range(heads):
                mask = half_mask(half)
                log_total = jnp.sum(
                    jnp.where(lane == head_place + half, log_ref[row * tile : (row + 1) * tile, :], 0.0),
                    -1, keepdims=True,
                )
                query_half = jnp.where(mask, query, 0)
                grad_half = jnp.where(mask, grad_out, 0)
                probability = jnp.exp(dot_nt(query_half, keys) * 0.125 - log_total)
                grad_prob = dot_nt(grad_half, values)
                mean = jnp.sum(probability * grad_prob, -1, keepdims=True)
                grad_scores = to_bf16(probability * (grad_prob - mean))
                grad_query = grad_query + dot_nn(grad_scores, jnp.where(mask, keys, 0))
                grad_keys[...] += dot_tn(grad_scores, query_half)
                grad_values[...] += dot_tn(to_bf16(probability), grad_half)
            out[row // per, rows, starts[0] : starts[0] + 128] = to_bf16(grad_query * 0.125)
        out[:, :, starts[1] : starts[1] + 128] = to_bf16(grad_keys[...] * 0.125).reshape(
            packed.shape[0], packed.shape[1], 128
        )
        out[:, :, starts[2] : starts[2] + 128] = to_bf16(grad_values[...]).reshape(
            packed.shape[0], packed.shape[1], 128
        )

    for copy in pair_copies:
        copy.wait()
    for pair in range(3):
        one_pair(pair_all, pair_mixed, pair * 128,
                 (pair * 128, HALF + pair * 128, 2 * HALF + pair * 128), 2 * pair, 2, pair_out, 3)
    back = [send_to(pair_out.at[1 - c], pair_grad.at[c], sems, 4, h ^ 1)]
    back[0].start()
    pair_grad[c] = pair_out[c]
    for copy in quad_copies:
        copy.wait()
    for pair in range(2):
        one_pair(quad_all, quad_mixed, pair * 128,
                 (pair * 128, WIDE + pair * 128, 2 * WIDE + pair * 128), 6 + 2 * pair, 2 - pair,
                 quad_out, 2)
    for other in (1, 2, 3):
        back.append(send_to(quad_out.at[h ^ other], quad_grad.at[h], sems, 4 + other, h ^ other))
        back[-1].start()
    quad_grad[h] = quad_out[h]
    for copy in back:
        copy.wait()


def attend_back(pair_all, quad_all, logs, pair_grad, quad_grad, collective_id):
    rows, tile = pair_all.shape[1], quad_all.shape[1]
    low = jnp.bfloat16
    return pl.pallas_call(
        attend_back_kernel,
        out_shape=[
            jax.ShapeDtypeStruct(pair_all.shape, low),
            jax.ShapeDtypeStruct(quad_all.shape, low),
        ],
        in_specs=[vmem()] * 5,
        out_specs=[vmem()] * 2,
        scratch_shapes=[
            pltpu.VMEM((2, rows, HALF), low),
            pltpu.VMEM((4, tile, WIDE), low),
            pltpu.VMEM(pair_all.shape, low),
            pltpu.VMEM(quad_all.shape, low),
            pltpu.VMEM((4 * tile, 128), jnp.float32),
            pltpu.VMEM((4 * tile, 128), jnp.float32),
            pltpu.SemaphoreType.DMA((8,)),
            pltpu.SemaphoreType.DMA((8,)),
        ],
        compiler_params=comm_params(collective_id),
        name="attend_back",
    )(pair_all, quad_all, logs, pair_grad, quad_grad)


def masked_scores(query_half, keys, keep):
    return jnp.where(keep, dot_nt(query_half, keys) * 0.125, -1e30)


def cross_kernel(query_ref, keys_ref, values_ref, len_ref, out_ref):
    tile = query_ref.shape[1]
    tokens = keys_ref.shape[1]
    token = lax.broadcasted_iota(jnp.int32, (1, tokens), 1)
    for row in range(3):
        clip = row // 2
        keep = token < len_ref[clip]
        keys, values = keys_ref[clip], values_ref[clip]
        mixed = jnp.zeros((tile, 128), jnp.float32)
        for half in range(2):
            mask = half_mask(half)
            scores = masked_scores(jnp.where(mask, query_ref[row], 0), keys, keep)
            exponent = jnp.exp(scores - jnp.max(scores, -1, keepdims=True))
            probability = to_bf16(exponent / jnp.sum(exponent, -1, keepdims=True))
            mixed = mixed + dot_nn(probability, jnp.where(mask, values, 0))
        out_ref[row] = to_bf16(mixed)


def cross(query, pair_kv, lengths):
    _, tile, width = query.shape
    blocks = width // 128
    tokens = pair_kv.shape[1]
    return pl.pallas_call(
        cross_kernel,
        grid=(blocks,),
        out_shape=jax.ShapeDtypeStruct(query.shape, jnp.bfloat16),
        in_specs=[
            pl.BlockSpec((3, tile, 128), lambda i: (0, 0, i)),
            pl.BlockSpec((2, tokens, 128), lambda i: (0, 0, i)),
            pl.BlockSpec((2, tokens, 128), lambda i: (0, 0, blocks + i)),
            pl.BlockSpec(memory_space=pltpu.SMEM),
        ],
        out_specs=pl.BlockSpec((3, tile, 128), lambda i: (0, 0, i)),
        compiler_params=pltpu.CompilerParams(vmem_limit_bytes=VMEM_BYTES),
        name="cross",
    )(query, pair_kv, pair_kv, lengths)


def cross_back_kernel(query_ref, keys_ref, values_ref, grad_ref, len_ref, grad_query_ref,
                      grad_keys_ref, grad_values_ref):
    tile = query_ref.shape[1]
    tokens = keys_ref.shape[1]
    token = lax.broadcasted_iota(jnp.int32, (1, tokens), 1)
    for clip in range(2):
        keep = token < len_ref[clip]
        keys, values = keys_ref[clip], values_ref[clip]
        grad_keys = jnp.zeros((tokens, 128), jnp.float32)
        grad_values = jnp.zeros((tokens, 128), jnp.float32)
        for row in range(2 * clip, 2 + clip):
            grad_query = jnp.zeros((tile, 128), jnp.float32)
            for half in range(2):
                mask = half_mask(half)
                query_half = jnp.where(mask, query_ref[row], 0)
                grad_half = jnp.where(mask, grad_ref[row], 0)
                scores = masked_scores(query_half, keys, keep)
                exponent = jnp.exp(scores - jnp.max(scores, -1, keepdims=True))
                probability = exponent / jnp.sum(exponent, -1, keepdims=True)
                grad_prob = dot_nt(grad_half, values)
                mean = jnp.sum(probability * grad_prob, -1, keepdims=True)
                grad_scores = to_bf16(probability * (grad_prob - mean))
                grad_query = grad_query + dot_nn(grad_scores, jnp.where(mask, keys, 0))
                grad_keys = grad_keys + dot_tn(grad_scores, query_half)
                grad_values = grad_values + dot_tn(to_bf16(probability), grad_half)
            grad_query_ref[row] = to_bf16(grad_query * 0.125)
        grad_keys_ref[clip] = to_bf16(grad_keys * 0.125)
        grad_values_ref[clip] = to_bf16(grad_values)


def cross_back(query, pair_kv, lengths, grad):
    _, tile, width = query.shape
    blocks = width // 128
    tokens = pair_kv.shape[1]
    rows_spec = pl.BlockSpec((3, tile, 128), lambda i: (0, 0, i))
    keys_spec = pl.BlockSpec((2, tokens, 128), lambda i: (0, 0, i))
    return pl.pallas_call(
        cross_back_kernel,
        grid=(blocks,),
        out_shape=[
            jax.ShapeDtypeStruct(query.shape, jnp.bfloat16),
            jax.ShapeDtypeStruct((2, tokens, width), jnp.bfloat16),
            jax.ShapeDtypeStruct((2, tokens, width), jnp.bfloat16),
        ],
        in_specs=[
            rows_spec,
            keys_spec,
            pl.BlockSpec((2, tokens, 128), lambda i: (0, 0, blocks + i)),
            rows_spec,
            pl.BlockSpec(memory_space=pltpu.SMEM),
        ],
        out_specs=[rows_spec, keys_spec, keys_spec],
        compiler_params=pltpu.CompilerParams(vmem_limit_bytes=VMEM_BYTES),
        name="cross_back",
    )(query, pair_kv, pair_kv, grad, lengths)


def body(
    clean_latents,
    noise_draw,
    timesteps,
    captions,
    cap_len,
    pairing,
    adam_step,
    qkv_weight,
    out_weight,
    up_weight,
    down_weight,
    ada_weight,
    time_weight,
    io_weight,
    qkv_moment,
    out_moment,
    up_moment,
    down_moment,
    ada_first,
    ada_second,
    time_first,
    time_second,
    io_first,
    io_second,
):
    data_count = lax.axis_size("dp")
    head_count = lax.axis_size("head")
    clip_count, tile, channels = clean_latents.shape
    length = tile * head_count
    rows_own = qkv_weight.shape[1]
    d, h = lax.axis_index("dp"), lax.axis_index("head")
    own_clip, core = h // 2, h % 2
    own_row = d * rows_own
    linked = data_count == 8 and rows_own == 96
    ids = iter(range(64))

    def swap(x, axis):
        return exchange(x, axis, True, next(ids))

    def spread(x, axis):
        return exchange(x, axis, False, next(ids))

    def by_tile(values):
        own = lax.dynamic_slice_in_dim(values, own_clip, 1, 0)
        return jnp.concatenate([own, own, values[2:3]])

    def by_clip(tiles):
        own = tiles[0:1] + tiles[1:2]
        none = jnp.zeros_like(own)
        return jnp.concatenate(
            [jnp.where(own_clip == 0, own, none), jnp.where(own_clip == 1, own, none), tiles[2:3]]
        )

    weight_groups = []
    for layer in range(2):
        weight_groups.append(
            to_bf16(jnp.concatenate([qkv_weight[layer], out_weight[layer]], 1))
        )
        weight_groups.append(to_bf16(up_weight[layer]))
        weight_groups.append(to_bf16(down_weight[layer]))
    time_cols = time_weight.shape[1]
    io_cols = io_weight.shape[2]
    io_flat = io_weight.transpose(1, 0, 2).reshape(rows_own, 2 * io_cols)
    table_rows = clip_count * D // WIDE
    small_rows = -(-(rows_own + table_rows) // 16) * 16
    small_own = jnp.concatenate(
        [
            jnp.pad(
                to_bf16(jnp.concatenate([time_weight, io_flat], 1)),
                ((0, 0), (0, WIDE - time_cols - 2 * io_cols)),
            ),
            to_bf16(time_table(timesteps, D)).reshape(table_rows, WIDE),
            jnp.zeros((small_rows - rows_own - table_rows, WIDE), jnp.bfloat16),
        ]
    )
    if linked:
        gathered = gather_whole([small_own] + weight_groups, next(ids))
    else:
        gathered = [gather_general(own) for own in [small_own] + weight_groups]
    small_all = gathered[0].reshape(data_count, small_rows, head_count, WIDE)
    qkv_out_full = [gathered[1], gathered[4]]
    up_full = [gathered[2], gathered[5]]
    down_full = [gathered[3], gathered[6]]
    time_full = small_all[:, :rows_own, :, :time_cols].reshape(D, D)
    io_full = (
        small_all[:, :rows_own, :, time_cols : time_cols + 2 * io_cols]
        .reshape(D, head_count, 2, io_cols)
        .transpose(2, 0, 1, 3)
        .reshape(2, D, channels)
    )
    table_bf = small_all[:, rows_own : rows_own + table_rows, 0].reshape(-1, D)
    out_full = [
        full.reshape(D, head_count, D)[:, :, 3 * D // head_count :].reshape(D, D)
        for full in qkv_out_full
    ]

    latents = jnp.concatenate([clean_latents, noise_draw], -1)
    latents_all = spread(latents.reshape(-1, 128), "head").reshape(
        head_count, clip_count, tile, 2 * channels
    )
    own_latents = lax.dynamic_slice(
        latents_all, (2 * core, own_clip, 0, 0), (2, 1, tile, 2 * channels)
    )[:, 0]
    latents = jnp.concatenate([own_latents, latents[2:3]])
    clean_rows, noise_rows = latents[..., :channels], latents[..., channels:]
    tile_times = by_tile(timesteps)[:, None, None]
    input_bf = to_bf16((1.0 - tile_times) * clean_rows + tile_times * noise_rows)
    target = noise_rows - clean_rows
    hidden = product("flc,dc->fld", input_bf, io_full[0])

    keep_mask = jnp.arange(CAP)[None, :] < cap_len[:, None]
    cap_mean = product("ft,ftd->fd", keep_mask.astype(jnp.bfloat16), captions) / cap_len[
        :, None
    ].astype(jnp.float32)
    cap_unit = cap_mean * lax.rsqrt(jnp.mean(cap_mean * cap_mean, -1, keepdims=True) + 1e-06)
    cap_all = spread(cap_unit, "dp").reshape(-1, D)
    own_captions = jnp.concatenate([lax.dynamic_slice_in_dim(captions, own_clip, 1, 0), captions[2:3]])
    own_lengths = jnp.concatenate([lax.dynamic_slice_in_dim(cap_len, own_clip, 1, 0), cap_len[2:3]])

    time_hidden = jnp.dot(table_bf, time_full, preferred_element_type=jnp.float32)
    signal_bf = to_bf16(double_silu(time_hidden))
    signal_own = lax.dynamic_slice_in_dim(signal_bf, own_row, rows_own, 1)
    table_own = lax.dynamic_slice_in_dim(table_bf, own_row, rows_own, 1)
    ada_bf = to_bf16(ada_weight)
    ada_cols = ada_weight.shape[2]
    mod_part = product("fd,ldn->fln", signal_own, ada_bf).reshape(
        data_count, clip_count, 2 * ada_cols
    )
    mod_own = jnp.sum(swap(mod_part, "dp"), 0)
    mod_all = (
        spread(mod_own, "head")
        .reshape(head_count, clip_count, 2, ada_cols)
        .transpose(1, 2, 0, 3)
        .reshape(clip_count, 2, 6 * D)
    )
    tile_mods = by_tile(mod_all)

    block = 3 * D // head_count

    def take_qkv(wide_rows):
        lead = wide_rows.shape[:-1]
        return wide_rows.reshape(lead + (head_count, D))[..., :block].reshape(lead + (3 * D,))

    def put_qkv(rows):
        blocks = rows.reshape(rows.shape[0], head_count, block)
        return jnp.pad(blocks, ((0, 0), (0, 0), (0, D - block))).reshape(rows.shape[0], -1)

    def put_out(rows):
        blocks = rows.reshape(rows.shape[0], head_count, D - block)
        return jnp.pad(blocks, ((0, 0), (0, 0), (block, 0))).reshape(rows.shape[0], -1)

    frames = clip_count * tile
    share = D // head_count

    def cut_rows(rows, parts):
        pair = rows[: 2 * tile].reshape(2 * tile, parts, 2, HALF)
        pair = pair.transpose(2, 0, 1, 3).reshape(2, 2 * tile, parts * HALF)
        quad = rows[2 * tile :].reshape(tile, parts, head_count, share)
        quad = jnp.pad(quad, ((0, 0), (0, 0), (0, 0), (0, WIDE - share)))
        return pair, quad.transpose(2, 0, 1, 3).reshape(head_count, tile, parts * WIDE)

    def join_rows(pair, quad, parts):
        pair = pair.reshape(2, 2 * tile, parts, HALF).transpose(1, 2, 0, 3)
        quad = quad.reshape(head_count, tile, parts, WIDE)[..., :share].transpose(1, 2, 0, 3)
        return jnp.concatenate(
            [pair.reshape(2 * tile, parts * D), quad.reshape(tile, parts * D)]
        )

    def layer_forward(layer_index, hidden):
        modulation = tile_mods[:, layer_index].reshape(clip_count, 1, 6, D)
        mod_parts = [modulation[:, :, member] for member in range(6)]
        normed = to_bf16(modulate(hidden, mod_parts[0], mod_parts[1]))
        weight = qkv_out_full[layer_index]
        if layer_index == 0:
            projected = take_qkv(to_bf16(product("fld,dn->fln", normed, weight)))
            pair, quad = cut_rows(projected.reshape(frames, 3 * D), 3)
            pair_mix, quad_mix, *attended = attend(pair, quad, next(ids))
            mixed = join_rows(pair_mix, quad_mix, 1).reshape(clip_count, tile, D)
        else:
            query = to_bf16(product("fld,dn->fln", normed, weight[:, : 2 * D]))
            query = jnp.concatenate([query[..., :block], query[..., D : 2 * D - block]], -1)
            pair_kv = take_qkv(to_bf16(product("ftd,dn->ftn", own_captions, weight)))[..., D:]
            attended = (query, pair_kv)
            mixed = cross(query, pair_kv, own_lengths)
        branch = product("fle,de->fld", mixed, out_full[layer_index])
        middle = hidden + mod_parts[2] * branch
        normed2 = to_bf16(modulate(middle, mod_parts[3], mod_parts[4]))
        upper = product("fld,dn->fln", normed2, up_full[layer_index])
        active = to_bf16(soft_gelu(upper))
        down_out = product("fln,dn->fld", active, down_full[layer_index])
        kept = (hidden, mod_parts, normed, attended, mixed, branch, middle, normed2, upper,
                active, down_out)
        return (middle + mod_parts[5] * down_out, kept)

    saved_layers = []
    for layer_index in range(2):
        hidden, kept = layer_forward(layer_index, hidden)
        saved_layers.append(kept)
    final = norm_rows(hidden)
    final_bf = to_bf16(final)
    predicted = product("fld,dc->flc", final_bf, io_full[1])
    errors = predicted - target
    flow_part = jnp.sum(jnp.mean(errors * errors, -1))
    grad_pred = to_bf16(2.0 * errors / errors.shape[-1])
    pool_sum = jnp.sum(spread(by_clip(jnp.sum(final, 1)), "head"), 0)
    pooled_out = pool_sum / length

    def contrast_of(pool_total):
        pooled = pool_total / length
        unit_rows = pooled * lax.rsqrt(jnp.mean(pooled * pooled, -1, keepdims=True) + 1e-06)
        logits = exact_product("id,jd->ij", unit_rows, cap_all) * (2.0 / math.sqrt(D))
        row_top = jnp.max(logits, -1, keepdims=True)
        log_total = row_top[:, 0] + jnp.log(jnp.sum(jnp.exp(logits - row_top), -1))
        picked = jnp.sum(
            jnp.where(jnp.arange(logits.shape[1])[None, :] == pairing[:, None], logits, 0.0), -1
        )
        return length * jnp.sum(log_total - picked)

    contrast_value, contrast_back = jax.vjp(contrast_of, pool_sum)
    grad_pool = by_tile(contrast_back(jnp.ones_like(contrast_value))[0])
    loss_part = flow_part + contrast_value / head_count
    grad_final = product("flc,dc->fld", grad_pred, io_full[1]) + grad_pool[:, None, :]
    final_value, final_back = jax.vjp(norm_rows, hidden)
    grad_hidden = final_back(grad_final)[0]
    fin_grad = product("flc,fld->dc", grad_pred, final_bf)
    grad_parts = [None] * 6
    mod_grads = [None, None]
    for layer_index in (1, 0):
        (
            layer_hidden,
            mod_parts,
            layer_normed,
            attended,
            layer_mixed,
            layer_branch,
            layer_middle,
            layer_normed2,
            layer_upper,
            layer_active,
            layer_down_out,
        ) = saved_layers[layer_index]
        weight = qkv_out_full[layer_index]
        d_gate2 = jnp.sum(layer_down_out * grad_hidden, axis=1, keepdims=True)
        grad_down = to_bf16(mod_parts[5] * grad_hidden)
        grad_active = product("fld,dn->fln", grad_down, down_full[layer_index])
        gelu_value, gelu_back = jax.vjp(soft_gelu, layer_upper)
        grad_upper = to_bf16(gelu_back(grad_active)[0])
        grad_parts[3 * layer_index + 2] = product("fld,fln->dn", grad_down, layer_active)
        grad_parts[3 * layer_index + 1] = product("fld,fln->dn", layer_normed2, grad_upper)
        grad_normed2 = product("fln,dn->fld", grad_upper, up_full[layer_index])
        mod_value, mod_back = jax.vjp(modulate, layer_middle, mod_parts[3], mod_parts[4])
        grad_middle, d_shift2, d_scale2 = mod_back(grad_normed2)
        grad_middle = grad_middle + grad_hidden
        d_gate1 = jnp.sum(layer_branch * grad_middle, axis=1, keepdims=True)
        grad_branch = to_bf16(mod_parts[2] * grad_middle)
        grad_mixed = to_bf16(product("fld,de->fle", grad_branch, out_full[layer_index]))
        left = [layer_normed.reshape(frames, D), grad_branch.reshape(frames, D)]
        right = [None, put_out(layer_mixed.reshape(frames, D))]
        if layer_index == 0:
            pair, quad = cut_rows(grad_mixed.reshape(frames, D), 1)
            pair_grad, quad_grad = attend_back(*attended, pair, quad, next(ids))
            grad_proj = put_qkv(join_rows(pair_grad, quad_grad, 3))
            right[0] = grad_proj
            grad_normed = product("fn,dn->fd", grad_proj, weight)
        else:
            query, pair_kv = attended
            grad_query, grad_keys, grad_values = cross_back(query, pair_kv, own_lengths, grad_mixed)
            tokens = 2 * CAP
            grad_kv = jnp.concatenate(
                [
                    jnp.zeros((tokens, D), jnp.bfloat16),
                    grad_keys.reshape(tokens, D),
                    grad_values.reshape(tokens, D),
                ],
                1,
            )
            grad_query = jnp.pad(grad_query.reshape(frames, D), ((0, 0), (0, 2 * D)))
            grad_proj = put_qkv(grad_query)
            right[0] = grad_proj
            left.append(own_captions.reshape(tokens, D))
            right.append(put_qkv(grad_kv))
            grad_normed = product("fn,dn->fd", grad_proj[:, : 2 * D], weight[:, : 2 * D])
        grad_parts[3 * layer_index] = product(
            "kd,kn->dn", jnp.concatenate(left), jnp.concatenate(right)
        )
        first_value, first_back = jax.vjp(modulate, layer_hidden, mod_parts[0], mod_parts[1])
        grad_in, d_shift1, d_scale1 = first_back(grad_normed.reshape(clip_count, tile, D))
        mod_grads[layer_index] = jnp.concatenate(
            [d_shift1, d_scale1, d_gate1, d_shift2, d_scale2, d_gate2], -1
        )[:, 0]
        grad_hidden = grad_in + grad_middle
    in_grad = product("fld,flc->dc", to_bf16(grad_hidden), input_bf)

    mod_size = clip_count * 2 * ada_cols
    io_size = rows_own * 2 * io_cols
    mod_grad = by_clip(jnp.stack(mod_grads, 1)).reshape(clip_count, 2, head_count, ada_cols)
    mod_grad = mod_grad.transpose(2, 0, 1, 3).reshape(head_count, mod_size)
    io_part = (
        jnp.stack([in_grad, fin_grad])
        .reshape(2, data_count, rows_own, head_count, io_cols)
        .transpose(3, 1, 0, 2, 4)
        .reshape(head_count, data_count * io_size)
    )
    packed = jnp.concatenate([mod_grad, io_part], 1).reshape(head_count, -1, 128)
    packed = jnp.sum(swap(packed, "head"), 0).reshape(-1)
    mod_grad = jnp.broadcast_to(packed[:mod_size], (data_count, mod_size))
    lines = -(-(mod_size + io_size) // 128)
    packed = jnp.concatenate([mod_grad, packed[mod_size:].reshape(data_count, io_size)], 1)
    packed = jnp.pad(packed, ((0, 0), (0, lines * 128 - mod_size - io_size)))
    packed = swap(packed.reshape(data_count, lines, 128), "dp").reshape(data_count, -1)
    mod_grad = packed[:, :mod_size].reshape(-1, 2, ada_cols)
    io_grad = jnp.sum(packed[:, mod_size : mod_size + io_size], 0).reshape(2, rows_own, io_cols)
    ada_grad = exact_product("fd,fln->ldn", signal_own.astype(jnp.float32), mod_grad)
    grad_signal = exact_product("fln,ldn->fd", mod_grad, ada_bf.astype(jnp.float32))
    grad_signal = jnp.sum(spread(grad_signal, "head"), 0)
    hidden_own = lax.dynamic_slice_in_dim(time_hidden, own_row, rows_own, 1)
    signal_own_value, signal_back = jax.vjp(double_silu, hidden_own)
    grad_cond = spread(signal_back(grad_signal)[0], "dp").transpose(1, 0, 2).reshape(-1, D)
    time_grad = exact_product(
        "fd,fn->dn",
        table_own.astype(jnp.float32),
        lax.dynamic_slice_in_dim(grad_cond, h * time_cols, time_cols, 1),
    )

    if linked:
        owned = reduce_whole(grad_parts, next(ids))
    else:
        owned = [reduce_general(part) for part in grad_parts]
    shards = (
        jnp.stack([owned[0][:, :block], owned[3][:, :block]]),
        jnp.stack([owned[0][:, block:], owned[3][:, block:]]),
        jnp.stack([owned[1], owned[4]]),
        jnp.stack([owned[2], owned[5]]),
        ada_grad,
        time_grad[None],
        io_grad,
    )
    square = sum((jnp.sum(shard * shard) for shard in shards))
    totals = jnp.pad(jnp.stack([square, loss_part])[None], ((0, 7), (0, 126)))
    totals = jnp.sum(spread(jnp.sum(spread(totals, "head"), 0), "dp"), 0)
    total_square, total_loss = totals[0, 0], totals[0, 1]
    old_moments = (qkv_moment, out_moment, up_moment, down_moment)
    grad_norm = jnp.sqrt(total_square)
    clip_scale = jnp.minimum(1.0, CLIP_NORM / (grad_norm + 1e-06))
    moments = tuple(
        (MUON_BETA * old_moments[member] + clip_scale * shards[member] for member in range(4))
    )
    coeff_a, coeff_b, coeff_c = NEWTON_COEFFS
    wide = max(moment.shape[2] for moment in moments)
    sent = jnp.concatenate(
        [jnp.pad(moment, ((0, 0), (0, 0), (0, wide - moment.shape[2]))) for moment in moments]
    )
    matrices = sent.shape[0]
    sent = jnp.pad(sent, ((0, data_count - matrices), (0, 0), (0, 0)))
    own_matrix = swap(sent, "dp").reshape(D, wide)

    def near_product(form, left, right):
        return jnp.einsum(form, left, right, precision=lax.Precision.HIGH)

    gram = lax.psum(near_product("rc,kc->rk", own_matrix, own_matrix), "head")
    unit = jnp.eye(D, dtype=jnp.float32)
    size_frob = jnp.sqrt(jnp.sum(gram * unit)) + 1e-07
    gram = gram / (size_frob * size_frob)
    factor = None
    for ns_step in range(NS_STEPS):
        poly = coeff_a * unit + coeff_b * gram + coeff_c * near_product("rk,kj->rj", gram, gram)
        factor = poly if factor is None else near_product("rk,kj->rj", poly, factor)
        if ns_step < NS_STEPS - 1:
            gram = near_product("rk,kj->rj", near_product("rk,kj->rj", poly, gram), poly)
    ortho_matrix = near_product("rk,kc->rc", factor, own_matrix) / size_frob
    ortho_back = swap(ortho_matrix.reshape(data_count, rows_own, wide), "dp")
    ortho_rows = tuple(
        (
            ortho_back[2 * member : 2 * member + 2, :, : moments[member].shape[2]]
            for member in range(4)
        )
    )
    muon_weights = (qkv_weight, out_weight, up_weight, down_weight)
    muon_new = tuple(
        (
            muon_weights[member] * (1.0 - MUON_RATE * MUON_DECAY)
            - MUON_RATE
            * 0.2
            * math.sqrt(max(D, muon_weights[member].shape[2] * head_count))
            * ortho_rows[member]
            for member in range(4)
        )
    )
    step_count = adam_step[0].astype(jnp.float32)
    ada_new, ada_first_new, ada_second_new = adam_update(
        ada_weight, clip_scale * shards[4], ada_first, ada_second, step_count
    )
    time_new, time_first_new, time_second_new = adam_update(
        time_weight, clip_scale * shards[5][0], time_first, time_second, step_count
    )
    io_new, io_first_new, io_second_new = adam_update(
        io_weight, clip_scale * shards[6], io_first, io_second, step_count
    )
    return (
        total_loss,
        grad_norm,
        pooled_out,
        muon_new[0],
        moments[0],
        muon_new[1],
        moments[1],
        muon_new[2],
        moments[2],
        muon_new[3],
        moments[3],
        ada_new,
        ada_first_new,
        ada_second_new,
        time_new,
        time_first_new,
        time_second_new,
        io_new,
        io_first_new,
        io_second_new,
    )


def solution(mesh):
    placed = (
        P("dp", "head", None),
        P("dp", "head", None),
        P("dp"),
        P("dp", None, None),
        P("dp"),
        P("dp"),
        P(),
        P(None, "dp", "head"),
        P(None, "dp", "head"),
        P(None, "dp", "head"),
        P(None, "dp", "head"),
        P(None, "dp", "head"),
        P("dp", "head"),
        P(None, "dp", "head"),
        P(None, "dp", "head"),
        P(None, "dp", "head"),
        P(None, "dp", "head"),
        P(None, "dp", "head"),
        P(None, "dp", "head"),
        P(None, "dp", "head"),
        P("dp", "head"),
        P("dp", "head"),
        P(None, "dp", "head"),
        P(None, "dp", "head"),
    )
    return jax.shard_map(
        body,
        mesh=mesh,
        in_specs=placed,
        out_specs=(
            P(),
            P(),
            P("dp", None),
            P(None, "dp", "head"),
            P(None, "dp", "head"),
            P(None, "dp", "head"),
            P(None, "dp", "head"),
            P(None, "dp", "head"),
            P(None, "dp", "head"),
            P(None, "dp", "head"),
            P(None, "dp", "head"),
            P(None, "dp", "head"),
            P(None, "dp", "head"),
            P(None, "dp", "head"),
            P("dp", "head"),
            P("dp", "head"),
            P("dp", "head"),
            P(None, "dp", "head"),
            P(None, "dp", "head"),
            P(None, "dp", "head"),
        ),
        check_vma=False,
    )
```

```python
import functools
import math

import jax
import jax.numpy as jnp
from jax import lax
from jax.experimental import pallas as pl
from jax.experimental.pallas import tpu as pltpu
from jax.sharding import PartitionSpec as P

D = 768
HEADS = 12
HDIM = 64
CAP = 256
NS_STEPS = 5


HIGHEST_PRECISION = lax.Precision.HIGHEST
NEWTON_COEFFS = (3.4445, -4.775, 2.0315)
CLIP_NORM = 1.0
MUON_RATE = 0.2
MUON_DECAY = 0.1
MUON_BETA = 0.95
ADAM_RATE = 0.02
ADAM_DECAY = 0.01
ADAM_FIRST = 0.9
ADAM_SECOND = 0.999


def to_bf16(values):
    return values.astype(jnp.bfloat16)


def sigmoid_unit(values):
    return values * jax.nn.sigmoid(values)


def double_silu(values):
    return sigmoid_unit(sigmoid_unit(values))


def soft_gelu(values):
    return (
        0.5
        * values
        * (1.0 + jnp.tanh(0.7978845608 * (values + 0.044715 * values * values * values)))
    )


def norm_rows(values):
    centre = values - jnp.mean(values, -1, keepdims=True)
    return centre * lax.rsqrt(jnp.mean(centre * centre, -1, keepdims=True) + 1e-06)


def modulate(hidden, shift, stretch):
    return norm_rows(hidden) * (1.0 + stretch) + shift


def time_table(timesteps, width):
    half_width = width // 2
    frequency = jnp.exp(
        -math.log(10000.0) * jnp.arange(half_width).astype(timesteps.dtype) / half_width
    )
    angles = 1000.0 * timesteps[:, None] * frequency[None, :]
    return jnp.concatenate([jnp.cos(angles), jnp.sin(angles)], axis=-1)


def product(form, left, right):
    return jnp.einsum(form, left, right, preferred_element_type=jnp.float32)


def exact_product(form, left, right):
    return jnp.einsum(form, left, right, precision=HIGHEST_PRECISION)


def adam_update(weight, grad_part, first_moment, second_moment, step_count):
    first_moment = ADAM_FIRST * first_moment + (1.0 - ADAM_FIRST) * grad_part
    second_moment = ADAM_SECOND * second_moment + (1.0 - ADAM_SECOND) * grad_part * grad_part
    first_fix = 1.0 - jnp.power(ADAM_FIRST, step_count)
    second_fix = 1.0 - jnp.power(ADAM_SECOND, step_count)
    direction = first_moment / first_fix / (jnp.sqrt(second_moment / second_fix) + 1e-08)
    return (weight - ADAM_RATE * (direction + ADAM_DECAY * weight), first_moment, second_moment)


MESH = pl.DeviceIdType.MESH
ROWS_A = 64
PIECE_COLS = 256
SLOTS = 4
HALF = 384
WIDE = 256
VMEM_BYTES = 56 * 1024 * 1024


def vmem():
    return pl.BlockSpec(memory_space=pltpu.VMEM)


def anywhere():
    return pl.BlockSpec(memory_space=pl.ANY)


def comm_params(collective_id):
    return pltpu.CompilerParams(
        collective_id=collective_id, has_side_effects=True, vmem_limit_bytes=VMEM_BYTES
    )


def greet(peers):
    barrier = pltpu.get_barrier_semaphore()
    for peer in peers:
        pl.semaphore_signal(barrier, inc=1, device_id=peer, device_id_type=MESH)
    pl.semaphore_wait(barrier, len(peers))


def exchange_kernel(axis, count, swapped, x_ref, out_ref, send_sem, recv_sem):
    me = lax.axis_index(axis)
    peers = [lax.rem(me + shift, count) for shift in range(1, count)]
    greet([{axis: peer} for peer in peers])
    copies = []
    for place, peer in enumerate(peers):
        copy = pltpu.make_async_remote_copy(
            src_ref=x_ref.at[peer] if swapped else x_ref,
            dst_ref=out_ref.at[me],
            send_sem=send_sem.at[place],
            recv_sem=recv_sem.at[place],
            device_id={axis: peer},
            device_id_type=MESH,
        )
        copy.start()
        copies.append(copy)
    out_ref[me] = x_ref[me] if swapped else x_ref[...]
    for copy in copies:
        copy.wait()


def exchange(x, axis, swapped, collective_id):
    count = lax.axis_size(axis)
    block = x.shape[1:] if swapped else x.shape
    return pl.pallas_call(
        functools.partial(exchange_kernel, axis, count, swapped),
        out_shape=jax.ShapeDtypeStruct((count,) + block, x.dtype),
        in_specs=[vmem()],
        out_specs=vmem(),
        scratch_shapes=[
            pltpu.SemaphoreType.DMA((count - 1,)),
            pltpu.SemaphoreType.DMA((count - 1,)),
        ],
        compiler_params=comm_params(collective_id),
        name="swap" if swapped else "spread",
    )(x)


def link_peers(d, h):
    return {
        "core": (d, h ^ 1),
        "y": (d, h ^ 2),
        "x": (d ^ 1, h),
        "zl": (d ^ 2, h),
        "zh": (d ^ 4, h),
    }


def gather_kernel(groups, *refs):
    own_refs, out_refs = refs[:groups], refs[groups : 2 * groups]
    send_sem, recv_sem, core_send, core_recv, local_sem = refs[2 * groups :]
    d = lax.axis_index("dp")
    h = lax.axis_index("head")
    peers = link_peers(d, h)
    greet(list(peers.values()))
    y, c = h // 2, h % 2
    zh, zl, x = d // 4, (d // 2) % 2, d % 2
    every = slice(None)
    pieces = [
        (group, start)
        for group in range(groups)
        for start in range(0, own_refs[group].shape[1], PIECE_COLS)
    ]
    order_a = (("zh", (zh, zl, x)), ("zl", (every, zl, x)), ("x", (every, every, x)),
               ("y", (every, every, every)))
    order_b = (("y", (zh, zl, x)), ("zh", (zh, zl, x)), ("zl", (every, zl, x)),
               ("x", (every, every, x)))

    def columns_of(piece, head):
        group, start = pieces[piece]
        width = own_refs[group].shape[1]
        return pl.ds(pl.multiple_of(head * width + start, 128), PIECE_COLS)

    def own_copy(piece):
        group, start = pieces[piece]
        return pltpu.make_async_copy(
            own_refs[group].at[:, pl.ds(start, PIECE_COLS)],
            out_refs[group].at[zh, zl, x, :, columns_of(piece, h)],
            local_sem.at[piece],
        )

    def hop(piece, step, stream):
        group, start = pieces[piece]
        rows_all = own_refs[group].shape[0]
        rows = pl.ds(0, ROWS_A) if stream == 0 else pl.ds(ROWS_A, rows_all - ROWS_A)
        head = h if stream < 2 else h ^ 2
        peer, index = (order_a if stream == 0 else order_b)[step]
        view = out_refs[group].at[index + (rows, columns_of(piece, head))]
        source = view
        if step == 0:
            source = own_refs[group].at[rows, pl.ds(start, PIECE_COLS)]
        return pltpu.make_async_remote_copy(
            src_ref=source,
            dst_ref=view,
            send_sem=send_sem.at[piece, step, stream],
            recv_sem=recv_sem.at[piece, step, stream],
            device_id=peers[peer],
            device_id_type=MESH,
        )

    def streams(step):
        return range(2) if step == 0 else range(3)

    def across(piece, side):
        group, start = pieces[piece]
        view = out_refs[group].at[:, :, :, :, columns_of(piece, h ^ (2 * side))]
        return pltpu.make_async_remote_copy(
            src_ref=view,
            dst_ref=view,
            send_sem=core_send.at[piece, side],
            recv_sem=core_recv.at[piece, side],
            device_id=peers["core"],
            device_id_type=MESH,
        )

    for piece in range(len(pieces)):
        own_copy(piece).start()
    for turn in range(len(pieces) + 4):
        for step in range(5):
            piece = turn - step
            if not 0 <= piece < len(pieces):
                continue
            if step == 1:
                own_copy(piece).wait()
            if step >= 1:
                for stream in streams(step - 1):
                    hop(piece, step - 1, stream).wait_recv()
            if step < 4:
                for stream in streams(step):
                    hop(piece, step, stream).start()
            else:
                for side in range(2):
                    across(piece, side).start()
    for piece in range(len(pieces)):
        for step in range(4):
            for stream in streams(step):
                hop(piece, step, stream).wait_send()
        for side in range(2):
            across(piece, side).wait()


def gather_whole(owns, collective_id):
    groups = len(owns)
    pieces = sum(own.shape[1] // PIECE_COLS for own in owns)
    wholes = pl.pallas_call(
        functools.partial(gather_kernel, groups),
        out_shape=[
            jax.ShapeDtypeStruct((2, 2, 2, own.shape[0], 4 * own.shape[1]), own.dtype)
            for own in owns
        ],
        in_specs=[anywhere()] * groups,
        out_specs=[anywhere()] * groups,
        scratch_shapes=[
            pltpu.SemaphoreType.DMA((pieces, 4, 3)),
            pltpu.SemaphoreType.DMA((pieces, 4, 3)),
            pltpu.SemaphoreType.DMA((pieces, 2)),
            pltpu.SemaphoreType.DMA((pieces, 2)),
            pltpu.SemaphoreType.DMA((pieces,)),
        ],
        compiler_params=pltpu.CompilerParams(collective_id=collective_id, has_side_effects=True),
        name="gather_weights",
    )(*owns)
    return [whole.reshape(8 * own.shape[0], -1) for whole, own in zip(wholes, owns)]


def gather_general(own):
    rows, columns = own.shape
    blocks = lax.all_gather(own, ("dp", "head"), axis=0, tiled=False)
    blocks = blocks.reshape(-1, lax.axis_size("head"), rows, columns)
    return blocks.transpose(0, 2, 1, 3).reshape(-1, lax.axis_size("head") * columns)


def reduce_kernel(layers, *refs):
    first_refs = refs[:layers]
    left_refs = refs[layers : 3 * layers]
    right_refs = refs[3 * layers : 5 * layers]
    extra_ref, out_ref, total_ref, edge_ref = refs[5 * layers : 5 * layers + 4]
    (own, near, made, left, left_t, right, send_a, send_b, got_a, got_b, keep_a, keep_b,
     mine, head_got, data_got, own_sem, near_send, near_recv, hop_send, hop_recv, left_sem,
     right_sem, edge_send, edge_recv, sum_send, sum_recv) = refs[5 * layers + 4 :]
    per_group = D // PIECE_COLS
    pieces = 3 * layers * per_group
    d = lax.axis_index("dp")
    h = lax.axis_index("head")
    peers = link_peers(d, h)
    across = [(d, h ^ other) for other in (1, 2, 3)] + [(d ^ other, h) for other in range(1, 8)]
    greet(across)
    y, c = h // 2, h % 2
    zh, zl, x = d // 4, (d // 2) % 2, d % 2
    order = (("y", "x"), ("x", "zl"), ("zl", "zh"), ("zh", "y"))
    rows_own = own.shape[-2]
    top, bottom = pl.ds(0, ROWS_A), pl.ds(ROWS_A, rows_own - ROWS_A)
    every = slice(None)

    def columns_of(piece, head):
        start = head * D + (piece % per_group) * PIECE_COLS
        return pl.ds(pl.multiple_of(start, PIECE_COLS), PIECE_COLS)

    def own_copy(piece, layer, side):
        return pltpu.make_async_copy(
            first_refs[layer].at[:, :, :, :, columns_of(piece, 2 * side + c)],
            own.at[piece % SLOTS, side],
            own_sem.at[piece % SLOTS, side],
        )

    def near_copy(piece, layer, side):
        slot = piece % SLOTS
        source = made.at[slot, side]
        if layer is not None:
            source = first_refs[layer].at[:, :, :, :, columns_of(piece, 2 * side + 1 - c)]
        return pltpu.make_async_remote_copy(
            src_ref=source,
            dst_ref=near.at[slot, side],
            send_sem=near_send.at[slot, side],
            recv_sem=near_recv.at[slot, side],
            device_id=peers["core"],
            device_id_type=MESH,
        )

    def left_copy(pair):
        return pltpu.make_async_copy(left_refs[pair], left.at[pair], left_sem.at[pair])

    def right_copy(piece, pair, head):
        return pltpu.make_async_copy(
            right_refs[pair].at[:, columns_of(piece, head)],
            right.at[piece % 2, head],
            right_sem.at[piece % 2, head],
        )

    def is_made(piece):
        return (piece // per_group) % 3 != 0

    def fetch(piece):
        for layer in range(layers):
            for member in range(2):

                @pl.when(piece // per_group == 3 * layer + 1 + member)
                def _():
                    for head in range(4):
                        right_copy(piece, 2 * layer + member, head).start()

    def bring(piece):
        slot = piece % SLOTS
        for layer in range(layers):

            @pl.when(piece // per_group == 3 * layer)
            def _():
                for side in range(2):
                    near_copy(piece, layer, side).start()
                    own_copy(piece, layer, side).start()

            for member in range(2):

                @pl.when(piece == (3 * layer + 1 + member) * per_group)
                def _():
                    pair = 2 * layer + member
                    left_copy(pair).wait()
                    left_t[...] = left[pair].T

        @pl.when(is_made(piece))
        def _():
            for head in range(4):
                right_copy(piece, 0, head).wait()
            shape = own.shape[2:]
            for side in range(2):
                made[slot, side] = dot_nn(left_t[...], right[piece % 2, 2 * side + 1 - c]).reshape(
                    shape
                )
                near_copy(piece, None, side).start()
            for side in range(2):
                own[slot, side] = dot_nn(left_t[...], right[piece % 2, 2 * side + c]).reshape(shape)

    def hop(piece, step, stream):
        slot = piece % SLOTS
        sent, got = (send_a, got_a) if stream == 0 else (send_b, got_b)
        return pltpu.make_async_remote_copy(
            src_ref=sent[step].at[slot],
            dst_ref=got[step].at[slot],
            send_sem=hop_send.at[step, stream, slot],
            recv_sem=hop_recv.at[step, stream, slot],
            device_id=peers[order[step][stream]],
            device_id_type=MESH,
        )

    def first(piece):
        slot = piece % SLOTS
        for side in range(2):
            near_copy(piece, None, side).wait()

        @pl.when(jnp.logical_not(is_made(piece)))
        def _():
            for side in range(2):
                own_copy(piece, 0, side).wait()

        def total(*index):
            return own[(slot,) + index] + near[(slot,) + index]

        send_a[0][slot] = to_bf16(total(1 - y, every, every, every, top))
        hop(piece, 0, 0).start()
        send_b[0][slot] = to_bf16(total(every, every, every, 1 - x, bottom))
        hop(piece, 0, 1).start()
        keep_a[0][slot] = total(y, every, every, every, top)
        keep_b[0][slot] = total(every, every, every, x, bottom)

    cut_a = (None, (2, x), (1, zl), (0, zh))
    cut_b = (None, (2, zl), (1, zh), (0, y))

    def later(piece, step):
        slot = piece % SLOTS
        for stream in range(2):
            keep, got, sent = (keep_a, got_a, send_a) if stream == 0 else (keep_b, got_b, send_b)
            axis, mine = (cut_a if stream == 0 else cut_b)[step]
            hop(piece, step - 1, stream).wait()

            def total(which):
                index = (slot,) + (every,) * axis + (which,)
                return keep[step - 1][index] + got[step - 1][index].astype(jnp.float32)

            sent[step][slot] = to_bf16(total(1 - mine))
            hop(piece, step, stream).start()
            keep[step][slot] = total(mine)

    def last(piece):
        slot = piece % SLOTS
        for stream in range(2):
            keep, got = (keep_a, got_a) if stream == 0 else (keep_b, got_b)
            hop(piece, 3, stream).wait()
            out_ref[piece, top if stream == 0 else bottom, :] = keep[3][slot] + got[3][
                slot
            ].astype(jnp.float32)

    for pair in range(2 * layers):
        left_copy(pair).start()
    bring(0)
    bring(1)

    @pl.loop(0, pieces + 4)
    def _(turn):
        @pl.when(turn + 3 < pieces)
        def _():
            fetch(turn + 3)

        @pl.when(turn < pieces)
        def _():
            first(turn)

        for step in (1, 2, 3):

            @pl.when((turn >= step) & (turn - step < pieces))
            def _():
                later(turn - step, step)

        @pl.when(turn >= 4)
        def _():
            last(turn - 4)

        @pl.when(turn + 2 < pieces)
        def _():
            bring(turn + 2)

    edges = []
    for layer in range(layers):
        piece = (3 * layer + 1) * per_group - 1
        edges.append(
            pltpu.make_async_remote_copy(
                src_ref=out_ref.at[piece, :, pl.ds(0, 128)],
                dst_ref=edge_ref.at[layer],
                send_sem=edge_send.at[layer],
                recv_sem=edge_recv.at[layer],
                device_id=peers["core"],
                device_id_type=MESH,
            )
        )
        edges[-1].start()

    squares = jnp.zeros((rows_own, PIECE_COLS), jnp.float32)
    for piece in range(pieces):
        squares = squares + out_ref[piece] * out_ref[piece]
    row = lax.broadcasted_iota(jnp.int32, (8, 128), 0)
    column = lax.broadcasted_iota(jnp.int32, (8, 128), 1)
    mine[0] = extra_ref[...] + jnp.where((row == 0) & (column == 0), jnp.sum(squares), 0.0)
    for phase, (got, me, count) in enumerate(((head_got, h, 4), (data_got, d, 8))):
        copies = []
        for other in range(1, count):
            place = 3 * phase + other - 1
            copies.append(
                pltpu.make_async_remote_copy(
                    src_ref=mine.at[phase],
                    dst_ref=got.at[me],
                    send_sem=sum_send.at[place],
                    recv_sem=sum_recv.at[place],
                    device_id=across[place],
                    device_id_type=MESH,
                )
            )
            copies[-1].start()
        got[me] = mine[phase]
        for copy in copies:
            copy.wait()
        total = got[0]
        for other in range(1, count):
            total = total + got[other]
        if phase == 0:
            mine[1] = total
        else:
            total_ref[...] = total
    for copy in edges:
        copy.wait()


def reduce_whole(firsts, pairs, extra, collective_id):
    layers = len(firsts)
    frames = pairs[0][0].shape[0]
    rows = firsts[0].shape[0] // 8
    per_group = D // PIECE_COLS
    pieces = 3 * layers * per_group
    views = [first.reshape(2, 2, 2, rows, first.shape[1]) for first in firsts]
    leads = ((2, 2, 2), (2, 2), (2,), ())

    def buffers(count, dtype):
        return [pltpu.VMEM((SLOTS,) + lead + (count, PIECE_COLS), dtype) for lead in leads]

    bottom_rows = rows - ROWS_A
    whole = (SLOTS, 2, 2, 2, 2, rows, PIECE_COLS)
    low = jnp.bfloat16
    summed, totals, edges = pl.pallas_call(
        functools.partial(reduce_kernel, layers),
        out_shape=[
            jax.ShapeDtypeStruct((pieces, rows, PIECE_COLS), jnp.float32),
            jax.ShapeDtypeStruct((8, 128), jnp.float32),
            jax.ShapeDtypeStruct((layers, rows, 128), jnp.float32),
        ],
        in_specs=[anywhere()] * (5 * layers) + [vmem()],
        out_specs=[vmem()] * 3,
        scratch_shapes=[
            pltpu.VMEM(whole, jnp.float32),
            pltpu.VMEM(whole, jnp.float32),
            pltpu.VMEM(whole, jnp.float32),
            pltpu.VMEM((2 * layers, frames, D), low),
            pltpu.VMEM((D, frames), low),
            pltpu.VMEM((2, 4, frames, PIECE_COLS), low),
            buffers(ROWS_A, low),
            buffers(bottom_rows, low),
            buffers(ROWS_A, low),
            buffers(bottom_rows, low),
            buffers(ROWS_A, jnp.float32),
            buffers(bottom_rows, jnp.float32),
            pltpu.VMEM((2, 8, 128), jnp.float32),
            pltpu.VMEM((4, 8, 128), jnp.float32),
            pltpu.VMEM((8, 8, 128), jnp.float32),
            pltpu.SemaphoreType.DMA((SLOTS, 2)),
            pltpu.SemaphoreType.DMA((SLOTS, 2)),
            pltpu.SemaphoreType.DMA((SLOTS, 2)),
            pltpu.SemaphoreType.DMA((4, 2, SLOTS)),
            pltpu.SemaphoreType.DMA((4, 2, SLOTS)),
            pltpu.SemaphoreType.DMA((2 * layers,)),
            pltpu.SemaphoreType.DMA((2, 4)),
            pltpu.SemaphoreType.DMA((layers,)),
            pltpu.SemaphoreType.DMA((layers,)),
            pltpu.SemaphoreType.DMA((10,)),
            pltpu.SemaphoreType.DMA((10,)),
        ],
        compiler_params=comm_params(collective_id),
        name="reduce_grads",
    )(*views, *[pair[0] for pair in pairs], *[pair[1] for pair in pairs], extra)
    summed = summed.reshape(3 * layers, per_group, rows, PIECE_COLS).transpose(0, 2, 1, 3)
    return list(summed.reshape(3 * layers, rows, D)), totals, edges


def reduce_general(part):
    data_count, head_count = lax.axis_size("dp"), lax.axis_size("head")
    blocks = part.reshape(
        data_count, part.shape[0] // data_count, head_count, part.shape[1] // head_count
    ).transpose(0, 2, 1, 3)
    blocks = blocks.reshape((-1,) + blocks.shape[2:])
    return lax.psum_scatter(blocks, ("dp", "head"), scatter_dimension=0, tiled=True)[0]


KIND_AT = (1, 2, 3, 0)


def owner_of(kind, layer):
    return 4 * layer + KIND_AT.index(kind)


def is_owner_of(me, kind):
    return (me % 4 == KIND_AT.index(kind)) & (me < 8)


def to_owner_kernel(count, *refs):
    block_refs, out_ref, send_sem, recv_sem = refs[:4], refs[4], refs[5], refs[6]
    me = lax.axis_index("dp")
    out_ref[...] = jnp.zeros_like(out_ref)
    greet([{"dp": lax.rem(me + shift, count)} for shift in range(1, count)])

    def copy(kind, layer, source):
        width = block_refs[kind].shape[-1]
        return pltpu.make_async_remote_copy(
            src_ref=block_refs[kind].at[layer],
            dst_ref=out_ref.at[source, :, pl.ds(0, width)],
            send_sem=send_sem.at[2 * kind + layer],
            recv_sem=recv_sem.at[source],
            device_id={"dp": owner_of(kind, layer)},
            device_id_type=MESH,
        )

    for kind in range(4):
        for layer in range(2):

            @pl.when(me != owner_of(kind, layer))
            def _():
                copy(kind, layer, me).start()

            @pl.when(me == owner_of(kind, layer))
            def _():
                out_ref[me, :, : block_refs[kind].shape[-1]] = block_refs[kind][layer]

    for kind in range(4):

        @pl.when(is_owner_of(me, kind))
        def _():
            @pl.loop(0, count)
            def _(source):
                @pl.when(source != me)
                def _():
                    copy(kind, 0, source).wait_recv()

        for layer in range(2):

            @pl.when(me != owner_of(kind, layer))
            def _():
                copy(kind, layer, me).wait_send()


def to_owner(blocks, collective_id):
    count = lax.axis_size("dp")
    rows = blocks[0].shape[1]
    wide = max(block.shape[2] for block in blocks)
    return pl.pallas_call(
        functools.partial(to_owner_kernel, count),
        out_shape=jax.ShapeDtypeStruct((count, rows, wide), jnp.float32),
        in_specs=[vmem()] * 4,
        out_specs=vmem(),
        scratch_shapes=[pltpu.SemaphoreType.DMA((8,)), pltpu.SemaphoreType.DMA((count,))],
        compiler_params=comm_params(collective_id),
        name="to_owner",
    )(*blocks)


def from_owner_kernel(count, widths, x_ref, out_ref, send_sem, recv_sem):
    me = lax.axis_index("dp")
    greet([{"dp": lax.rem(me + shift, count)} for shift in range(1, count)])

    def copy(kind, matrix, target):
        columns = pl.ds(0, widths[kind])
        return pltpu.make_async_remote_copy(
            src_ref=x_ref.at[target, :, columns],
            dst_ref=out_ref.at[matrix, :, columns],
            send_sem=send_sem.at[target],
            recv_sem=recv_sem.at[matrix],
            device_id={"dp": target},
            device_id_type=MESH,
        )

    for kind in range(4):

        @pl.when(is_owner_of(me, kind))
        def _():
            @pl.loop(0, count)
            def _(target):
                @pl.when(target != me)
                def _():
                    copy(kind, me, target).start()

            out_ref[me] = x_ref[me]

    for kind in range(4):
        for layer in range(2):
            matrix = owner_of(kind, layer)

            @pl.when(me != matrix)
            def _():
                copy(kind, matrix, me).wait_recv()

        @pl.when(is_owner_of(me, kind))
        def _():
            @pl.loop(0, count)
            def _(target):
                @pl.when(target != me)
                def _():
                    copy(kind, me, target).wait_send()


def from_owner(x, widths, collective_id):
    count = lax.axis_size("dp")
    return pl.pallas_call(
        functools.partial(from_owner_kernel, count, widths),
        out_shape=jax.ShapeDtypeStruct((8,) + x.shape[1:], x.dtype),
        in_specs=[vmem()],
        out_specs=vmem(),
        scratch_shapes=[pltpu.SemaphoreType.DMA((count,)), pltpu.SemaphoreType.DMA((8,))],
        compiler_params=comm_params(collective_id),
        name="from_owner",
    )(x)


def gram_kernel(x_ref, out_ref, high, rest, upper, chip, got, whole, send_sem, recv_sem):
    h = lax.axis_index("head")
    c = h % 2
    greet([{"head": h ^ other} for other in (1, 2)])
    third = PIECE_COLS
    values = x_ref[...]
    high[...] = to_bf16(values)
    rest[...] = to_bf16(values - high[...].astype(jnp.float32))

    def dots(first, second):
        return (
            dot_nt(high[first], high[second])
            + dot_nt(high[first], rest[second])
            + dot_nt(rest[first], high[second])
        )

    r0, r1, r2 = (pl.ds(third * place, third) for place in range(3))
    upper[0] = dots(r0, pl.ds(0, 3 * third))
    upper[1, :, : 2 * third] = dots(r1, pl.ds(third, 2 * third))
    upper[1, :, 2 * third :] = dots(r2, r2)

    def step(place, source, target, peer):
        copy = send_to(source, target, (send_sem, recv_sem), place, peer)
        copy.start()
        copy.wait()

    step(0, upper.at[1 - c], got.at[0], h ^ 1)
    chip[...] = upper[c] + got[0]
    step(1, chip, got.at[1], h ^ 2)
    whole[c] = chip[...] + got[1]
    step(2, whole.at[c], whole.at[c], h ^ 1)
    out_ref[r0, :] = whole[0]
    out_ref[r1, pl.ds(third, 2 * third)] = whole[1, :, : 2 * third]
    out_ref[r2, r2] = whole[1, :, 2 * third :]
    out_ref[r1, r0] = whole[0, :, third : 2 * third].T
    out_ref[r2, r0] = whole[0, :, 2 * third :].T
    out_ref[r2, r1] = whole[1, :, third : 2 * third].T


def gram_sum(x, collective_id):
    rows, columns = x.shape
    third = PIECE_COLS
    return pl.pallas_call(
        gram_kernel,
        out_shape=jax.ShapeDtypeStruct((rows, rows), jnp.float32),
        in_specs=[vmem()],
        out_specs=vmem(),
        scratch_shapes=[
            pltpu.VMEM((rows, columns), jnp.bfloat16),
            pltpu.VMEM((rows, columns), jnp.bfloat16),
            pltpu.VMEM((2, third, rows), jnp.float32),
            pltpu.VMEM((third, rows), jnp.float32),
            pltpu.VMEM((2, third, rows), jnp.float32),
            pltpu.VMEM((2, third, rows), jnp.float32),
            pltpu.SemaphoreType.DMA((3,)),
            pltpu.SemaphoreType.DMA((3,)),
        ],
        compiler_params=comm_params(collective_id),
        name="gram_sum",
    )(x)


def send_to(source, target, sems, place, peer):
    return pltpu.make_async_remote_copy(
        src_ref=source,
        dst_ref=target,
        send_sem=sems[0].at[place],
        recv_sem=sems[1].at[place],
        device_id={"head": peer},
        device_id_type=MESH,
    )


def half_mask(half):
    lane = lax.broadcasted_iota(jnp.int32, (1, 128), 1)
    return (lane // 64) == half


def dot_nt(left, right):
    return lax.dot_general(
        left, right, (((1,), (1,)), ((), ())), preferred_element_type=jnp.float32
    )


def dot_nn(left, right):
    return lax.dot_general(
        left, right, (((1,), (0,)), ((), ())), preferred_element_type=jnp.float32
    )


def dot_tn(left, right):
    return lax.dot_general(
        left, right, (((0,), (0,)), ((), ())), preferred_element_type=jnp.float32
    )


def lanes(start, size):
    return pl.ds(pl.multiple_of(start, 128), size)


def window(head):
    return 128 * ((3 * head) // 2)


def bring_heads(h, rows_ref, pair_all, quad_all, parts, sems):
    c = h % 2
    tile = quad_all.shape[1]
    own, shared = pl.ds(0, 2 * tile), pl.ds(2 * tile, tile)
    pair, quad = [], []
    for part in range(parts):
        pair.append(
            send_to(
                rows_ref.at[own, lanes(part * D + (1 - c) * HALF, HALF)],
                pair_all.at[c, :, pl.ds(part * HALF, HALF)],
                sems, part, h ^ 1,
            )
        )
        for other in (1, 2, 3):
            quad.append(
                send_to(
                    rows_ref.at[shared, lanes(part * D + window(h ^ other), WIDE)],
                    quad_all.at[h, :, pl.ds(part * WIDE, WIDE)],
                    sems, 3 * other + part, h ^ other,
                )
            )
    for copy in pair + quad:
        copy.start()
    for part in range(parts):
        pair_all[c, :, part * HALF : (part + 1) * HALF] = rows_ref[
            own, lanes(part * D + c * HALF, HALF)
        ]
        quad_all[h, :, part * WIDE : (part + 1) * WIDE] = rows_ref[
            shared, lanes(part * D + window(h), WIDE)
        ]
    return pair, quad


def return_pair(h, pair_out, rows_ref, parts, sems):
    c = h % 2
    own = pl.ds(0, pair_out.shape[1])
    copies = []
    for part in range(parts):
        columns = lanes(part * D + c * HALF, HALF)
        copies.append(
            send_to(
                pair_out.at[1 - c, :, pl.ds(part * HALF, HALF)], rows_ref.at[own, columns],
                sems, 12 + part, h ^ 1,
            )
        )
        copies[-1].start()
        rows_ref[own, columns] = pair_out[c, :, part * HALF : (part + 1) * HALF]
    return copies


def return_quad(h, quad_out, quad_got, sems):
    copies = []
    for other in (1, 2, 3):
        copies.append(
            send_to(quad_out.at[h ^ other], quad_got.at[h], sems, 14 + other, h ^ other)
        )
        copies[-1].start()
    quad_got[h] = quad_out[h]
    return copies


def merge_quad(quad_got, rows_ref, parts):
    tile = quad_got.shape[1]
    shared = slice(2 * tile, 3 * tile)
    for part in range(parts):
        base, start = part * WIDE, part * D
        for side in range(2):
            left, right = quad_got.at[2 * side], quad_got.at[2 * side + 1]
            at = start + side * HALF
            rows_ref[shared, at : at + 128] = left[:, base : base + 128]
            rows_ref[shared, at + 128 : at + 256] = (
                left[:, base + 128 : base + 256] + right[:, base : base + 128]
            )
            rows_ref[shared, at + 256 : at + 384] = right[:, base + 128 : base + 256]


def attend_kernel(rows_ref, mixed_ref, pair_all, quad_all, log_ref, pair_out, quad_out, quad_got,
                  send_sem, recv_sem):
    h = lax.axis_index("head")
    sems = (send_sem, recv_sem)
    greet([{"head": h ^ other} for other in (1, 2, 3)])
    pair_copies, quad_copies = bring_heads(h, rows_ref, pair_all, quad_all, 3, sems)
    tile = quad_all.shape[1]
    length = 4 * tile
    lane = lax.broadcasted_iota(jnp.int32, (1, 128), 1)

    def one_head(query, keys, values, mask):
        scores = dot_nt(jnp.where(mask, query, 0) * 0.125, keys)
        top = jnp.max(scores, -1, keepdims=True)
        exponent = jnp.exp(scores - top)
        total = jnp.sum(exponent, -1, keepdims=True)
        probability = to_bf16(exponent * (1.0 / total))
        return dot_nn(probability, jnp.where(mask, values, 0)), top + jnp.log(total)

    log_ref[...] = jnp.zeros_like(log_ref)
    quad_out[...] = jnp.zeros_like(quad_out)
    for copy in pair_copies:
        copy.wait()
    for pair in range(3):
        keys = pair_all[:, :, HALF + pair * 128 : HALF + pair * 128 + 128].reshape(length, 128)
        values = pair_all[:, :, 2 * HALF + pair * 128 : 2 * HALF + pair * 128 + 128].reshape(
            length, 128
        )
        for row in range(4):
            rows = slice((row % 2) * tile, (row % 2 + 1) * tile)
            out_rows = slice(row * tile, (row + 1) * tile)
            query = pair_all[row // 2, rows, pair * 128 : pair * 128 + 128]
            mixed = jnp.zeros((tile, 128), jnp.float32)
            logs = log_ref[out_rows, :]
            for half in range(2):
                part, log_total = one_head(query, keys, values, half_mask(half))
                mixed = mixed + part
                logs = jnp.where(lane == 2 * pair + half, log_total, logs)
            log_ref[out_rows, :] = logs
            pair_out[row // 2, rows, pair * 128 : pair * 128 + 128] = to_bf16(mixed)
    back = return_pair(h, pair_out, mixed_ref, 1, sems)
    for copy in quad_copies:
        copy.wait()
    for member in range(3):
        place = h % 2 + member
        mask = half_mask(place % 2)
        at = (place // 2) * 128
        keys = quad_all[:, :, lanes(WIDE + at, 128)].reshape(length, 128)
        values = quad_all[:, :, lanes(2 * WIDE + at, 128)].reshape(length, 128)
        for row in range(4):
            out_rows = slice(row * tile, (row + 1) * tile)
            mixed, log_total = one_head(quad_all[row, :, lanes(at, 128)], keys, values, mask)
            log_ref[out_rows, :] = jnp.where(lane == 6 + member, log_total, log_ref[out_rows, :])
            quad_out[row, :, lanes(at, 128)] += to_bf16(mixed)
    back_quad = return_quad(h, quad_out, quad_got, sems)
    for copy in back + back_quad:
        copy.wait()
    merge_quad(quad_got, mixed_ref, 1)


def attend(rows, collective_id):
    frames = rows.shape[0]
    tile = frames // 3
    low = jnp.bfloat16
    return pl.pallas_call(
        attend_kernel,
        out_shape=[
            jax.ShapeDtypeStruct((frames, D), low),
            jax.ShapeDtypeStruct((2, 2 * tile, 3 * HALF), low),
            jax.ShapeDtypeStruct((4, tile, 3 * WIDE), low),
            jax.ShapeDtypeStruct((4 * tile, 128), jnp.float32),
        ],
        in_specs=[vmem()],
        out_specs=[vmem()] * 4,
        scratch_shapes=[
            pltpu.VMEM((2, 2 * tile, HALF), low),
            pltpu.VMEM((4, tile, WIDE), low),
            pltpu.VMEM((4, tile, WIDE), low),
            pltpu.SemaphoreType.DMA((18,)),
            pltpu.SemaphoreType.DMA((18,)),
        ],
        compiler_params=comm_params(collective_id),
        name="attend",
    )(rows)


def attend_back_kernel(pair_all, quad_all, log_ref, grad_ref, rows_ref, pair_mixed, quad_mixed,
                       pair_out, quad_out, quad_got, grad_keys, grad_values, send_sem, recv_sem):
    h = lax.axis_index("head")
    sems = (send_sem, recv_sem)
    greet([{"head": h ^ other} for other in (1, 2, 3)])
    pair_copies, quad_copies = bring_heads(h, grad_ref, pair_mixed, quad_mixed, 1, sems)
    tile = quad_all.shape[1]
    length = 4 * tile
    lane = lax.broadcasted_iota(jnp.int32, (1, 128), 1)

    def one_head(query, keys, values, grad_out, mask, out_rows, log_lane):
        log_total = jnp.sum(
            jnp.where(lane == log_lane, log_ref[out_rows, :], 0.0), -1, keepdims=True
        )
        query = jnp.where(mask, query, 0) * 0.125
        grad_out = jnp.where(mask, grad_out, 0)
        probability = jnp.exp(dot_nt(query, keys) - log_total)
        grad_prob = dot_nt(grad_out, values)
        mean = jnp.sum(probability * grad_prob, -1, keepdims=True)
        grad_scores = to_bf16(probability * (grad_prob - mean))
        grad_keys[...] += dot_tn(grad_scores, query)
        grad_values[...] += dot_tn(to_bf16(probability), grad_out)
        return dot_nn(grad_scores, jnp.where(mask, keys, 0)) * 0.125

    quad_out[...] = jnp.zeros_like(quad_out)
    for copy in pair_copies:
        copy.wait()
    for pair in range(3):
        at = [part * HALF + pair * 128 for part in range(3)]
        keys = pair_all[:, :, at[1] : at[1] + 128].reshape(length, 128)
        values = pair_all[:, :, at[2] : at[2] + 128].reshape(length, 128)
        grad_keys[...] = jnp.zeros_like(grad_keys)
        grad_values[...] = jnp.zeros_like(grad_values)
        for row in range(4):
            rows = slice((row % 2) * tile, (row % 2 + 1) * tile)
            query = pair_all[row // 2, rows, at[0] : at[0] + 128]
            grad_out = pair_mixed[row // 2, rows, at[0] : at[0] + 128]
            grad_query = jnp.zeros((tile, 128), jnp.float32)
            for half in range(2):
                grad_query = grad_query + one_head(
                    query, keys, values, grad_out, half_mask(half),
                    slice(row * tile, (row + 1) * tile), 2 * pair + half,
                )
            pair_out[row // 2, rows, at[0] : at[0] + 128] = to_bf16(grad_query)
        for part, total in ((1, grad_keys), (2, grad_values)):
            pair_out[:, :, at[part] : at[part] + 128] = to_bf16(total[...]).reshape(
                2, 2 * tile, 128
            )
    back = return_pair(h, pair_out, rows_ref, 3, sems)
    for copy in quad_copies:
        copy.wait()
    for member in range(3):
        place = h % 2 + member
        mask = half_mask(place % 2)
        at = (place // 2) * 128
        keys = quad_all[:, :, lanes(WIDE + at, 128)].reshape(length, 128)
        values = quad_all[:, :, lanes(2 * WIDE + at, 128)].reshape(length, 128)
        grad_keys[...] = jnp.zeros_like(grad_keys)
        grad_values[...] = jnp.zeros_like(grad_values)
        for row in range(4):
            grad_query = one_head(
                quad_all[row, :, lanes(at, 128)], keys, values, quad_mixed[row, :, lanes(at, 128)],
                mask, slice(row * tile, (row + 1) * tile), 6 + member,
            )
            quad_out[row, :, lanes(at, 128)] += to_bf16(grad_query)
        for part, total in ((1, grad_keys), (2, grad_values)):
            quad_out[:, :, lanes(part * WIDE + at, 128)] += to_bf16(total[...]).reshape(
                4, tile, 128
            )
    back_quad = return_quad(h, quad_out, quad_got, sems)
    for copy in back + back_quad:
        copy.wait()
    merge_quad(quad_got, rows_ref, 3)


def attend_back(pair_all, quad_all, logs, grad_mixed, collective_id):
    rows, tile = pair_all.shape[1], quad_all.shape[1]
    low = jnp.bfloat16
    return pl.pallas_call(
        attend_back_kernel,
        out_shape=jax.ShapeDtypeStruct((3 * tile, 3 * D), low),
        in_specs=[vmem()] * 4,
        out_specs=vmem(),
        scratch_shapes=[
            pltpu.VMEM((2, rows, HALF), low),
            pltpu.VMEM((4, tile, WIDE), low),
            pltpu.VMEM(pair_all.shape, low),
            pltpu.VMEM(quad_all.shape, low),
            pltpu.VMEM(quad_all.shape, low),
            pltpu.VMEM((4 * tile, 128), jnp.float32),
            pltpu.VMEM((4 * tile, 128), jnp.float32),
            pltpu.SemaphoreType.DMA((18,)),
            pltpu.SemaphoreType.DMA((18,)),
        ],
        compiler_params=comm_params(collective_id),
        name="attend_back",
    )(pair_all, quad_all, logs, grad_mixed)


def masked_scores(query_half, keys, keep):
    return jnp.where(keep, dot_nt(query_half, keys) * 0.125, -1e30)


def cross_kernel(query_ref, keys_ref, values_ref, len_ref, out_ref):
    tile = query_ref.shape[1]
    tokens = keys_ref.shape[1]
    token = lax.broadcasted_iota(jnp.int32, (1, tokens), 1)
    for row in range(3):
        clip = row // 2
        keep = token < len_ref[clip]
        keys, values = keys_ref[clip], values_ref[clip]
        mixed = jnp.zeros((tile, 128), jnp.float32)
        for half in range(2):
            mask = half_mask(half)
            scores = masked_scores(jnp.where(mask, query_ref[row], 0), keys, keep)
            exponent = jnp.exp(scores - jnp.max(scores, -1, keepdims=True))
            probability = to_bf16(exponent / jnp.sum(exponent, -1, keepdims=True))
            mixed = mixed + dot_nn(probability, jnp.where(mask, values, 0))
        out_ref[row] = to_bf16(mixed)


def cross(query, pair_kv, lengths):
    _, tile, width = query.shape
    blocks = width // 128
    tokens = pair_kv.shape[1]
    return pl.pallas_call(
        cross_kernel,
        grid=(blocks,),
        out_shape=jax.ShapeDtypeStruct(query.shape, jnp.bfloat16),
        in_specs=[
            pl.BlockSpec((3, tile, 128), lambda i: (0, 0, i)),
            pl.BlockSpec((2, tokens, 128), lambda i: (0, 0, i)),
            pl.BlockSpec((2, tokens, 128), lambda i: (0, 0, blocks + i)),
            pl.BlockSpec(memory_space=pltpu.SMEM),
        ],
        out_specs=pl.BlockSpec((3, tile, 128), lambda i: (0, 0, i)),
        compiler_params=pltpu.CompilerParams(vmem_limit_bytes=VMEM_BYTES),
        name="cross",
    )(query, pair_kv, pair_kv, lengths)


def cross_back_kernel(query_ref, keys_ref, values_ref, grad_ref, len_ref, grad_query_ref,
                      grad_keys_ref, grad_values_ref):
    tile = query_ref.shape[1]
    tokens = keys_ref.shape[1]
    token = lax.broadcasted_iota(jnp.int32, (1, tokens), 1)
    for clip in range(2):
        keep = token < len_ref[clip]
        keys, values = keys_ref[clip], values_ref[clip]
        grad_keys = jnp.zeros((tokens, 128), jnp.float32)
        grad_values = jnp.zeros((tokens, 128), jnp.float32)
        for row in range(2 * clip, 2 + clip):
            grad_query = jnp.zeros((tile, 128), jnp.float32)
            for half in range(2):
                mask = half_mask(half)
                query_half = jnp.where(mask, query_ref[row], 0)
                grad_half = jnp.where(mask, grad_ref[row], 0)
                scores = masked_scores(query_half, keys, keep)
                exponent = jnp.exp(scores - jnp.max(scores, -1, keepdims=True))
                probability = exponent / jnp.sum(exponent, -1, keepdims=True)
                grad_prob = dot_nt(grad_half, values)
                mean = jnp.sum(probability * grad_prob, -1, keepdims=True)
                grad_scores = to_bf16(probability * (grad_prob - mean))
                grad_query = grad_query + dot_nn(grad_scores, jnp.where(mask, keys, 0))
                grad_keys = grad_keys + dot_tn(grad_scores, query_half)
                grad_values = grad_values + dot_tn(to_bf16(probability), grad_half)
            grad_query_ref[row] = to_bf16(grad_query * 0.125)
        grad_keys_ref[clip] = to_bf16(grad_keys * 0.125)
        grad_values_ref[clip] = to_bf16(grad_values)


def cross_back(query, pair_kv, lengths, grad):
    _, tile, width = query.shape
    blocks = width // 128
    tokens = pair_kv.shape[1]
    rows_spec = pl.BlockSpec((3, tile, 128), lambda i: (0, 0, i))
    keys_spec = pl.BlockSpec((2, tokens, 128), lambda i: (0, 0, i))
    return pl.pallas_call(
        cross_back_kernel,
        grid=(blocks,),
        out_shape=[
            jax.ShapeDtypeStruct(query.shape, jnp.bfloat16),
            jax.ShapeDtypeStruct((2, tokens, width), jnp.bfloat16),
            jax.ShapeDtypeStruct((2, tokens, width), jnp.bfloat16),
        ],
        in_specs=[
            rows_spec,
            keys_spec,
            pl.BlockSpec((2, tokens, 128), lambda i: (0, 0, blocks + i)),
            rows_spec,
            pl.BlockSpec(memory_space=pltpu.SMEM),
        ],
        out_specs=[rows_spec, keys_spec, keys_spec],
        compiler_params=pltpu.CompilerParams(vmem_limit_bytes=VMEM_BYTES),
        name="cross_back",
    )(query, pair_kv, pair_kv, grad, lengths)


def body(
    clean_latents,
    noise_draw,
    timesteps,
    captions,
    cap_len,
    pairing,
    adam_step,
    qkv_weight,
    out_weight,
    up_weight,
    down_weight,
    ada_weight,
    time_weight,
    io_weight,
    qkv_moment,
    out_moment,
    up_moment,
    down_moment,
    ada_first,
    ada_second,
    time_first,
    time_second,
    io_first,
    io_second,
):
    data_count = lax.axis_size("dp")
    head_count = lax.axis_size("head")
    clip_count, tile, channels = clean_latents.shape
    length = tile * head_count
    rows_own = qkv_weight.shape[1]
    d, h = lax.axis_index("dp"), lax.axis_index("head")
    own_clip, core = h // 2, h % 2
    own_row = d * rows_own
    linked = data_count == 8 and rows_own == 96
    ids = iter(range(64))

    def swap(x, axis):
        return exchange(x, axis, True, next(ids))

    def spread(x, axis):
        return exchange(x, axis, False, next(ids))

    def by_tile(values):
        own = lax.dynamic_slice_in_dim(values, own_clip, 1, 0)
        return jnp.concatenate([own, own, values[2:3]])

    def by_clip(tiles):
        own = tiles[0:1] + tiles[1:2]
        none = jnp.zeros_like(own)
        return jnp.concatenate(
            [jnp.where(own_clip == 0, own, none), jnp.where(own_clip == 1, own, none), tiles[2:3]]
        )

    block = 3 * D // head_count
    share = D // head_count
    is_first = core == 0
    edge = jnp.where(is_first, out_weight[..., 128:], qkv_weight[..., :64])
    latents = jnp.concatenate([clean_latents, noise_draw], -1)
    latents_size = latents.size
    packed = jnp.concatenate([latents.reshape(-1), edge.reshape(-1)]).reshape(-1, 128)
    packed = spread(packed, "head").reshape(head_count, -1)
    latents_all = packed[:, :latents_size].reshape(head_count, clip_count, tile, 2 * channels)
    edge = lax.dynamic_slice_in_dim(packed[:, latents_size:], h ^ 1, 1, 0).reshape(edge.shape)

    def with_edge(qkv, out, edge):
        return jnp.where(
            is_first,
            jnp.concatenate([qkv, edge, out[..., :128]], -1),
            jnp.concatenate([qkv[..., 64:], edge, out], -1),
        )

    def without_edge(own, edge):
        qkv = jnp.where(
            is_first, own[..., :block], jnp.concatenate([edge, own[..., : block - 64]], -1)
        )
        out = jnp.where(
            is_first, jnp.concatenate([own[..., block + 64 :], edge], -1), own[..., block:]
        )
        return qkv, out

    first_groups = to_bf16(with_edge(qkv_weight, out_weight, edge))
    weight_groups = []
    for layer in range(2):
        weight_groups.append(first_groups[layer])
        weight_groups.append(to_bf16(up_weight[layer]))
        weight_groups.append(to_bf16(down_weight[layer]))
    time_cols = time_weight.shape[1]
    io_cols = io_weight.shape[2]
    io_flat = io_weight.transpose(1, 0, 2).reshape(rows_own, 2 * io_cols)
    table_rows = clip_count * D // WIDE
    small_rows = -(-(rows_own + table_rows) // 16) * 16
    small_own = jnp.concatenate(
        [
            jnp.pad(
                to_bf16(jnp.concatenate([time_weight, io_flat], 1)),
                ((0, 0), (0, WIDE - time_cols - 2 * io_cols)),
            ),
            to_bf16(time_table(timesteps, D)).reshape(table_rows, WIDE),
            jnp.zeros((small_rows - rows_own - table_rows, WIDE), jnp.bfloat16),
        ]
    )
    if linked:
        gathered = gather_whole([small_own] + weight_groups, next(ids))
    else:
        gathered = [gather_general(own) for own in [small_own] + weight_groups]
    small_all = gathered[0].reshape(data_count, small_rows, head_count, WIDE)
    up_full = [gathered[2], gathered[5]]
    down_full = [gathered[3], gathered[6]]
    time_full = small_all[:, :rows_own, :, :time_cols].reshape(D, D)
    io_full = (
        small_all[:, :rows_own, :, time_cols : time_cols + 2 * io_cols]
        .reshape(D, head_count, 2, io_cols)
        .transpose(2, 0, 1, 3)
        .reshape(2, D, channels)
    )
    table_bf = small_all[:, rows_own : rows_own + table_rows, 0].reshape(-1, D)

    def split_first(whole):
        qkv, out = [], []
        for side in range(2):
            at = 2 * side * D
            qkv += [whole[:, at : at + 640], whole[:, at + D : at + D + 512]]
            out += [whole[:, at + 640 : at + D], whole[:, at + D + 512 : at + 2 * D]]
        return jnp.concatenate(qkv, 1), jnp.concatenate(out, 1)

    def join_first(qkv, out):
        columns = []
        for side in range(2):
            q, o = side * 2 * block, side * 2 * share
            columns += [qkv[:, q : q + 640], out[:, o : o + 128]]
            columns += [qkv[:, q + 640 : q + 1152], out[:, o + 128 : o + 384]]
        return jnp.concatenate(columns, 1)

    qkv_full, out_full = zip(*[split_first(gathered[1 + 3 * layer]) for layer in range(2)])

    own_latents = lax.dynamic_slice(
        latents_all, (2 * core, own_clip, 0, 0), (2, 1, tile, 2 * channels)
    )[:, 0]
    latents = jnp.concatenate([own_latents, latents[2:3]])
    clean_rows, noise_rows = latents[..., :channels], latents[..., channels:]
    tile_times = by_tile(timesteps)[:, None, None]
    input_bf = to_bf16((1.0 - tile_times) * clean_rows + tile_times * noise_rows)
    target = noise_rows - clean_rows
    hidden = product("flc,dc->fld", input_bf, io_full[0])

    keep_mask = jnp.arange(CAP)[None, :] < cap_len[:, None]
    cap_mean = product("ft,ftd->fd", keep_mask.astype(jnp.bfloat16), captions) / cap_len[
        :, None
    ].astype(jnp.float32)
    cap_unit = cap_mean * lax.rsqrt(jnp.mean(cap_mean * cap_mean, -1, keepdims=True) + 1e-06)
    own_captions = jnp.concatenate([lax.dynamic_slice_in_dim(captions, own_clip, 1, 0), captions[2:3]])
    own_lengths = jnp.concatenate([lax.dynamic_slice_in_dim(cap_len, own_clip, 1, 0), cap_len[2:3]])

    time_hidden = jnp.dot(table_bf, time_full, preferred_element_type=jnp.float32)
    signal_bf = to_bf16(double_silu(time_hidden))
    signal_own = lax.dynamic_slice_in_dim(signal_bf, own_row, rows_own, 1)
    table_own = lax.dynamic_slice_in_dim(table_bf, own_row, rows_own, 1)
    ada_bf = to_bf16(ada_weight)
    ada_cols = ada_weight.shape[2]
    mod_part = product("fd,ldn->fln", signal_own, ada_bf).reshape(
        data_count, clip_count, 2 * ada_cols
    )
    mod_part = jnp.concatenate(
        [mod_part, jnp.broadcast_to(cap_unit, (data_count, clip_count, D))], -1
    )
    mod_part = swap(mod_part, "dp")
    cap_all = mod_part[:, :, 2 * ada_cols :].reshape(-1, D)
    mod_own = jnp.sum(mod_part[:, :, : 2 * ada_cols], 0)
    mod_all = (
        spread(mod_own, "head")
        .reshape(head_count, clip_count, 2, ada_cols)
        .transpose(1, 2, 0, 3)
        .reshape(clip_count, 2, 6 * D)
    )
    tile_mods = by_tile(mod_all)

    frames = clip_count * tile

    def layer_forward(layer_index, hidden):
        modulation = tile_mods[:, layer_index].reshape(clip_count, 1, 6, D)
        mod_parts = [modulation[:, :, member] for member in range(6)]
        normed = to_bf16(modulate(hidden, mod_parts[0], mod_parts[1]))
        weight = qkv_full[layer_index]
        if layer_index == 0:
            projected = to_bf16(product("fld,dn->fln", normed, weight))
            mixed, *attended = attend(projected.reshape(frames, 3 * D), next(ids))
            mixed = mixed.reshape(clip_count, tile, D)
        else:
            query = to_bf16(product("fld,dn->fln", normed, weight[:, :D]))
            pair_kv = to_bf16(product("ftd,dn->ftn", own_captions, weight[:, D:]))
            attended = (query, pair_kv)
            mixed = cross(query, pair_kv, own_lengths)
        branch = product("fle,de->fld", mixed, out_full[layer_index])
        middle = hidden + mod_parts[2] * branch
        normed2 = to_bf16(modulate(middle, mod_parts[3], mod_parts[4]))
        upper = product("fld,dn->fln", normed2, up_full[layer_index])
        active = to_bf16(soft_gelu(upper))
        down_out = product("fln,dn->fld", active, down_full[layer_index])
        kept = (hidden, mod_parts, normed, attended, mixed, branch, middle, normed2, upper,
                active, down_out)
        return (middle + mod_parts[5] * down_out, kept)

    saved_layers = []
    for layer_index in range(2):
        hidden, kept = layer_forward(layer_index, hidden)
        saved_layers.append(kept)
    final = norm_rows(hidden)
    final_bf = to_bf16(final)
    predicted = product("fld,dc->flc", final_bf, io_full[1])
    errors = predicted - target
    flow_part = jnp.sum(jnp.mean(errors * errors, -1))
    grad_pred = to_bf16(2.0 * errors / errors.shape[-1])
    pool_sum = jnp.sum(spread(by_clip(jnp.sum(final, 1)), "head"), 0)
    pooled_out = pool_sum / length

    def contrast_of(pool_total):
        pooled = pool_total / length
        unit_rows = pooled * lax.rsqrt(jnp.mean(pooled * pooled, -1, keepdims=True) + 1e-06)
        logits = exact_product("id,jd->ij", unit_rows, cap_all) * (2.0 / math.sqrt(D))
        row_top = jnp.max(logits, -1, keepdims=True)
        log_total = row_top[:, 0] + jnp.log(jnp.sum(jnp.exp(logits - row_top), -1))
        picked = jnp.sum(
            jnp.where(jnp.arange(logits.shape[1])[None, :] == pairing[:, None], logits, 0.0), -1
        )
        return length * jnp.sum(log_total - picked)

    contrast_value, contrast_back = jax.vjp(contrast_of, pool_sum)
    grad_pool = by_tile(contrast_back(jnp.ones_like(contrast_value))[0])
    loss_part = flow_part + contrast_value / head_count
    grad_final = product("flc,dc->fld", grad_pred, io_full[1]) + grad_pool[:, None, :]
    final_value, final_back = jax.vjp(norm_rows, hidden)
    grad_hidden = final_back(grad_final)[0]
    fin_grad = product("flc,fld->dc", grad_pred, final_bf)
    firsts, pairs = [], []
    mod_grads = [None, None]
    for layer_index in (1, 0):
        (
            layer_hidden,
            mod_parts,
            layer_normed,
            attended,
            layer_mixed,
            layer_branch,
            layer_middle,
            layer_normed2,
            layer_upper,
            layer_active,
            layer_down_out,
        ) = saved_layers[layer_index]
        weight = qkv_full[layer_index]
        d_gate2 = jnp.sum(layer_down_out * grad_hidden, axis=1, keepdims=True)
        grad_down = to_bf16(mod_parts[5] * grad_hidden)
        grad_active = product("fld,dn->fln", grad_down, down_full[layer_index])
        gelu_value, gelu_back = jax.vjp(soft_gelu, layer_upper)
        grad_upper = to_bf16(gelu_back(grad_active)[0])
        pairs += [
            (layer_normed2.reshape(frames, D), grad_upper.reshape(frames, -1)),
            (grad_down.reshape(frames, D), layer_active.reshape(frames, -1)),
        ]
        grad_normed2 = product("fln,dn->fld", grad_upper, up_full[layer_index])
        mod_value, mod_back = jax.vjp(modulate, layer_middle, mod_parts[3], mod_parts[4])
        grad_middle, d_shift2, d_scale2 = mod_back(grad_normed2)
        grad_middle = grad_middle + grad_hidden
        d_gate1 = jnp.sum(layer_branch * grad_middle, axis=1, keepdims=True)
        grad_branch = to_bf16(mod_parts[2] * grad_middle)
        grad_mixed = to_bf16(product("fld,de->fle", grad_branch, out_full[layer_index]))
        out_grad = product("fld,fle->de", grad_branch, layer_mixed)
        if layer_index == 0:
            grad_proj = attend_back(*attended, grad_mixed.reshape(frames, D), next(ids))
            grad_normed = product("fn,dn->fd", grad_proj, weight)
            qkv_grad = product("fd,fn->dn", layer_normed.reshape(frames, D), grad_proj)
        else:
            query, pair_kv = attended
            grad_query, grad_keys, grad_values = cross_back(query, pair_kv, own_lengths, grad_mixed)
            grad_normed = product("fln,dn->fld", grad_query, weight[:, :D])
            qkv_grad = jnp.concatenate(
                [
                    product("fld,fln->dn", layer_normed, grad_query),
                    product("ftd,ftn->dn", own_captions, grad_keys),
                    product("ftd,ftn->dn", own_captions, grad_values),
                ],
                1,
            )
        firsts.append(join_first(qkv_grad, out_grad))
        first_value, first_back = jax.vjp(modulate, layer_hidden, mod_parts[0], mod_parts[1])
        grad_in, d_shift1, d_scale1 = first_back(grad_normed.reshape(clip_count, tile, D))
        mod_grads[layer_index] = jnp.concatenate(
            [d_shift1, d_scale1, d_gate1, d_shift2, d_scale2, d_gate2], -1
        )[:, 0]
        grad_hidden = grad_in + grad_middle
    in_grad = product("fld,flc->dc", to_bf16(grad_hidden), input_bf)

    mod_size = clip_count * 2 * ada_cols
    io_size = rows_own * 2 * io_cols
    mod_grad = by_clip(jnp.stack(mod_grads, 1)).reshape(clip_count, 2, head_count, ada_cols)
    mod_grad = mod_grad.transpose(2, 0, 1, 3).reshape(head_count, mod_size)
    io_part = (
        jnp.stack([in_grad, fin_grad])
        .reshape(2, data_count, rows_own, head_count, io_cols)
        .transpose(3, 1, 0, 2, 4)
        .reshape(head_count, data_count * io_size)
    )
    packed = jnp.concatenate([mod_grad, io_part], 1).reshape(head_count, -1, 128)
    packed = jnp.sum(swap(packed, "head"), 0).reshape(-1)
    mod_grad = jnp.broadcast_to(packed[:mod_size], (data_count, mod_size))
    lines = -(-(mod_size + io_size) // 128)
    packed = jnp.concatenate([mod_grad, packed[mod_size:].reshape(data_count, io_size)], 1)
    packed = jnp.pad(packed, ((0, 0), (0, lines * 128 - mod_size - io_size)))
    packed = swap(packed.reshape(data_count, lines, 128), "dp").reshape(data_count, -1)
    mod_grad = packed[:, :mod_size].reshape(-1, 2, ada_cols)
    io_grad = jnp.sum(packed[:, mod_size : mod_size + io_size], 0).reshape(2, rows_own, io_cols)
    ada_grad = exact_product("fd,fln->ldn", signal_own.astype(jnp.float32), mod_grad)
    grad_signal = exact_product("fln,ldn->fd", mod_grad, ada_bf.astype(jnp.float32))
    grad_signal = jnp.sum(spread(grad_signal, "head"), 0)
    hidden_own = lax.dynamic_slice_in_dim(time_hidden, own_row, rows_own, 1)
    signal_own_value, signal_back = jax.vjp(double_silu, hidden_own)
    grad_cond = spread(signal_back(grad_signal)[0], "dp").transpose(1, 0, 2).reshape(-1, D)
    time_grad = exact_product(
        "fd,fn->dn",
        table_own.astype(jnp.float32),
        lax.dynamic_slice_in_dim(grad_cond, h * time_cols, time_cols, 1),
    )

    square = sum((jnp.sum(grad * grad) for grad in (ada_grad, time_grad, io_grad)))
    if linked:
        extra = jnp.pad(jnp.stack([square, loss_part])[None], ((0, 7), (0, 126)))
        owned, totals, edge = reduce_whole(firsts, pairs, extra, next(ids))
        totals = totals[0, :2]
        edge = edge[::-1]
        edge = jnp.where(is_first, edge[..., :64], edge[..., 64:])
    else:
        parts = []
        for place in range(2):
            parts.append(firsts[place])
            parts += [product("fd,fn->dn", *pair) for pair in pairs[2 * place : 2 * place + 2]]
        owned = [reduce_general(part) for part in parts]
        square = square + sum((jnp.sum(part * part) for part in owned))
        totals = lax.psum(jnp.stack([square, loss_part]), ("dp", "head"))
        edge = jnp.stack([owned[3], owned[0]])
        edge = jnp.where(is_first, edge[..., block : block + 64], edge[..., block - 64 : block])
        edge = spread(edge.reshape(-1, 128), "head")
        edge = lax.dynamic_slice_in_dim(edge, h ^ 1, 1, 0).reshape(2, rows_own, 64)
    first_own = jnp.stack([owned[3], owned[0]])
    total_square, total_loss = totals[0], totals[1]
    qkv_shard, out_shard = without_edge(first_own, edge)
    shards = (
        qkv_shard,
        out_shard,
        jnp.stack([owned[4], owned[1]]),
        jnp.stack([owned[5], owned[2]]),
        ada_grad,
        time_grad[None],
        io_grad,
    )
    old_moments = (qkv_moment, out_moment, up_moment, down_moment)
    grad_norm = jnp.sqrt(total_square)
    clip_scale = jnp.minimum(1.0, CLIP_NORM / (grad_norm + 1e-06))
    moments = tuple(
        (MUON_BETA * old_moments[member] + clip_scale * shards[member] for member in range(4))
    )
    coeff_a, coeff_b, coeff_c = NEWTON_COEFFS
    widths = [-(-moment.shape[2] // 128) * 128 for moment in moments]
    padded = [
        jnp.pad(moment, ((0, 0), (0, 0), (0, width - moment.shape[2])))
        for moment, width in zip(moments, widths)
    ]
    own_matrix = to_owner(padded, next(ids)).reshape(D, -1)

    def near_product(form, left, right):
        return jnp.einsum(form, left, right, precision=lax.Precision.HIGH)

    gram = gram_sum(own_matrix, next(ids))
    unit = jnp.eye(D, dtype=jnp.float32)
    size_frob = jnp.sqrt(jnp.sum(gram * unit)) + 1e-07
    gram = gram / (size_frob * size_frob)
    factor = None
    for ns_step in range(NS_STEPS):
        poly = coeff_a * unit + coeff_b * gram + coeff_c * near_product("rk,kj->rj", gram, gram)
        factor = poly if factor is None else near_product("rk,kj->rj", poly, factor)
        if ns_step < NS_STEPS - 1:
            gram = near_product("rk,kj->rj", near_product("rk,kj->rj", poly, gram), poly)
    ortho_matrix = near_product("rk,kc->rc", factor, own_matrix) / size_frob
    ortho_back = to_bf16(ortho_matrix).reshape(data_count, rows_own, -1)
    ortho_back = from_owner(ortho_back, tuple(widths), next(ids)).astype(jnp.float32)
    ortho_rows = tuple(
        (
            jnp.stack(
                [
                    ortho_back[owner_of(member, layer), :, : moments[member].shape[2]]
                    for layer in range(2)
                ]
            )
            for member in range(4)
        )
    )
    muon_weights = (qkv_weight, out_weight, up_weight, down_weight)
    muon_new = tuple(
        (
            muon_weights[member] * (1.0 - MUON_RATE * MUON_DECAY)
            - MUON_RATE
            * 0.2
            * math.sqrt(max(D, muon_weights[member].shape[2] * head_count))
            * ortho_rows[member]
            for member in range(4)
        )
    )
    step_count = adam_step[0].astype(jnp.float32)
    ada_new, ada_first_new, ada_second_new = adam_update(
        ada_weight, clip_scale * shards[4], ada_first, ada_second, step_count
    )
    time_new, time_first_new, time_second_new = adam_update(
        time_weight, clip_scale * shards[5][0], time_first, time_second, step_count
    )
    io_new, io_first_new, io_second_new = adam_update(
        io_weight, clip_scale * shards[6], io_first, io_second, step_count
    )
    return (
        total_loss,
        grad_norm,
        pooled_out,
        muon_new[0],
        moments[0],
        muon_new[1],
        moments[1],
        muon_new[2],
        moments[2],
        muon_new[3],
        moments[3],
        ada_new,
        ada_first_new,
        ada_second_new,
        time_new,
        time_first_new,
        time_second_new,
        io_new,
        io_first_new,
        io_second_new,
    )


def solution(mesh):
    placed = (
        P("dp", "head", None),
        P("dp", "head", None),
        P("dp"),
        P("dp", None, None),
        P("dp"),
        P("dp"),
        P(),
        P(None, "dp", "head"),
        P(None, "dp", "head"),
        P(None, "dp", "head"),
        P(None, "dp", "head"),
        P(None, "dp", "head"),
        P("dp", "head"),
        P(None, "dp", "head"),
        P(None, "dp", "head"),
        P(None, "dp", "head"),
        P(None, "dp", "head"),
        P(None, "dp", "head"),
        P(None, "dp", "head"),
        P(None, "dp", "head"),
        P("dp", "head"),
        P("dp", "head"),
        P(None, "dp", "head"),
        P(None, "dp", "head"),
    )
    return jax.shard_map(
        body,
        mesh=mesh,
        in_specs=placed,
        out_specs=(
            P(),
            P(),
            P("dp", None),
            P(None, "dp", "head"),
            P(None, "dp", "head"),
            P(None, "dp", "head"),
            P(None, "dp", "head"),
            P(None, "dp", "head"),
            P(None, "dp", "head"),
            P(None, "dp", "head"),
            P(None, "dp", "head"),
            P(None, "dp", "head"),
            P(None, "dp", "head"),
            P(None, "dp", "head"),
            P("dp", "head"),
            P("dp", "head"),
            P("dp", "head"),
            P(None, "dp", "head"),
            P(None, "dp", "head"),
            P(None, "dp", "head"),
        ),
        check_vma=False,
    )
```

```python
import functools
import math

import jax
import jax.numpy as jnp
from jax import lax
from jax.experimental import pallas as pl
from jax.experimental.pallas import tpu as pltpu
from jax.sharding import PartitionSpec as P

D = 768
HEADS = 12
HDIM = 64
CAP = 256
NS_STEPS = 5


HIGHEST_PRECISION = lax.Precision.HIGHEST
NEWTON_COEFFS = (3.4445, -4.775, 2.0315)
CLIP_NORM = 1.0
MUON_RATE = 0.2
MUON_DECAY = 0.1
MUON_BETA = 0.95
ADAM_RATE = 0.02
ADAM_DECAY = 0.01
ADAM_FIRST = 0.9
ADAM_SECOND = 0.999


def to_bf16(values):
    return values.astype(jnp.bfloat16)


def sigmoid_unit(values):
    return values * jax.nn.sigmoid(values)


def double_silu(values):
    return sigmoid_unit(sigmoid_unit(values))


def soft_gelu(values):
    return (
        0.5
        * values
        * (1.0 + jnp.tanh(0.7978845608 * (values + 0.044715 * values * values * values)))
    )


def norm_rows(values):
    centre = values - jnp.mean(values, -1, keepdims=True)
    return centre * lax.rsqrt(jnp.mean(centre * centre, -1, keepdims=True) + 1e-06)


def modulate(hidden, shift, stretch):
    return norm_rows(hidden) * (1.0 + stretch) + shift


def time_table(timesteps, width):
    half_width = width // 2
    frequency = jnp.exp(
        -math.log(10000.0) * jnp.arange(half_width).astype(timesteps.dtype) / half_width
    )
    angles = 1000.0 * timesteps[:, None] * frequency[None, :]
    return jnp.concatenate([jnp.cos(angles), jnp.sin(angles)], axis=-1)


def product(form, left, right):
    return jnp.einsum(form, left, right, preferred_element_type=jnp.float32)


def exact_product(form, left, right):
    return jnp.einsum(form, left, right, precision=HIGHEST_PRECISION)


def adam_update(weight, grad_part, first_moment, second_moment, step_count):
    first_moment = ADAM_FIRST * first_moment + (1.0 - ADAM_FIRST) * grad_part
    second_moment = ADAM_SECOND * second_moment + (1.0 - ADAM_SECOND) * grad_part * grad_part
    first_fix = 1.0 - jnp.power(ADAM_FIRST, step_count)
    second_fix = 1.0 - jnp.power(ADAM_SECOND, step_count)
    direction = first_moment / first_fix / (jnp.sqrt(second_moment / second_fix) + 1e-08)
    return (weight - ADAM_RATE * (direction + ADAM_DECAY * weight), first_moment, second_moment)


MESH = pl.DeviceIdType.MESH
ROWS_A = 64
PIECE_COLS = 256
SLOTS = 4
HALF = 384
WIDE = 256
VMEM_BYTES = 56 * 1024 * 1024


def vmem():
    return pl.BlockSpec(memory_space=pltpu.VMEM)


def anywhere():
    return pl.BlockSpec(memory_space=pl.ANY)


def comm_params(collective_id):
    return pltpu.CompilerParams(
        collective_id=collective_id, has_side_effects=True, vmem_limit_bytes=VMEM_BYTES
    )


def greet(peers):
    barrier = pltpu.get_barrier_semaphore()
    for peer in peers:
        pl.semaphore_signal(barrier, inc=1, device_id=peer, device_id_type=MESH)
    pl.semaphore_wait(barrier, len(peers))


def exchange_kernel(axis, count, swapped, x_ref, out_ref, send_sem, recv_sem):
    me = lax.axis_index(axis)
    peers = [lax.rem(me + shift, count) for shift in range(1, count)]
    greet([{axis: peer} for peer in peers])
    copies = []
    for place, peer in enumerate(peers):
        copy = pltpu.make_async_remote_copy(
            src_ref=x_ref.at[peer] if swapped else x_ref,
            dst_ref=out_ref.at[me],
            send_sem=send_sem.at[place],
            recv_sem=recv_sem.at[place],
            device_id={axis: peer},
            device_id_type=MESH,
        )
        copy.start()
        copies.append(copy)
    out_ref[me] = x_ref[me] if swapped else x_ref[...]
    for copy in copies:
        copy.wait()


def exchange(x, axis, swapped, collective_id):
    count = lax.axis_size(axis)
    block = x.shape[1:] if swapped else x.shape
    return pl.pallas_call(
        functools.partial(exchange_kernel, axis, count, swapped),
        out_shape=jax.ShapeDtypeStruct((count,) + block, x.dtype),
        in_specs=[vmem()],
        out_specs=vmem(),
        scratch_shapes=[
            pltpu.SemaphoreType.DMA((count - 1,)),
            pltpu.SemaphoreType.DMA((count - 1,)),
        ],
        compiler_params=comm_params(collective_id),
        name="swap" if swapped else "spread",
    )(x)


def link_peers(d, h):
    return {
        "core": (d, h ^ 1),
        "y": (d, h ^ 2),
        "x": (d ^ 1, h),
        "zl": (d ^ 2, h),
        "zh": (d ^ 4, h),
    }


def first_column(side, core, start):
    if start < 512:
        return side * 1152 + core * 640 + start
    if start == 512:
        return (1 - core) * (side * 1152 + 512) + core * (3 * D + side * HALF + 128)
    return 3 * D + side * HALF + core * 256


def gather_pieces(widths, firsts):
    pieces = []
    for group, width in enumerate(widths):
        for start in range(0, width, PIECE_COLS):
            if group in firsts and start == 512:
                pieces += [(group, 512, 128), (group, 640, 128)]
            else:
                pieces.append((group, start, PIECE_COLS))
    return pieces


def gather_kernel(groups, firsts, *refs):
    own_refs = refs[:groups]
    edge_ref, latents_ref, shared_ref, table_ref, ada_ref = refs[groups : groups + 5]
    out_refs = refs[groups + 5 : 2 * groups + 5]
    latents_out, shared_out, mods_out = refs[2 * groups + 5 : 2 * groups + 8]
    (tail, edge_got, times, parts, parts_got, mine, send_sem, recv_sem, core_send, core_recv,
     local_sem, tail_sem, small_send, small_recv) = refs[2 * groups + 8 :]
    d = lax.axis_index("dp")
    h = lax.axis_index("head")
    peers = link_peers(d, h)
    heads = [(d, h ^ other) for other in (1, 2, 3)]
    datas = [(d ^ other, h) for other in range(1, 8)]
    greet(heads + datas)
    y, c = h // 2, h % 2
    zh, zl, x = d // 4, (d // 2) % 2, d % 2
    every = slice(None)
    pieces = gather_pieces([own.shape[1] for own in own_refs], firsts)
    order_a = (("zh", (zh, zl, x)), ("zl", (every, zl, x)), ("x", (every, every, x)),
               ("y", (every, every, every)))
    order_b = (("y", (zh, zl, x)), ("zh", (zh, zl, x)), ("zl", (every, zl, x)),
               ("x", (every, every, x)))

    def tail_of(piece):
        group, start, size = pieces[piece]
        if group in firsts and start == 2 * PIECE_COLS:
            return firsts.index(group)
        return None

    def source_of(piece, rows):
        group, start, size = pieces[piece]
        place = tail_of(piece)
        if place is not None:
            return tail.at[place, rows]
        return own_refs[group].at[rows, pl.ds(start, size)]

    def columns_of(piece, head):
        group, start, size = pieces[piece]
        if group in firsts:
            return pl.ds(pl.multiple_of(first_column(head // 2, head % 2, start), 128), size)
        return pl.ds(pl.multiple_of(head * own_refs[group].shape[1] + start, 128), size)

    def own_copy(piece):
        group = pieces[piece][0]
        return pltpu.make_async_copy(
            source_of(piece, pl.ds(0, own_refs[group].shape[0])),
            out_refs[group].at[zh, zl, x, :, columns_of(piece, h)],
            local_sem.at[piece],
        )

    def hop(piece, step, stream):
        group = pieces[piece][0]
        rows_all = own_refs[group].shape[0]
        rows = pl.ds(0, ROWS_A) if stream == 0 else pl.ds(ROWS_A, rows_all - ROWS_A)
        head = h if stream < 2 else h ^ 2
        peer, index = (order_a if stream == 0 else order_b)[step]
        view = out_refs[group].at[index + (rows, columns_of(piece, head))]
        return pltpu.make_async_remote_copy(
            src_ref=source_of(piece, rows) if step == 0 else view,
            dst_ref=view,
            send_sem=send_sem.at[piece, step, stream],
            recv_sem=recv_sem.at[piece, step, stream],
            device_id=peers[peer],
            device_id_type=MESH,
        )

    def streams(step):
        return range(2) if step == 0 else range(3)

    def across(piece, side):
        group = pieces[piece][0]
        view = out_refs[group].at[:, :, :, :, columns_of(piece, h ^ (2 * side))]
        return pltpu.make_async_remote_copy(
            src_ref=view,
            dst_ref=view,
            send_sem=core_send.at[piece, side],
            recv_sem=core_recv.at[piece, side],
            device_id=peers["core"],
            device_id_type=MESH,
        )

    def small(place, source, target, peer):
        return pltpu.make_async_remote_copy(
            src_ref=source,
            dst_ref=target,
            send_sem=small_send.at[place],
            recv_sem=small_recv.at[place],
            device_id=peer,
            device_id_type=MESH,
        )

    edge = small(0, edge_ref, edge_got, peers["core"])
    edge.start()
    tails = [
        pltpu.make_async_copy(
            own_refs[group].at[:, pl.ds(2 * PIECE_COLS, 128)], tail.at[place],
            tail_sem.at[place],
        )
        for place, group in enumerate(firsts)
    ]
    for copy in tails:
        copy.start()
    latents = [
        small(1 + place, latents_ref, latents_out.at[h], peer) for place, peer in enumerate(heads)
    ]
    for copy in latents:
        copy.start()
    latents_out[h] = latents_ref[...]
    bring_times = pltpu.make_async_copy(out_refs[0], times, tail_sem.at[len(firsts)])
    shares = [
        small(4 + place, mine, shared_out.at[d], peer) for place, peer in enumerate(datas)
    ]
    swaps = [
        small(11 + place, parts.at[d ^ (1 + place)], parts_got.at[d], peer)
        for place, peer in enumerate(datas)
    ]
    spreads = [
        small(18 + place, mods_out.at[h], mods_out.at[h], peer) for place, peer in enumerate(heads)
    ]

    def condition(turn):
        if turn == 2:
            edge.wait()
            for copy in tails:
                copy.wait()
            tail[...] = tail[...] + edge_got[...]
            for piece in range(len(pieces)):
                if tail_of(piece) is not None:
                    own_copy(piece).start()
        if turn == 6:
            for side in range(2):
                across(0, side).wait_recv()
            bring_times.start()
        if turn == 7:
            bring_times.wait()
            rows = times.shape[-2]
            mine[...] = shared_ref[...] + dot_nn(
                table_ref[...], times[...].reshape(8 * rows, times.shape[-1])
            )
            for copy in shares:
                copy.start()
            shared_out[d] = mine[...]
        if turn == 9:
            for copy in shares:
                copy.wait()
            count, lines, width = shared_out.shape
            signal = to_bf16(double_silu(shared_out[...])).reshape(count * lines, width)
            first = (d // 2) * WIDE + (d % 2) * ada_ref.shape[1]
            at = lax.broadcasted_iota(jnp.int32, (width, 128), 0)
            to = lax.broadcasted_iota(jnp.int32, (width, 128), 1)
            chosen = jnp.where((at == first + to) & (to < ada_ref.shape[1]), 1.0, 0.0)
            own = to_bf16(dot_nn(signal, to_bf16(chosen)))[:, : ada_ref.shape[1]]
            columns = ada_ref.shape[2]
            for layer in range(2):
                part = dot_nn(own, ada_ref[layer]).reshape(count, lines, columns)
                parts[:, :, layer * columns : (layer + 1) * columns] = part[:, :8]
            for copy in swaps:
                copy.start()
            parts_got[d] = parts[d]
        if turn == 11:
            for copy in swaps:
                copy.wait()
            total = parts_got[0]
            for place in range(1, 8):
                total = total + parts_got[place]
            mods_out[h] = total
            for copy in spreads:
                copy.start()
        if turn == 13:
            for copy in spreads + latents:
                copy.wait()

    for piece in range(len(pieces)):
        if tail_of(piece) is None:
            own_copy(piece).start()
    for turn in range(len(pieces) + 4):
        for step in range(5):
            piece = turn - step
            if not 0 <= piece < len(pieces):
                continue
            if step == 1:
                own_copy(piece).wait()
            if step >= 1:
                for stream in streams(step - 1):
                    hop(piece, step - 1, stream).wait_recv()
            if step < 4:
                for stream in streams(step):
                    hop(piece, step, stream).start()
            else:
                for side in range(2):
                    across(piece, side).start()
        condition(turn)
    for piece in range(len(pieces)):
        for step in range(4):
            for stream in streams(step):
                hop(piece, step, stream).wait_send()
        for side in range(2):
            if piece > 0:
                across(piece, side).wait_recv()
            across(piece, side).wait_send()


def gather_whole(owns, firsts, edge, latents, shared, table, ada, collective_id):
    groups = len(owns)
    pieces = len(gather_pieces([own.shape[1] for own in owns], firsts))
    rows = owns[0].shape[0]
    low = jnp.bfloat16
    mod_cols = 2 * ada.shape[2]
    *wholes, latents_all, shared_all, mods = pl.pallas_call(
        functools.partial(gather_kernel, groups, firsts),
        out_shape=[
            jax.ShapeDtypeStruct((2, 2, 2, own.shape[0], 4 * own.shape[1]), own.dtype)
            for own in owns
        ]
        + [
            jax.ShapeDtypeStruct((4,) + latents.shape, jnp.float32),
            jax.ShapeDtypeStruct((8,) + shared.shape, jnp.float32),
            jax.ShapeDtypeStruct((4, 8, mod_cols), jnp.float32),
        ],
        in_specs=[anywhere()] * groups + [vmem()] * 5,
        out_specs=[anywhere()] * groups + [vmem()] * 3,
        scratch_shapes=[
            pltpu.VMEM(edge.shape, low),
            pltpu.VMEM(edge.shape, low),
            pltpu.VMEM((2, 2, 2, rows, 4 * owns[0].shape[1]), low),
            pltpu.VMEM((8, 8, mod_cols), jnp.float32),
            pltpu.VMEM((8, 8, mod_cols), jnp.float32),
            pltpu.VMEM(shared.shape, jnp.float32),
            pltpu.SemaphoreType.DMA((pieces, 4, 3)),
            pltpu.SemaphoreType.DMA((pieces, 4, 3)),
            pltpu.SemaphoreType.DMA((pieces, 2)),
            pltpu.SemaphoreType.DMA((pieces, 2)),
            pltpu.SemaphoreType.DMA((pieces,)),
            pltpu.SemaphoreType.DMA((len(firsts) + 1,)),
            pltpu.SemaphoreType.DMA((21,)),
            pltpu.SemaphoreType.DMA((21,)),
        ],
        compiler_params=comm_params(collective_id),
        name="gather_weights",
    )(*owns, edge, latents, shared, table, ada)
    wholes = [whole.reshape(8 * own.shape[0], -1) for whole, own in zip(wholes, owns)]
    return wholes, latents_all, shared_all, mods


def gather_general(own):
    rows, columns = own.shape
    blocks = lax.all_gather(own, ("dp", "head"), axis=0, tiled=False)
    blocks = blocks.reshape(-1, lax.axis_size("head"), rows, columns)
    return blocks.transpose(0, 2, 1, 3).reshape(-1, lax.axis_size("head") * columns)


def reduce_kernel(plan, lefts, rights, *refs):
    left_refs, right_refs = refs[:lefts], refs[lefts : lefts + rights]
    extra_ref, out_ref, total_ref, edge_ref = refs[lefts + rights : lefts + rights + 4]
    (made, near, left, left_t, right, send_a, send_b, got_a, got_b, keep_a, keep_b,
     mine, head_got, data_got, near_send, near_recv, hop_send, hop_recv, left_sem,
     right_sem, edge_send, edge_recv, sum_send, sum_recv) = refs[lefts + rights + 4 :]
    layers = len(plan)
    per_group = D // PIECE_COLS
    pieces = 3 * layers * per_group
    d = lax.axis_index("dp")
    h = lax.axis_index("head")
    peers = link_peers(d, h)
    across = [(d, h ^ other) for other in (1, 2, 3)] + [(d ^ other, h) for other in range(1, 8)]
    greet(across)
    y, c = h // 2, h % 2
    zh, zl, x = d // 4, (d // 2) % 2, d % 2
    order = (("y", "x"), ("x", "zl"), ("zl", "zh"), ("zh", "y"))
    shape = made.shape[3:]
    rows_own = shape[-2]
    top, bottom = pl.ds(0, ROWS_A), pl.ds(ROWS_A, rows_own - ROWS_A)
    every = slice(None)

    def near_copy(piece, side):
        slot = piece % SLOTS
        return pltpu.make_async_remote_copy(
            src_ref=made.at[slot, side, 1 - c],
            dst_ref=near.at[slot, side],
            send_sem=near_send.at[slot, side],
            recv_sem=near_recv.at[slot, side],
            device_id=peers["core"],
            device_id_type=MESH,
        )

    def left_copy(place):
        rows = left_refs[place].shape[0]
        return pltpu.make_async_copy(
            left_refs[place], left.at[place, pl.ds(0, rows)], left_sem.at[place]
        )

    def turn_left(place, at):
        rows = left_refs[place].shape[0]
        left_copy(place).wait()
        left_t[at, :, :rows] = left[place, :rows].T

    def sources(layer, part, head, half):
        column = first_column(head // 2, head % 2, part * PIECE_COLS + (128 * half if part == 2 else 0))
        if part < 2:
            column += 128 * half
        for at, (left_place, right_place, start, stop) in enumerate(plan[layer][0]):
            if start <= column < stop:
                return left_place, right_place, column - start

    def right_copies(piece, layer, part):
        copies = []
        for head in range(4):
            for half in range(2):
                left_place, right_place, column = sources(layer, part, head, half)
                rows = right_refs[right_place].shape[0]
                copies.append(
                    pltpu.make_async_copy(
                        right_refs[right_place].at[:, pl.ds(column, 128)],
                        right.at[piece % 2, head, pl.ds(0, rows), pl.ds(128 * half, 128)],
                        right_sem.at[piece % 2, head, half],
                    )
                )
        return copies

    def right_copy(piece, right_place, head):
        start = head * D + (piece % per_group) * PIECE_COLS
        return pltpu.make_async_copy(
            right_refs[right_place].at[:, pl.ds(pl.multiple_of(start, PIECE_COLS), PIECE_COLS)],
            right.at[piece % 2, head],
            right_sem.at[piece % 2, head, 0],
        )

    def fetch(piece):
        for layer in range(layers):
            for part in range(per_group):

                @pl.when(piece == 3 * layer * per_group + part)
                def _():
                    for copy in right_copies(piece, layer, part):
                        copy.start()

            for member in range(2):

                @pl.when(piece // per_group == 3 * layer + 1 + member)
                def _():
                    for head in range(4):
                        right_copy(piece, plan[layer][1 + member][1], head).start()

    def bring(piece):
        slot = piece % SLOTS
        for layer in range(layers):
            used = []
            for left_place, _, _, _ in plan[layer][0]:
                if left_place not in used:
                    used.append(left_place)

            @pl.when(piece == 3 * layer * per_group)
            def _():
                for at, left_place in enumerate(used):
                    turn_left(left_place, at)

            for part in range(per_group):

                @pl.when(piece == 3 * layer * per_group + part)
                def _():
                    for copy in right_copies(piece, layer, part):
                        copy.wait()
                    for head in range(4):
                        pair = [sources(layer, part, head, half) for half in range(2)]
                        spans = [(0, 2)] if pair[0][0] == pair[1][0] else [(0, 1), (1, 2)]
                        for first, stop in spans:
                            left_place, right_place, _ = pair[first]
                            rows = right_refs[right_place].shape[0]
                            columns = slice(128 * first, 128 * stop)
                            made[slot, head // 2, head % 2, :, :, :, :, columns] = dot_nn(
                                left_t[used.index(left_place), :, :rows],
                                right[piece % 2, head, :rows, columns],
                            ).reshape(shape[:-1] + (128 * (stop - first),))

            for member in range(2):

                @pl.when(piece == (3 * layer + 1 + member) * per_group)
                def _():
                    turn_left(plan[layer][1 + member][0], 0)

        @pl.when((piece // per_group) % 3 != 0)
        def _():
            for head in range(4):
                right_copy(piece, plan[0][1][1], head).wait()
            for head in range(4):
                made[slot, head // 2, head % 2] = dot_nn(
                    left_t[0], right[piece % 2, head]
                ).reshape(shape)

        for side in range(2):
            near_copy(piece, side).start()

    def hop(piece, step, stream):
        slot = piece % SLOTS
        sent, got = (send_a, got_a) if stream == 0 else (send_b, got_b)
        return pltpu.make_async_remote_copy(
            src_ref=sent[step].at[slot],
            dst_ref=got[step].at[slot],
            send_sem=hop_send.at[step, stream, slot],
            recv_sem=hop_recv.at[step, stream, slot],
            device_id=peers[order[step][stream]],
            device_id_type=MESH,
        )

    def first(piece):
        slot = piece % SLOTS
        for side in range(2):
            near_copy(piece, side).wait()

        def total(side, *index):
            return made[(slot, side, c) + index] + near[(slot, side) + index]

        send_a[0][slot] = to_bf16(total(1 - y, every, every, every, top))
        hop(piece, 0, 0).start()
        send_b[0][slot] = to_bf16(total(every, every, every, 1 - x, bottom))
        hop(piece, 0, 1).start()
        keep_a[0][slot] = total(y, every, every, every, top)
        keep_b[0][slot] = total(every, every, every, x, bottom)

    cut_a = (None, (2, x), (1, zl), (0, zh))
    cut_b = (None, (2, zl), (1, zh), (0, y))

    def later(piece, step):
        slot = piece % SLOTS
        for stream in range(2):
            keep, got, sent = (keep_a, got_a, send_a) if stream == 0 else (keep_b, got_b, send_b)
            axis, mine = (cut_a if stream == 0 else cut_b)[step]
            hop(piece, step - 1, stream).wait()

            def total(which):
                index = (slot,) + (every,) * axis + (which,)
                return keep[step - 1][index] + got[step - 1][index].astype(jnp.float32)

            sent[step][slot] = to_bf16(total(1 - mine))
            hop(piece, step, stream).start()
            keep[step][slot] = total(mine)

    def last(piece):
        slot = piece % SLOTS
        for stream in range(2):
            keep, got = (keep_a, got_a) if stream == 0 else (keep_b, got_b)
            hop(piece, 3, stream).wait()
            out_ref[piece, top if stream == 0 else bottom, :] = keep[3][slot] + got[3][
                slot
            ].astype(jnp.float32)

    for place in range(lefts):
        left_copy(place).start()
    fetch(0)
    fetch(1)
    bring(0)
    fetch(2)
    bring(1)

    @pl.loop(0, pieces + 4)
    def _(turn):
        @pl.when(turn + 3 < pieces)
        def _():
            fetch(turn + 3)

        @pl.when(turn < pieces)
        def _():
            first(turn)

        for step in (1, 2, 3):

            @pl.when((turn >= step) & (turn - step < pieces))
            def _():
                later(turn - step, step)

        @pl.when(turn >= 4)
        def _():
            last(turn - 4)

        @pl.when(turn + 2 < pieces)
        def _():
            bring(turn + 2)

    edges = []
    for layer in range(layers):
        piece = (3 * layer + 1) * per_group - 1
        edges.append(
            pltpu.make_async_remote_copy(
                src_ref=out_ref.at[piece, :, pl.ds(0, 128)],
                dst_ref=edge_ref.at[layer],
                send_sem=edge_send.at[layer],
                recv_sem=edge_recv.at[layer],
                device_id=peers["core"],
                device_id_type=MESH,
            )
        )
        edges[-1].start()

    squares = jnp.zeros((rows_own, PIECE_COLS), jnp.float32)
    for piece in range(pieces):
        squares = squares + out_ref[piece] * out_ref[piece]
    row = lax.broadcasted_iota(jnp.int32, (8, 128), 0)
    column = lax.broadcasted_iota(jnp.int32, (8, 128), 1)
    mine[0] = extra_ref[...] + jnp.where((row == 0) & (column == 0), jnp.sum(squares), 0.0)
    for phase, (got, me, count) in enumerate(((head_got, h, 4), (data_got, d, 8))):
        copies = []
        for other in range(1, count):
            place = 3 * phase + other - 1
            copies.append(
                pltpu.make_async_remote_copy(
                    src_ref=mine.at[phase],
                    dst_ref=got.at[me],
                    send_sem=sum_send.at[place],
                    recv_sem=sum_recv.at[place],
                    device_id=across[place],
                    device_id_type=MESH,
                )
            )
            copies[-1].start()
        got[me] = mine[phase]
        for copy in copies:
            copy.wait()
        total = got[0]
        for other in range(1, count):
            total = total + got[other]
        if phase == 0:
            mine[1] = total
        else:
            total_ref[...] = total
    for copy in edges:
        copy.wait()


def reduce_whole(plan, lefts, rights, extra, collective_id):
    layers = len(plan)
    frames = lefts[0].shape[0]
    rows = D // 8
    per_group = D // PIECE_COLS
    pieces = 3 * layers * per_group
    leads = ((2, 2, 2), (2, 2), (2,), ())

    def buffers(count, dtype):
        return [pltpu.VMEM((SLOTS,) + lead + (count, PIECE_COLS), dtype) for lead in leads]

    bottom_rows = rows - ROWS_A
    blocks = (2, 2, 2, rows, PIECE_COLS)
    low = jnp.bfloat16
    summed, totals, edges = pl.pallas_call(
        functools.partial(reduce_kernel, plan, len(lefts), len(rights)),
        out_shape=[
            jax.ShapeDtypeStruct((pieces, rows, PIECE_COLS), jnp.float32),
            jax.ShapeDtypeStruct((8, 128), jnp.float32),
            jax.ShapeDtypeStruct((layers, rows, 128), jnp.float32),
        ],
        in_specs=[anywhere()] * (len(lefts) + len(rights)) + [vmem()],
        out_specs=[vmem()] * 3,
        scratch_shapes=[
            pltpu.VMEM((SLOTS, 2, 2) + blocks, jnp.float32),
            pltpu.VMEM((SLOTS, 2) + blocks, jnp.float32),
            pltpu.VMEM((len(lefts), frames, D), low),
            pltpu.VMEM((3, D, frames), low),
            pltpu.VMEM((2, 4, frames, PIECE_COLS), low),
            buffers(ROWS_A, low),
            buffers(bottom_rows, low),
            buffers(ROWS_A, low),
            buffers(bottom_rows, low),
            buffers(ROWS_A, jnp.float32),
            buffers(bottom_rows, jnp.float32),
            pltpu.VMEM((2, 8, 128), jnp.float32),
            pltpu.VMEM((4, 8, 128), jnp.float32),
            pltpu.VMEM((8, 8, 128), jnp.float32),
            pltpu.SemaphoreType.DMA((SLOTS, 2)),
            pltpu.SemaphoreType.DMA((SLOTS, 2)),
            pltpu.SemaphoreType.DMA((4, 2, SLOTS)),
            pltpu.SemaphoreType.DMA((4, 2, SLOTS)),
            pltpu.SemaphoreType.DMA((len(lefts),)),
            pltpu.SemaphoreType.DMA((2, 4, 2)),
            pltpu.SemaphoreType.DMA((layers,)),
            pltpu.SemaphoreType.DMA((layers,)),
            pltpu.SemaphoreType.DMA((10,)),
            pltpu.SemaphoreType.DMA((10,)),
        ],
        compiler_params=comm_params(collective_id),
        name="reduce_grads",
    )(*lefts, *rights, extra)
    summed = summed.reshape(3 * layers, per_group, rows, PIECE_COLS).transpose(0, 2, 1, 3)
    return list(summed.reshape(3 * layers, rows, D)), totals, edges


def reduce_general(part):
    data_count, head_count = lax.axis_size("dp"), lax.axis_size("head")
    blocks = part.reshape(
        data_count, part.shape[0] // data_count, head_count, part.shape[1] // head_count
    ).transpose(0, 2, 1, 3)
    blocks = blocks.reshape((-1,) + blocks.shape[2:])
    return lax.psum_scatter(blocks, ("dp", "head"), scatter_dimension=0, tiled=True)[0]


KIND_AT = (1, 2, 3, 0)


def owner_of(kind, layer):
    return 4 * layer + KIND_AT.index(kind)


def is_owner_of(me, kind):
    return (me % 4 == KIND_AT.index(kind)) & (me < 8)


def to_owner_kernel(count, *refs):
    block_refs, out_ref, send_sem, recv_sem = refs[:4], refs[4], refs[5], refs[6]
    me = lax.axis_index("dp")
    out_ref[...] = jnp.zeros_like(out_ref)
    greet([{"dp": lax.rem(me + shift, count)} for shift in range(1, count)])

    def copy(kind, layer, source):
        width = block_refs[kind].shape[-1]
        return pltpu.make_async_remote_copy(
            src_ref=block_refs[kind].at[layer],
            dst_ref=out_ref.at[source, :, pl.ds(0, width)],
            send_sem=send_sem.at[2 * kind + layer],
            recv_sem=recv_sem.at[source],
            device_id={"dp": owner_of(kind, layer)},
            device_id_type=MESH,
        )

    for kind in range(4):
        for layer in range(2):

            @pl.when(me != owner_of(kind, layer))
            def _():
                copy(kind, layer, me).start()

            @pl.when(me == owner_of(kind, layer))
            def _():
                out_ref[me, :, : block_refs[kind].shape[-1]] = block_refs[kind][layer]

    for kind in range(4):

        @pl.when(is_owner_of(me, kind))
        def _():
            @pl.loop(0, count)
            def _(source):
                @pl.when(source != me)
                def _():
                    copy(kind, 0, source).wait_recv()

        for layer in range(2):

            @pl.when(me != owner_of(kind, layer))
            def _():
                copy(kind, layer, me).wait_send()


def to_owner(blocks, collective_id):
    count = lax.axis_size("dp")
    rows = blocks[0].shape[1]
    wide = max(block.shape[2] for block in blocks)
    return pl.pallas_call(
        functools.partial(to_owner_kernel, count),
        out_shape=jax.ShapeDtypeStruct((count, rows, wide), jnp.float32),
        in_specs=[vmem()] * 4,
        out_specs=vmem(),
        scratch_shapes=[pltpu.SemaphoreType.DMA((8,)), pltpu.SemaphoreType.DMA((count,))],
        compiler_params=comm_params(collective_id),
        name="to_owner",
    )(*blocks)


def from_owner_kernel(count, widths, x_ref, out_ref, send_sem, recv_sem):
    me = lax.axis_index("dp")
    greet([{"dp": lax.rem(me + shift, count)} for shift in range(1, count)])

    def copy(kind, matrix, target):
        columns = pl.ds(0, widths[kind])
        return pltpu.make_async_remote_copy(
            src_ref=x_ref.at[target, :, columns],
            dst_ref=out_ref.at[matrix, :, columns],
            send_sem=send_sem.at[target],
            recv_sem=recv_sem.at[matrix],
            device_id={"dp": target},
            device_id_type=MESH,
        )

    for kind in range(4):

        @pl.when(is_owner_of(me, kind))
        def _():
            @pl.loop(0, count)
            def _(target):
                @pl.when(target != me)
                def _():
                    copy(kind, me, target).start()

            out_ref[me] = x_ref[me]

    for kind in range(4):
        for layer in range(2):
            matrix = owner_of(kind, layer)

            @pl.when(me != matrix)
            def _():
                copy(kind, matrix, me).wait_recv()

        @pl.when(is_owner_of(me, kind))
        def _():
            @pl.loop(0, count)
            def _(target):
                @pl.when(target != me)
                def _():
                    copy(kind, me, target).wait_send()


def from_owner(x, widths, collective_id):
    count = lax.axis_size("dp")
    return pl.pallas_call(
        functools.partial(from_owner_kernel, count, widths),
        out_shape=jax.ShapeDtypeStruct((8,) + x.shape[1:], x.dtype),
        in_specs=[vmem()],
        out_specs=vmem(),
        scratch_shapes=[pltpu.SemaphoreType.DMA((count,)), pltpu.SemaphoreType.DMA((8,))],
        compiler_params=comm_params(collective_id),
        name="from_owner",
    )(x)


def gram_kernel(x_ref, out_ref, high, rest, upper, chip, got, whole, send_sem, recv_sem):
    h = lax.axis_index("head")
    c = h % 2
    greet([{"head": h ^ other} for other in (1, 2)])
    third = PIECE_COLS
    values = x_ref[...]
    high[...] = to_bf16(values)
    rest[...] = to_bf16(values - high[...].astype(jnp.float32))

    def dots(first, second):
        return (
            dot_nt(high[first], high[second])
            + dot_nt(high[first], rest[second])
            + dot_nt(rest[first], high[second])
        )

    r0, r1, r2 = (pl.ds(third * place, third) for place in range(3))
    upper[0] = dots(r0, pl.ds(0, 3 * third))
    upper[1, :, : 2 * third] = dots(r1, pl.ds(third, 2 * third))
    upper[1, :, 2 * third :] = dots(r2, r2)

    def step(place, source, target, peer):
        copy = send_to(source, target, (send_sem, recv_sem), place, peer)
        copy.start()
        copy.wait()

    step(0, upper.at[1 - c], got.at[0], h ^ 1)
    chip[...] = upper[c] + got[0]
    step(1, chip, got.at[1], h ^ 2)
    whole[c] = chip[...] + got[1]
    step(2, whole.at[c], whole.at[c], h ^ 1)
    out_ref[r0, :] = whole[0]
    out_ref[r1, pl.ds(third, 2 * third)] = whole[1, :, : 2 * third]
    out_ref[r2, r2] = whole[1, :, 2 * third :]
    out_ref[r1, r0] = whole[0, :, third : 2 * third].T
    out_ref[r2, r0] = whole[0, :, 2 * third :].T
    out_ref[r2, r1] = whole[1, :, third : 2 * third].T


def gram_sum(x, collective_id):
    rows, columns = x.shape
    third = PIECE_COLS
    return pl.pallas_call(
        gram_kernel,
        out_shape=jax.ShapeDtypeStruct((rows, rows), jnp.float32),
        in_specs=[vmem()],
        out_specs=vmem(),
        scratch_shapes=[
            pltpu.VMEM((rows, columns), jnp.bfloat16),
            pltpu.VMEM((rows, columns), jnp.bfloat16),
            pltpu.VMEM((2, third, rows), jnp.float32),
            pltpu.VMEM((third, rows), jnp.float32),
            pltpu.VMEM((2, third, rows), jnp.float32),
            pltpu.VMEM((2, third, rows), jnp.float32),
            pltpu.SemaphoreType.DMA((3,)),
            pltpu.SemaphoreType.DMA((3,)),
        ],
        compiler_params=comm_params(collective_id),
        name="gram_sum",
    )(x)


def send_to(source, target, sems, place, peer):
    return pltpu.make_async_remote_copy(
        src_ref=source,
        dst_ref=target,
        send_sem=sems[0].at[place],
        recv_sem=sems[1].at[place],
        device_id={"head": peer},
        device_id_type=MESH,
    )


def half_mask(half):
    lane = lax.broadcasted_iota(jnp.int32, (1, 128), 1)
    return (lane // 64) == half


def dot_nt(left, right):
    return lax.dot_general(
        left, right, (((1,), (1,)), ((), ())), preferred_element_type=jnp.float32
    )


def dot_nn(left, right):
    return lax.dot_general(
        left, right, (((1,), (0,)), ((), ())), preferred_element_type=jnp.float32
    )


def dot_tn(left, right):
    return lax.dot_general(
        left, right, (((0,), (0,)), ((), ())), preferred_element_type=jnp.float32
    )


def lanes(start, size):
    return pl.ds(pl.multiple_of(start, 128), size)


def window(head):
    return 128 * ((3 * head) // 2)


def bring_heads(h, rows_ref, pair_all, quad_all, parts, sems):
    c = h % 2
    tile = quad_all.shape[1]
    own, shared = pl.ds(0, 2 * tile), pl.ds(2 * tile, tile)
    pair, quad = [], []
    for part in range(parts):
        pair.append(
            send_to(
                rows_ref.at[own, lanes(part * D + (1 - c) * HALF, HALF)],
                pair_all.at[c, :, pl.ds(part * HALF, HALF)],
                sems, part, h ^ 1,
            )
        )
        for other in (1, 2, 3):
            quad.append(
                send_to(
                    rows_ref.at[shared, lanes(part * D + window(h ^ other), WIDE)],
                    quad_all.at[h, :, pl.ds(part * WIDE, WIDE)],
                    sems, 3 * other + part, h ^ other,
                )
            )
    for copy in pair + quad:
        copy.start()
    for part in range(parts):
        pair_all[c, :, part * HALF : (part + 1) * HALF] = rows_ref[
            own, lanes(part * D + c * HALF, HALF)
        ]
        quad_all[h, :, part * WIDE : (part + 1) * WIDE] = rows_ref[
            shared, lanes(part * D + window(h), WIDE)
        ]
    return pair, quad


def return_pair(h, pair_out, rows_ref, parts, sems):
    c = h % 2
    own = pl.ds(0, pair_out.shape[1])
    copies = []
    for part in range(parts):
        columns = lanes(part * D + c * HALF, HALF)
        copies.append(
            send_to(
                pair_out.at[1 - c, :, pl.ds(part * HALF, HALF)], rows_ref.at[own, columns],
                sems, 12 + part, h ^ 1,
            )
        )
        copies[-1].start()
        rows_ref[own, columns] = pair_out[c, :, part * HALF : (part + 1) * HALF]
    return copies


def return_quad(h, quad_out, quad_got, sems):
    copies = []
    for other in (1, 2, 3):
        copies.append(
            send_to(quad_out.at[h ^ other], quad_got.at[h], sems, 14 + other, h ^ other)
        )
        copies[-1].start()
    quad_got[h] = quad_out[h]
    return copies


def merge_quad(quad_got, rows_ref, parts):
    tile = quad_got.shape[1]
    shared = slice(2 * tile, 3 * tile)
    for part in range(parts):
        base, start = part * WIDE, part * D
        for side in range(2):
            left, right = quad_got.at[2 * side], quad_got.at[2 * side + 1]
            at = start + side * HALF
            rows_ref[shared, at : at + 128] = left[:, base : base + 128]
            rows_ref[shared, at + 128 : at + 256] = (
                left[:, base + 128 : base + 256] + right[:, base : base + 128]
            )
            rows_ref[shared, at + 256 : at + 384] = right[:, base + 128 : base + 256]


def attend_kernel(rows_ref, mixed_ref, pair_all, quad_all, log_ref, pair_out, quad_out, quad_got,
                  send_sem, recv_sem):
    h = lax.axis_index("head")
    sems = (send_sem, recv_sem)
    greet([{"head": h ^ other} for other in (1, 2, 3)])
    pair_copies, quad_copies = bring_heads(h, rows_ref, pair_all, quad_all, 3, sems)
    tile = quad_all.shape[1]
    length = 4 * tile
    lane = lax.broadcasted_iota(jnp.int32, (1, 128), 1)

    def one_head(query, keys, values, mask):
        scores = dot_nt(jnp.where(mask, query, 0) * 0.125, keys)
        top = jnp.max(scores, -1, keepdims=True)
        exponent = jnp.exp(scores - top)
        total = jnp.sum(exponent, -1, keepdims=True)
        probability = to_bf16(exponent * (1.0 / total))
        return dot_nn(probability, jnp.where(mask, values, 0)), top + jnp.log(total)

    log_ref[...] = jnp.zeros_like(log_ref)
    quad_out[...] = jnp.zeros_like(quad_out)
    for copy in pair_copies:
        copy.wait()
    for pair in range(3):
        keys = pair_all[:, :, HALF + pair * 128 : HALF + pair * 128 + 128].reshape(length, 128)
        values = pair_all[:, :, 2 * HALF + pair * 128 : 2 * HALF + pair * 128 + 128].reshape(
            length, 128
        )
        for row in range(4):
            rows = slice((row % 2) * tile, (row % 2 + 1) * tile)
            out_rows = slice(row * tile, (row + 1) * tile)
            query = pair_all[row // 2, rows, pair * 128 : pair * 128 + 128]
            mixed = jnp.zeros((tile, 128), jnp.float32)
            logs = log_ref[out_rows, :]
            for half in range(2):
                part, log_total = one_head(query, keys, values, half_mask(half))
                mixed = mixed + part
                logs = jnp.where(lane == 2 * pair + half, log_total, logs)
            log_ref[out_rows, :] = logs
            pair_out[row // 2, rows, pair * 128 : pair * 128 + 128] = to_bf16(mixed)
    back = return_pair(h, pair_out, mixed_ref, 1, sems)
    for copy in quad_copies:
        copy.wait()
    for member in range(3):
        place = h % 2 + member
        mask = half_mask(place % 2)
        at = (place // 2) * 128
        keys = quad_all[:, :, lanes(WIDE + at, 128)].reshape(length, 128)
        values = quad_all[:, :, lanes(2 * WIDE + at, 128)].reshape(length, 128)
        for row in range(4):
            out_rows = slice(row * tile, (row + 1) * tile)
            mixed, log_total = one_head(quad_all[row, :, lanes(at, 128)], keys, values, mask)
            log_ref[out_rows, :] = jnp.where(lane == 6 + member, log_total, log_ref[out_rows, :])
            quad_out[row, :, lanes(at, 128)] += to_bf16(mixed)
    back_quad = return_quad(h, quad_out, quad_got, sems)
    for copy in back + back_quad:
        copy.wait()
    merge_quad(quad_got, mixed_ref, 1)


def attend(rows, collective_id):
    frames = rows.shape[0]
    tile = frames // 3
    low = jnp.bfloat16
    return pl.pallas_call(
        attend_kernel,
        out_shape=[
            jax.ShapeDtypeStruct((frames, D), low),
            jax.ShapeDtypeStruct((2, 2 * tile, 3 * HALF), low),
            jax.ShapeDtypeStruct((4, tile, 3 * WIDE), low),
            jax.ShapeDtypeStruct((4 * tile, 128), jnp.float32),
        ],
        in_specs=[vmem()],
        out_specs=[vmem()] * 4,
        scratch_shapes=[
            pltpu.VMEM((2, 2 * tile, HALF), low),
            pltpu.VMEM((4, tile, WIDE), low),
            pltpu.VMEM((4, tile, WIDE), low),
            pltpu.SemaphoreType.DMA((18,)),
            pltpu.SemaphoreType.DMA((18,)),
        ],
        compiler_params=comm_params(collective_id),
        name="attend",
    )(rows)


def attend_back_kernel(pair_all, quad_all, log_ref, grad_ref, rows_ref, pair_mixed, quad_mixed,
                       pair_out, quad_out, quad_got, grad_keys, grad_values, send_sem, recv_sem):
    h = lax.axis_index("head")
    sems = (send_sem, recv_sem)
    greet([{"head": h ^ other} for other in (1, 2, 3)])
    pair_copies, quad_copies = bring_heads(h, grad_ref, pair_mixed, quad_mixed, 1, sems)
    tile = quad_all.shape[1]
    length = 4 * tile
    lane = lax.broadcasted_iota(jnp.int32, (1, 128), 1)

    def one_head(query, keys, values, grad_out, mask, out_rows, log_lane):
        log_total = jnp.sum(
            jnp.where(lane == log_lane, log_ref[out_rows, :], 0.0), -1, keepdims=True
        )
        query = jnp.where(mask, query, 0) * 0.125
        grad_out = jnp.where(mask, grad_out, 0)
        probability = jnp.exp(dot_nt(query, keys) - log_total)
        grad_prob = dot_nt(grad_out, values)
        mean = jnp.sum(probability * grad_prob, -1, keepdims=True)
        grad_scores = to_bf16(probability * (grad_prob - mean))
        grad_keys[...] += dot_tn(grad_scores, query)
        grad_values[...] += dot_tn(to_bf16(probability), grad_out)
        return dot_nn(grad_scores, jnp.where(mask, keys, 0)) * 0.125

    quad_out[...] = jnp.zeros_like(quad_out)
    for copy in pair_copies:
        copy.wait()
    for pair in range(3):
        at = [part * HALF + pair * 128 for part in range(3)]
        keys = pair_all[:, :, at[1] : at[1] + 128].reshape(length, 128)
        values = pair_all[:, :, at[2] : at[2] + 128].reshape(length, 128)
        grad_keys[...] = jnp.zeros_like(grad_keys)
        grad_values[...] = jnp.zeros_like(grad_values)
        for row in range(4):
            rows = slice((row % 2) * tile, (row % 2 + 1) * tile)
            query = pair_all[row // 2, rows, at[0] : at[0] + 128]
            grad_out = pair_mixed[row // 2, rows, at[0] : at[0] + 128]
            grad_query = jnp.zeros((tile, 128), jnp.float32)
            for half in range(2):
                grad_query = grad_query + one_head(
                    query, keys, values, grad_out, half_mask(half),
                    slice(row * tile, (row + 1) * tile), 2 * pair + half,
                )
            pair_out[row // 2, rows, at[0] : at[0] + 128] = to_bf16(grad_query)
        for part, total in ((1, grad_keys), (2, grad_values)):
            pair_out[:, :, at[part] : at[part] + 128] = to_bf16(total[...]).reshape(
                2, 2 * tile, 128
            )
    back = return_pair(h, pair_out, rows_ref, 3, sems)
    for copy in quad_copies:
        copy.wait()
    for member in range(3):
        place = h % 2 + member
        mask = half_mask(place % 2)
        at = (place // 2) * 128
        keys = quad_all[:, :, lanes(WIDE + at, 128)].reshape(length, 128)
        values = quad_all[:, :, lanes(2 * WIDE + at, 128)].reshape(length, 128)
        grad_keys[...] = jnp.zeros_like(grad_keys)
        grad_values[...] = jnp.zeros_like(grad_values)
        for row in range(4):
            grad_query = one_head(
                quad_all[row, :, lanes(at, 128)], keys, values, quad_mixed[row, :, lanes(at, 128)],
                mask, slice(row * tile, (row + 1) * tile), 6 + member,
            )
            quad_out[row, :, lanes(at, 128)] += to_bf16(grad_query)
        for part, total in ((1, grad_keys), (2, grad_values)):
            quad_out[:, :, lanes(part * WIDE + at, 128)] += to_bf16(total[...]).reshape(
                4, tile, 128
            )
    back_quad = return_quad(h, quad_out, quad_got, sems)
    for copy in back + back_quad:
        copy.wait()
    merge_quad(quad_got, rows_ref, 3)


def attend_back(pair_all, quad_all, logs, grad_mixed, collective_id):
    rows, tile = pair_all.shape[1], quad_all.shape[1]
    low = jnp.bfloat16
    return pl.pallas_call(
        attend_back_kernel,
        out_shape=jax.ShapeDtypeStruct((3 * tile, 3 * D), low),
        in_specs=[vmem()] * 4,
        out_specs=vmem(),
        scratch_shapes=[
            pltpu.VMEM((2, rows, HALF), low),
            pltpu.VMEM((4, tile, WIDE), low),
            pltpu.VMEM(pair_all.shape, low),
            pltpu.VMEM(quad_all.shape, low),
            pltpu.VMEM(quad_all.shape, low),
            pltpu.VMEM((4 * tile, 128), jnp.float32),
            pltpu.VMEM((4 * tile, 128), jnp.float32),
            pltpu.SemaphoreType.DMA((18,)),
            pltpu.SemaphoreType.DMA((18,)),
        ],
        compiler_params=comm_params(collective_id),
        name="attend_back",
    )(pair_all, quad_all, logs, grad_mixed)


def masked_scores(query_half, keys, keep):
    return jnp.where(keep, dot_nt(query_half, keys) * 0.125, -1e30)


def cross_kernel(query_ref, keys_ref, values_ref, len_ref, out_ref):
    tile = query_ref.shape[1]
    tokens = keys_ref.shape[1]
    token = lax.broadcasted_iota(jnp.int32, (1, tokens), 1)
    for row in range(3):
        clip = row // 2
        keep = token < len_ref[clip]
        keys, values = keys_ref[clip], values_ref[clip]
        mixed = jnp.zeros((tile, 128), jnp.float32)
        for half in range(2):
            mask = half_mask(half)
            scores = masked_scores(jnp.where(mask, query_ref[row], 0), keys, keep)
            exponent = jnp.exp(scores - jnp.max(scores, -1, keepdims=True))
            probability = to_bf16(exponent / jnp.sum(exponent, -1, keepdims=True))
            mixed = mixed + dot_nn(probability, jnp.where(mask, values, 0))
        out_ref[row] = to_bf16(mixed)


def cross(query, pair_kv, lengths):
    _, tile, width = query.shape
    blocks = width // 128
    tokens = pair_kv.shape[1]
    return pl.pallas_call(
        cross_kernel,
        grid=(blocks,),
        out_shape=jax.ShapeDtypeStruct(query.shape, jnp.bfloat16),
        in_specs=[
            pl.BlockSpec((3, tile, 128), lambda i: (0, 0, i)),
            pl.BlockSpec((2, tokens, 128), lambda i: (0, 0, i)),
            pl.BlockSpec((2, tokens, 128), lambda i: (0, 0, blocks + i)),
            pl.BlockSpec(memory_space=pltpu.SMEM),
        ],
        out_specs=pl.BlockSpec((3, tile, 128), lambda i: (0, 0, i)),
        compiler_params=pltpu.CompilerParams(vmem_limit_bytes=VMEM_BYTES),
        name="cross",
    )(query, pair_kv, pair_kv, lengths)


def cross_back_kernel(query_ref, keys_ref, values_ref, grad_ref, len_ref, grad_query_ref,
                      grad_keys_ref, grad_values_ref):
    tile = query_ref.shape[1]
    tokens = keys_ref.shape[1]
    token = lax.broadcasted_iota(jnp.int32, (1, tokens), 1)
    for clip in range(2):
        keep = token < len_ref[clip]
        keys, values = keys_ref[clip], values_ref[clip]
        grad_keys = jnp.zeros((tokens, 128), jnp.float32)
        grad_values = jnp.zeros((tokens, 128), jnp.float32)
        for row in range(2 * clip, 2 + clip):
            grad_query = jnp.zeros((tile, 128), jnp.float32)
            for half in range(2):
                mask = half_mask(half)
                query_half = jnp.where(mask, query_ref[row], 0)
                grad_half = jnp.where(mask, grad_ref[row], 0)
                scores = masked_scores(query_half, keys, keep)
                exponent = jnp.exp(scores - jnp.max(scores, -1, keepdims=True))
                probability = exponent / jnp.sum(exponent, -1, keepdims=True)
                grad_prob = dot_nt(grad_half, values)
                mean = jnp.sum(probability * grad_prob, -1, keepdims=True)
                grad_scores = to_bf16(probability * (grad_prob - mean))
                grad_query = grad_query + dot_nn(grad_scores, jnp.where(mask, keys, 0))
                grad_keys = grad_keys + dot_tn(grad_scores, query_half)
                grad_values = grad_values + dot_tn(to_bf16(probability), grad_half)
            grad_query_ref[row] = to_bf16(grad_query * 0.125)
        grad_keys_ref[clip] = to_bf16(grad_keys * 0.125)
        grad_values_ref[clip] = to_bf16(grad_values)


def cross_back(query, pair_kv, lengths, grad):
    _, tile, width = query.shape
    blocks = width // 128
    tokens = pair_kv.shape[1]
    rows_spec = pl.BlockSpec((3, tile, 128), lambda i: (0, 0, i))
    keys_spec = pl.BlockSpec((2, tokens, 128), lambda i: (0, 0, i))
    return pl.pallas_call(
        cross_back_kernel,
        grid=(blocks,),
        out_shape=[
            jax.ShapeDtypeStruct(query.shape, jnp.bfloat16),
            jax.ShapeDtypeStruct((2, tokens, width), jnp.bfloat16),
            jax.ShapeDtypeStruct((2, tokens, width), jnp.bfloat16),
        ],
        in_specs=[
            rows_spec,
            keys_spec,
            pl.BlockSpec((2, tokens, 128), lambda i: (0, 0, blocks + i)),
            rows_spec,
            pl.BlockSpec(memory_space=pltpu.SMEM),
        ],
        out_specs=[rows_spec, keys_spec, keys_spec],
        compiler_params=pltpu.CompilerParams(vmem_limit_bytes=VMEM_BYTES),
        name="cross_back",
    )(query, pair_kv, pair_kv, grad, lengths)


def body(
    clean_latents,
    noise_draw,
    timesteps,
    captions,
    cap_len,
    pairing,
    adam_step,
    qkv_weight,
    out_weight,
    up_weight,
    down_weight,
    ada_weight,
    time_weight,
    io_weight,
    qkv_moment,
    out_moment,
    up_moment,
    down_moment,
    ada_first,
    ada_second,
    time_first,
    time_second,
    io_first,
    io_second,
):
    data_count = lax.axis_size("dp")
    head_count = lax.axis_size("head")
    clip_count, tile, channels = clean_latents.shape
    length = tile * head_count
    rows_own = qkv_weight.shape[1]
    d, h = lax.axis_index("dp"), lax.axis_index("head")
    own_clip, core = h // 2, h % 2
    own_row = d * rows_own
    linked = data_count == 8 and rows_own == 96
    ids = iter(range(64))

    def swap(x, axis):
        return exchange(x, axis, True, next(ids))

    def spread(x, axis):
        return exchange(x, axis, False, next(ids))

    def by_tile(values):
        own = lax.dynamic_slice_in_dim(values, own_clip, 1, 0)
        return jnp.concatenate([own, own, values[2:3]])

    def by_clip(tiles):
        own = tiles[0:1] + tiles[1:2]
        none = jnp.zeros_like(own)
        return jnp.concatenate(
            [jnp.where(own_clip == 0, own, none), jnp.where(own_clip == 1, own, none), tiles[2:3]]
        )

    block = 3 * D // head_count
    share = D // head_count
    is_first = core == 0
    latents = jnp.concatenate([clean_latents, noise_draw], -1).transpose(0, 2, 1)
    latents = latents.reshape(-1, tile)

    def with_edge(qkv, out, edge):
        return jnp.where(
            is_first,
            jnp.concatenate([qkv, edge, out[..., :128]], -1),
            jnp.concatenate([qkv[..., 64:], edge, out], -1),
        )

    def without_edge(own, edge):
        qkv = jnp.where(
            is_first, own[..., :block], jnp.concatenate([edge, own[..., : block - 64]], -1)
        )
        out = jnp.where(
            is_first, jnp.concatenate([own[..., block + 64 :], edge], -1), own[..., block:]
        )
        return qkv, out

    keep_mask = jnp.arange(CAP)[None, :] < cap_len[:, None]
    cap_mean = product("ft,ftd->fd", keep_mask.astype(jnp.bfloat16), captions) / cap_len[
        :, None
    ].astype(jnp.float32)
    cap_unit = cap_mean * lax.rsqrt(jnp.mean(cap_mean * cap_mean, -1, keepdims=True) + 1e-06)
    own_captions = jnp.concatenate([lax.dynamic_slice_in_dim(captions, own_clip, 1, 0), captions[2:3]])
    own_lengths = jnp.concatenate([lax.dynamic_slice_in_dim(cap_len, own_clip, 1, 0), cap_len[2:3]])

    qkv_low, out_low = to_bf16(qkv_weight), to_bf16(out_weight)
    edge = jnp.where(is_first, out_low[..., 128:], qkv_low[..., :64])
    time_cols = time_weight.shape[1]
    io_cols = io_weight.shape[2]
    ada_cols = ada_weight.shape[2]
    ada_bf = to_bf16(ada_weight)
    io_flat = io_weight.transpose(1, 0, 2).reshape(rows_own, 2 * io_cols)
    small_own = jnp.pad(
        to_bf16(jnp.concatenate([time_weight, io_flat], 1)),
        ((0, 0), (0, WIDE - time_cols - 2 * io_cols)),
    )
    table_bf = to_bf16(time_table(timesteps, D))

    def listed(first_groups):
        listed_groups = [small_own]
        for layer in range(2):
            listed_groups.append(first_groups[layer])
            listed_groups.append(to_bf16(up_weight[layer]))
            listed_groups.append(to_bf16(down_weight[layer]))
        return listed_groups

    if linked:
        none = jnp.zeros_like(edge)
        edge = jnp.where(
            is_first, jnp.concatenate([edge, none], -1), jnp.concatenate([none, edge], -1)
        )
        shared = jnp.concatenate(
            [
                jnp.zeros((clip_count, D)),
                table_bf.astype(jnp.float32),
                cap_unit,
                jnp.zeros((16 - 3 * clip_count, D)),
            ]
        )
        gathered, latents_all, shared_all, mods = gather_whole(
            listed(with_edge(qkv_low, out_low, none)),
            (1, 4),
            edge,
            latents,
            jnp.pad(shared, ((0, 0), (0, head_count * WIDE - D))),
            jnp.pad(table_bf, ((0, 16 - clip_count), (0, 0))),
            ada_bf,
            next(ids),
        )
        start = (d // 2) * WIDE + (d % 2) * rows_own
        hidden_own = lax.dynamic_slice(
            shared_all, (0, 0, start), (data_count, clip_count, rows_own)
        ).reshape(-1, rows_own)
        table_own = lax.dynamic_slice(
            shared_all, (0, clip_count, own_row), (data_count, clip_count, rows_own)
        ).reshape(-1, rows_own)
        cap_all = shared_all[:, 2 * clip_count : 3 * clip_count, :D].reshape(-1, D)
        signal_own = to_bf16(double_silu(hidden_own))
        mods = mods[:, :clip_count]
    else:
        edge = lax.ppermute(edge, "head", [(place, place ^ 1) for place in range(head_count)])
        gathered = [gather_general(own) for own in listed(with_edge(qkv_low, out_low, edge))]
        latents_all = spread(latents, "head")
        time_full = gathered[0].reshape(D, head_count, WIDE)[:, :, :time_cols].reshape(D, D)
        time_hidden = jnp.dot(table_bf, time_full, preferred_element_type=jnp.float32)
        shared = jnp.concatenate([time_hidden, table_bf.astype(jnp.float32), cap_unit], 1)
        shared_all = spread(shared, "dp").reshape(-1, 3 * D)
        hidden_own = lax.dynamic_slice_in_dim(shared_all, own_row, rows_own, 1)
        table_own = lax.dynamic_slice_in_dim(shared_all, D + own_row, rows_own, 1)
        cap_all = shared_all[:, 2 * D :]
        signal_own = to_bf16(double_silu(hidden_own))
        mod_part = product("fd,ldn->fln", signal_own, ada_bf)
        mod_part = mod_part.reshape(data_count, clip_count, 2 * ada_cols)
        mods = spread(jnp.sum(swap(mod_part, "dp"), 0), "head")
    up_full = [gathered[2], gathered[5]]
    down_full = [gathered[3], gathered[6]]
    io_full = (
        gathered[0]
        .reshape(D, head_count, WIDE)[:, :, time_cols : time_cols + 2 * io_cols]
        .reshape(D, head_count, 2, io_cols)
        .transpose(2, 0, 1, 3)
        .reshape(2, D, channels)
    )
    mod_all = (
        mods.reshape(head_count, clip_count, 2, ada_cols)
        .transpose(1, 2, 0, 3)
        .reshape(clip_count, 2, 6 * D)
    )
    tile_mods = by_tile(mod_all)

    def split_first(whole):
        qkv, out = [], []
        for side in range(2):
            at = 2 * side * D
            qkv += [whole[:, at : at + 640], whole[:, at + D : at + D + 512]]
            out += [whole[:, at + 640 : at + D], whole[:, at + D + 512 : at + 2 * D]]
        return jnp.concatenate(qkv, 1), jnp.concatenate(out, 1)

    def join_first(qkv, out):
        columns = []
        for side in range(2):
            q, o = side * 2 * block, side * 2 * share
            columns += [qkv[:, q : q + 640], out[:, o : o + 128]]
            columns += [qkv[:, q + 640 : q + 1152], out[:, o + 128 : o + 384]]
        return jnp.concatenate(columns, 1)

    if linked:
        qkv_full = [gathered[1 + 3 * layer][:, : 3 * D] for layer in range(2)]
        out_full = [gathered[1 + 3 * layer][:, 3 * D :] for layer in range(2)]
    else:
        qkv_full, out_full = zip(*[split_first(gathered[1 + 3 * layer]) for layer in range(2)])

    latents_all = latents_all.reshape(head_count, clip_count, 2 * channels, tile)
    own_latents = lax.dynamic_slice(
        latents_all, (2 * core, own_clip, 0, 0), (2, 1, 2 * channels, tile)
    )[:, 0]
    latents = jnp.concatenate(
        [own_latents, lax.dynamic_slice_in_dim(latents_all, h, 1, 0)[0, 2:3]]
    )
    clean_rows, noise_rows = latents[:, :channels], latents[:, channels:]
    tile_times = by_tile(timesteps)[:, None, None]
    input_bf = to_bf16((1.0 - tile_times) * clean_rows + tile_times * noise_rows)
    target = noise_rows - clean_rows
    hidden = product("fcl,dc->fld", input_bf, io_full[0])

    frames = clip_count * tile

    def layer_forward(layer_index, hidden):
        modulation = tile_mods[:, layer_index].reshape(clip_count, 1, 6, D)
        mod_parts = [modulation[:, :, member] for member in range(6)]
        normed = to_bf16(modulate(hidden, mod_parts[0], mod_parts[1]))
        weight = qkv_full[layer_index]
        if layer_index == 0:
            projected = to_bf16(product("fld,dn->fln", normed, weight))
            mixed, *attended = attend(projected.reshape(frames, 3 * D), next(ids))
            mixed = mixed.reshape(clip_count, tile, D)
        else:
            query = to_bf16(product("fld,dn->fln", normed, weight[:, :D]))
            pair_kv = to_bf16(product("ftd,dn->ftn", own_captions, weight[:, D:]))
            attended = (query, pair_kv)
            mixed = cross(query, pair_kv, own_lengths)
        branch = product("fle,de->fld", mixed, out_full[layer_index])
        middle = hidden + mod_parts[2] * branch
        normed2 = to_bf16(modulate(middle, mod_parts[3], mod_parts[4]))
        upper = product("fld,dn->fln", normed2, up_full[layer_index])
        active = to_bf16(soft_gelu(upper))
        down_out = product("fln,dn->fld", active, down_full[layer_index])
        kept = (hidden, mod_parts, normed, attended, mixed, branch, middle, normed2, upper,
                active, down_out)
        return (middle + mod_parts[5] * down_out, kept)

    saved_layers = []
    for layer_index in range(2):
        hidden, kept = layer_forward(layer_index, hidden)
        saved_layers.append(kept)
    final = norm_rows(hidden)
    final_bf = to_bf16(final)
    predicted = product("fld,dc->fcl", final_bf, io_full[1])
    errors = predicted - target
    flow_part = jnp.sum(jnp.mean(errors * errors, 1))
    grad_pred = to_bf16(2.0 * errors / channels)
    pool_sum = jnp.sum(spread(by_clip(jnp.sum(final, 1)), "head"), 0)
    pooled_out = pool_sum / length

    def contrast_of(pool_total):
        pooled = pool_total / length
        unit_rows = pooled * lax.rsqrt(jnp.mean(pooled * pooled, -1, keepdims=True) + 1e-06)
        logits = exact_product("id,jd->ij", unit_rows, cap_all) * (2.0 / math.sqrt(D))
        row_top = jnp.max(logits, -1, keepdims=True)
        log_total = row_top[:, 0] + jnp.log(jnp.sum(jnp.exp(logits - row_top), -1))
        picked = jnp.sum(
            jnp.where(jnp.arange(logits.shape[1])[None, :] == pairing[:, None], logits, 0.0), -1
        )
        return length * jnp.sum(log_total - picked)

    contrast_value, contrast_back = jax.vjp(contrast_of, pool_sum)
    grad_pool = by_tile(contrast_back(jnp.ones_like(contrast_value))[0])
    loss_part = flow_part + contrast_value / head_count
    grad_final = product("fcl,dc->fld", grad_pred, io_full[1]) + grad_pool[:, None, :]
    final_value, final_back = jax.vjp(norm_rows, hidden)
    grad_hidden = final_back(grad_final)[0]
    fin_grad = product("fcl,fld->dc", grad_pred, final_bf)
    plan, lefts, rights = [], [], []

    def listed_factors(factors, factor):
        factors.append(factor.reshape(-1, factor.shape[-1]))
        return len(factors) - 1

    mod_grads = [None, None]
    for layer_index in (1, 0):
        (
            layer_hidden,
            mod_parts,
            layer_normed,
            attended,
            layer_mixed,
            layer_branch,
            layer_middle,
            layer_normed2,
            layer_upper,
            layer_active,
            layer_down_out,
        ) = saved_layers[layer_index]
        weight = qkv_full[layer_index]
        d_gate2 = jnp.sum(layer_down_out * grad_hidden, axis=1, keepdims=True)
        grad_down = to_bf16(mod_parts[5] * grad_hidden)
        grad_active = product("fld,dn->fln", grad_down, down_full[layer_index])
        gelu_value, gelu_back = jax.vjp(soft_gelu, layer_upper)
        grad_upper = to_bf16(gelu_back(grad_active)[0])
        grad_normed2 = product("fln,dn->fld", grad_upper, up_full[layer_index])
        mod_value, mod_back = jax.vjp(modulate, layer_middle, mod_parts[3], mod_parts[4])
        grad_middle, d_shift2, d_scale2 = mod_back(grad_normed2)
        grad_middle = grad_middle + grad_hidden
        d_gate1 = jnp.sum(layer_branch * grad_middle, axis=1, keepdims=True)
        grad_branch = to_bf16(mod_parts[2] * grad_middle)
        grad_mixed = to_bf16(product("fld,de->fle", grad_branch, out_full[layer_index]))
        branch_place, branch_right = listed_factors(lefts, grad_branch), listed_factors(rights, layer_mixed)
        normed_place = listed_factors(lefts, layer_normed)
        if layer_index == 0:
            grad_proj = attend_back(*attended, grad_mixed.reshape(frames, D), next(ids))
            grad_normed = product("fn,dn->fd", grad_proj, weight)
            first = [(normed_place, listed_factors(rights, grad_proj), 0, 3 * D)]
        else:
            query, pair_kv = attended
            grad_query, grad_keys, grad_values = cross_back(query, pair_kv, own_lengths, grad_mixed)
            grad_normed = product("fln,dn->fld", grad_query, weight[:, :D])
            caption_place = listed_factors(lefts, own_captions)
            first = [
                (normed_place, listed_factors(rights, grad_query), 0, D),
                (caption_place, listed_factors(rights, grad_keys), D, 2 * D),
                (caption_place, listed_factors(rights, grad_values), 2 * D, 3 * D),
            ]
        first.append((branch_place, branch_right, 3 * D, 4 * D))
        plan.append(
            (
                tuple(first),
                (listed_factors(lefts, layer_normed2), listed_factors(rights, grad_upper)),
                (listed_factors(lefts, grad_down), listed_factors(rights, layer_active)),
            )
        )
        first_value, first_back = jax.vjp(modulate, layer_hidden, mod_parts[0], mod_parts[1])
        grad_in, d_shift1, d_scale1 = first_back(grad_normed.reshape(clip_count, tile, D))
        mod_grads[layer_index] = jnp.concatenate(
            [d_shift1, d_scale1, d_gate1, d_shift2, d_scale2, d_gate2], -1
        )[:, 0]
        grad_hidden = grad_in + grad_middle
    in_grad = product("fld,fcl->dc", to_bf16(grad_hidden), input_bf)

    mod_size = clip_count * 2 * ada_cols
    io_size = rows_own * 2 * io_cols
    mod_grad = by_clip(jnp.stack(mod_grads, 1)).reshape(clip_count, 2, head_count, ada_cols)
    mod_grad = mod_grad.transpose(2, 0, 1, 3).reshape(head_count, mod_size)
    io_part = (
        jnp.stack([in_grad, fin_grad])
        .reshape(2, data_count, rows_own, head_count, io_cols)
        .transpose(3, 1, 0, 2, 4)
        .reshape(head_count, data_count * io_size)
    )
    packed = jnp.concatenate([mod_grad, io_part], 1).reshape(head_count, -1, 128)
    packed = jnp.sum(swap(packed, "head"), 0).reshape(-1)
    mod_grad = jnp.broadcast_to(packed[:mod_size], (data_count, mod_size))
    lines = -(-(mod_size + io_size) // 128)
    packed = jnp.concatenate([mod_grad, packed[mod_size:].reshape(data_count, io_size)], 1)
    packed = jnp.pad(packed, ((0, 0), (0, lines * 128 - mod_size - io_size)))
    packed = swap(packed.reshape(data_count, lines, 128), "dp").reshape(data_count, -1)
    mod_grad = packed[:, :mod_size].reshape(-1, 2, ada_cols)
    io_grad = jnp.sum(packed[:, mod_size : mod_size + io_size], 0).reshape(2, rows_own, io_cols)
    ada_grad = exact_product("fd,fln->ldn", signal_own.astype(jnp.float32), mod_grad)
    grad_signal = exact_product("fln,ldn->fd", mod_grad, ada_bf.astype(jnp.float32))
    grad_signal = jnp.sum(spread(grad_signal, "head"), 0)
    signal_own_value, signal_back = jax.vjp(double_silu, hidden_own)
    grad_cond = spread(signal_back(grad_signal)[0], "dp").transpose(1, 0, 2).reshape(-1, D)
    time_grad = exact_product(
        "fd,fn->dn",
        table_own,
        lax.dynamic_slice_in_dim(grad_cond, h * time_cols, time_cols, 1),
    )

    square = sum((jnp.sum(grad * grad) for grad in (ada_grad, time_grad, io_grad)))
    if linked:
        extra = jnp.pad(jnp.stack([square, loss_part])[None], ((0, 7), (0, 126)))
        owned, totals, edge = reduce_whole(tuple(plan), lefts, rights, extra, next(ids))
        totals = totals[0, :2]
        edge = edge[::-1]
        edge = jnp.where(is_first, edge[..., :64], edge[..., 64:])
    else:

        def made(left_place, right_place):
            return product("fd,fn->dn", lefts[left_place], rights[right_place])

        owned = []
        for first, *pairs in plan:
            columns = jnp.concatenate([made(*source[:2]) for source in first], 1)
            owned.append(join_first(columns[:, : 3 * D], columns[:, 3 * D :]))
            owned += [made(*pair) for pair in pairs]
        owned = [reduce_general(part) for part in owned]
        square = square + sum((jnp.sum(part * part) for part in owned))
        totals = lax.psum(jnp.stack([square, loss_part]), ("dp", "head"))
        edge = jnp.stack([owned[3], owned[0]])
        edge = jnp.where(is_first, edge[..., block : block + 64], edge[..., block - 64 : block])
        edge = spread(edge.reshape(-1, 128), "head")
        edge = lax.dynamic_slice_in_dim(edge, h ^ 1, 1, 0).reshape(2, rows_own, 64)
    first_own = jnp.stack([owned[3], owned[0]])
    total_square, total_loss = totals[0], totals[1]
    qkv_shard, out_shard = without_edge(first_own, edge)
    shards = (
        qkv_shard,
        out_shard,
        jnp.stack([owned[4], owned[1]]),
        jnp.stack([owned[5], owned[2]]),
        ada_grad,
        time_grad[None],
        io_grad,
    )
    old_moments = (qkv_moment, out_moment, up_moment, down_moment)
    grad_norm = jnp.sqrt(total_square)
    clip_scale = jnp.minimum(1.0, CLIP_NORM / (grad_norm + 1e-06))
    moments = tuple(
        (MUON_BETA * old_moments[member] + clip_scale * shards[member] for member in range(4))
    )
    coeff_a, coeff_b, coeff_c = NEWTON_COEFFS
    widths = [-(-moment.shape[2] // 128) * 128 for moment in moments]
    padded = [
        jnp.pad(moment, ((0, 0), (0, 0), (0, width - moment.shape[2])))
        for moment, width in zip(moments, widths)
    ]
    own_matrix = to_owner(padded, next(ids)).reshape(D, -1)

    def near_product(form, left, right):
        return jnp.einsum(form, left, right, precision=lax.Precision.HIGH)

    gram = gram_sum(own_matrix, next(ids))
    unit = jnp.eye(D, dtype=jnp.float32)
    size_frob = jnp.sqrt(jnp.sum(gram * unit)) + 1e-07
    gram = gram / (size_frob * size_frob)
    factor = None
    for ns_step in range(NS_STEPS):
        poly = coeff_a * unit + coeff_b * gram + coeff_c * near_product("rk,kj->rj", gram, gram)
        factor = poly if factor is None else near_product("rk,kj->rj", poly, factor)
        if ns_step < NS_STEPS - 1:
            gram = near_product("rk,kj->rj", near_product("rk,kj->rj", poly, gram), poly)
    ortho_matrix = near_product("rk,kc->rc", factor, own_matrix) / size_frob
    ortho_back = to_bf16(ortho_matrix).reshape(data_count, rows_own, -1)
    ortho_back = from_owner(ortho_back, tuple(widths), next(ids)).astype(jnp.float32)
    ortho_rows = tuple(
        (
            jnp.stack(
                [
                    ortho_back[owner_of(member, layer), :, : moments[member].shape[2]]
                    for layer in range(2)
                ]
            )
            for member in range(4)
        )
    )
    muon_weights = (qkv_weight, out_weight, up_weight, down_weight)
    muon_new = tuple(
        (
            muon_weights[member] * (1.0 - MUON_RATE * MUON_DECAY)
            - MUON_RATE
            * 0.2
            * math.sqrt(max(D, muon_weights[member].shape[2] * head_count))
            * ortho_rows[member]
            for member in range(4)
        )
    )
    step_count = adam_step[0].astype(jnp.float32)
    ada_new, ada_first_new, ada_second_new = adam_update(
        ada_weight, clip_scale * shards[4], ada_first, ada_second, step_count
    )
    time_new, time_first_new, time_second_new = adam_update(
        time_weight, clip_scale * shards[5][0], time_first, time_second, step_count
    )
    io_new, io_first_new, io_second_new = adam_update(
        io_weight, clip_scale * shards[6], io_first, io_second, step_count
    )
    return (
        total_loss,
        grad_norm,
        pooled_out,
        muon_new[0],
        moments[0],
        muon_new[1],
        moments[1],
        muon_new[2],
        moments[2],
        muon_new[3],
        moments[3],
        ada_new,
        ada_first_new,
        ada_second_new,
        time_new,
        time_first_new,
        time_second_new,
        io_new,
        io_first_new,
        io_second_new,
    )


def solution(mesh):
    placed = (
        P("dp", "head", None),
        P("dp", "head", None),
        P("dp"),
        P("dp", None, None),
        P("dp"),
        P("dp"),
        P(),
        P(None, "dp", "head"),
        P(None, "dp", "head"),
        P(None, "dp", "head"),
        P(None, "dp", "head"),
        P(None, "dp", "head"),
        P("dp", "head"),
        P(None, "dp", "head"),
        P(None, "dp", "head"),
        P(None, "dp", "head"),
        P(None, "dp", "head"),
        P(None, "dp", "head"),
        P(None, "dp", "head"),
        P(None, "dp", "head"),
        P("dp", "head"),
        P("dp", "head"),
        P(None, "dp", "head"),
        P(None, "dp", "head"),
    )
    return jax.shard_map(
        body,
        mesh=mesh,
        in_specs=placed,
        out_specs=(
            P(),
            P(),
            P("dp", None),
            P(None, "dp", "head"),
            P(None, "dp", "head"),
            P(None, "dp", "head"),
            P(None, "dp", "head"),
            P(None, "dp", "head"),
            P(None, "dp", "head"),
            P(None, "dp", "head"),
            P(None, "dp", "head"),
            P(None, "dp", "head"),
            P(None, "dp", "head"),
            P(None, "dp", "head"),
            P("dp", "head"),
            P("dp", "head"),
            P("dp", "head"),
            P(None, "dp", "head"),
            P(None, "dp", "head"),
            P(None, "dp", "head"),
        ),
        check_vma=False,
    )
```

```python
import functools
import math

import jax
import jax.numpy as jnp
from jax import lax
from jax.experimental import pallas as pl
from jax.experimental.pallas import tpu as pltpu
from jax.sharding import PartitionSpec as P

D = 768
HEADS = 12
HDIM = 64
CAP = 256
NS_STEPS = 5


HIGHEST_PRECISION = lax.Precision.HIGHEST
NEWTON_COEFFS = (3.4445, -4.775, 2.0315)
CLIP_NORM = 1.0
MUON_RATE = 0.2
MUON_DECAY = 0.1
MUON_BETA = 0.95
ADAM_RATE = 0.02
ADAM_DECAY = 0.01
ADAM_FIRST = 0.9
ADAM_SECOND = 0.999


def to_bf16(values):
    return values.astype(jnp.bfloat16)


def sigmoid_unit(values):
    return values * jax.nn.sigmoid(values)


def double_silu(values):
    return sigmoid_unit(sigmoid_unit(values))


def soft_gelu(values):
    return (
        0.5
        * values
        * (1.0 + jnp.tanh(0.7978845608 * (values + 0.044715 * values * values * values)))
    )


def norm_rows(values):
    centre = values - jnp.mean(values, -1, keepdims=True)
    return centre * lax.rsqrt(jnp.mean(centre * centre, -1, keepdims=True) + 1e-06)


def modulate(hidden, shift, stretch):
    return norm_rows(hidden) * (1.0 + stretch) + shift


def time_table(timesteps, width):
    half_width = width // 2
    frequency = jnp.exp(
        -math.log(10000.0) * jnp.arange(half_width).astype(timesteps.dtype) / half_width
    )
    angles = 1000.0 * timesteps[:, None] * frequency[None, :]
    return jnp.concatenate([jnp.cos(angles), jnp.sin(angles)], axis=-1)


def product(form, left, right):
    return jnp.einsum(form, left, right, preferred_element_type=jnp.float32)


def exact_product(form, left, right):
    return jnp.einsum(form, left, right, precision=HIGHEST_PRECISION)


def adam_update(weight, grad_part, first_moment, second_moment, step_count):
    first_moment = ADAM_FIRST * first_moment + (1.0 - ADAM_FIRST) * grad_part
    second_moment = ADAM_SECOND * second_moment + (1.0 - ADAM_SECOND) * grad_part * grad_part
    first_fix = 1.0 - jnp.power(ADAM_FIRST, step_count)
    second_fix = 1.0 - jnp.power(ADAM_SECOND, step_count)
    direction = first_moment / first_fix / (jnp.sqrt(second_moment / second_fix) + 1e-08)
    return (weight - ADAM_RATE * (direction + ADAM_DECAY * weight), first_moment, second_moment)


MESH = pl.DeviceIdType.MESH
ROWS_A = 64
PIECE_COLS = 256
SLOTS = 4
HALF = 384
WIDE = 256
VMEM_BYTES = 56 * 1024 * 1024


def vmem():
    return pl.BlockSpec(memory_space=pltpu.VMEM)


def anywhere():
    return pl.BlockSpec(memory_space=pl.ANY)


def comm_params(collective_id):
    return pltpu.CompilerParams(
        collective_id=collective_id, has_side_effects=True, vmem_limit_bytes=VMEM_BYTES
    )


def greet(peers):
    barrier = pltpu.get_barrier_semaphore()
    for peer in peers:
        pl.semaphore_signal(barrier, inc=1, device_id=peer, device_id_type=MESH)
    pl.semaphore_wait(barrier, len(peers))


def exchange_kernel(axis, count, swapped, x_ref, out_ref, send_sem, recv_sem):
    me = lax.axis_index(axis)
    peers = [lax.rem(me + shift, count) for shift in range(1, count)]
    greet([{axis: peer} for peer in peers])
    copies = []
    for place, peer in enumerate(peers):
        copy = pltpu.make_async_remote_copy(
            src_ref=x_ref.at[peer] if swapped else x_ref,
            dst_ref=out_ref.at[me],
            send_sem=send_sem.at[place],
            recv_sem=recv_sem.at[place],
            device_id={axis: peer},
            device_id_type=MESH,
        )
        copy.start()
        copies.append(copy)
    out_ref[me] = x_ref[me] if swapped else x_ref[...]
    for copy in copies:
        copy.wait()


def exchange(x, axis, swapped, collective_id):
    count = lax.axis_size(axis)
    block = x.shape[1:] if swapped else x.shape
    return pl.pallas_call(
        functools.partial(exchange_kernel, axis, count, swapped),
        out_shape=jax.ShapeDtypeStruct((count,) + block, x.dtype),
        in_specs=[vmem()],
        out_specs=vmem(),
        scratch_shapes=[
            pltpu.SemaphoreType.DMA((count - 1,)),
            pltpu.SemaphoreType.DMA((count - 1,)),
        ],
        compiler_params=comm_params(collective_id),
        name="swap" if swapped else "spread",
    )(x)


def link_peers(d, h):
    return {
        "core": (d, h ^ 1),
        "y": (d, h ^ 2),
        "x": (d ^ 1, h),
        "zl": (d ^ 2, h),
        "zh": (d ^ 4, h),
    }


def first_column(side, core, start):
    if start < 512:
        return side * 1152 + core * 640 + start
    if start == 512:
        return (1 - core) * (side * 1152 + 512) + core * (3 * D + side * HALF + 128)
    return 3 * D + side * HALF + core * 256


def gather_pieces(widths, firsts):
    pieces = []
    for group, width in enumerate(widths):
        for start in range(0, width, PIECE_COLS):
            if group in firsts and start == 512:
                pieces += [(group, 512, 128), (group, 640, 128)]
            else:
                pieces.append((group, start, PIECE_COLS))
    return pieces


def gather_kernel(groups, firsts, *refs):
    own_refs = refs[:groups]
    edge_ref, latents_ref, shared_ref, table_ref, ada_ref = refs[groups : groups + 5]
    out_refs = refs[groups + 5 : 2 * groups + 5]
    latents_out, shared_out, mods_out = refs[2 * groups + 5 : 2 * groups + 8]
    (tail, edge_got, times, parts, parts_got, mine, send_sem, recv_sem, core_send, core_recv,
     local_sem, tail_sem, small_send, small_recv) = refs[2 * groups + 8 :]
    d = lax.axis_index("dp")
    h = lax.axis_index("head")
    peers = link_peers(d, h)
    heads = [(d, h ^ other) for other in (1, 2, 3)]
    datas = [(d ^ other, h) for other in range(1, 8)]
    greet(heads + datas)
    y, c = h // 2, h % 2
    zh, zl, x = d // 4, (d // 2) % 2, d % 2
    every = slice(None)
    pieces = gather_pieces([own.shape[1] for own in own_refs], firsts)
    order_a = (("zh", (zh, zl, x)), ("zl", (every, zl, x)), ("x", (every, every, x)),
               ("y", (every, every, every)))
    order_b = (("y", (zh, zl, x)), ("zh", (zh, zl, x)), ("zl", (every, zl, x)),
               ("x", (every, every, x)))

    def tail_of(piece):
        group, start, size = pieces[piece]
        if group in firsts and start == 2 * PIECE_COLS:
            return firsts.index(group)
        return None

    def source_of(piece, rows):
        group, start, size = pieces[piece]
        place = tail_of(piece)
        if place is not None:
            return tail.at[place, rows]
        return own_refs[group].at[rows, pl.ds(start, size)]

    def columns_of(piece, head):
        group, start, size = pieces[piece]
        if group in firsts:
            return pl.ds(pl.multiple_of(first_column(head // 2, head % 2, start), 128), size)
        return pl.ds(pl.multiple_of(head * own_refs[group].shape[1] + start, 128), size)

    def own_copy(piece):
        group = pieces[piece][0]
        return pltpu.make_async_copy(
            source_of(piece, pl.ds(0, own_refs[group].shape[0])),
            out_refs[group].at[zh, zl, x, :, columns_of(piece, h)],
            local_sem.at[piece],
        )

    def hop(piece, step, stream):
        group = pieces[piece][0]
        rows_all = own_refs[group].shape[0]
        rows = pl.ds(0, ROWS_A) if stream == 0 else pl.ds(ROWS_A, rows_all - ROWS_A)
        head = h if stream < 2 else h ^ 2
        peer, index = (order_a if stream == 0 else order_b)[step]
        view = out_refs[group].at[index + (rows, columns_of(piece, head))]
        return pltpu.make_async_remote_copy(
            src_ref=source_of(piece, rows) if step == 0 else view,
            dst_ref=view,
            send_sem=send_sem.at[piece, step, stream],
            recv_sem=recv_sem.at[piece, step, stream],
            device_id=peers[peer],
            device_id_type=MESH,
        )

    def streams(step):
        return range(2) if step == 0 else range(3)

    def across(piece, side):
        group = pieces[piece][0]
        view = out_refs[group].at[:, :, :, :, columns_of(piece, h ^ (2 * side))]
        return pltpu.make_async_remote_copy(
            src_ref=view,
            dst_ref=view,
            send_sem=core_send.at[piece, side],
            recv_sem=core_recv.at[piece, side],
            device_id=peers["core"],
            device_id_type=MESH,
        )

    def small(place, source, target, peer):
        return pltpu.make_async_remote_copy(
            src_ref=source,
            dst_ref=target,
            send_sem=small_send.at[place],
            recv_sem=small_recv.at[place],
            device_id=peer,
            device_id_type=MESH,
        )

    edge = small(0, edge_ref, edge_got, peers["core"])
    edge.start()
    tails = [
        pltpu.make_async_copy(
            own_refs[group].at[:, pl.ds(2 * PIECE_COLS, 128)], tail.at[place],
            tail_sem.at[place],
        )
        for place, group in enumerate(firsts)
    ]
    for copy in tails:
        copy.start()
    latents = [
        small(1 + place, latents_ref, latents_out.at[h], peer) for place, peer in enumerate(heads)
    ]
    for copy in latents:
        copy.start()
    latents_out[h] = latents_ref[...]
    bring_times = pltpu.make_async_copy(out_refs[0], times, tail_sem.at[len(firsts)])
    shares = [
        small(4 + place, mine, shared_out.at[d], peer) for place, peer in enumerate(datas)
    ]
    swaps = [
        small(11 + place, parts.at[d ^ (1 + place)], parts_got.at[d], peer)
        for place, peer in enumerate(datas)
    ]
    spreads = [
        small(18 + place, mods_out.at[h], mods_out.at[h], peer) for place, peer in enumerate(heads)
    ]

    def condition(turn):
        if turn == 2:
            edge.wait()
            for copy in tails:
                copy.wait()
            tail[...] = tail[...] + edge_got[...]
            for piece in range(len(pieces)):
                if tail_of(piece) is not None:
                    own_copy(piece).start()
        if turn == 6:
            for side in range(2):
                across(0, side).wait_recv()
            bring_times.start()
        if turn == 7:
            bring_times.wait()
            rows = times.shape[-2]
            mine[...] = shared_ref[...] + dot_nn(
                table_ref[...], times[...].reshape(8 * rows, times.shape[-1])
            )
            for copy in shares:
                copy.start()
            shared_out[d] = mine[...]
        if turn == 11:
            for copy in shares:
                copy.wait()
            count, lines, width = shared_out.shape
            signal = to_bf16(double_silu(shared_out[...])).reshape(count * lines, width)
            first = (d // 2) * WIDE + (d % 2) * ada_ref.shape[1]
            at = lax.broadcasted_iota(jnp.int32, (width, 128), 0)
            to = lax.broadcasted_iota(jnp.int32, (width, 128), 1)
            chosen = jnp.where((at == first + to) & (to < ada_ref.shape[1]), 1.0, 0.0)
            own = to_bf16(dot_nn(signal, to_bf16(chosen)))[:, : ada_ref.shape[1]]
            columns = ada_ref.shape[2]
            for layer in range(2):
                part = dot_nn(own, ada_ref[layer]).reshape(count, lines, columns)
                parts[:, :, layer * columns : (layer + 1) * columns] = part[:, :8]
            for copy in swaps:
                copy.start()
            parts_got[d] = parts[d]
        if turn == 15:
            for copy in swaps:
                copy.wait()
            total = parts_got[0]
            for place in range(1, 8):
                total = total + parts_got[place]
            mods_out[h] = total
            for copy in spreads:
                copy.start()
        if turn == 19:
            for copy in spreads + latents:
                copy.wait()

    for piece in range(len(pieces)):
        if tail_of(piece) is None:
            own_copy(piece).start()
    for turn in range(len(pieces) + 4):
        for step in range(5):
            piece = turn - step
            if not 0 <= piece < len(pieces):
                continue
            if step == 1:
                own_copy(piece).wait()
            if step >= 1:
                for stream in streams(step - 1):
                    hop(piece, step - 1, stream).wait_recv()
            if step < 4:
                for stream in streams(step):
                    hop(piece, step, stream).start()
            else:
                for side in range(2):
                    across(piece, side).start()
        condition(turn)
    for piece in range(len(pieces)):
        for step in range(4):
            for stream in streams(step):
                hop(piece, step, stream).wait_send()
        for side in range(2):
            if piece > 0:
                across(piece, side).wait_recv()
            across(piece, side).wait_send()


def gather_whole(owns, firsts, edge, latents, shared, table, ada, collective_id):
    groups = len(owns)
    pieces = len(gather_pieces([own.shape[1] for own in owns], firsts))
    rows = owns[0].shape[0]
    low = jnp.bfloat16
    mod_cols = 2 * ada.shape[2]
    *wholes, latents_all, shared_all, mods = pl.pallas_call(
        functools.partial(gather_kernel, groups, firsts),
        out_shape=[
            jax.ShapeDtypeStruct((2, 2, 2, own.shape[0], 4 * own.shape[1]), own.dtype)
            for own in owns
        ]
        + [
            jax.ShapeDtypeStruct((4,) + latents.shape, jnp.float32),
            jax.ShapeDtypeStruct((8,) + shared.shape, jnp.float32),
            jax.ShapeDtypeStruct((4, 8, mod_cols), jnp.float32),
        ],
        in_specs=[anywhere()] * groups + [vmem()] * 5,
        out_specs=[anywhere()] * groups + [vmem()] * 3,
        scratch_shapes=[
            pltpu.VMEM(edge.shape, low),
            pltpu.VMEM(edge.shape, low),
            pltpu.VMEM((2, 2, 2, rows, 4 * owns[0].shape[1]), low),
            pltpu.VMEM((8, 8, mod_cols), jnp.float32),
            pltpu.VMEM((8, 8, mod_cols), jnp.float32),
            pltpu.VMEM(shared.shape, jnp.float32),
            pltpu.SemaphoreType.DMA((pieces, 4, 3)),
            pltpu.SemaphoreType.DMA((pieces, 4, 3)),
            pltpu.SemaphoreType.DMA((pieces, 2)),
            pltpu.SemaphoreType.DMA((pieces, 2)),
            pltpu.SemaphoreType.DMA((pieces,)),
            pltpu.SemaphoreType.DMA((len(firsts) + 1,)),
            pltpu.SemaphoreType.DMA((21,)),
            pltpu.SemaphoreType.DMA((21,)),
        ],
        compiler_params=comm_params(collective_id),
        name="gather_weights",
    )(*owns, edge, latents, shared, table, ada)
    wholes = [whole.reshape(8 * own.shape[0], -1) for whole, own in zip(wholes, owns)]
    return wholes, latents_all, shared_all, mods


def gather_general(own):
    rows, columns = own.shape
    blocks = lax.all_gather(own, ("dp", "head"), axis=0, tiled=False)
    blocks = blocks.reshape(-1, lax.axis_size("head"), rows, columns)
    return blocks.transpose(0, 2, 1, 3).reshape(-1, lax.axis_size("head") * columns)


def reduce_kernel(plan, lefts, rights, *refs):
    left_refs, right_refs = refs[:lefts], refs[lefts : lefts + rights]
    (extra_ref, mod_ref, io_ref, signal_ref, slope_ref, table_ref, ada_ref, out_ref, total_ref,
     edge_ref, ada_out, time_out, io_out) = refs[lefts + rights : lefts + rights + 13]
    (made, near, left, left_t, right, send_a, send_b, got_a, got_b, keep_a, keep_b,
     mine, head_got, data_got, mod_got, io_got, mod_sum, io_sum, mod_all, io_all, part, part_got,
     inner, inner_all, near_send, near_recv, hop_send, hop_recv, left_sem,
     right_sem, edge_send, edge_recv, sum_send, sum_recv, small_send, small_recv) = refs[
        lefts + rights + 13 :
    ]
    layers = len(plan)
    per_group = D // PIECE_COLS
    pieces = 3 * layers * per_group
    d = lax.axis_index("dp")
    h = lax.axis_index("head")
    peers = link_peers(d, h)
    across = [(d, h ^ other) for other in (1, 2, 3)] + [(d ^ other, h) for other in range(1, 8)]
    greet(across)
    y, c = h // 2, h % 2
    zh, zl, x = d // 4, (d // 2) % 2, d % 2
    order = (("y", "x"), ("x", "zl"), ("zl", "zh"), ("zh", "y"))
    shape = made.shape[3:]
    rows_own = shape[-2]
    top, bottom = pl.ds(0, ROWS_A), pl.ds(ROWS_A, rows_own - ROWS_A)
    every = slice(None)

    def near_copy(piece, side):
        slot = piece % SLOTS
        return pltpu.make_async_remote_copy(
            src_ref=made.at[slot, side, 1 - c],
            dst_ref=near.at[slot, side],
            send_sem=near_send.at[slot, side],
            recv_sem=near_recv.at[slot, side],
            device_id=peers["core"],
            device_id_type=MESH,
        )

    def left_copy(place):
        rows = left_refs[place].shape[0]
        return pltpu.make_async_copy(
            left_refs[place], left.at[place, pl.ds(0, rows)], left_sem.at[place]
        )

    def turn_left(place, at):
        rows = left_refs[place].shape[0]
        left_copy(place).wait()
        left_t[at, :, :rows] = left[place, :rows].T

    def sources(layer, part, head, half):
        column = first_column(head // 2, head % 2, part * PIECE_COLS + (128 * half if part == 2 else 0))
        if part < 2:
            column += 128 * half
        for at, (left_place, right_place, start, stop) in enumerate(plan[layer][0]):
            if start <= column < stop:
                return left_place, right_place, column - start

    def right_copies(piece, layer, part):
        copies = []
        for head in range(4):
            for half in range(2):
                left_place, right_place, column = sources(layer, part, head, half)
                rows = right_refs[right_place].shape[0]
                copies.append(
                    pltpu.make_async_copy(
                        right_refs[right_place].at[:, pl.ds(column, 128)],
                        right.at[piece % 2, head, pl.ds(0, rows), pl.ds(128 * half, 128)],
                        right_sem.at[piece % 2, head, half],
                    )
                )
        return copies

    def right_copy(piece, right_place, head):
        start = head * D + (piece % per_group) * PIECE_COLS
        return pltpu.make_async_copy(
            right_refs[right_place].at[:, pl.ds(pl.multiple_of(start, PIECE_COLS), PIECE_COLS)],
            right.at[piece % 2, head],
            right_sem.at[piece % 2, head, 0],
        )

    def fetch(piece):
        for layer in range(layers):
            for part in range(per_group):

                @pl.when(piece == 3 * layer * per_group + part)
                def _():
                    for copy in right_copies(piece, layer, part):
                        copy.start()

            for member in range(2):

                @pl.when(piece // per_group == 3 * layer + 1 + member)
                def _():
                    for head in range(4):
                        right_copy(piece, plan[layer][1 + member][1], head).start()

    def bring(piece):
        slot = piece % SLOTS
        for layer in range(layers):
            used = []
            for left_place, _, _, _ in plan[layer][0]:
                if left_place not in used:
                    used.append(left_place)

            @pl.when(piece == 3 * layer * per_group)
            def _():
                for at, left_place in enumerate(used):
                    turn_left(left_place, at)

            for part in range(per_group):

                @pl.when(piece == 3 * layer * per_group + part)
                def _():
                    for copy in right_copies(piece, layer, part):
                        copy.wait()
                    for head in range(4):
                        pair = [sources(layer, part, head, half) for half in range(2)]
                        spans = [(0, 2)] if pair[0][0] == pair[1][0] else [(0, 1), (1, 2)]
                        for first, stop in spans:
                            left_place, right_place, _ = pair[first]
                            rows = right_refs[right_place].shape[0]
                            columns = slice(128 * first, 128 * stop)
                            made[slot, head // 2, head % 2, :, :, :, :, columns] = dot_nn(
                                left_t[used.index(left_place), :, :rows],
                                right[piece % 2, head, :rows, columns],
                            ).reshape(shape[:-1] + (128 * (stop - first),))

            for member in range(2):

                @pl.when(piece == (3 * layer + 1 + member) * per_group)
                def _():
                    turn_left(plan[layer][1 + member][0], 0)

        @pl.when((piece // per_group) % 3 != 0)
        def _():
            for head in range(4):
                right_copy(piece, plan[0][1][1], head).wait()
            for head in range(4):
                made[slot, head // 2, head % 2] = dot_nn(
                    left_t[0], right[piece % 2, head]
                ).reshape(shape)

        for side in range(2):
            near_copy(piece, side).start()

    def hop(piece, step, stream):
        slot = piece % SLOTS
        sent, got = (send_a, got_a) if stream == 0 else (send_b, got_b)
        return pltpu.make_async_remote_copy(
            src_ref=sent[step].at[slot],
            dst_ref=got[step].at[slot],
            send_sem=hop_send.at[step, stream, slot],
            recv_sem=hop_recv.at[step, stream, slot],
            device_id=peers[order[step][stream]],
            device_id_type=MESH,
        )

    def first(piece):
        slot = piece % SLOTS
        for side in range(2):
            near_copy(piece, side).wait()

        def total(side, *index):
            return made[(slot, side, c) + index] + near[(slot, side) + index]

        send_a[0][slot] = to_bf16(total(1 - y, every, every, every, top))
        hop(piece, 0, 0).start()
        send_b[0][slot] = to_bf16(total(every, every, every, 1 - x, bottom))
        hop(piece, 0, 1).start()
        keep_a[0][slot] = total(y, every, every, every, top)
        keep_b[0][slot] = total(every, every, every, x, bottom)

    cut_a = (None, (2, x), (1, zl), (0, zh))
    cut_b = (None, (2, zl), (1, zh), (0, y))

    def later(piece, step):
        slot = piece % SLOTS
        for stream in range(2):
            keep, got, sent = (keep_a, got_a, send_a) if stream == 0 else (keep_b, got_b, send_b)
            axis, mine = (cut_a if stream == 0 else cut_b)[step]
            hop(piece, step - 1, stream).wait()

            def total(which):
                index = (slot,) + (every,) * axis + (which,)
                return keep[step - 1][index] + got[step - 1][index].astype(jnp.float32)

            sent[step][slot] = to_bf16(total(1 - mine))
            hop(piece, step, stream).start()
            keep[step][slot] = total(mine)

    def last(piece):
        slot = piece % SLOTS
        for stream in range(2):
            keep, got = (keep_a, got_a) if stream == 0 else (keep_b, got_b)
            hop(piece, 3, stream).wait()
            out_ref[piece, top if stream == 0 else bottom, :] = keep[3][slot] + got[3][
                slot
            ].astype(jnp.float32)

    def small(place, source, target, peer):
        return pltpu.make_async_remote_copy(
            src_ref=source,
            dst_ref=target,
            send_sem=small_send.at[place],
            recv_sem=small_recv.at[place],
            device_id=peer,
            device_id_type=MESH,
        )

    heads = [(across[other - 1], h ^ other, other - 1) for other in (1, 2, 3)]
    datas = [(across[2 + other], d ^ other, other - 1) for other in range(1, 8)]
    mod_swaps = [small(at, mod_ref.at[place], mod_got.at[h], peer) for peer, place, at in heads]
    io_swaps = [small(3 + at, io_ref.at[place], io_got.at[h], peer) for peer, place, at in heads]
    mod_spreads = [small(6 + at, mod_sum, mod_all.at[d], peer) for peer, _, at in datas]
    io_moves = [small(13 + at, io_sum.at[place], io_all.at[d], peer) for peer, place, at in datas]
    part_spreads = [small(20 + at, part, part_got.at[h], peer) for peer, _, at in heads]
    inner_spreads = [small(23 + at, inner, inner_all.at[d], peer) for peer, _, at in datas]

    def total_of(ref):
        total = ref[0]
        for place in range(1, ref.shape[0]):
            total = total + ref[place]
        return total

    def exact(left, right, contract):
        return lax.dot_general(
            left, right, (contract, ((), ())), precision=HIGHEST_PRECISION,
            preferred_element_type=jnp.float32,
        )

    def condition(turn):
        @pl.when(turn == 2)
        def _():
            for copy in mod_swaps + io_swaps:
                copy.wait()
            mod_sum[...] = total_of(mod_got)
            io_sum[...] = total_of(io_got)
            for copy in mod_spreads + io_moves:
                copy.start()
            mod_all[d] = mod_sum[...]
            io_all[d] = io_sum[d]

        @pl.when(turn == 6)
        def _():
            for copy in mod_spreads + io_moves:
                copy.wait()
            io_out[...] = total_of(io_all)
            columns = ada_ref.shape[2]
            total = jnp.zeros(part.shape, jnp.float32)
            for layer in range(2):
                grads = mod_all[:, :, layer * columns : (layer + 1) * columns].reshape(
                    part.shape[0], columns
                )
                ada_out[layer] = exact(signal_ref[...], grads, ((0,), (0,)))
                total = total + exact(grads, ada_ref[layer].astype(jnp.float32), ((1,), (1,)))
            part[...] = total
            for copy in part_spreads:
                copy.start()
            part_got[h] = total

        @pl.when(turn == 10)
        def _():
            for copy in part_spreads:
                copy.wait()
            inner[...] = total_of(part_got) * slope_ref[...]
            for copy in inner_spreads:
                copy.start()
            inner_all[d] = inner[...]

        @pl.when(turn == 14)
        def _():
            for copy in inner_spreads:
                copy.wait()
            for place in range(2):
                time_out[place] = exact(table_ref[...], inner_all[2 * h + place], ((0,), (0,)))

    for copy in mod_swaps + io_swaps:
        copy.start()
    mod_got[h] = mod_ref[h]
    io_got[h] = io_ref[h]
    for place in range(lefts):
        left_copy(place).start()
    fetch(0)
    fetch(1)
    bring(0)
    fetch(2)
    bring(1)

    @pl.loop(0, pieces + 4)
    def _(turn):
        @pl.when(turn + 3 < pieces)
        def _():
            fetch(turn + 3)

        @pl.when(turn < pieces)
        def _():
            first(turn)

        for step in (1, 2, 3):

            @pl.when((turn >= step) & (turn - step < pieces))
            def _():
                later(turn - step, step)

        @pl.when(turn >= 4)
        def _():
            last(turn - 4)

        @pl.when(turn + 2 < pieces)
        def _():
            bring(turn + 2)

        condition(turn)

    edges = []
    for layer in range(layers):
        piece = (3 * layer + 1) * per_group - 1
        edges.append(
            pltpu.make_async_remote_copy(
                src_ref=out_ref.at[piece, :, pl.ds(0, 128)],
                dst_ref=edge_ref.at[layer],
                send_sem=edge_send.at[layer],
                recv_sem=edge_recv.at[layer],
                device_id=peers["core"],
                device_id_type=MESH,
            )
        )
        edges[-1].start()

    squares = jnp.zeros((rows_own, PIECE_COLS), jnp.float32)
    for piece in range(pieces):
        squares = squares + out_ref[piece] * out_ref[piece]
    row = lax.broadcasted_iota(jnp.int32, (8, 128), 0)
    column = lax.broadcasted_iota(jnp.int32, (8, 128), 1)
    square = jnp.sum(squares)
    for ref in (ada_out, time_out, io_out):
        square = square + jnp.sum(ref[...] * ref[...])
    mine[0] = extra_ref[...] + jnp.where((row == 0) & (column == 0), square, 0.0)
    for phase, (got, me, count) in enumerate(((head_got, h, 4), (data_got, d, 8))):
        copies = []
        for other in range(1, count):
            place = 3 * phase + other - 1
            copies.append(
                pltpu.make_async_remote_copy(
                    src_ref=mine.at[phase],
                    dst_ref=got.at[me],
                    send_sem=sum_send.at[place],
                    recv_sem=sum_recv.at[place],
                    device_id=across[place],
                    device_id_type=MESH,
                )
            )
            copies[-1].start()
        got[me] = mine[phase]
        for copy in copies:
            copy.wait()
        total = got[0]
        for other in range(1, count):
            total = total + got[other]
        if phase == 0:
            mine[1] = total
        else:
            total_ref[...] = total
    for copy in edges:
        copy.wait()


def reduce_whole(plan, lefts, rights, smalls, collective_id):
    layers = len(plan)
    frames = lefts[0].shape[0]
    rows = D // 8
    per_group = D // PIECE_COLS
    pieces = 3 * layers * per_group
    leads = ((2, 2, 2), (2, 2), (2,), ())

    def buffers(count, dtype):
        return [pltpu.VMEM((SLOTS,) + lead + (count, PIECE_COLS), dtype) for lead in leads]

    bottom_rows = rows - ROWS_A
    blocks = (2, 2, 2, rows, PIECE_COLS)
    low = jnp.bfloat16
    mod, io, signal, ada = smalls[1], smalls[2], smalls[3], smalls[6]
    summed, *others = pl.pallas_call(
        functools.partial(reduce_kernel, plan, len(lefts), len(rights)),
        out_shape=[
            jax.ShapeDtypeStruct((pieces, rows, PIECE_COLS), jnp.float32),
            jax.ShapeDtypeStruct((8, 128), jnp.float32),
            jax.ShapeDtypeStruct((layers, rows, 128), jnp.float32),
            jax.ShapeDtypeStruct(ada.shape, jnp.float32),
            jax.ShapeDtypeStruct((2, rows, rows), jnp.float32),
            jax.ShapeDtypeStruct(io.shape[2:], jnp.float32),
        ],
        in_specs=[anywhere()] * (len(lefts) + len(rights)) + [vmem()] * 7,
        out_specs=[vmem()] * 6,
        scratch_shapes=[
            pltpu.VMEM((SLOTS, 2, 2) + blocks, jnp.float32),
            pltpu.VMEM((SLOTS, 2) + blocks, jnp.float32),
            pltpu.VMEM((len(lefts), frames, D), low),
            pltpu.VMEM((3, D, frames), low),
            pltpu.VMEM((2, 4, frames, PIECE_COLS), low),
            buffers(ROWS_A, low),
            buffers(bottom_rows, low),
            buffers(ROWS_A, low),
            buffers(bottom_rows, low),
            buffers(ROWS_A, jnp.float32),
            buffers(bottom_rows, jnp.float32),
            pltpu.VMEM((2, 8, 128), jnp.float32),
            pltpu.VMEM((4, 8, 128), jnp.float32),
            pltpu.VMEM((8, 8, 128), jnp.float32),
            pltpu.VMEM(mod.shape, jnp.float32),
            pltpu.VMEM(io.shape, jnp.float32),
            pltpu.VMEM(mod.shape[1:], jnp.float32),
            pltpu.VMEM(io.shape[1:], jnp.float32),
            pltpu.VMEM((8,) + mod.shape[1:], jnp.float32),
            pltpu.VMEM(io.shape[1:], jnp.float32),
            pltpu.VMEM(signal.shape, jnp.float32),
            pltpu.VMEM((4,) + signal.shape, jnp.float32),
            pltpu.VMEM(signal.shape, jnp.float32),
            pltpu.VMEM((8,) + signal.shape, jnp.float32),
            pltpu.SemaphoreType.DMA((SLOTS, 2)),
            pltpu.SemaphoreType.DMA((SLOTS, 2)),
            pltpu.SemaphoreType.DMA((4, 2, SLOTS)),
            pltpu.SemaphoreType.DMA((4, 2, SLOTS)),
            pltpu.SemaphoreType.DMA((len(lefts),)),
            pltpu.SemaphoreType.DMA((2, 4, 2)),
            pltpu.SemaphoreType.DMA((layers,)),
            pltpu.SemaphoreType.DMA((layers,)),
            pltpu.SemaphoreType.DMA((10,)),
            pltpu.SemaphoreType.DMA((10,)),
            pltpu.SemaphoreType.DMA((30,)),
            pltpu.SemaphoreType.DMA((30,)),
        ],
        compiler_params=comm_params(collective_id),
        name="reduce_grads",
    )(*lefts, *rights, *smalls)
    summed = summed.reshape(3 * layers, per_group, rows, PIECE_COLS).transpose(0, 2, 1, 3)
    return list(summed.reshape(3 * layers, rows, D)), *others


def reduce_general(part):
    data_count, head_count = lax.axis_size("dp"), lax.axis_size("head")
    blocks = part.reshape(
        data_count, part.shape[0] // data_count, head_count, part.shape[1] // head_count
    ).transpose(0, 2, 1, 3)
    blocks = blocks.reshape((-1,) + blocks.shape[2:])
    return lax.psum_scatter(blocks, ("dp", "head"), scatter_dimension=0, tiled=True)[0]


KIND_AT = (1, 2, 3, 0)


def owner_of(kind, layer):
    return 4 * layer + KIND_AT.index(kind)


def is_owner_of(me, kind):
    return (me % 4 == KIND_AT.index(kind)) & (me < 8)


def to_owner_kernel(count, *refs):
    block_refs, out_ref, send_sem, recv_sem = refs[:4], refs[4], refs[5], refs[6]
    me = lax.axis_index("dp")
    out_ref[...] = jnp.zeros_like(out_ref)
    greet([{"dp": lax.rem(me + shift, count)} for shift in range(1, count)])

    def copy(kind, layer, source):
        width = block_refs[kind].shape[-1]
        return pltpu.make_async_remote_copy(
            src_ref=block_refs[kind].at[layer],
            dst_ref=out_ref.at[source, :, pl.ds(0, width)],
            send_sem=send_sem.at[2 * kind + layer],
            recv_sem=recv_sem.at[source],
            device_id={"dp": owner_of(kind, layer)},
            device_id_type=MESH,
        )

    for kind in range(4):
        for layer in range(2):

            @pl.when(me != owner_of(kind, layer))
            def _():
                copy(kind, layer, me).start()

            @pl.when(me == owner_of(kind, layer))
            def _():
                out_ref[me, :, : block_refs[kind].shape[-1]] = block_refs[kind][layer]

    for kind in range(4):

        @pl.when(is_owner_of(me, kind))
        def _():
            @pl.loop(0, count)
            def _(source):
                @pl.when(source != me)
                def _():
                    copy(kind, 0, source).wait_recv()

        for layer in range(2):

            @pl.when(me != owner_of(kind, layer))
            def _():
                copy(kind, layer, me).wait_send()


def to_owner(blocks, collective_id):
    count = lax.axis_size("dp")
    rows = blocks[0].shape[1]
    wide = max(block.shape[2] for block in blocks)
    return pl.pallas_call(
        functools.partial(to_owner_kernel, count),
        out_shape=jax.ShapeDtypeStruct((count, rows, wide), jnp.float32),
        in_specs=[vmem()] * 4,
        out_specs=vmem(),
        scratch_shapes=[pltpu.SemaphoreType.DMA((8,)), pltpu.SemaphoreType.DMA((count,))],
        compiler_params=comm_params(collective_id),
        name="to_owner",
    )(*blocks)


def from_owner_kernel(count, widths, x_ref, out_ref, send_sem, recv_sem):
    me = lax.axis_index("dp")
    greet([{"dp": lax.rem(me + shift, count)} for shift in range(1, count)])

    def copy(kind, matrix, target):
        columns = pl.ds(0, widths[kind])
        return pltpu.make_async_remote_copy(
            src_ref=x_ref.at[target, :, columns],
            dst_ref=out_ref.at[matrix, :, columns],
            send_sem=send_sem.at[target],
            recv_sem=recv_sem.at[matrix],
            device_id={"dp": target},
            device_id_type=MESH,
        )

    for kind in range(4):

        @pl.when(is_owner_of(me, kind))
        def _():
            @pl.loop(0, count)
            def _(target):
                @pl.when(target != me)
                def _():
                    copy(kind, me, target).start()

            out_ref[me] = x_ref[me]

    for kind in range(4):
        for layer in range(2):
            matrix = owner_of(kind, layer)

            @pl.when(me != matrix)
            def _():
                copy(kind, matrix, me).wait_recv()

        @pl.when(is_owner_of(me, kind))
        def _():
            @pl.loop(0, count)
            def _(target):
                @pl.when(target != me)
                def _():
                    copy(kind, me, target).wait_send()


def from_owner(x, widths, collective_id):
    count = lax.axis_size("dp")
    return pl.pallas_call(
        functools.partial(from_owner_kernel, count, widths),
        out_shape=jax.ShapeDtypeStruct((8,) + x.shape[1:], x.dtype),
        in_specs=[vmem()],
        out_specs=vmem(),
        scratch_shapes=[pltpu.SemaphoreType.DMA((count,)), pltpu.SemaphoreType.DMA((8,))],
        compiler_params=comm_params(collective_id),
        name="from_owner",
    )(x)


def gram_kernel(x_ref, out_ref, high, rest, upper, chip, got, whole, send_sem, recv_sem):
    h = lax.axis_index("head")
    c = h % 2
    greet([{"head": h ^ other} for other in (1, 2)])
    third = PIECE_COLS
    values = x_ref[...]
    high[...] = to_bf16(values)
    rest[...] = to_bf16(values - high[...].astype(jnp.float32))

    def dots(first, second):
        return (
            dot_nt(high[first], high[second])
            + dot_nt(high[first], rest[second])
            + dot_nt(rest[first], high[second])
        )

    r0, r1, r2 = (pl.ds(third * place, third) for place in range(3))
    upper[0] = dots(r0, pl.ds(0, 3 * third))
    upper[1, :, : 2 * third] = dots(r1, pl.ds(third, 2 * third))
    upper[1, :, 2 * third :] = dots(r2, r2)

    def step(place, source, target, peer):
        copy = send_to(source, target, (send_sem, recv_sem), place, peer)
        copy.start()
        copy.wait()

    step(0, upper.at[1 - c], got.at[0], h ^ 1)
    chip[...] = upper[c] + got[0]
    step(1, chip, got.at[1], h ^ 2)
    whole[c] = chip[...] + got[1]
    step(2, whole.at[c], whole.at[c], h ^ 1)
    out_ref[r0, :] = whole[0]
    out_ref[r1, pl.ds(third, 2 * third)] = whole[1, :, : 2 * third]
    out_ref[r2, r2] = whole[1, :, 2 * third :]
    out_ref[r1, r0] = whole[0, :, third : 2 * third].T
    out_ref[r2, r0] = whole[0, :, 2 * third :].T
    out_ref[r2, r1] = whole[1, :, third : 2 * third].T


def gram_sum(x, collective_id):
    rows, columns = x.shape
    third = PIECE_COLS
    return pl.pallas_call(
        gram_kernel,
        out_shape=jax.ShapeDtypeStruct((rows, rows), jnp.float32),
        in_specs=[vmem()],
        out_specs=vmem(),
        scratch_shapes=[
            pltpu.VMEM((rows, columns), jnp.bfloat16),
            pltpu.VMEM((rows, columns), jnp.bfloat16),
            pltpu.VMEM((2, third, rows), jnp.float32),
            pltpu.VMEM((third, rows), jnp.float32),
            pltpu.VMEM((2, third, rows), jnp.float32),
            pltpu.VMEM((2, third, rows), jnp.float32),
            pltpu.SemaphoreType.DMA((3,)),
            pltpu.SemaphoreType.DMA((3,)),
        ],
        compiler_params=comm_params(collective_id),
        name="gram_sum",
    )(x)


def send_to(source, target, sems, place, peer):
    return pltpu.make_async_remote_copy(
        src_ref=source,
        dst_ref=target,
        send_sem=sems[0].at[place],
        recv_sem=sems[1].at[place],
        device_id={"head": peer},
        device_id_type=MESH,
    )


def half_mask(half):
    lane = lax.broadcasted_iota(jnp.int32, (1, 128), 1)
    return (lane // 64) == half


def dot_nt(left, right):
    return lax.dot_general(
        left, right, (((1,), (1,)), ((), ())), preferred_element_type=jnp.float32
    )


def dot_nn(left, right):
    return lax.dot_general(
        left, right, (((1,), (0,)), ((), ())), preferred_element_type=jnp.float32
    )


def dot_tn(left, right):
    return lax.dot_general(
        left, right, (((0,), (0,)), ((), ())), preferred_element_type=jnp.float32
    )


def lanes(start, size):
    return pl.ds(pl.multiple_of(start, 128), size)


def window(head):
    return 128 * ((3 * head) // 2)


def bring_heads(h, rows_ref, pair_all, quad_all, parts, sems):
    c = h % 2
    tile = quad_all.shape[1]
    own, shared = pl.ds(0, 2 * tile), pl.ds(2 * tile, tile)
    pair, quad = [], []
    for part in range(parts):
        pair.append(
            send_to(
                rows_ref.at[own, lanes(part * D + (1 - c) * HALF, HALF)],
                pair_all.at[c, :, pl.ds(part * HALF, HALF)],
                sems, part, h ^ 1,
            )
        )
        for other in (1, 2, 3):
            quad.append(
                send_to(
                    rows_ref.at[shared, lanes(part * D + window(h ^ other), WIDE)],
                    quad_all.at[h, :, pl.ds(part * WIDE, WIDE)],
                    sems, 3 * other + part, h ^ other,
                )
            )
    for copy in pair + quad:
        copy.start()
    for part in range(parts):
        pair_all[c, :, part * HALF : (part + 1) * HALF] = rows_ref[
            own, lanes(part * D + c * HALF, HALF)
        ]
        quad_all[h, :, part * WIDE : (part + 1) * WIDE] = rows_ref[
            shared, lanes(part * D + window(h), WIDE)
        ]
    return pair, quad


def return_pair(h, pair_out, rows_ref, parts, sems):
    c = h % 2
    own = pl.ds(0, pair_out.shape[1])
    copies = []
    for part in range(parts):
        columns = lanes(part * D + c * HALF, HALF)
        copies.append(
            send_to(
                pair_out.at[1 - c, :, pl.ds(part * HALF, HALF)], rows_ref.at[own, columns],
                sems, 12 + part, h ^ 1,
            )
        )
        copies[-1].start()
        rows_ref[own, columns] = pair_out[c, :, part * HALF : (part + 1) * HALF]
    return copies


def return_quad(h, quad_out, quad_got, sems):
    copies = []
    for other in (1, 2, 3):
        copies.append(
            send_to(quad_out.at[h ^ other], quad_got.at[h], sems, 14 + other, h ^ other)
        )
        copies[-1].start()
    quad_got[h] = quad_out[h]
    return copies


def merge_quad(quad_got, rows_ref, parts):
    tile = quad_got.shape[1]
    shared = slice(2 * tile, 3 * tile)
    for part in range(parts):
        base, start = part * WIDE, part * D
        for side in range(2):
            left, right = quad_got.at[2 * side], quad_got.at[2 * side + 1]
            at = start + side * HALF
            rows_ref[shared, at : at + 128] = left[:, base : base + 128]
            rows_ref[shared, at + 128 : at + 256] = (
                left[:, base + 128 : base + 256] + right[:, base : base + 128]
            )
            rows_ref[shared, at + 256 : at + 384] = right[:, base + 128 : base + 256]


def row_half(half):
    row = lax.broadcasted_iota(jnp.int32, (128, 1), 0)
    return (row // 64) == half


CHUNKS = ((0, 384), (384, 832))


def probabilities(scores):
    top = jnp.max(scores, 0, keepdims=True)
    exponent = jnp.exp(scores - top)
    total = jnp.sum(exponent, 0, keepdims=True)
    return exponent * (1.0 / total), top + jnp.log(total)


def attend_kernel(rows_ref, mixed_ref, pair_all, quad_all, log_ref, pair_out, quad_out, quad_got,
                  joined, send_sem, recv_sem):
    h = lax.axis_index("head")
    sems = (send_sem, recv_sem)
    greet([{"head": h ^ other} for other in (1, 2, 3)])
    pair_copies, quad_copies = bring_heads(h, rows_ref, pair_all, quad_all, 3, sems)
    tile = quad_all.shape[1]
    length = 4 * tile

    def heads(query, keys, values, members):
        values_t = values.T
        for start, stop in CHUNKS:
            mixed = jnp.zeros((128, stop - start), jnp.float32)
            for half, log_row in members:
                chunk = jnp.where(half_mask(half), query[start:stop], 0) * 0.125
                probability, logs = probabilities(dot_nt(keys, chunk))
                mixed = mixed + dot_nn(
                    jnp.where(row_half(half), values_t, 0), to_bf16(probability)
                )
                log_ref[log_row : log_row + 1, start:stop] = logs
            joined[start:stop, :] = to_bf16(mixed.T)

    log_ref[...] = jnp.zeros_like(log_ref)
    quad_out[...] = jnp.zeros_like(quad_out)
    for copy in pair_copies:
        copy.wait()
    for pair in range(3):
        query, keys, values = (
            pair_all[:, :, part * HALF + pair * 128 : part * HALF + pair * 128 + 128].reshape(
                length, 128
            )
            for part in range(3)
        )
        heads(query, keys, values, ((0, 2 * pair), (1, 2 * pair + 1)))
        pair_out[:, :, pair * 128 : pair * 128 + 128] = joined[...].reshape(2, 2 * tile, 128)
    back = return_pair(h, pair_out, mixed_ref, 1, sems)
    for copy in quad_copies:
        copy.wait()
    for member in range(3):
        place = h % 2 + member
        at = (place // 2) * 128
        query, keys, values = (
            quad_all[:, :, lanes(part * WIDE + at, 128)].reshape(length, 128) for part in range(3)
        )
        heads(query, keys, values, ((place % 2, 6 + member),))
        quad_out[:, :, lanes(at, 128)] += joined[...].reshape(4, tile, 128)
    back_quad = return_quad(h, quad_out, quad_got, sems)
    for copy in back + back_quad:
        copy.wait()
    merge_quad(quad_got, mixed_ref, 1)


def attend(rows, collective_id):
    frames = rows.shape[0]
    tile = frames // 3
    low = jnp.bfloat16
    return pl.pallas_call(
        attend_kernel,
        out_shape=[
            jax.ShapeDtypeStruct((frames, D), low),
            jax.ShapeDtypeStruct((2, 2 * tile, 3 * HALF), low),
            jax.ShapeDtypeStruct((4, tile, 3 * WIDE), low),
            jax.ShapeDtypeStruct((16, 4 * tile), jnp.float32),
        ],
        in_specs=[vmem()],
        out_specs=[vmem()] * 4,
        scratch_shapes=[
            pltpu.VMEM((2, 2 * tile, HALF), low),
            pltpu.VMEM((4, tile, WIDE), low),
            pltpu.VMEM((4, tile, WIDE), low),
            pltpu.VMEM((4 * tile, 128), low),
            pltpu.SemaphoreType.DMA((18,)),
            pltpu.SemaphoreType.DMA((18,)),
        ],
        compiler_params=comm_params(collective_id),
        name="attend",
    )(rows)


def attend_back_kernel(pair_all, quad_all, log_ref, grad_ref, rows_ref, pair_mixed, quad_mixed,
                       pair_out, quad_out, quad_got, grad_keys, grad_values, grads, send_sem,
                       recv_sem):
    h = lax.axis_index("head")
    sems = (send_sem, recv_sem)
    greet([{"head": h ^ other} for other in (1, 2, 3)])
    pair_copies, quad_copies = bring_heads(h, grad_ref, pair_mixed, quad_mixed, 1, sems)
    tile = quad_all.shape[1]
    length = 4 * tile

    def heads(query, keys, values, grad_out, members):
        keys_t = keys.T
        grad_keys[...] = jnp.zeros_like(grad_keys)
        grad_values[...] = jnp.zeros_like(grad_values)
        for start, stop in CHUNKS:
            grad_query = jnp.zeros((128, stop - start), jnp.float32)
            for half, log_row in members:
                mask = half_mask(half)
                chunk = jnp.where(mask, query[start:stop], 0) * 0.125
                grad_chunk = jnp.where(mask, grad_out[start:stop], 0)
                probability = jnp.exp(
                    dot_nt(keys, chunk) - log_ref[log_row : log_row + 1, start:stop]
                )
                grad_prob = dot_nt(values, grad_chunk)
                mean = jnp.sum(probability * grad_prob, 0, keepdims=True)
                grad_scores = to_bf16(probability * (grad_prob - mean))
                grad_keys[...] += dot_nn(grad_scores, chunk)
                grad_values[...] += dot_nn(to_bf16(probability), grad_chunk)
                grad_query = grad_query + dot_nn(
                    jnp.where(row_half(half), keys_t, 0), grad_scores
                )
            grads[0, start:stop, :] = to_bf16(grad_query.T * 0.125)
        grads[1] = to_bf16(grad_keys[...])
        grads[2] = to_bf16(grad_values[...])

    quad_out[...] = jnp.zeros_like(quad_out)
    for copy in pair_copies:
        copy.wait()
    for pair in range(3):
        at = [part * HALF + pair * 128 for part in range(3)]
        query, keys, values = (
            pair_all[:, :, start : start + 128].reshape(length, 128) for start in at
        )
        grad_out = pair_mixed[:, :, at[0] : at[0] + 128].reshape(length, 128)
        heads(query, keys, values, grad_out, ((0, 2 * pair), (1, 2 * pair + 1)))
        for part in range(3):
            pair_out[:, :, at[part] : at[part] + 128] = grads[part].reshape(2, 2 * tile, 128)
    back = return_pair(h, pair_out, rows_ref, 3, sems)
    for copy in quad_copies:
        copy.wait()
    for member in range(3):
        place = h % 2 + member
        at = (place // 2) * 128
        query, keys, values = (
            quad_all[:, :, lanes(part * WIDE + at, 128)].reshape(length, 128) for part in range(3)
        )
        grad_out = quad_mixed[:, :, lanes(at, 128)].reshape(length, 128)
        heads(query, keys, values, grad_out, ((place % 2, 6 + member),))
        for part in range(3):
            quad_out[:, :, lanes(part * WIDE + at, 128)] += grads[part].reshape(4, tile, 128)
    back_quad = return_quad(h, quad_out, quad_got, sems)
    for copy in back + back_quad:
        copy.wait()
    merge_quad(quad_got, rows_ref, 3)


def attend_back(pair_all, quad_all, logs, grad_mixed, collective_id):
    rows, tile = pair_all.shape[1], quad_all.shape[1]
    low = jnp.bfloat16
    return pl.pallas_call(
        attend_back_kernel,
        out_shape=jax.ShapeDtypeStruct((3 * tile, 3 * D), low),
        in_specs=[vmem()] * 4,
        out_specs=vmem(),
        scratch_shapes=[
            pltpu.VMEM((2, rows, HALF), low),
            pltpu.VMEM((4, tile, WIDE), low),
            pltpu.VMEM(pair_all.shape, low),
            pltpu.VMEM(quad_all.shape, low),
            pltpu.VMEM(quad_all.shape, low),
            pltpu.VMEM((4 * tile, 128), jnp.float32),
            pltpu.VMEM((4 * tile, 128), jnp.float32),
            pltpu.VMEM((3, 4 * tile, 128), low),
            pltpu.SemaphoreType.DMA((18,)),
            pltpu.SemaphoreType.DMA((18,)),
        ],
        compiler_params=comm_params(collective_id),
        name="attend_back",
    )(pair_all, quad_all, logs, grad_mixed)


def cross_frames(clip, tile):
    return slice(2 * clip, 2 + clip), (2 - clip) * tile


def masked_scores(keys, query_half, length):
    token = lax.broadcasted_iota(jnp.int32, (keys.shape[0], 1), 0)
    return jnp.where(token < length, dot_nt(keys, query_half), -1e30)


def cross_kernel(query_ref, keys_ref, values_ref, len_ref, out_ref):
    tile = query_ref.shape[1]
    for clip in range(2):
        tiles, count = cross_frames(clip, tile)
        query = query_ref[tiles].reshape(count, 128)
        values_t = values_ref[clip].T
        mixed = jnp.zeros((128, count), jnp.float32)
        for half in range(2):
            chunk = jnp.where(half_mask(half), query, 0) * 0.125
            probability, _ = probabilities(masked_scores(keys_ref[clip], chunk, len_ref[clip]))
            mixed = mixed + dot_nn(jnp.where(row_half(half), values_t, 0), to_bf16(probability))
        out_ref[tiles] = to_bf16(mixed.T).reshape(2 - clip, tile, 128)


def cross(query, pair_kv, lengths):
    _, tile, width = query.shape
    blocks = width // 128
    tokens = pair_kv.shape[1]
    return pl.pallas_call(
        cross_kernel,
        grid=(blocks,),
        out_shape=jax.ShapeDtypeStruct(query.shape, jnp.bfloat16),
        in_specs=[
            pl.BlockSpec((3, tile, 128), lambda i: (0, 0, i)),
            pl.BlockSpec((2, tokens, 128), lambda i: (0, 0, i)),
            pl.BlockSpec((2, tokens, 128), lambda i: (0, 0, blocks + i)),
            pl.BlockSpec(memory_space=pltpu.SMEM),
        ],
        out_specs=pl.BlockSpec((3, tile, 128), lambda i: (0, 0, i)),
        compiler_params=pltpu.CompilerParams(vmem_limit_bytes=VMEM_BYTES),
        name="cross",
    )(query, pair_kv, pair_kv, lengths)


def cross_back_kernel(query_ref, keys_ref, values_ref, grad_ref, len_ref, grad_query_ref,
                      grad_keys_ref, grad_values_ref):
    tile = query_ref.shape[1]
    tokens = keys_ref.shape[1]
    for clip in range(2):
        tiles, count = cross_frames(clip, tile)
        keys, values = keys_ref[clip], values_ref[clip]
        query = query_ref[tiles].reshape(count, 128)
        grad = grad_ref[tiles].reshape(count, 128)
        keys_t = keys.T
        grad_keys = jnp.zeros((tokens, 128), jnp.float32)
        grad_values = jnp.zeros((tokens, 128), jnp.float32)
        grad_query = jnp.zeros((128, count), jnp.float32)
        for half in range(2):
            mask = half_mask(half)
            chunk = jnp.where(mask, query, 0) * 0.125
            grad_half = jnp.where(mask, grad, 0)
            probability, _ = probabilities(masked_scores(keys, chunk, len_ref[clip]))
            grad_prob = dot_nt(values, grad_half)
            mean = jnp.sum(probability * grad_prob, 0, keepdims=True)
            grad_scores = to_bf16(probability * (grad_prob - mean))
            grad_keys = grad_keys + dot_nn(grad_scores, chunk)
            grad_values = grad_values + dot_nn(to_bf16(probability), grad_half)
            grad_query = grad_query + dot_nn(jnp.where(row_half(half), keys_t, 0), grad_scores)
        grad_query_ref[tiles] = to_bf16(grad_query.T * 0.125).reshape(2 - clip, tile, 128)
        grad_keys_ref[clip] = to_bf16(grad_keys)
        grad_values_ref[clip] = to_bf16(grad_values)


def cross_back(query, pair_kv, lengths, grad):
    _, tile, width = query.shape
    blocks = width // 128
    tokens = pair_kv.shape[1]
    rows_spec = pl.BlockSpec((3, tile, 128), lambda i: (0, 0, i))
    keys_spec = pl.BlockSpec((2, tokens, 128), lambda i: (0, 0, i))
    return pl.pallas_call(
        cross_back_kernel,
        grid=(blocks,),
        out_shape=[
            jax.ShapeDtypeStruct(query.shape, jnp.bfloat16),
            jax.ShapeDtypeStruct((2, tokens, width), jnp.bfloat16),
            jax.ShapeDtypeStruct((2, tokens, width), jnp.bfloat16),
        ],
        in_specs=[
            rows_spec,
            keys_spec,
            pl.BlockSpec((2, tokens, 128), lambda i: (0, 0, blocks + i)),
            rows_spec,
            pl.BlockSpec(memory_space=pltpu.SMEM),
        ],
        out_specs=[rows_spec, keys_spec, keys_spec],
        compiler_params=pltpu.CompilerParams(vmem_limit_bytes=VMEM_BYTES),
        name="cross_back",
    )(query, pair_kv, pair_kv, grad, lengths)


def body(
    clean_latents,
    noise_draw,
    timesteps,
    captions,
    cap_len,
    pairing,
    adam_step,
    qkv_weight,
    out_weight,
    up_weight,
    down_weight,
    ada_weight,
    time_weight,
    io_weight,
    qkv_moment,
    out_moment,
    up_moment,
    down_moment,
    ada_first,
    ada_second,
    time_first,
    time_second,
    io_first,
    io_second,
):
    data_count = lax.axis_size("dp")
    head_count = lax.axis_size("head")
    clip_count, tile, channels = clean_latents.shape
    length = tile * head_count
    rows_own = qkv_weight.shape[1]
    d, h = lax.axis_index("dp"), lax.axis_index("head")
    own_clip, core = h // 2, h % 2
    own_row = d * rows_own
    linked = data_count == 8 and rows_own == 96
    ids = iter(range(64))

    def swap(x, axis):
        return exchange(x, axis, True, next(ids))

    def spread(x, axis):
        return exchange(x, axis, False, next(ids))

    def by_tile(values):
        own = lax.dynamic_slice_in_dim(values, own_clip, 1, 0)
        return jnp.concatenate([own, own, values[2:3]])

    def by_clip(tiles):
        own = tiles[0:1] + tiles[1:2]
        none = jnp.zeros_like(own)
        return jnp.concatenate(
            [jnp.where(own_clip == 0, own, none), jnp.where(own_clip == 1, own, none), tiles[2:3]]
        )

    block = 3 * D // head_count
    share = D // head_count
    is_first = core == 0
    latents = jnp.concatenate([clean_latents, noise_draw], -1).transpose(0, 2, 1)
    latents = latents.reshape(-1, tile)

    def with_edge(qkv, out, edge):
        return jnp.where(
            is_first,
            jnp.concatenate([qkv, edge, out[..., :128]], -1),
            jnp.concatenate([qkv[..., 64:], edge, out], -1),
        )

    def without_edge(own, edge):
        qkv = jnp.where(
            is_first, own[..., :block], jnp.concatenate([edge, own[..., : block - 64]], -1)
        )
        out = jnp.where(
            is_first, jnp.concatenate([own[..., block + 64 :], edge], -1), own[..., block:]
        )
        return qkv, out

    keep_mask = jnp.arange(CAP)[None, :] < cap_len[:, None]
    cap_mean = product("ft,ftd->fd", keep_mask.astype(jnp.bfloat16), captions) / cap_len[
        :, None
    ].astype(jnp.float32)
    cap_unit = cap_mean * lax.rsqrt(jnp.mean(cap_mean * cap_mean, -1, keepdims=True) + 1e-06)
    own_captions = jnp.concatenate([lax.dynamic_slice_in_dim(captions, own_clip, 1, 0), captions[2:3]])
    own_lengths = jnp.concatenate([lax.dynamic_slice_in_dim(cap_len, own_clip, 1, 0), cap_len[2:3]])

    qkv_low, out_low = to_bf16(qkv_weight), to_bf16(out_weight)
    edge = jnp.where(is_first, out_low[..., 128:], qkv_low[..., :64])
    time_cols = time_weight.shape[1]
    io_cols = io_weight.shape[2]
    ada_cols = ada_weight.shape[2]
    ada_bf = to_bf16(ada_weight)
    io_flat = io_weight.transpose(1, 0, 2).reshape(rows_own, 2 * io_cols)
    small_own = jnp.pad(
        to_bf16(jnp.concatenate([time_weight, io_flat], 1)),
        ((0, 0), (0, WIDE - time_cols - 2 * io_cols)),
    )
    table_bf = to_bf16(time_table(timesteps, D))

    def listed(first_groups):
        listed_groups = [small_own]
        for layer in range(2):
            listed_groups.append(first_groups[layer])
            listed_groups.append(to_bf16(up_weight[layer]))
            listed_groups.append(to_bf16(down_weight[layer]))
        return listed_groups

    if linked:
        none = jnp.zeros_like(edge)
        edge = jnp.where(
            is_first, jnp.concatenate([edge, none], -1), jnp.concatenate([none, edge], -1)
        )
        shared = jnp.concatenate(
            [
                jnp.zeros((clip_count, D)),
                table_bf.astype(jnp.float32),
                cap_unit,
                jnp.zeros((16 - 3 * clip_count, D)),
            ]
        )
        gathered, latents_all, shared_all, mods = gather_whole(
            listed(with_edge(qkv_low, out_low, none)),
            (1, 4),
            edge,
            latents,
            jnp.pad(shared, ((0, 0), (0, head_count * WIDE - D))),
            jnp.pad(table_bf, ((0, 16 - clip_count), (0, 0))),
            ada_bf,
            next(ids),
        )
        start = (d // 2) * WIDE + (d % 2) * rows_own
        hidden_own = lax.dynamic_slice(
            shared_all, (0, 0, start), (data_count, clip_count, rows_own)
        ).reshape(-1, rows_own)
        table_own = lax.dynamic_slice(
            shared_all, (0, clip_count, own_row), (data_count, clip_count, rows_own)
        ).reshape(-1, rows_own)
        cap_all = shared_all[:, 2 * clip_count : 3 * clip_count, :D].reshape(-1, D)
        signal_own = to_bf16(double_silu(hidden_own))
        mods = mods[:, :clip_count]
    else:
        edge = lax.ppermute(edge, "head", [(place, place ^ 1) for place in range(head_count)])
        gathered = [gather_general(own) for own in listed(with_edge(qkv_low, out_low, edge))]
        latents_all = spread(latents, "head")
        time_full = gathered[0].reshape(D, head_count, WIDE)[:, :, :time_cols].reshape(D, D)
        time_hidden = jnp.dot(table_bf, time_full, preferred_element_type=jnp.float32)
        shared = jnp.concatenate([time_hidden, table_bf.astype(jnp.float32), cap_unit], 1)
        shared_all = spread(shared, "dp").reshape(-1, 3 * D)
        hidden_own = lax.dynamic_slice_in_dim(shared_all, own_row, rows_own, 1)
        table_own = lax.dynamic_slice_in_dim(shared_all, D + own_row, rows_own, 1)
        cap_all = shared_all[:, 2 * D :]
        signal_own = to_bf16(double_silu(hidden_own))
        mod_part = product("fd,ldn->fln", signal_own, ada_bf)
        mod_part = mod_part.reshape(data_count, clip_count, 2 * ada_cols)
        mods = spread(jnp.sum(swap(mod_part, "dp"), 0), "head")
    up_full = [gathered[2], gathered[5]]
    down_full = [gathered[3], gathered[6]]
    io_full = (
        gathered[0]
        .reshape(D, head_count, WIDE)[:, :, time_cols : time_cols + 2 * io_cols]
        .reshape(D, head_count, 2, io_cols)
        .transpose(2, 0, 1, 3)
        .reshape(2, D, channels)
    )
    mod_all = (
        mods.reshape(head_count, clip_count, 2, ada_cols)
        .transpose(1, 2, 0, 3)
        .reshape(clip_count, 2, 6 * D)
    )
    tile_mods = by_tile(mod_all)

    def split_first(whole):
        qkv, out = [], []
        for side in range(2):
            at = 2 * side * D
            qkv += [whole[:, at : at + 640], whole[:, at + D : at + D + 512]]
            out += [whole[:, at + 640 : at + D], whole[:, at + D + 512 : at + 2 * D]]
        return jnp.concatenate(qkv, 1), jnp.concatenate(out, 1)

    def join_first(qkv, out):
        columns = []
        for side in range(2):
            q, o = side * 2 * block, side * 2 * share
            columns += [qkv[:, q : q + 640], out[:, o : o + 128]]
            columns += [qkv[:, q + 640 : q + 1152], out[:, o + 128 : o + 384]]
        return jnp.concatenate(columns, 1)

    if linked:
        qkv_full = [gathered[1 + 3 * layer][:, : 3 * D] for layer in range(2)]
        out_full = [gathered[1 + 3 * layer][:, 3 * D :] for layer in range(2)]
    else:
        qkv_full, out_full = zip(*[split_first(gathered[1 + 3 * layer]) for layer in range(2)])

    latents_all = latents_all.reshape(head_count, clip_count, 2 * channels, tile)
    own_latents = lax.dynamic_slice(
        latents_all, (2 * core, own_clip, 0, 0), (2, 1, 2 * channels, tile)
    )[:, 0]
    latents = jnp.concatenate(
        [own_latents, lax.dynamic_slice_in_dim(latents_all, h, 1, 0)[0, 2:3]]
    )
    clean_rows, noise_rows = latents[:, :channels], latents[:, channels:]
    tile_times = by_tile(timesteps)[:, None, None]
    input_bf = to_bf16((1.0 - tile_times) * clean_rows + tile_times * noise_rows)
    target = noise_rows - clean_rows
    hidden = product("fcl,dc->fld", input_bf, io_full[0])

    frames = clip_count * tile

    def layer_forward(layer_index, hidden):
        modulation = tile_mods[:, layer_index].reshape(clip_count, 1, 6, D)
        mod_parts = [modulation[:, :, member] for member in range(6)]
        normed = to_bf16(modulate(hidden, mod_parts[0], mod_parts[1]))
        weight = qkv_full[layer_index]
        if layer_index == 0:
            projected = to_bf16(product("fld,dn->fln", normed, weight))
            mixed, *attended = attend(projected.reshape(frames, 3 * D), next(ids))
            mixed = mixed.reshape(clip_count, tile, D)
        else:
            query = to_bf16(product("fld,dn->fln", normed, weight[:, :D]))
            pair_kv = to_bf16(product("ftd,dn->ftn", own_captions, weight[:, D:]))
            attended = (query, pair_kv)
            mixed = cross(query, pair_kv, own_lengths)
        branch = product("fle,de->fld", mixed, out_full[layer_index])
        middle = hidden + mod_parts[2] * branch
        normed2 = to_bf16(modulate(middle, mod_parts[3], mod_parts[4]))
        upper = product("fld,dn->fln", normed2, up_full[layer_index])
        active = to_bf16(soft_gelu(upper))
        down_out = product("fln,dn->fld", active, down_full[layer_index])
        kept = (hidden, mod_parts, normed, attended, mixed, branch, middle, normed2, upper,
                active, down_out)
        return (middle + mod_parts[5] * down_out, kept)

    saved_layers = []
    for layer_index in range(2):
        hidden, kept = layer_forward(layer_index, hidden)
        saved_layers.append(kept)
    final = norm_rows(hidden)
    final_bf = to_bf16(final)
    predicted = product("fld,dc->fcl", final_bf, io_full[1])
    errors = predicted - target
    flow_part = jnp.sum(jnp.mean(errors * errors, 1))
    grad_pred = to_bf16(2.0 * errors / channels)
    pool_sum = jnp.sum(spread(by_clip(jnp.sum(final, 1)), "head"), 0)
    pooled_out = pool_sum / length

    def contrast_of(pool_total):
        pooled = pool_total / length
        unit_rows = pooled * lax.rsqrt(jnp.mean(pooled * pooled, -1, keepdims=True) + 1e-06)
        logits = exact_product("id,jd->ij", unit_rows, cap_all) * (2.0 / math.sqrt(D))
        row_top = jnp.max(logits, -1, keepdims=True)
        log_total = row_top[:, 0] + jnp.log(jnp.sum(jnp.exp(logits - row_top), -1))
        picked = jnp.sum(
            jnp.where(jnp.arange(logits.shape[1])[None, :] == pairing[:, None], logits, 0.0), -1
        )
        return length * jnp.sum(log_total - picked)

    contrast_value, contrast_back = jax.vjp(contrast_of, pool_sum)
    grad_pool = by_tile(contrast_back(jnp.ones_like(contrast_value))[0])
    loss_part = flow_part + contrast_value / head_count
    grad_final = product("fcl,dc->fld", grad_pred, io_full[1]) + grad_pool[:, None, :]
    final_value, final_back = jax.vjp(norm_rows, hidden)
    grad_hidden = final_back(grad_final)[0]
    fin_grad = product("fcl,fld->dc", grad_pred, final_bf)
    plan, lefts, rights = [], [], []

    def listed_factors(factors, factor):
        factors.append(factor.reshape(-1, factor.shape[-1]))
        return len(factors) - 1

    mod_grads = [None, None]
    for layer_index in (1, 0):
        (
            layer_hidden,
            mod_parts,
            layer_normed,
            attended,
            layer_mixed,
            layer_branch,
            layer_middle,
            layer_normed2,
            layer_upper,
            layer_active,
            layer_down_out,
        ) = saved_layers[layer_index]
        weight = qkv_full[layer_index]
        d_gate2 = jnp.sum(layer_down_out * grad_hidden, axis=1, keepdims=True)
        grad_down = to_bf16(mod_parts[5] * grad_hidden)
        grad_active = product("fld,dn->fln", grad_down, down_full[layer_index])
        gelu_value, gelu_back = jax.vjp(soft_gelu, layer_upper)
        grad_upper = to_bf16(gelu_back(grad_active)[0])
        grad_normed2 = product("fln,dn->fld", grad_upper, up_full[layer_index])
        mod_value, mod_back = jax.vjp(modulate, layer_middle, mod_parts[3], mod_parts[4])
        grad_middle, d_shift2, d_scale2 = mod_back(grad_normed2)
        grad_middle = grad_middle + grad_hidden
        d_gate1 = jnp.sum(layer_branch * grad_middle, axis=1, keepdims=True)
        grad_branch = to_bf16(mod_parts[2] * grad_middle)
        grad_mixed = to_bf16(product("fld,de->fle", grad_branch, out_full[layer_index]))
        branch_place, branch_right = listed_factors(lefts, grad_branch), listed_factors(rights, layer_mixed)
        normed_place = listed_factors(lefts, layer_normed)
        if layer_index == 0:
            grad_proj = attend_back(*attended, grad_mixed.reshape(frames, D), next(ids))
            grad_normed = product("fn,dn->fd", grad_proj, weight)
            first = [(normed_place, listed_factors(rights, grad_proj), 0, 3 * D)]
        else:
            query, pair_kv = attended
            grad_query, grad_keys, grad_values = cross_back(query, pair_kv, own_lengths, grad_mixed)
            grad_normed = product("fln,dn->fld", grad_query, weight[:, :D])
            caption_place = listed_factors(lefts, own_captions)
            first = [
                (normed_place, listed_factors(rights, grad_query), 0, D),
                (caption_place, listed_factors(rights, grad_keys), D, 2 * D),
                (caption_place, listed_factors(rights, grad_values), 2 * D, 3 * D),
            ]
        first.append((branch_place, branch_right, 3 * D, 4 * D))
        plan.append(
            (
                tuple(first),
                (listed_factors(lefts, layer_normed2), listed_factors(rights, grad_upper)),
                (listed_factors(lefts, grad_down), listed_factors(rights, layer_active)),
            )
        )
        first_value, first_back = jax.vjp(modulate, layer_hidden, mod_parts[0], mod_parts[1])
        grad_in, d_shift1, d_scale1 = first_back(grad_normed.reshape(clip_count, tile, D))
        mod_grads[layer_index] = jnp.concatenate(
            [d_shift1, d_scale1, d_gate1, d_shift2, d_scale2, d_gate2], -1
        )[:, 0]
        grad_hidden = grad_in + grad_middle
    in_grad = product("fld,fcl->dc", to_bf16(grad_hidden), input_bf)

    mod_size = clip_count * 2 * ada_cols
    io_size = rows_own * 2 * io_cols
    mod_grad = by_clip(jnp.stack(mod_grads, 1)).reshape(clip_count, 2, head_count, ada_cols)
    mod_grad = mod_grad.transpose(2, 0, 1, 3).reshape(head_count, clip_count, 2 * ada_cols)
    io_part = (
        jnp.stack([in_grad, fin_grad])
        .reshape(2, data_count, rows_own, head_count, io_cols)
        .transpose(3, 1, 0, 2, 4)
        .reshape(head_count, data_count, io_size)
    )
    signal_own_value, signal_back = jax.vjp(double_silu, hidden_own)
    if linked:

        def padded_clips(values):
            values = values.reshape(data_count, clip_count, rows_own)
            values = jnp.pad(values, ((0, 0), (0, 8 - clip_count), (0, 0)))
            return values.reshape(-1, rows_own)

        io_lines = -(-io_size // 1024) * 8
        io_part = jnp.pad(io_part, ((0, 0), (0, 0), (0, io_lines * 128 - io_size)))
        smalls = (
            jnp.pad(loss_part.reshape(1, 1), ((0, 7), (1, 126))),
            jnp.pad(mod_grad, ((0, 0), (0, 8 - clip_count), (0, 0))),
            io_part.reshape(head_count, data_count, io_lines, 128),
            padded_clips(signal_own.astype(jnp.float32)),
            padded_clips(signal_back(jnp.ones_like(hidden_own))[0]),
            padded_clips(table_own),
            ada_bf,
        )
        owned, totals, edge, ada_grad, time_grad, io_grad = reduce_whole(
            tuple(plan), lefts, rights, smalls, next(ids)
        )
        totals = totals[0, :2]
        edge = edge[::-1]
        edge = jnp.where(is_first, edge[..., :64], edge[..., 64:])
        time_grad = jnp.concatenate([time_grad[0], time_grad[1]], 1)
        io_grad = io_grad.reshape(-1)[:io_size].reshape(2, rows_own, io_cols)
    else:
        io_grad = lax.psum(io_part, ("dp", "head"))
        io_grad = lax.dynamic_slice(io_grad, (h, d, 0), (1, 1, io_size))
        io_grad = io_grad.reshape(2, rows_own, io_cols)
        mod_grad = jnp.sum(swap(mod_grad, "head"), 0)
        mod_grad = spread(mod_grad, "dp").reshape(-1, 2, ada_cols)
        ada_grad = exact_product("fd,fln->ldn", signal_own.astype(jnp.float32), mod_grad)
        grad_signal = exact_product("fln,ldn->fd", mod_grad, ada_bf.astype(jnp.float32))
        grad_signal = jnp.sum(spread(grad_signal, "head"), 0)
        grad_cond = spread(signal_back(grad_signal)[0], "dp").transpose(1, 0, 2).reshape(-1, D)
        time_grad = exact_product(
            "fd,fn->dn",
            table_own,
            lax.dynamic_slice_in_dim(grad_cond, h * time_cols, time_cols, 1),
        )

        def made(left_place, right_place):
            return product("fd,fn->dn", lefts[left_place], rights[right_place])

        owned = []
        for first, *pairs in plan:
            columns = jnp.concatenate([made(*source[:2]) for source in first], 1)
            owned.append(join_first(columns[:, : 3 * D], columns[:, 3 * D :]))
            owned += [made(*pair) for pair in pairs]
        owned = [reduce_general(part) for part in owned]
        square = sum((jnp.sum(part * part) for part in owned + [ada_grad, time_grad, io_grad]))
        totals = lax.psum(jnp.stack([square, loss_part]), ("dp", "head"))
        edge = jnp.stack([owned[3], owned[0]])
        edge = jnp.where(is_first, edge[..., block : block + 64], edge[..., block - 64 : block])
        edge = spread(edge.reshape(-1, 128), "head")
        edge = lax.dynamic_slice_in_dim(edge, h ^ 1, 1, 0).reshape(2, rows_own, 64)
    first_own = jnp.stack([owned[3], owned[0]])
    total_square, total_loss = totals[0], totals[1]
    qkv_shard, out_shard = without_edge(first_own, edge)
    shards = (
        qkv_shard,
        out_shard,
        jnp.stack([owned[4], owned[1]]),
        jnp.stack([owned[5], owned[2]]),
        ada_grad,
        time_grad[None],
        io_grad,
    )
    old_moments = (qkv_moment, out_moment, up_moment, down_moment)
    grad_norm = jnp.sqrt(total_square)
    clip_scale = jnp.minimum(1.0, CLIP_NORM / (grad_norm + 1e-06))
    moments = tuple(
        (MUON_BETA * old_moments[member] + clip_scale * shards[member] for member in range(4))
    )
    coeff_a, coeff_b, coeff_c = NEWTON_COEFFS
    widths = [-(-moment.shape[2] // 128) * 128 for moment in moments]
    padded = [
        jnp.pad(moment, ((0, 0), (0, 0), (0, width - moment.shape[2])))
        for moment, width in zip(moments, widths)
    ]
    own_matrix = to_owner(padded, next(ids)).reshape(D, -1)

    def near_product(form, left, right):
        return jnp.einsum(form, left, right, precision=lax.Precision.HIGH)

    gram = gram_sum(own_matrix, next(ids))
    unit = jnp.eye(D, dtype=jnp.float32)
    size_frob = jnp.sqrt(jnp.sum(gram * unit)) + 1e-07
    gram = gram / (size_frob * size_frob)
    factor = None
    for ns_step in range(NS_STEPS):
        poly = coeff_a * unit + coeff_b * gram + coeff_c * near_product("rk,kj->rj", gram, gram)
        factor = poly if factor is None else near_product("rk,kj->rj", poly, factor)
        if ns_step < NS_STEPS - 1:
            gram = near_product("rk,kj->rj", near_product("rk,kj->rj", poly, gram), poly)
    ortho_matrix = near_product("rk,kc->rc", factor, own_matrix) / size_frob
    ortho_back = to_bf16(ortho_matrix).reshape(data_count, rows_own, -1)
    ortho_back = from_owner(ortho_back, tuple(widths), next(ids)).astype(jnp.float32)
    ortho_rows = tuple(
        (
            jnp.stack(
                [
                    ortho_back[owner_of(member, layer), :, : moments[member].shape[2]]
                    for layer in range(2)
                ]
            )
            for member in range(4)
        )
    )
    muon_weights = (qkv_weight, out_weight, up_weight, down_weight)
    muon_new = tuple(
        (
            muon_weights[member] * (1.0 - MUON_RATE * MUON_DECAY)
            - MUON_RATE
            * 0.2
            * math.sqrt(max(D, muon_weights[member].shape[2] * head_count))
            * ortho_rows[member]
            for member in range(4)
        )
    )
    step_count = adam_step[0].astype(jnp.float32)
    ada_new, ada_first_new, ada_second_new = adam_update(
        ada_weight, clip_scale * shards[4], ada_first, ada_second, step_count
    )
    time_new, time_first_new, time_second_new = adam_update(
        time_weight, clip_scale * shards[5][0], time_first, time_second, step_count
    )
    io_new, io_first_new, io_second_new = adam_update(
        io_weight, clip_scale * shards[6], io_first, io_second, step_count
    )
    return (
        total_loss,
        grad_norm,
        pooled_out,
        muon_new[0],
        moments[0],
        muon_new[1],
        moments[1],
        muon_new[2],
        moments[2],
        muon_new[3],
        moments[3],
        ada_new,
        ada_first_new,
        ada_second_new,
        time_new,
        time_first_new,
        time_second_new,
        io_new,
        io_first_new,
        io_second_new,
    )


def solution(mesh):
    placed = (
        P("dp", "head", None),
        P("dp", "head", None),
        P("dp"),
        P("dp", None, None),
        P("dp"),
        P("dp"),
        P(),
        P(None, "dp", "head"),
        P(None, "dp", "head"),
        P(None, "dp", "head"),
        P(None, "dp", "head"),
        P(None, "dp", "head"),
        P("dp", "head"),
        P(None, "dp", "head"),
        P(None, "dp", "head"),
        P(None, "dp", "head"),
        P(None, "dp", "head"),
        P(None, "dp", "head"),
        P(None, "dp", "head"),
        P(None, "dp", "head"),
        P("dp", "head"),
        P("dp", "head"),
        P(None, "dp", "head"),
        P(None, "dp", "head"),
    )
    return jax.shard_map(
        body,
        mesh=mesh,
        in_specs=placed,
        out_specs=(
            P(),
            P(),
            P("dp", None),
            P(None, "dp", "head"),
            P(None, "dp", "head"),
            P(None, "dp", "head"),
            P(None, "dp", "head"),
            P(None, "dp", "head"),
            P(None, "dp", "head"),
            P(None, "dp", "head"),
            P(None, "dp", "head"),
            P(None, "dp", "head"),
            P(None, "dp", "head"),
            P(None, "dp", "head"),
            P("dp", "head"),
            P("dp", "head"),
            P("dp", "head"),
            P(None, "dp", "head"),
            P(None, "dp", "head"),
            P(None, "dp", "head"),
        ),
        check_vma=False,
    )
```

```python
import functools
import math

import jax
import jax.numpy as jnp
from jax import lax
from jax.experimental import pallas as pl
from jax.experimental.pallas import tpu as pltpu
from jax.sharding import PartitionSpec as P

D = 768
HEADS = 12
HDIM = 64
CAP = 256
NS_STEPS = 5


HIGHEST_PRECISION = lax.Precision.HIGHEST
NEWTON_COEFFS = (3.4445, -4.775, 2.0315)
CLIP_NORM = 1.0
MUON_RATE = 0.2
MUON_DECAY = 0.1
MUON_BETA = 0.95
ADAM_RATE = 0.02
ADAM_DECAY = 0.01
ADAM_FIRST = 0.9
ADAM_SECOND = 0.999


def to_bf16(values):
    return values.astype(jnp.bfloat16)


def sigmoid_unit(values):
    return values * jax.nn.sigmoid(values)


def double_silu(values):
    return sigmoid_unit(sigmoid_unit(values))


def soft_gelu(values):
    return (
        0.5
        * values
        * (1.0 + jnp.tanh(0.7978845608 * (values + 0.044715 * values * values * values)))
    )


def norm_rows(values):
    centre = values - jnp.mean(values, -1, keepdims=True)
    return centre * lax.rsqrt(jnp.mean(centre * centre, -1, keepdims=True) + 1e-06)


def modulate(hidden, shift, stretch):
    return norm_rows(hidden) * (1.0 + stretch) + shift


def time_table(timesteps, width):
    half_width = width // 2
    frequency = jnp.exp(
        -math.log(10000.0) * jnp.arange(half_width).astype(timesteps.dtype) / half_width
    )
    angles = 1000.0 * timesteps[:, None] * frequency[None, :]
    return jnp.concatenate([jnp.cos(angles), jnp.sin(angles)], axis=-1)


def product(form, left, right):
    return jnp.einsum(form, left, right, preferred_element_type=jnp.float32)


def exact_product(form, left, right):
    return jnp.einsum(form, left, right, precision=HIGHEST_PRECISION)


def adam_update(weight, grad_part, first_moment, second_moment, step_count):
    first_moment = ADAM_FIRST * first_moment + (1.0 - ADAM_FIRST) * grad_part
    second_moment = ADAM_SECOND * second_moment + (1.0 - ADAM_SECOND) * grad_part * grad_part
    first_fix = 1.0 - jnp.power(ADAM_FIRST, step_count)
    second_fix = 1.0 - jnp.power(ADAM_SECOND, step_count)
    direction = first_moment / first_fix / (jnp.sqrt(second_moment / second_fix) + 1e-08)
    return (weight - ADAM_RATE * (direction + ADAM_DECAY * weight), first_moment, second_moment)


MESH = pl.DeviceIdType.MESH
ROWS_A = 64
PIECE_COLS = 256
SLOTS = 4
HALF = 384
WIDE = 256
VMEM_BYTES = 56 * 1024 * 1024


def vmem():
    return pl.BlockSpec(memory_space=pltpu.VMEM)


def anywhere():
    return pl.BlockSpec(memory_space=pl.ANY)


def comm_params(collective_id):
    return pltpu.CompilerParams(
        collective_id=collective_id, has_side_effects=True, vmem_limit_bytes=VMEM_BYTES
    )


def greet(peers):
    barrier = pltpu.get_barrier_semaphore()
    for peer in peers:
        pl.semaphore_signal(barrier, inc=1, device_id=peer, device_id_type=MESH)
    pl.semaphore_wait(barrier, len(peers))


def exchange_kernel(axis, count, swapped, x_ref, out_ref, send_sem, recv_sem):
    me = lax.axis_index(axis)
    peers = [lax.rem(me + shift, count) for shift in range(1, count)]
    greet([{axis: peer} for peer in peers])
    copies = []
    for place, peer in enumerate(peers):
        copy = pltpu.make_async_remote_copy(
            src_ref=x_ref.at[peer] if swapped else x_ref,
            dst_ref=out_ref.at[me],
            send_sem=send_sem.at[place],
            recv_sem=recv_sem.at[place],
            device_id={axis: peer},
            device_id_type=MESH,
        )
        copy.start()
        copies.append(copy)
    out_ref[me] = x_ref[me] if swapped else x_ref[...]
    for copy in copies:
        copy.wait()


def exchange(x, axis, swapped, collective_id):
    count = lax.axis_size(axis)
    block = x.shape[1:] if swapped else x.shape
    return pl.pallas_call(
        functools.partial(exchange_kernel, axis, count, swapped),
        out_shape=jax.ShapeDtypeStruct((count,) + block, x.dtype),
        in_specs=[vmem()],
        out_specs=vmem(),
        scratch_shapes=[
            pltpu.SemaphoreType.DMA((count - 1,)),
            pltpu.SemaphoreType.DMA((count - 1,)),
        ],
        compiler_params=comm_params(collective_id),
        name="swap" if swapped else "spread",
    )(x)


def link_peers(d, h):
    return {
        "core": (d, h ^ 1),
        "y": (d, h ^ 2),
        "x": (d ^ 1, h),
        "zl": (d ^ 2, h),
        "zh": (d ^ 4, h),
    }


def first_column(side, core, start):
    if start < 512:
        return side * 1152 + core * 640 + start
    if start == 512:
        return (1 - core) * (side * 1152 + 512) + core * (3 * D + side * HALF + 128)
    return 3 * D + side * HALF + core * 256


def gather_pieces(widths, firsts):
    pieces = []
    for group, width in enumerate(widths):
        for start in range(0, width, PIECE_COLS):
            if group in firsts and start == 512:
                pieces += [(group, 512, 128), (group, 640, 128)]
            else:
                pieces.append((group, start, PIECE_COLS))
    return pieces


def gather_kernel(groups, firsts, *refs):
    own_refs = refs[:groups]
    edge_ref, latents_ref, shared_ref, table_ref, ada_ref = refs[groups : groups + 5]
    out_refs = refs[groups + 5 : 2 * groups + 5]
    latents_out, shared_out, mods_out = refs[2 * groups + 5 : 2 * groups + 8]
    (tail, edge_got, times, parts, parts_got, mine, send_sem, recv_sem, core_send, core_recv,
     local_sem, tail_sem, small_send, small_recv) = refs[2 * groups + 8 :]
    d = lax.axis_index("dp")
    h = lax.axis_index("head")
    peers = link_peers(d, h)
    heads = [(d, h ^ other) for other in (1, 2, 3)]
    datas = [(d ^ other, h) for other in range(1, 8)]
    greet(heads + datas)
    y, c = h // 2, h % 2
    zh, zl, x = d // 4, (d // 2) % 2, d % 2
    every = slice(None)
    pieces = gather_pieces([own.shape[1] for own in own_refs], firsts)
    order_a = (("zh", (zh, zl, x)), ("zl", (every, zl, x)), ("x", (every, every, x)),
               ("y", (every, every, every)))
    order_b = (("y", (zh, zl, x)), ("zh", (zh, zl, x)), ("zl", (every, zl, x)),
               ("x", (every, every, x)))

    def tail_of(piece):
        group, start, size = pieces[piece]
        if group in firsts and start == 2 * PIECE_COLS:
            return firsts.index(group)
        return None

    def source_of(piece, rows):
        group, start, size = pieces[piece]
        place = tail_of(piece)
        if place is not None:
            return tail.at[place, rows]
        return own_refs[group].at[rows, pl.ds(start, size)]

    def columns_of(piece, head):
        group, start, size = pieces[piece]
        if group in firsts:
            return pl.ds(pl.multiple_of(first_column(head // 2, head % 2, start), 128), size)
        return pl.ds(pl.multiple_of(head * own_refs[group].shape[1] + start, 128), size)

    def own_copy(piece):
        group = pieces[piece][0]
        return pltpu.make_async_copy(
            source_of(piece, pl.ds(0, own_refs[group].shape[0])),
            out_refs[group].at[zh, zl, x, :, columns_of(piece, h)],
            local_sem.at[piece],
        )

    def hop(piece, step, stream):
        group = pieces[piece][0]
        rows_all = own_refs[group].shape[0]
        rows = pl.ds(0, ROWS_A) if stream == 0 else pl.ds(ROWS_A, rows_all - ROWS_A)
        head = h if stream < 2 else h ^ 2
        peer, index = (order_a if stream == 0 else order_b)[step]
        view = out_refs[group].at[index + (rows, columns_of(piece, head))]
        return pltpu.make_async_remote_copy(
            src_ref=source_of(piece, rows) if step == 0 else view,
            dst_ref=view,
            send_sem=send_sem.at[piece, step, stream],
            recv_sem=recv_sem.at[piece, step, stream],
            device_id=peers[peer],
            device_id_type=MESH,
        )

    def streams(step):
        return range(2) if step == 0 else range(3)

    def across(piece, side):
        group = pieces[piece][0]
        view = out_refs[group].at[:, :, :, :, columns_of(piece, h ^ (2 * side))]
        return pltpu.make_async_remote_copy(
            src_ref=view,
            dst_ref=view,
            send_sem=core_send.at[piece, side],
            recv_sem=core_recv.at[piece, side],
            device_id=peers["core"],
            device_id_type=MESH,
        )

    def small(place, source, target, peer):
        return pltpu.make_async_remote_copy(
            src_ref=source,
            dst_ref=target,
            send_sem=small_send.at[place],
            recv_sem=small_recv.at[place],
            device_id=peer,
            device_id_type=MESH,
        )

    edge = small(0, edge_ref, edge_got, peers["core"])
    edge.start()
    tails = [
        pltpu.make_async_copy(
            own_refs[group].at[:, pl.ds(2 * PIECE_COLS, 128)], tail.at[place],
            tail_sem.at[place],
        )
        for place, group in enumerate(firsts)
    ]
    for copy in tails:
        copy.start()
    latents = [
        small(1 + place, latents_ref, latents_out.at[h], peer) for place, peer in enumerate(heads)
    ]
    for copy in latents:
        copy.start()
    latents_out[h] = latents_ref[...]
    bring_times = pltpu.make_async_copy(out_refs[0], times, tail_sem.at[len(firsts)])
    shares = [
        small(4 + place, mine, shared_out.at[d], peer) for place, peer in enumerate(datas)
    ]
    swaps = [
        small(11 + place, parts.at[d ^ (1 + place)], parts_got.at[d], peer)
        for place, peer in enumerate(datas)
    ]
    spreads = [
        small(18 + place, mods_out.at[h], mods_out.at[h], peer) for place, peer in enumerate(heads)
    ]

    def condition(turn):
        if turn == 2:
            edge.wait()
            for copy in tails:
                copy.wait()
            tail[...] = tail[...] + edge_got[...]
            for piece in range(len(pieces)):
                if tail_of(piece) is not None:
                    own_copy(piece).start()
        if turn == 6:
            for side in range(2):
                across(0, side).wait_recv()
            bring_times.start()
        if turn == 7:
            bring_times.wait()
            rows = times.shape[-2]
            mine[...] = shared_ref[...] + dot_nn(
                table_ref[...], times[...].reshape(8 * rows, times.shape[-1])
            )
            for copy in shares:
                copy.start()
            shared_out[d] = mine[...]
        if turn == 11:
            for copy in shares:
                copy.wait()
            count, lines, width = shared_out.shape
            signal = to_bf16(double_silu(shared_out[...])).reshape(count * lines, width)
            first = (d // 2) * WIDE + (d % 2) * ada_ref.shape[1]
            at = lax.broadcasted_iota(jnp.int32, (width, 128), 0)
            to = lax.broadcasted_iota(jnp.int32, (width, 128), 1)
            chosen = jnp.where((at == first + to) & (to < ada_ref.shape[1]), 1.0, 0.0)
            own = to_bf16(dot_nn(signal, to_bf16(chosen)))
            row = lax.broadcasted_iota(jnp.int32, (count * lines, count * lines), 0)
            source = lax.broadcasted_iota(jnp.int32, (count * lines, count * lines), 1)
            within = row % lines
            repeat = (source == row) & (within < 3) | (source == row - 3) & (within >= 3) & (within < 6)
            own = to_bf16(dot_nn(to_bf16(jnp.where(repeat, 1.0, 0.0)), own))[:, : ada_ref.shape[1]]
            within = lax.broadcasted_iota(jnp.int32, (count * lines, 1), 0) % lines
            part = jnp.where(within < 3, dot_nn(own, ada_ref[0]), dot_nn(own, ada_ref[1]))
            parts[...] = part.reshape(parts.shape)
            for copy in swaps:
                copy.start()
            parts_got[d] = parts[d]
        if turn == 15:
            for copy in swaps:
                copy.wait()
            total = parts_got[0]
            for place in range(1, 8):
                total = total + parts_got[place]
            mods_out[h] = total
            for copy in spreads:
                copy.start()
        if turn == 19:
            for copy in spreads + latents:
                copy.wait()

    for piece in range(len(pieces)):
        if tail_of(piece) is None:
            own_copy(piece).start()
    for turn in range(len(pieces) + 4):
        for step in range(5):
            piece = turn - step
            if not 0 <= piece < len(pieces):
                continue
            if step == 1:
                own_copy(piece).wait()
            if step >= 1:
                for stream in streams(step - 1):
                    hop(piece, step - 1, stream).wait_recv()
            if step < 4:
                for stream in streams(step):
                    hop(piece, step, stream).start()
            else:
                for side in range(2):
                    across(piece, side).start()
        condition(turn)
    for piece in range(len(pieces)):
        for step in range(4):
            for stream in streams(step):
                hop(piece, step, stream).wait_send()
        for side in range(2):
            if piece > 0:
                across(piece, side).wait_recv()
            across(piece, side).wait_send()


def gather_whole(owns, firsts, edge, latents, shared, table, ada, collective_id):
    groups = len(owns)
    pieces = len(gather_pieces([own.shape[1] for own in owns], firsts))
    rows = owns[0].shape[0]
    low = jnp.bfloat16
    mod_cols = ada.shape[2]
    *wholes, latents_all, shared_all, mods = pl.pallas_call(
        functools.partial(gather_kernel, groups, firsts),
        out_shape=[
            jax.ShapeDtypeStruct((2, 2, 2, own.shape[0], 4 * own.shape[1]), own.dtype)
            for own in owns
        ]
        + [
            jax.ShapeDtypeStruct((4,) + latents.shape, jnp.float32),
            jax.ShapeDtypeStruct((8,) + shared.shape, jnp.float32),
            jax.ShapeDtypeStruct((4, 8, mod_cols), jnp.float32),
        ],
        in_specs=[anywhere()] * groups + [vmem()] * 5,
        out_specs=[anywhere()] * groups + [vmem()] * 3,
        scratch_shapes=[
            pltpu.VMEM(edge.shape, low),
            pltpu.VMEM(edge.shape, low),
            pltpu.VMEM((2, 2, 2, rows, 4 * owns[0].shape[1]), low),
            pltpu.VMEM((8, 8, mod_cols), jnp.float32),
            pltpu.VMEM((8, 8, mod_cols), jnp.float32),
            pltpu.VMEM(shared.shape, jnp.float32),
            pltpu.SemaphoreType.DMA((pieces, 4, 3)),
            pltpu.SemaphoreType.DMA((pieces, 4, 3)),
            pltpu.SemaphoreType.DMA((pieces, 2)),
            pltpu.SemaphoreType.DMA((pieces, 2)),
            pltpu.SemaphoreType.DMA((pieces,)),
            pltpu.SemaphoreType.DMA((len(firsts) + 1,)),
            pltpu.SemaphoreType.DMA((21,)),
            pltpu.SemaphoreType.DMA((21,)),
        ],
        compiler_params=comm_params(collective_id),
        name="gather_weights",
    )(*owns, edge, latents, shared, table, ada)
    wholes = [whole.reshape(8 * own.shape[0], -1) for whole, own in zip(wholes, owns)]
    return wholes, latents_all, shared_all, mods


def gather_general(own):
    rows, columns = own.shape
    blocks = lax.all_gather(own, ("dp", "head"), axis=0, tiled=False)
    blocks = blocks.reshape(-1, lax.axis_size("head"), rows, columns)
    return blocks.transpose(0, 2, 1, 3).reshape(-1, lax.axis_size("head") * columns)


def reduce_kernel(plan, lefts, rights, *refs):
    left_refs, right_refs = refs[:lefts], refs[lefts : lefts + rights]
    (extra_ref, mod_ref, io_ref, signal_ref, slope_ref, table_ref, ada_ref, out_ref, total_ref,
     edge_ref, ada_out, time_out, io_out) = refs[lefts + rights : lefts + rights + 13]
    (made, near, left, left_t, right, send_a, send_b, got_a, got_b, keep_a, keep_b,
     mine, head_got, data_got, mod_got, io_got, mod_sum, io_sum, mod_all, io_all, part, part_got,
     inner, inner_all, near_send, near_recv, hop_send, hop_recv, left_sem,
     right_sem, edge_send, edge_recv, sum_send, sum_recv, small_send, small_recv) = refs[
        lefts + rights + 13 :
    ]
    layers = len(plan)
    per_group = D // PIECE_COLS
    pieces = 3 * layers * per_group
    d = lax.axis_index("dp")
    h = lax.axis_index("head")
    peers = link_peers(d, h)
    across = [(d, h ^ other) for other in (1, 2, 3)] + [(d ^ other, h) for other in range(1, 8)]
    greet(across)
    y, c = h // 2, h % 2
    zh, zl, x = d // 4, (d // 2) % 2, d % 2
    order = (("y", "x"), ("x", "zl"), ("zl", "zh"), ("zh", "y"))
    shape = made.shape[3:]
    rows_own = shape[-2]
    top, bottom = pl.ds(0, ROWS_A), pl.ds(ROWS_A, rows_own - ROWS_A)
    every = slice(None)

    def near_copy(piece, side):
        slot = piece % SLOTS
        return pltpu.make_async_remote_copy(
            src_ref=made.at[slot, side, 1 - c],
            dst_ref=near.at[slot, side],
            send_sem=near_send.at[slot, side],
            recv_sem=near_recv.at[slot, side],
            device_id=peers["core"],
            device_id_type=MESH,
        )

    def left_copy(place):
        rows = left_refs[place].shape[0]
        return pltpu.make_async_copy(
            left_refs[place], left.at[place, pl.ds(0, rows)], left_sem.at[place]
        )

    def turn_left(place, at):
        rows = left_refs[place].shape[0]
        left_copy(place).wait()
        left_t[at, :, :rows] = left[place, :rows].T

    def sources(layer, part, head, half):
        column = first_column(head // 2, head % 2, part * PIECE_COLS + (128 * half if part == 2 else 0))
        if part < 2:
            column += 128 * half
        for at, (left_place, right_place, start, stop) in enumerate(plan[layer][0]):
            if start <= column < stop:
                return left_place, right_place, column - start

    def right_copies(piece, layer, part):
        copies = []
        for head in range(4):
            for half in range(2):
                left_place, right_place, column = sources(layer, part, head, half)
                rows = right_refs[right_place].shape[0]
                copies.append(
                    pltpu.make_async_copy(
                        right_refs[right_place].at[:, pl.ds(column, 128)],
                        right.at[piece % 2, head, pl.ds(0, rows), pl.ds(128 * half, 128)],
                        right_sem.at[piece % 2, head, half],
                    )
                )
        return copies

    def right_copy(piece, right_place, head):
        start = head * D + (piece % per_group) * PIECE_COLS
        return pltpu.make_async_copy(
            right_refs[right_place].at[:, pl.ds(pl.multiple_of(start, PIECE_COLS), PIECE_COLS)],
            right.at[piece % 2, head],
            right_sem.at[piece % 2, head, 0],
        )

    def fetch(piece):
        for layer in range(layers):
            for part in range(per_group):

                @pl.when(piece == 3 * layer * per_group + part)
                def _():
                    for copy in right_copies(piece, layer, part):
                        copy.start()

            for member in range(2):

                @pl.when(piece // per_group == 3 * layer + 1 + member)
                def _():
                    for head in range(4):
                        right_copy(piece, plan[layer][1 + member][1], head).start()

    def bring(piece):
        slot = piece % SLOTS
        for layer in range(layers):
            used = []
            for left_place, _, _, _ in plan[layer][0]:
                if left_place not in used:
                    used.append(left_place)

            @pl.when(piece == 3 * layer * per_group)
            def _():
                for at, left_place in enumerate(used):
                    turn_left(left_place, at)

            for part in range(per_group):

                @pl.when(piece == 3 * layer * per_group + part)
                def _():
                    for copy in right_copies(piece, layer, part):
                        copy.wait()
                    for head in range(4):
                        pair = [sources(layer, part, head, half) for half in range(2)]
                        spans = [(0, 2)] if pair[0][0] == pair[1][0] else [(0, 1), (1, 2)]
                        for first, stop in spans:
                            left_place, right_place, _ = pair[first]
                            rows = right_refs[right_place].shape[0]
                            columns = slice(128 * first, 128 * stop)
                            made[slot, head // 2, head % 2, :, :, :, :, columns] = dot_nn(
                                left_t[used.index(left_place), :, :rows],
                                right[piece % 2, head, :rows, columns],
                            ).reshape(shape[:-1] + (128 * (stop - first),))

            for member in range(2):

                @pl.when(piece == (3 * layer + 1 + member) * per_group)
                def _():
                    turn_left(plan[layer][1 + member][0], 0)

        @pl.when((piece // per_group) % 3 != 0)
        def _():
            for head in range(4):
                right_copy(piece, plan[0][1][1], head).wait()
            for head in range(4):
                made[slot, head // 2, head % 2] = dot_nn(
                    left_t[0], right[piece % 2, head]
                ).reshape(shape)

        for side in range(2):
            near_copy(piece, side).start()

    def hop(piece, step, stream):
        slot = piece % SLOTS
        sent, got = (send_a, got_a) if stream == 0 else (send_b, got_b)
        return pltpu.make_async_remote_copy(
            src_ref=sent[step].at[slot],
            dst_ref=got[step].at[slot],
            send_sem=hop_send.at[step, stream, slot],
            recv_sem=hop_recv.at[step, stream, slot],
            device_id=peers[order[step][stream]],
            device_id_type=MESH,
        )

    def first(piece):
        slot = piece % SLOTS
        for side in range(2):
            near_copy(piece, side).wait()

        def total(side, *index):
            return made[(slot, side, c) + index] + near[(slot, side) + index]

        send_a[0][slot] = to_bf16(total(1 - y, every, every, every, top))
        hop(piece, 0, 0).start()
        send_b[0][slot] = to_bf16(total(every, every, every, 1 - x, bottom))
        hop(piece, 0, 1).start()
        keep_a[0][slot] = total(y, every, every, every, top)
        keep_b[0][slot] = total(every, every, every, x, bottom)

    cut_a = (None, (2, x), (1, zl), (0, zh))
    cut_b = (None, (2, zl), (1, zh), (0, y))

    def later(piece, step):
        slot = piece % SLOTS
        for stream in range(2):
            keep, got, sent = (keep_a, got_a, send_a) if stream == 0 else (keep_b, got_b, send_b)
            axis, mine = (cut_a if stream == 0 else cut_b)[step]
            hop(piece, step - 1, stream).wait()

            def total(which):
                index = (slot,) + (every,) * axis + (which,)
                return keep[step - 1][index] + got[step - 1][index].astype(jnp.float32)

            sent[step][slot] = to_bf16(total(1 - mine))
            hop(piece, step, stream).start()
            keep[step][slot] = total(mine)

    def last(piece):
        slot = piece % SLOTS
        for stream in range(2):
            keep, got = (keep_a, got_a) if stream == 0 else (keep_b, got_b)
            hop(piece, 3, stream).wait()
            out_ref[piece, top if stream == 0 else bottom, :] = keep[3][slot] + got[3][
                slot
            ].astype(jnp.float32)

    def small(place, source, target, peer):
        return pltpu.make_async_remote_copy(
            src_ref=source,
            dst_ref=target,
            send_sem=small_send.at[place],
            recv_sem=small_recv.at[place],
            device_id=peer,
            device_id_type=MESH,
        )

    heads = [(across[other - 1], h ^ other, other - 1) for other in (1, 2, 3)]
    datas = [(across[2 + other], d ^ other, other - 1) for other in range(1, 8)]
    mod_swaps = [small(at, mod_ref.at[place], mod_got.at[h], peer) for peer, place, at in heads]
    io_swaps = [small(3 + at, io_ref.at[place], io_got.at[h], peer) for peer, place, at in heads]
    mod_spreads = [small(6 + at, mod_sum, mod_all.at[d], peer) for peer, _, at in datas]
    io_moves = [small(13 + at, io_sum.at[place], io_all.at[d], peer) for peer, place, at in datas]
    part_spreads = [small(20 + at, part, part_got.at[h], peer) for peer, _, at in heads]
    inner_spreads = [small(23 + at, inner, inner_all.at[d], peer) for peer, _, at in datas]

    def total_of(ref):
        total = ref[0]
        for place in range(1, ref.shape[0]):
            total = total + ref[place]
        return total

    def exact(left, right, contract):
        return lax.dot_general(
            left, right, (contract, ((), ())), precision=HIGHEST_PRECISION,
            preferred_element_type=jnp.float32,
        )

    def condition(turn):
        @pl.when(turn == 2)
        def _():
            for copy in mod_swaps + io_swaps:
                copy.wait()
            mod_sum[...] = total_of(mod_got)
            io_sum[...] = total_of(io_got)
            for copy in mod_spreads + io_moves:
                copy.start()
            mod_all[d] = mod_sum[...]
            io_all[d] = io_sum[d]

        @pl.when(turn == 6)
        def _():
            for copy in mod_spreads + io_moves:
                copy.wait()
            io_out[...] = total_of(io_all)
            columns = ada_ref.shape[2]
            total = jnp.zeros(part.shape, jnp.float32)
            for layer in range(2):
                grads = mod_all[:, :, layer * columns : (layer + 1) * columns].reshape(
                    part.shape[0], columns
                )
                ada_out[layer] = exact(signal_ref[...], grads, ((0,), (0,)))
                total = total + exact(grads, ada_ref[layer].astype(jnp.float32), ((1,), (1,)))
            part[...] = total
            for copy in part_spreads:
                copy.start()
            part_got[h] = total

        @pl.when(turn == 10)
        def _():
            for copy in part_spreads:
                copy.wait()
            inner[...] = total_of(part_got) * slope_ref[...]
            for copy in inner_spreads:
                copy.start()
            inner_all[d] = inner[...]

        @pl.when(turn == 14)
        def _():
            for copy in inner_spreads:
                copy.wait()
            for place in range(2):
                time_out[place] = exact(table_ref[...], inner_all[2 * h + place], ((0,), (0,)))

    for copy in mod_swaps + io_swaps:
        copy.start()
    mod_got[h] = mod_ref[h]
    io_got[h] = io_ref[h]
    for place in range(lefts):
        left_copy(place).start()
    fetch(0)
    fetch(1)
    bring(0)
    fetch(2)
    bring(1)

    @pl.loop(0, pieces + 4)
    def _(turn):
        @pl.when(turn + 3 < pieces)
        def _():
            fetch(turn + 3)

        @pl.when(turn < pieces)
        def _():
            first(turn)

        for step in (1, 2, 3):

            @pl.when((turn >= step) & (turn - step < pieces))
            def _():
                later(turn - step, step)

        @pl.when(turn >= 4)
        def _():
            last(turn - 4)

        @pl.when(turn + 2 < pieces)
        def _():
            bring(turn + 2)

        condition(turn)

    edges = []
    for layer in range(layers):
        piece = (3 * layer + 1) * per_group - 1
        edges.append(
            pltpu.make_async_remote_copy(
                src_ref=out_ref.at[piece, :, pl.ds(0, 128)],
                dst_ref=edge_ref.at[layer],
                send_sem=edge_send.at[layer],
                recv_sem=edge_recv.at[layer],
                device_id=peers["core"],
                device_id_type=MESH,
            )
        )
        edges[-1].start()

    squares = jnp.zeros((rows_own, PIECE_COLS), jnp.float32)
    for piece in range(pieces):
        squares = squares + out_ref[piece] * out_ref[piece]
    row = lax.broadcasted_iota(jnp.int32, (8, 128), 0)
    column = lax.broadcasted_iota(jnp.int32, (8, 128), 1)
    square = jnp.sum(squares)
    for ref in (ada_out, time_out, io_out):
        square = square + jnp.sum(ref[...] * ref[...])
    mine[0] = extra_ref[...] + jnp.where((row == 0) & (column == 0), square, 0.0)
    for phase, (got, me, count) in enumerate(((head_got, h, 4), (data_got, d, 8))):
        copies = []
        for other in range(1, count):
            place = 3 * phase + other - 1
            copies.append(
                pltpu.make_async_remote_copy(
                    src_ref=mine.at[phase],
                    dst_ref=got.at[me],
                    send_sem=sum_send.at[place],
                    recv_sem=sum_recv.at[place],
                    device_id=across[place],
                    device_id_type=MESH,
                )
            )
            copies[-1].start()
        got[me] = mine[phase]
        for copy in copies:
            copy.wait()
        total = got[0]
        for other in range(1, count):
            total = total + got[other]
        if phase == 0:
            mine[1] = total
        else:
            total_ref[...] = total
    for copy in edges:
        copy.wait()


def reduce_whole(plan, lefts, rights, smalls, collective_id):
    layers = len(plan)
    frames = lefts[0].shape[0]
    rows = D // 8
    per_group = D // PIECE_COLS
    pieces = 3 * layers * per_group
    leads = ((2, 2, 2), (2, 2), (2,), ())

    def buffers(count, dtype):
        return [pltpu.VMEM((SLOTS,) + lead + (count, PIECE_COLS), dtype) for lead in leads]

    bottom_rows = rows - ROWS_A
    blocks = (2, 2, 2, rows, PIECE_COLS)
    low = jnp.bfloat16
    mod, io, signal, ada = smalls[1], smalls[2], smalls[3], smalls[6]
    summed, *others = pl.pallas_call(
        functools.partial(reduce_kernel, plan, len(lefts), len(rights)),
        out_shape=[
            jax.ShapeDtypeStruct((pieces, rows, PIECE_COLS), jnp.float32),
            jax.ShapeDtypeStruct((8, 128), jnp.float32),
            jax.ShapeDtypeStruct((layers, rows, 128), jnp.float32),
            jax.ShapeDtypeStruct(ada.shape, jnp.float32),
            jax.ShapeDtypeStruct((2, rows, rows), jnp.float32),
            jax.ShapeDtypeStruct(io.shape[2:], jnp.float32),
        ],
        in_specs=[anywhere()] * (len(lefts) + len(rights)) + [vmem()] * 7,
        out_specs=[vmem()] * 6,
        scratch_shapes=[
            pltpu.VMEM((SLOTS, 2, 2) + blocks, jnp.float32),
            pltpu.VMEM((SLOTS, 2) + blocks, jnp.float32),
            pltpu.VMEM((len(lefts), frames, D), low),
            pltpu.VMEM((3, D, frames), low),
            pltpu.VMEM((2, 4, frames, PIECE_COLS), low),
            buffers(ROWS_A, low),
            buffers(bottom_rows, low),
            buffers(ROWS_A, low),
            buffers(bottom_rows, low),
            buffers(ROWS_A, jnp.float32),
            buffers(bottom_rows, jnp.float32),
            pltpu.VMEM((2, 8, 128), jnp.float32),
            pltpu.VMEM((4, 8, 128), jnp.float32),
            pltpu.VMEM((8, 8, 128), jnp.float32),
            pltpu.VMEM(mod.shape, jnp.float32),
            pltpu.VMEM(io.shape, jnp.float32),
            pltpu.VMEM(mod.shape[1:], jnp.float32),
            pltpu.VMEM(io.shape[1:], jnp.float32),
            pltpu.VMEM((8,) + mod.shape[1:], jnp.float32),
            pltpu.VMEM(io.shape[1:], jnp.float32),
            pltpu.VMEM(signal.shape, jnp.float32),
            pltpu.VMEM((4,) + signal.shape, jnp.float32),
            pltpu.VMEM(signal.shape, jnp.float32),
            pltpu.VMEM((8,) + signal.shape, jnp.float32),
            pltpu.SemaphoreType.DMA((SLOTS, 2)),
            pltpu.SemaphoreType.DMA((SLOTS, 2)),
            pltpu.SemaphoreType.DMA((4, 2, SLOTS)),
            pltpu.SemaphoreType.DMA((4, 2, SLOTS)),
            pltpu.SemaphoreType.DMA((len(lefts),)),
            pltpu.SemaphoreType.DMA((2, 4, 2)),
            pltpu.SemaphoreType.DMA((layers,)),
            pltpu.SemaphoreType.DMA((layers,)),
            pltpu.SemaphoreType.DMA((10,)),
            pltpu.SemaphoreType.DMA((10,)),
            pltpu.SemaphoreType.DMA((30,)),
            pltpu.SemaphoreType.DMA((30,)),
        ],
        compiler_params=comm_params(collective_id),
        name="reduce_grads",
    )(*lefts, *rights, *smalls)
    summed = summed.reshape(3 * layers, per_group, rows, PIECE_COLS).transpose(0, 2, 1, 3)
    return list(summed.reshape(3 * layers, rows, D)), *others


def reduce_general(part):
    data_count, head_count = lax.axis_size("dp"), lax.axis_size("head")
    blocks = part.reshape(
        data_count, part.shape[0] // data_count, head_count, part.shape[1] // head_count
    ).transpose(0, 2, 1, 3)
    blocks = blocks.reshape((-1,) + blocks.shape[2:])
    return lax.psum_scatter(blocks, ("dp", "head"), scatter_dimension=0, tiled=True)[0]


KIND_AT = (1, 2, 3, 0)


def owner_of(kind, layer):
    return 4 * layer + KIND_AT.index(kind)


def is_owner_of(me, kind):
    return (me % 4 == KIND_AT.index(kind)) & (me < 8)


def to_owner_kernel(count, *refs):
    block_refs, out_ref, send_sem, recv_sem = refs[:4], refs[4], refs[5], refs[6]
    me = lax.axis_index("dp")
    out_ref[...] = jnp.zeros_like(out_ref)
    greet([{"dp": lax.rem(me + shift, count)} for shift in range(1, count)])

    def copy(kind, layer, source):
        width = block_refs[kind].shape[-1]
        return pltpu.make_async_remote_copy(
            src_ref=block_refs[kind].at[layer],
            dst_ref=out_ref.at[source, :, pl.ds(0, width)],
            send_sem=send_sem.at[2 * kind + layer],
            recv_sem=recv_sem.at[source],
            device_id={"dp": owner_of(kind, layer)},
            device_id_type=MESH,
        )

    for kind in range(4):
        for layer in range(2):

            @pl.when(me != owner_of(kind, layer))
            def _():
                copy(kind, layer, me).start()

            @pl.when(me == owner_of(kind, layer))
            def _():
                out_ref[me, :, : block_refs[kind].shape[-1]] = block_refs[kind][layer]

    for kind in range(4):

        @pl.when(is_owner_of(me, kind))
        def _():
            @pl.loop(0, count)
            def _(source):
                @pl.when(source != me)
                def _():
                    copy(kind, 0, source).wait_recv()

        for layer in range(2):

            @pl.when(me != owner_of(kind, layer))
            def _():
                copy(kind, layer, me).wait_send()


def to_owner(blocks, collective_id):
    count = lax.axis_size("dp")
    rows = blocks[0].shape[1]
    wide = max(block.shape[2] for block in blocks)
    return pl.pallas_call(
        functools.partial(to_owner_kernel, count),
        out_shape=jax.ShapeDtypeStruct((count, rows, wide), jnp.float32),
        in_specs=[vmem()] * 4,
        out_specs=vmem(),
        scratch_shapes=[pltpu.SemaphoreType.DMA((8,)), pltpu.SemaphoreType.DMA((count,))],
        compiler_params=comm_params(collective_id),
        name="to_owner",
    )(*blocks)


def from_owner_kernel(count, widths, x_ref, out_ref, send_sem, recv_sem):
    me = lax.axis_index("dp")
    greet([{"dp": lax.rem(me + shift, count)} for shift in range(1, count)])

    def copy(kind, matrix, target):
        columns = pl.ds(0, widths[kind])
        return pltpu.make_async_remote_copy(
            src_ref=x_ref.at[target, :, columns],
            dst_ref=out_ref.at[matrix, :, columns],
            send_sem=send_sem.at[target],
            recv_sem=recv_sem.at[matrix],
            device_id={"dp": target},
            device_id_type=MESH,
        )

    for kind in range(4):

        @pl.when(is_owner_of(me, kind))
        def _():
            @pl.loop(0, count)
            def _(target):
                @pl.when(target != me)
                def _():
                    copy(kind, me, target).start()

            out_ref[me] = x_ref[me]

    for kind in range(4):
        for layer in range(2):
            matrix = owner_of(kind, layer)

            @pl.when(me != matrix)
            def _():
                copy(kind, matrix, me).wait_recv()

        @pl.when(is_owner_of(me, kind))
        def _():
            @pl.loop(0, count)
            def _(target):
                @pl.when(target != me)
                def _():
                    copy(kind, me, target).wait_send()


def from_owner(x, widths, collective_id):
    count = lax.axis_size("dp")
    return pl.pallas_call(
        functools.partial(from_owner_kernel, count, widths),
        out_shape=jax.ShapeDtypeStruct((8,) + x.shape[1:], x.dtype),
        in_specs=[vmem()],
        out_specs=vmem(),
        scratch_shapes=[pltpu.SemaphoreType.DMA((count,)), pltpu.SemaphoreType.DMA((8,))],
        compiler_params=comm_params(collective_id),
        name="from_owner",
    )(x)


def gram_kernel(x_ref, out_ref, high, rest, upper, chip, got, whole, send_sem, recv_sem):
    h = lax.axis_index("head")
    c = h % 2
    greet([{"head": h ^ other} for other in (1, 2)])
    third = PIECE_COLS
    values = x_ref[...]
    high[...] = to_bf16(values)
    rest[...] = to_bf16(values - high[...].astype(jnp.float32))

    def dots(first, second):
        return (
            dot_nt(high[first], high[second])
            + dot_nt(high[first], rest[second])
            + dot_nt(rest[first], high[second])
        )

    r0, r1, r2 = (pl.ds(third * place, third) for place in range(3))
    upper[0] = dots(r0, pl.ds(0, 3 * third))
    upper[1, :, : 2 * third] = dots(r1, pl.ds(third, 2 * third))
    upper[1, :, 2 * third :] = dots(r2, r2)

    def step(place, source, target, peer):
        copy = send_to(source, target, (send_sem, recv_sem), place, peer)
        copy.start()
        copy.wait()

    step(0, upper.at[1 - c], got.at[0], h ^ 1)
    chip[...] = upper[c] + got[0]
    step(1, chip, got.at[1], h ^ 2)
    whole[c] = chip[...] + got[1]
    step(2, whole.at[c], whole.at[c], h ^ 1)
    out_ref[r0, :] = whole[0]
    out_ref[r1, pl.ds(third, 2 * third)] = whole[1, :, : 2 * third]
    out_ref[r2, r2] = whole[1, :, 2 * third :]
    out_ref[r1, r0] = whole[0, :, third : 2 * third].T
    out_ref[r2, r0] = whole[0, :, 2 * third :].T
    out_ref[r2, r1] = whole[1, :, third : 2 * third].T


def gram_sum(x, collective_id):
    rows, columns = x.shape
    third = PIECE_COLS
    return pl.pallas_call(
        gram_kernel,
        out_shape=jax.ShapeDtypeStruct((rows, rows), jnp.float32),
        in_specs=[vmem()],
        out_specs=vmem(),
        scratch_shapes=[
            pltpu.VMEM((rows, columns), jnp.bfloat16),
            pltpu.VMEM((rows, columns), jnp.bfloat16),
            pltpu.VMEM((2, third, rows), jnp.float32),
            pltpu.VMEM((third, rows), jnp.float32),
            pltpu.VMEM((2, third, rows), jnp.float32),
            pltpu.VMEM((2, third, rows), jnp.float32),
            pltpu.SemaphoreType.DMA((3,)),
            pltpu.SemaphoreType.DMA((3,)),
        ],
        compiler_params=comm_params(collective_id),
        name="gram_sum",
    )(x)


def send_to(source, target, sems, place, peer):
    return pltpu.make_async_remote_copy(
        src_ref=source,
        dst_ref=target,
        send_sem=sems[0].at[place],
        recv_sem=sems[1].at[place],
        device_id={"head": peer},
        device_id_type=MESH,
    )


def half_mask(half):
    lane = lax.broadcasted_iota(jnp.int32, (1, 128), 1)
    return (lane // 64) == half


def dot_nt(left, right):
    return lax.dot_general(
        left, right, (((1,), (1,)), ((), ())), preferred_element_type=jnp.float32
    )


def dot_nn(left, right):
    return lax.dot_general(
        left, right, (((1,), (0,)), ((), ())), preferred_element_type=jnp.float32
    )


def dot_tn(left, right):
    return lax.dot_general(
        left, right, (((0,), (0,)), ((), ())), preferred_element_type=jnp.float32
    )


def lanes(start, size):
    return pl.ds(pl.multiple_of(start, 128), size)


def window(head):
    return 128 * ((3 * head) // 2)


def bring_heads(h, rows_ref, pair_all, quad_all, parts, sems):
    c = h % 2
    tile = quad_all.shape[1]
    own, shared = pl.ds(0, 2 * tile), pl.ds(2 * tile, tile)
    pair, quad = [], []
    for part in range(parts):
        pair.append(
            send_to(
                rows_ref.at[own, lanes(part * D + (1 - c) * HALF, HALF)],
                pair_all.at[c, :, pl.ds(part * HALF, HALF)],
                sems, part, h ^ 1,
            )
        )
        for other in (1, 2, 3):
            quad.append(
                send_to(
                    rows_ref.at[shared, lanes(part * D + window(h ^ other), WIDE)],
                    quad_all.at[h, :, pl.ds(part * WIDE, WIDE)],
                    sems, 3 * other + part, h ^ other,
                )
            )
    for copy in pair + quad:
        copy.start()
    for part in range(parts):
        pair_all[c, :, part * HALF : (part + 1) * HALF] = rows_ref[
            own, lanes(part * D + c * HALF, HALF)
        ]
        quad_all[h, :, part * WIDE : (part + 1) * WIDE] = rows_ref[
            shared, lanes(part * D + window(h), WIDE)
        ]
    return pair, quad


def return_pair(h, pair_out, rows_ref, parts, sems):
    c = h % 2
    own = pl.ds(0, pair_out.shape[1])
    copies = []
    for part in range(parts):
        columns = lanes(part * D + c * HALF, HALF)
        copies.append(
            send_to(
                pair_out.at[1 - c, :, pl.ds(part * HALF, HALF)], rows_ref.at[own, columns],
                sems, 12 + part, h ^ 1,
            )
        )
        copies[-1].start()
        rows_ref[own, columns] = pair_out[c, :, part * HALF : (part + 1) * HALF]
    return copies


def return_quad(h, quad_out, quad_got, sems):
    copies = []
    for other in (1, 2, 3):
        copies.append(
            send_to(quad_out.at[h ^ other], quad_got.at[h], sems, 14 + other, h ^ other)
        )
        copies[-1].start()
    quad_got[h] = quad_out[h]
    return copies


def merge_quad(quad_got, rows_ref, parts):
    tile = quad_got.shape[1]
    shared = slice(2 * tile, 3 * tile)
    for part in range(parts):
        base, start = part * WIDE, part * D
        for side in range(2):
            left, right = quad_got.at[2 * side], quad_got.at[2 * side + 1]
            at = start + side * HALF
            rows_ref[shared, at : at + 128] = left[:, base : base + 128]
            rows_ref[shared, at + 128 : at + 256] = (
                left[:, base + 128 : base + 256] + right[:, base : base + 128]
            )
            rows_ref[shared, at + 256 : at + 384] = right[:, base + 128 : base + 256]


def row_half(half):
    row = lax.broadcasted_iota(jnp.int32, (128, 1), 0)
    return (row // 64) == half


CHUNKS = ((0, 384), (384, 832))


def probabilities(scores):
    top = jnp.max(scores, 0, keepdims=True)
    exponent = jnp.exp(scores - top)
    total = jnp.sum(exponent, 0, keepdims=True)
    return exponent * (1.0 / total), top + jnp.log(total)


def attend_kernel(rows_ref, mixed_ref, pair_all, quad_all, log_ref, pair_out, quad_out, quad_got,
                  joined, send_sem, recv_sem):
    h = lax.axis_index("head")
    sems = (send_sem, recv_sem)
    greet([{"head": h ^ other} for other in (1, 2, 3)])
    pair_copies, quad_copies = bring_heads(h, rows_ref, pair_all, quad_all, 3, sems)
    tile = quad_all.shape[1]
    length = 4 * tile

    def heads(query, keys, values, members):
        values_t = values.T
        for start, stop in CHUNKS:
            mixed = jnp.zeros((128, stop - start), jnp.float32)
            for half, log_row in members:
                chunk = jnp.where(half_mask(half), query[start:stop], 0) * 0.125
                probability, logs = probabilities(dot_nt(keys, chunk))
                mixed = mixed + dot_nn(
                    jnp.where(row_half(half), values_t, 0), to_bf16(probability)
                )
                log_ref[log_row : log_row + 1, start:stop] = logs
            joined[start:stop, :] = to_bf16(mixed.T)

    log_ref[...] = jnp.zeros_like(log_ref)
    quad_out[...] = jnp.zeros_like(quad_out)
    def pair_heads(pair):
        query, keys, values = (
            pair_all[:, :, part * HALF + pair * 128 : part * HALF + pair * 128 + 128].reshape(
                length, 128
            )
            for part in range(3)
        )
        heads(query, keys, values, ((0, 2 * pair), (1, 2 * pair + 1)))
        pair_out[:, :, pair * 128 : pair * 128 + 128] = joined[...].reshape(2, 2 * tile, 128)

    for copy in pair_copies:
        copy.wait()
    pair_heads(0)
    pair_heads(1)
    for copy in quad_copies:
        copy.wait()
    for member in range(3):
        place = h % 2 + member
        at = (place // 2) * 128
        query, keys, values = (
            quad_all[:, :, lanes(part * WIDE + at, 128)].reshape(length, 128) for part in range(3)
        )
        heads(query, keys, values, ((place % 2, 6 + member),))
        quad_out[:, :, lanes(at, 128)] += joined[...].reshape(4, tile, 128)
    back_quad = return_quad(h, quad_out, quad_got, sems)
    pair_heads(2)
    back = return_pair(h, pair_out, mixed_ref, 1, sems)
    for copy in back + back_quad:
        copy.wait()
    merge_quad(quad_got, mixed_ref, 1)


def attend(rows, collective_id):
    frames = rows.shape[0]
    tile = frames // 3
    low = jnp.bfloat16
    return pl.pallas_call(
        attend_kernel,
        out_shape=[
            jax.ShapeDtypeStruct((frames, D), low),
            jax.ShapeDtypeStruct((2, 2 * tile, 3 * HALF), low),
            jax.ShapeDtypeStruct((4, tile, 3 * WIDE), low),
            jax.ShapeDtypeStruct((16, 4 * tile), jnp.float32),
        ],
        in_specs=[vmem()],
        out_specs=[vmem()] * 4,
        scratch_shapes=[
            pltpu.VMEM((2, 2 * tile, HALF), low),
            pltpu.VMEM((4, tile, WIDE), low),
            pltpu.VMEM((4, tile, WIDE), low),
            pltpu.VMEM((4 * tile, 128), low),
            pltpu.SemaphoreType.DMA((18,)),
            pltpu.SemaphoreType.DMA((18,)),
        ],
        compiler_params=comm_params(collective_id),
        name="attend",
    )(rows)


def attend_back_kernel(pair_all, quad_all, log_ref, grad_ref, rows_ref, pair_mixed, quad_mixed,
                       pair_out, quad_out, quad_got, grad_keys, grad_values, grads, send_sem,
                       recv_sem):
    h = lax.axis_index("head")
    sems = (send_sem, recv_sem)
    greet([{"head": h ^ other} for other in (1, 2, 3)])
    pair_copies, quad_copies = bring_heads(h, grad_ref, pair_mixed, quad_mixed, 1, sems)
    tile = quad_all.shape[1]
    length = 4 * tile

    def heads(query, keys, values, grad_out, members):
        keys_t = keys.T
        grad_keys[...] = jnp.zeros_like(grad_keys)
        grad_values[...] = jnp.zeros_like(grad_values)
        for start, stop in CHUNKS:
            grad_query = jnp.zeros((128, stop - start), jnp.float32)
            for half, log_row in members:
                mask = half_mask(half)
                chunk = jnp.where(mask, query[start:stop], 0) * 0.125
                grad_chunk = jnp.where(mask, grad_out[start:stop], 0)
                probability = jnp.exp(
                    dot_nt(keys, chunk) - log_ref[log_row : log_row + 1, start:stop]
                )
                grad_prob = dot_nt(values, grad_chunk)
                mean = jnp.sum(probability * grad_prob, 0, keepdims=True)
                grad_scores = to_bf16(probability * (grad_prob - mean))
                grad_keys[...] += dot_nn(grad_scores, chunk)
                grad_values[...] += dot_nn(to_bf16(probability), grad_chunk)
                grad_query = grad_query + dot_nn(
                    jnp.where(row_half(half), keys_t, 0), grad_scores
                )
            grads[0, start:stop, :] = to_bf16(grad_query.T * 0.125)
        grads[1] = to_bf16(grad_keys[...])
        grads[2] = to_bf16(grad_values[...])

    quad_out[...] = jnp.zeros_like(quad_out)
    def pair_heads(pair):
        at = [part * HALF + pair * 128 for part in range(3)]
        query, keys, values = (
            pair_all[:, :, start : start + 128].reshape(length, 128) for start in at
        )
        grad_out = pair_mixed[:, :, at[0] : at[0] + 128].reshape(length, 128)
        heads(query, keys, values, grad_out, ((0, 2 * pair), (1, 2 * pair + 1)))
        for part in range(3):
            pair_out[:, :, at[part] : at[part] + 128] = grads[part].reshape(2, 2 * tile, 128)

    for copy in pair_copies:
        copy.wait()
    pair_heads(0)
    for copy in quad_copies:
        copy.wait()
    for member in range(3):
        place = h % 2 + member
        at = (place // 2) * 128
        query, keys, values = (
            quad_all[:, :, lanes(part * WIDE + at, 128)].reshape(length, 128) for part in range(3)
        )
        grad_out = quad_mixed[:, :, lanes(at, 128)].reshape(length, 128)
        heads(query, keys, values, grad_out, ((place % 2, 6 + member),))
        for part in range(3):
            quad_out[:, :, lanes(part * WIDE + at, 128)] += grads[part].reshape(4, tile, 128)
    back_quad = return_quad(h, quad_out, quad_got, sems)
    pair_heads(1)
    pair_heads(2)
    back = return_pair(h, pair_out, rows_ref, 3, sems)
    for copy in back + back_quad:
        copy.wait()
    merge_quad(quad_got, rows_ref, 3)


def attend_back(pair_all, quad_all, logs, grad_mixed, collective_id):
    rows, tile = pair_all.shape[1], quad_all.shape[1]
    low = jnp.bfloat16
    return pl.pallas_call(
        attend_back_kernel,
        out_shape=jax.ShapeDtypeStruct((3 * tile, 3 * D), low),
        in_specs=[vmem()] * 4,
        out_specs=vmem(),
        scratch_shapes=[
            pltpu.VMEM((2, rows, HALF), low),
            pltpu.VMEM((4, tile, WIDE), low),
            pltpu.VMEM(pair_all.shape, low),
            pltpu.VMEM(quad_all.shape, low),
            pltpu.VMEM(quad_all.shape, low),
            pltpu.VMEM((4 * tile, 128), jnp.float32),
            pltpu.VMEM((4 * tile, 128), jnp.float32),
            pltpu.VMEM((3, 4 * tile, 128), low),
            pltpu.SemaphoreType.DMA((18,)),
            pltpu.SemaphoreType.DMA((18,)),
        ],
        compiler_params=comm_params(collective_id),
        name="attend_back",
    )(pair_all, quad_all, logs, grad_mixed)


def cross_frames(clip, tile):
    return slice(2 * clip, 2 + clip), (2 - clip) * tile


def masked_scores(keys, query_half, length):
    token = lax.broadcasted_iota(jnp.int32, (keys.shape[0], 1), 0)
    return jnp.where(token < length, dot_nt(keys, query_half), -1e30)


def cross_kernel(query_ref, keys_ref, values_ref, len_ref, out_ref):
    tile = query_ref.shape[1]
    for clip in range(2):
        tiles, count = cross_frames(clip, tile)
        query = query_ref[tiles].reshape(count, 128)
        values_t = values_ref[clip].T
        mixed = jnp.zeros((128, count), jnp.float32)
        for half in range(2):
            chunk = jnp.where(half_mask(half), query, 0) * 0.125
            probability, _ = probabilities(masked_scores(keys_ref[clip], chunk, len_ref[clip]))
            mixed = mixed + dot_nn(jnp.where(row_half(half), values_t, 0), to_bf16(probability))
        out_ref[tiles] = to_bf16(mixed.T).reshape(2 - clip, tile, 128)


def cross(query, pair_kv, lengths):
    _, tile, width = query.shape
    blocks = width // 128
    tokens = pair_kv.shape[1]
    return pl.pallas_call(
        cross_kernel,
        grid=(blocks,),
        out_shape=jax.ShapeDtypeStruct(query.shape, jnp.bfloat16),
        in_specs=[
            pl.BlockSpec((3, tile, 128), lambda i: (0, 0, i)),
            pl.BlockSpec((2, tokens, 128), lambda i: (0, 0, i)),
            pl.BlockSpec((2, tokens, 128), lambda i: (0, 0, blocks + i)),
            pl.BlockSpec(memory_space=pltpu.SMEM),
        ],
        out_specs=pl.BlockSpec((3, tile, 128), lambda i: (0, 0, i)),
        compiler_params=pltpu.CompilerParams(vmem_limit_bytes=VMEM_BYTES),
        name="cross",
    )(query, pair_kv, pair_kv, lengths)


def cross_back_kernel(query_ref, keys_ref, values_ref, grad_ref, len_ref, grad_query_ref,
                      grad_keys_ref, grad_values_ref):
    tile = query_ref.shape[1]
    tokens = keys_ref.shape[1]
    for clip in range(2):
        tiles, count = cross_frames(clip, tile)
        keys, values = keys_ref[clip], values_ref[clip]
        query = query_ref[tiles].reshape(count, 128)
        grad = grad_ref[tiles].reshape(count, 128)
        keys_t = keys.T
        grad_keys = jnp.zeros((tokens, 128), jnp.float32)
        grad_values = jnp.zeros((tokens, 128), jnp.float32)
        grad_query = jnp.zeros((128, count), jnp.float32)
        for half in range(2):
            mask = half_mask(half)
            chunk = jnp.where(mask, query, 0) * 0.125
            grad_half = jnp.where(mask, grad, 0)
            probability, _ = probabilities(masked_scores(keys, chunk, len_ref[clip]))
            grad_prob = dot_nt(values, grad_half)
            mean = jnp.sum(probability * grad_prob, 0, keepdims=True)
            grad_scores = to_bf16(probability * (grad_prob - mean))
            grad_keys = grad_keys + dot_nn(grad_scores, chunk)
            grad_values = grad_values + dot_nn(to_bf16(probability), grad_half)
            grad_query = grad_query + dot_nn(jnp.where(row_half(half), keys_t, 0), grad_scores)
        grad_query_ref[tiles] = to_bf16(grad_query.T * 0.125).reshape(2 - clip, tile, 128)
        grad_keys_ref[clip] = to_bf16(grad_keys)
        grad_values_ref[clip] = to_bf16(grad_values)


def cross_back(query, pair_kv, lengths, grad):
    _, tile, width = query.shape
    blocks = width // 128
    tokens = pair_kv.shape[1]
    rows_spec = pl.BlockSpec((3, tile, 128), lambda i: (0, 0, i))
    keys_spec = pl.BlockSpec((2, tokens, 128), lambda i: (0, 0, i))
    return pl.pallas_call(
        cross_back_kernel,
        grid=(blocks,),
        out_shape=[
            jax.ShapeDtypeStruct(query.shape, jnp.bfloat16),
            jax.ShapeDtypeStruct((2, tokens, width), jnp.bfloat16),
            jax.ShapeDtypeStruct((2, tokens, width), jnp.bfloat16),
        ],
        in_specs=[
            rows_spec,
            keys_spec,
            pl.BlockSpec((2, tokens, 128), lambda i: (0, 0, blocks + i)),
            rows_spec,
            pl.BlockSpec(memory_space=pltpu.SMEM),
        ],
        out_specs=[rows_spec, keys_spec, keys_spec],
        compiler_params=pltpu.CompilerParams(vmem_limit_bytes=VMEM_BYTES),
        name="cross_back",
    )(query, pair_kv, pair_kv, grad, lengths)


def body(
    clean_latents,
    noise_draw,
    timesteps,
    captions,
    cap_len,
    pairing,
    adam_step,
    qkv_weight,
    out_weight,
    up_weight,
    down_weight,
    ada_weight,
    time_weight,
    io_weight,
    qkv_moment,
    out_moment,
    up_moment,
    down_moment,
    ada_first,
    ada_second,
    time_first,
    time_second,
    io_first,
    io_second,
):
    data_count = lax.axis_size("dp")
    head_count = lax.axis_size("head")
    clip_count, tile, channels = clean_latents.shape
    length = tile * head_count
    rows_own = qkv_weight.shape[1]
    d, h = lax.axis_index("dp"), lax.axis_index("head")
    own_clip, core = h // 2, h % 2
    own_row = d * rows_own
    linked = data_count == 8 and rows_own == 96
    ids = iter(range(64))

    def swap(x, axis):
        return exchange(x, axis, True, next(ids))

    def spread(x, axis):
        return exchange(x, axis, False, next(ids))

    def by_tile(values):
        own = lax.dynamic_slice_in_dim(values, own_clip, 1, 0)
        return jnp.concatenate([own, own, values[2:3]])

    def by_clip(tiles):
        own = tiles[0:1] + tiles[1:2]
        none = jnp.zeros_like(own)
        return jnp.concatenate(
            [jnp.where(own_clip == 0, own, none), jnp.where(own_clip == 1, own, none), tiles[2:3]]
        )

    block = 3 * D // head_count
    share = D // head_count
    is_first = core == 0
    latents = jnp.concatenate([clean_latents, noise_draw], -1).transpose(0, 2, 1)
    latents = latents.reshape(-1, tile)

    def with_edge(qkv, out, edge):
        return jnp.where(
            is_first,
            jnp.concatenate([qkv, edge, out[..., :128]], -1),
            jnp.concatenate([qkv[..., 64:], edge, out], -1),
        )

    def without_edge(own, edge):
        qkv = jnp.where(
            is_first, own[..., :block], jnp.concatenate([edge, own[..., : block - 64]], -1)
        )
        out = jnp.where(
            is_first, jnp.concatenate([own[..., block + 64 :], edge], -1), own[..., block:]
        )
        return qkv, out

    keep_mask = jnp.arange(CAP)[None, :] < cap_len[:, None]
    cap_mean = product("ft,ftd->fd", keep_mask.astype(jnp.bfloat16), captions) / cap_len[
        :, None
    ].astype(jnp.float32)
    cap_unit = cap_mean * lax.rsqrt(jnp.mean(cap_mean * cap_mean, -1, keepdims=True) + 1e-06)
    own_captions = jnp.concatenate([lax.dynamic_slice_in_dim(captions, own_clip, 1, 0), captions[2:3]])
    own_lengths = jnp.concatenate([lax.dynamic_slice_in_dim(cap_len, own_clip, 1, 0), cap_len[2:3]])

    qkv_low, out_low = to_bf16(qkv_weight), to_bf16(out_weight)
    edge = jnp.where(is_first, out_low[..., 128:], qkv_low[..., :64])
    time_cols = time_weight.shape[1]
    io_cols = io_weight.shape[2]
    ada_cols = ada_weight.shape[2]
    ada_bf = to_bf16(ada_weight)
    io_flat = io_weight.transpose(1, 0, 2).reshape(rows_own, 2 * io_cols)
    small_own = jnp.pad(
        to_bf16(jnp.concatenate([time_weight, io_flat], 1)),
        ((0, 0), (0, WIDE - time_cols - 2 * io_cols)),
    )
    table_bf = to_bf16(time_table(timesteps, D))

    def listed(first_groups):
        listed_groups = [small_own]
        for layer in range(2):
            listed_groups.append(first_groups[layer])
            listed_groups.append(to_bf16(up_weight[layer]))
            listed_groups.append(to_bf16(down_weight[layer]))
        return listed_groups

    if linked:
        none = jnp.zeros_like(edge)
        edge = jnp.where(
            is_first, jnp.concatenate([edge, none], -1), jnp.concatenate([none, edge], -1)
        )
        shared = jnp.concatenate(
            [
                jnp.zeros((clip_count, D)),
                cap_unit,
                jnp.pad(timesteps[None], ((0, 7 - 2 * clip_count), (0, D - clip_count))),
            ]
        )
        shared = jnp.pad(shared, ((0, 8 - shared.shape[0]), (0, head_count * WIDE - D)))
        gathered, latents_all, shared_all, mods = gather_whole(
            listed(with_edge(qkv_low, out_low, none)),
            (1, 4),
            edge,
            latents,
            shared,
            jnp.pad(table_bf, ((0, 8 - clip_count), (0, 0))),
            ada_bf,
            next(ids),
        )
        start = (d // 2) * WIDE + (d % 2) * rows_own
        hidden_own = lax.dynamic_slice(
            shared_all, (0, 0, start), (data_count, clip_count, rows_own)
        ).reshape(-1, rows_own)
        times_all = shared_all[:, 2 * clip_count, :clip_count].reshape(-1)
        table_own = to_bf16(time_table(times_all, D)).astype(jnp.float32)
        table_own = lax.dynamic_slice_in_dim(table_own, own_row, rows_own, 1)
        cap_all = shared_all[:, clip_count : 2 * clip_count, :D].reshape(-1, D)
        signal_own = to_bf16(double_silu(hidden_own))
        mods = mods[:, : 2 * clip_count].reshape(head_count, 2, clip_count, ada_cols)
        mods = mods.transpose(0, 2, 1, 3)
    else:
        edge = lax.ppermute(edge, "head", [(place, place ^ 1) for place in range(head_count)])
        gathered = [gather_general(own) for own in listed(with_edge(qkv_low, out_low, edge))]
        latents_all = spread(latents, "head")
        time_full = gathered[0].reshape(D, head_count, WIDE)[:, :, :time_cols].reshape(D, D)
        time_hidden = jnp.dot(table_bf, time_full, preferred_element_type=jnp.float32)
        shared = jnp.concatenate([time_hidden, table_bf.astype(jnp.float32), cap_unit], 1)
        shared_all = spread(shared, "dp").reshape(-1, 3 * D)
        hidden_own = lax.dynamic_slice_in_dim(shared_all, own_row, rows_own, 1)
        table_own = lax.dynamic_slice_in_dim(shared_all, D + own_row, rows_own, 1)
        cap_all = shared_all[:, 2 * D :]
        signal_own = to_bf16(double_silu(hidden_own))
        mod_part = product("fd,ldn->fln", signal_own, ada_bf)
        mod_part = mod_part.reshape(data_count, clip_count, 2 * ada_cols)
        mods = spread(jnp.sum(swap(mod_part, "dp"), 0), "head")
    up_full = [gathered[2], gathered[5]]
    down_full = [gathered[3], gathered[6]]
    io_full = (
        gathered[0]
        .reshape(D, head_count, WIDE)[:, :, time_cols : time_cols + 2 * io_cols]
        .reshape(D, head_count, 2, io_cols)
        .transpose(2, 0, 1, 3)
        .reshape(2, D, channels)
    )
    mod_all = (
        mods.reshape(head_count, clip_count, 2, ada_cols)
        .transpose(1, 2, 0, 3)
        .reshape(clip_count, 2, 6 * D)
    )
    tile_mods = by_tile(mod_all)

    def split_first(whole):
        qkv, out = [], []
        for side in range(2):
            at = 2 * side * D
            qkv += [whole[:, at : at + 640], whole[:, at + D : at + D + 512]]
            out += [whole[:, at + 640 : at + D], whole[:, at + D + 512 : at + 2 * D]]
        return jnp.concatenate(qkv, 1), jnp.concatenate(out, 1)

    def join_first(qkv, out):
        columns = []
        for side in range(2):
            q, o = side * 2 * block, side * 2 * share
            columns += [qkv[:, q : q + 640], out[:, o : o + 128]]
            columns += [qkv[:, q + 640 : q + 1152], out[:, o + 128 : o + 384]]
        return jnp.concatenate(columns, 1)

    if linked:
        qkv_full = [gathered[1 + 3 * layer][:, : 3 * D] for layer in range(2)]
        out_full = [gathered[1 + 3 * layer][:, 3 * D :] for layer in range(2)]
    else:
        qkv_full, out_full = zip(*[split_first(gathered[1 + 3 * layer]) for layer in range(2)])

    latents_all = latents_all.reshape(head_count, clip_count, 2 * channels, tile)
    own_latents = lax.dynamic_slice(
        latents_all, (2 * core, own_clip, 0, 0), (2, 1, 2 * channels, tile)
    )[:, 0]
    latents = jnp.concatenate(
        [own_latents, lax.dynamic_slice_in_dim(latents_all, h, 1, 0)[0, 2:3]]
    )
    clean_rows, noise_rows = latents[:, :channels], latents[:, channels:]
    tile_times = by_tile(timesteps)[:, None, None]
    input_bf = to_bf16((1.0 - tile_times) * clean_rows + tile_times * noise_rows)
    target = noise_rows - clean_rows
    hidden = product("fcl,dc->fld", input_bf, io_full[0])

    frames = clip_count * tile

    def layer_forward(layer_index, hidden):
        modulation = tile_mods[:, layer_index].reshape(clip_count, 1, 6, D)
        mod_parts = [modulation[:, :, member] for member in range(6)]
        normed = to_bf16(modulate(hidden, mod_parts[0], mod_parts[1]))
        weight = qkv_full[layer_index]
        if layer_index == 0:
            projected = to_bf16(product("fld,dn->fln", normed, weight))
            mixed, *attended = attend(projected.reshape(frames, 3 * D), next(ids))
            mixed = mixed.reshape(clip_count, tile, D)
        else:
            query = to_bf16(product("fld,dn->fln", normed, weight[:, :D]))
            pair_kv = to_bf16(product("ftd,dn->ftn", own_captions, weight[:, D:]))
            attended = (query, pair_kv)
            mixed = cross(query, pair_kv, own_lengths)
        branch = product("fle,de->fld", mixed, out_full[layer_index])
        middle = hidden + mod_parts[2] * branch
        normed2 = to_bf16(modulate(middle, mod_parts[3], mod_parts[4]))
        upper = product("fld,dn->fln", normed2, up_full[layer_index])
        active = to_bf16(soft_gelu(upper))
        down_out = product("fln,dn->fld", active, down_full[layer_index])
        kept = (hidden, mod_parts, normed, attended, mixed, branch, middle, normed2, upper,
                active, down_out)
        return (middle + mod_parts[5] * down_out, kept)

    saved_layers = []
    for layer_index in range(2):
        hidden, kept = layer_forward(layer_index, hidden)
        saved_layers.append(kept)
    final = norm_rows(hidden)
    final_bf = to_bf16(final)
    predicted = product("fld,dc->fcl", final_bf, io_full[1])
    errors = predicted - target
    flow_part = jnp.sum(jnp.mean(errors * errors, 1))
    grad_pred = to_bf16(2.0 * errors / channels)
    pool_sum = jnp.sum(spread(by_clip(jnp.sum(final, 1)), "head"), 0)
    pooled_out = pool_sum / length

    def contrast_of(pool_total):
        pooled = pool_total / length
        unit_rows = pooled * lax.rsqrt(jnp.mean(pooled * pooled, -1, keepdims=True) + 1e-06)
        logits = exact_product("id,jd->ij", unit_rows, cap_all) * (2.0 / math.sqrt(D))
        row_top = jnp.max(logits, -1, keepdims=True)
        log_total = row_top[:, 0] + jnp.log(jnp.sum(jnp.exp(logits - row_top), -1))
        picked = jnp.sum(
            jnp.where(jnp.arange(logits.shape[1])[None, :] == pairing[:, None], logits, 0.0), -1
        )
        return length * jnp.sum(log_total - picked)

    contrast_value, contrast_back = jax.vjp(contrast_of, pool_sum)
    grad_pool = by_tile(contrast_back(jnp.ones_like(contrast_value))[0])
    loss_part = flow_part + contrast_value / head_count
    grad_final = product("fcl,dc->fld", grad_pred, io_full[1]) + grad_pool[:, None, :]
    final_value, final_back = jax.vjp(norm_rows, hidden)
    grad_hidden = final_back(grad_final)[0]
    fin_grad = product("fcl,fld->dc", grad_pred, final_bf)
    plan, lefts, rights = [], [], []

    def listed_factors(factors, factor):
        factors.append(factor.reshape(-1, factor.shape[-1]))
        return len(factors) - 1

    mod_grads = [None, None]
    for layer_index in (1, 0):
        (
            layer_hidden,
            mod_parts,
            layer_normed,
            attended,
            layer_mixed,
            layer_branch,
            layer_middle,
            layer_normed2,
            layer_upper,
            layer_active,
            layer_down_out,
        ) = saved_layers[layer_index]
        weight = qkv_full[layer_index]
        d_gate2 = jnp.sum(layer_down_out * grad_hidden, axis=1, keepdims=True)
        grad_down = to_bf16(mod_parts[5] * grad_hidden)
        grad_active = product("fld,dn->fln", grad_down, down_full[layer_index])
        gelu_value, gelu_back = jax.vjp(soft_gelu, layer_upper)
        grad_upper = to_bf16(gelu_back(grad_active)[0])
        grad_normed2 = product("fln,dn->fld", grad_upper, up_full[layer_index])
        mod_value, mod_back = jax.vjp(modulate, layer_middle, mod_parts[3], mod_parts[4])
        grad_middle, d_shift2, d_scale2 = mod_back(grad_normed2)
        grad_middle = grad_middle + grad_hidden
        d_gate1 = jnp.sum(layer_branch * grad_middle, axis=1, keepdims=True)
        grad_branch = to_bf16(mod_parts[2] * grad_middle)
        grad_mixed = to_bf16(product("fld,de->fle", grad_branch, out_full[layer_index]))
        branch_place, branch_right = listed_factors(lefts, grad_branch), listed_factors(rights, layer_mixed)
        normed_place = listed_factors(lefts, layer_normed)
        if layer_index == 0:
            grad_proj = attend_back(*attended, grad_mixed.reshape(frames, D), next(ids))
            grad_normed = product("fn,dn->fd", grad_proj, weight)
            first = [(normed_place, listed_factors(rights, grad_proj), 0, 3 * D)]
        else:
            query, pair_kv = attended
            grad_query, grad_keys, grad_values = cross_back(query, pair_kv, own_lengths, grad_mixed)
            grad_normed = product("fln,dn->fld", grad_query, weight[:, :D])
            caption_place = listed_factors(lefts, own_captions)
            first = [
                (normed_place, listed_factors(rights, grad_query), 0, D),
                (caption_place, listed_factors(rights, grad_keys), D, 2 * D),
                (caption_place, listed_factors(rights, grad_values), 2 * D, 3 * D),
            ]
        first.append((branch_place, branch_right, 3 * D, 4 * D))
        plan.append(
            (
                tuple(first),
                (listed_factors(lefts, layer_normed2), listed_factors(rights, grad_upper)),
                (listed_factors(lefts, grad_down), listed_factors(rights, layer_active)),
            )
        )
        first_value, first_back = jax.vjp(modulate, layer_hidden, mod_parts[0], mod_parts[1])
        grad_in, d_shift1, d_scale1 = first_back(grad_normed.reshape(clip_count, tile, D))
        mod_grads[layer_index] = jnp.concatenate(
            [d_shift1, d_scale1, d_gate1, d_shift2, d_scale2, d_gate2], -1
        )[:, 0]
        grad_hidden = grad_in + grad_middle
    in_grad = product("fld,fcl->dc", to_bf16(grad_hidden), input_bf)

    mod_size = clip_count * 2 * ada_cols
    io_size = rows_own * 2 * io_cols
    mod_grad = by_clip(jnp.stack(mod_grads, 1)).reshape(clip_count, 2, head_count, ada_cols)
    mod_grad = mod_grad.transpose(2, 0, 1, 3).reshape(head_count, clip_count, 2 * ada_cols)
    io_part = (
        jnp.stack([in_grad, fin_grad])
        .reshape(2, data_count, rows_own, head_count, io_cols)
        .transpose(3, 1, 0, 2, 4)
        .reshape(head_count, data_count, io_size)
    )
    signal_own_value, signal_back = jax.vjp(double_silu, hidden_own)
    if linked:

        def padded_clips(values):
            values = values.reshape(data_count, clip_count, rows_own)
            values = jnp.pad(values, ((0, 0), (0, 8 - clip_count), (0, 0)))
            return values.reshape(-1, rows_own)

        io_lines = -(-io_size // 1024) * 8
        io_part = jnp.pad(io_part, ((0, 0), (0, 0), (0, io_lines * 128 - io_size)))
        smalls = (
            jnp.pad(loss_part.reshape(1, 1), ((0, 7), (1, 126))),
            jnp.pad(mod_grad, ((0, 0), (0, 8 - clip_count), (0, 0))),
            io_part.reshape(head_count, data_count, io_lines, 128),
            padded_clips(signal_own.astype(jnp.float32)),
            padded_clips(signal_back(jnp.ones_like(hidden_own))[0]),
            padded_clips(table_own),
            ada_bf,
        )
        owned, totals, edge, ada_grad, time_grad, io_grad = reduce_whole(
            tuple(plan), lefts, rights, smalls, next(ids)
        )
        totals = totals[0, :2]
        edge = edge[::-1]
        edge = jnp.where(is_first, edge[..., :64], edge[..., 64:])
        time_grad = jnp.concatenate([time_grad[0], time_grad[1]], 1)
        io_grad = io_grad.reshape(-1)[:io_size].reshape(2, rows_own, io_cols)
    else:
        io_grad = lax.psum(io_part, ("dp", "head"))
        io_grad = lax.dynamic_slice(io_grad, (h, d, 0), (1, 1, io_size))
        io_grad = io_grad.reshape(2, rows_own, io_cols)
        mod_grad = jnp.sum(swap(mod_grad, "head"), 0)
        mod_grad = spread(mod_grad, "dp").reshape(-1, 2, ada_cols)
        ada_grad = exact_product("fd,fln->ldn", signal_own.astype(jnp.float32), mod_grad)
        grad_signal = exact_product("fln,ldn->fd", mod_grad, ada_bf.astype(jnp.float32))
        grad_signal = jnp.sum(spread(grad_signal, "head"), 0)
        grad_cond = spread(signal_back(grad_signal)[0], "dp").transpose(1, 0, 2).reshape(-1, D)
        time_grad = exact_product(
            "fd,fn->dn",
            table_own,
            lax.dynamic_slice_in_dim(grad_cond, h * time_cols, time_cols, 1),
        )

        def made(left_place, right_place):
            return product("fd,fn->dn", lefts[left_place], rights[right_place])

        owned = []
        for first, *pairs in plan:
            columns = jnp.concatenate([made(*source[:2]) for source in first], 1)
            owned.append(join_first(columns[:, : 3 * D], columns[:, 3 * D :]))
            owned += [made(*pair) for pair in pairs]
        owned = [reduce_general(part) for part in owned]
        square = sum((jnp.sum(part * part) for part in owned + [ada_grad, time_grad, io_grad]))
        totals = lax.psum(jnp.stack([square, loss_part]), ("dp", "head"))
        edge = jnp.stack([owned[3], owned[0]])
        edge = jnp.where(is_first, edge[..., block : block + 64], edge[..., block - 64 : block])
        edge = spread(edge.reshape(-1, 128), "head")
        edge = lax.dynamic_slice_in_dim(edge, h ^ 1, 1, 0).reshape(2, rows_own, 64)
    first_own = jnp.stack([owned[3], owned[0]])
    total_square, total_loss = totals[0], totals[1]
    qkv_shard, out_shard = without_edge(first_own, edge)
    shards = (
        qkv_shard,
        out_shard,
        jnp.stack([owned[4], owned[1]]),
        jnp.stack([owned[5], owned[2]]),
        ada_grad,
        time_grad[None],
        io_grad,
    )
    old_moments = (qkv_moment, out_moment, up_moment, down_moment)
    grad_norm = jnp.sqrt(total_square)
    clip_scale = jnp.minimum(1.0, CLIP_NORM / (grad_norm + 1e-06))
    moments = tuple(
        (MUON_BETA * old_moments[member] + clip_scale * shards[member] for member in range(4))
    )
    coeff_a, coeff_b, coeff_c = NEWTON_COEFFS
    widths = [-(-moment.shape[2] // 128) * 128 for moment in moments]
    padded = [
        jnp.pad(moment, ((0, 0), (0, 0), (0, width - moment.shape[2])))
        for moment, width in zip(moments, widths)
    ]
    own_matrix = to_owner(padded, next(ids)).reshape(D, -1)

    def near_product(form, left, right):
        return jnp.einsum(form, left, right, precision=lax.Precision.HIGH)

    gram = gram_sum(own_matrix, next(ids))
    unit = jnp.eye(D, dtype=jnp.float32)
    size_frob = jnp.sqrt(jnp.sum(gram * unit)) + 1e-07
    gram = gram / (size_frob * size_frob)
    factor = None
    for ns_step in range(NS_STEPS):
        poly = coeff_a * unit + coeff_b * gram + coeff_c * near_product("rk,kj->rj", gram, gram)
        factor = poly if factor is None else near_product("rk,kj->rj", poly, factor)
        if ns_step < NS_STEPS - 1:
            gram = near_product("rk,kj->rj", near_product("rk,kj->rj", poly, gram), poly)
    ortho_matrix = near_product("rk,kc->rc", factor, own_matrix) / size_frob
    ortho_back = to_bf16(ortho_matrix).reshape(data_count, rows_own, -1)
    ortho_back = from_owner(ortho_back, tuple(widths), next(ids)).astype(jnp.float32)
    ortho_rows = tuple(
        (
            jnp.stack(
                [
                    ortho_back[owner_of(member, layer), :, : moments[member].shape[2]]
                    for layer in range(2)
                ]
            )
            for member in range(4)
        )
    )
    muon_weights = (qkv_weight, out_weight, up_weight, down_weight)
    muon_new = tuple(
        (
            muon_weights[member] * (1.0 - MUON_RATE * MUON_DECAY)
            - MUON_RATE
            * 0.2
            * math.sqrt(max(D, muon_weights[member].shape[2] * head_count))
            * ortho_rows[member]
            for member in range(4)
        )
    )
    step_count = adam_step[0].astype(jnp.float32)
    ada_new, ada_first_new, ada_second_new = adam_update(
        ada_weight, clip_scale * shards[4], ada_first, ada_second, step_count
    )
    time_new, time_first_new, time_second_new = adam_update(
        time_weight, clip_scale * shards[5][0], time_first, time_second, step_count
    )
    io_new, io_first_new, io_second_new = adam_update(
        io_weight, clip_scale * shards[6], io_first, io_second, step_count
    )
    return (
        total_loss,
        grad_norm,
        pooled_out,
        muon_new[0],
        moments[0],
        muon_new[1],
        moments[1],
        muon_new[2],
        moments[2],
        muon_new[3],
        moments[3],
        ada_new,
        ada_first_new,
        ada_second_new,
        time_new,
        time_first_new,
        time_second_new,
        io_new,
        io_first_new,
        io_second_new,
    )


def solution(mesh):
    placed = (
        P("dp", "head", None),
        P("dp", "head", None),
        P("dp"),
        P("dp", None, None),
        P("dp"),
        P("dp"),
        P(),
        P(None, "dp", "head"),
        P(None, "dp", "head"),
        P(None, "dp", "head"),
        P(None, "dp", "head"),
        P(None, "dp", "head"),
        P("dp", "head"),
        P(None, "dp", "head"),
        P(None, "dp", "head"),
        P(None, "dp", "head"),
        P(None, "dp", "head"),
        P(None, "dp", "head"),
        P(None, "dp", "head"),
        P(None, "dp", "head"),
        P("dp", "head"),
        P("dp", "head"),
        P(None, "dp", "head"),
        P(None, "dp", "head"),
    )
    return jax.shard_map(
        body,
        mesh=mesh,
        in_specs=placed,
        out_specs=(
            P(),
            P(),
            P("dp", None),
            P(None, "dp", "head"),
            P(None, "dp", "head"),
            P(None, "dp", "head"),
            P(None, "dp", "head"),
            P(None, "dp", "head"),
            P(None, "dp", "head"),
            P(None, "dp", "head"),
            P(None, "dp", "head"),
            P(None, "dp", "head"),
            P(None, "dp", "head"),
            P(None, "dp", "head"),
            P("dp", "head"),
            P("dp", "head"),
            P("dp", "head"),
            P(None, "dp", "head"),
            P(None, "dp", "head"),
            P(None, "dp", "head"),
        ),
        check_vma=False,
    )
```

```python
import functools
import math

import jax
import jax.numpy as jnp
from jax import lax
from jax.experimental import pallas as pl
from jax.experimental.pallas import tpu as pltpu
from jax.sharding import PartitionSpec as P

D = 768
HEADS = 12
HDIM = 64
CAP = 256
NS_STEPS = 5


HIGHEST_PRECISION = lax.Precision.HIGHEST
NEWTON_COEFFS = (3.4445, -4.775, 2.0315)
CLIP_NORM = 1.0
MUON_RATE = 0.2
MUON_DECAY = 0.1
MUON_BETA = 0.95
ADAM_RATE = 0.02
ADAM_DECAY = 0.01
ADAM_FIRST = 0.9
ADAM_SECOND = 0.999


def to_bf16(values):
    return values.astype(jnp.bfloat16)


def sigmoid_unit(values):
    return values * jax.nn.sigmoid(values)


def double_silu(values):
    return sigmoid_unit(sigmoid_unit(values))


GELU_RATE = 0.7978845608
GELU_CUBE = 0.7978845608 * 0.044715


def soft_gelu(values):
    return 0.5 * values * (1.0 + jnp.tanh(values * (GELU_RATE + GELU_CUBE * (values * values))))


def soft_gelu_slope(values):
    square = values * values
    bend = jnp.tanh(values * (GELU_RATE + GELU_CUBE * square))
    steep = values * (GELU_RATE + (3.0 * GELU_CUBE) * square)
    return 0.5 * ((1.0 + bend) + (1.0 - bend * bend) * steep)


def norm_rows(values):
    centre = values - jnp.mean(values, -1, keepdims=True)
    return centre * lax.rsqrt(jnp.mean(centre * centre, -1, keepdims=True) + 1e-06)


def modulate(hidden, shift, stretch):
    return norm_rows(hidden) * (1.0 + stretch) + shift


def time_table(timesteps, width):
    half_width = width // 2
    frequency = jnp.exp(
        -math.log(10000.0) * jnp.arange(half_width).astype(timesteps.dtype) / half_width
    )
    angles = 1000.0 * timesteps[:, None] * frequency[None, :]
    return jnp.concatenate([jnp.cos(angles), jnp.sin(angles)], axis=-1)


def product(form, left, right):
    return jnp.einsum(form, left, right, preferred_element_type=jnp.float32)


def exact_product(form, left, right):
    return jnp.einsum(form, left, right, precision=HIGHEST_PRECISION)


def adam_update(weight, grad_part, first_moment, second_moment, step_count):
    first_moment = ADAM_FIRST * first_moment + (1.0 - ADAM_FIRST) * grad_part
    second_moment = ADAM_SECOND * second_moment + (1.0 - ADAM_SECOND) * grad_part * grad_part
    first_fix = 1.0 - jnp.power(ADAM_FIRST, step_count)
    second_fix = 1.0 - jnp.power(ADAM_SECOND, step_count)
    direction = first_moment / first_fix / (jnp.sqrt(second_moment / second_fix) + 1e-08)
    return (weight - ADAM_RATE * (direction + ADAM_DECAY * weight), first_moment, second_moment)


MESH = pl.DeviceIdType.MESH
ROWS_A = 64
PIECE_COLS = 256
SLOTS = 4
HALF = 384
WIDE = 256
VMEM_BYTES = 56 * 1024 * 1024


def vmem():
    return pl.BlockSpec(memory_space=pltpu.VMEM)


def anywhere():
    return pl.BlockSpec(memory_space=pl.ANY)


def comm_params(collective_id):
    return pltpu.CompilerParams(
        collective_id=collective_id, has_side_effects=True, vmem_limit_bytes=VMEM_BYTES
    )


def greet(peers):
    barrier = pltpu.get_barrier_semaphore()
    for peer in peers:
        pl.semaphore_signal(barrier, inc=1, device_id=peer, device_id_type=MESH)
    pl.semaphore_wait(barrier, len(peers))


def exchange_kernel(axis, count, swapped, x_ref, out_ref, send_sem, recv_sem):
    me = lax.axis_index(axis)
    peers = [lax.rem(me + shift, count) for shift in range(1, count)]
    greet([{axis: peer} for peer in peers])
    copies = []
    for place, peer in enumerate(peers):
        copy = pltpu.make_async_remote_copy(
            src_ref=x_ref.at[peer] if swapped else x_ref,
            dst_ref=out_ref.at[me],
            send_sem=send_sem.at[place],
            recv_sem=recv_sem.at[place],
            device_id={axis: peer},
            device_id_type=MESH,
        )
        copy.start()
        copies.append(copy)
    out_ref[me] = x_ref[me] if swapped else x_ref[...]
    for copy in copies:
        copy.wait()


def exchange(x, axis, swapped, collective_id):
    count = lax.axis_size(axis)
    block = x.shape[1:] if swapped else x.shape
    return pl.pallas_call(
        functools.partial(exchange_kernel, axis, count, swapped),
        out_shape=jax.ShapeDtypeStruct((count,) + block, x.dtype),
        in_specs=[vmem()],
        out_specs=vmem(),
        scratch_shapes=[
            pltpu.SemaphoreType.DMA((count - 1,)),
            pltpu.SemaphoreType.DMA((count - 1,)),
        ],
        compiler_params=comm_params(collective_id),
        name="swap" if swapped else "spread",
    )(x)


def link_peers(d, h):
    return {
        "core": (d, h ^ 1),
        "y": (d, h ^ 2),
        "x": (d ^ 1, h),
        "zl": (d ^ 2, h),
        "zh": (d ^ 4, h),
    }


def first_column(side, core, start):
    if start < 512:
        return side * 1152 + core * 640 + start
    if start == 512:
        return (1 - core) * (side * 1152 + 512) + core * (3 * D + side * HALF + 128)
    return 3 * D + side * HALF + core * 256


def gather_pieces(widths, firsts):
    pieces = []
    for group, width in enumerate(widths):
        for start in range(0, width, PIECE_COLS):
            if group in firsts and start == 512:
                pieces += [(group, 512, 128), (group, 640, 128)]
            else:
                pieces.append((group, start, PIECE_COLS))
    return pieces


def gather_kernel(groups, firsts, *refs):
    own_refs = refs[:groups]
    edge_ref, latents_ref, shared_ref, table_ref, ada_ref = refs[groups : groups + 5]
    out_refs = refs[groups + 5 : 2 * groups + 5]
    latents_out, shared_out, mods_out = refs[2 * groups + 5 : 2 * groups + 8]
    (tail, edge_got, times, parts, parts_got, mine, send_sem, recv_sem, core_send, core_recv,
     local_sem, tail_sem, small_send, small_recv) = refs[2 * groups + 8 :]
    d = lax.axis_index("dp")
    h = lax.axis_index("head")
    peers = link_peers(d, h)
    heads = [(d, h ^ other) for other in (1, 2, 3)]
    datas = [(d ^ other, h) for other in range(1, 8)]
    greet(heads + datas)
    y, c = h // 2, h % 2
    zh, zl, x = d // 4, (d // 2) % 2, d % 2
    every = slice(None)
    pieces = gather_pieces([own.shape[1] for own in own_refs], firsts)
    order_a = (("zh", (zh, zl, x)), ("zl", (every, zl, x)), ("x", (every, every, x)),
               ("y", (every, every, every)))
    order_b = (("y", (zh, zl, x)), ("zh", (zh, zl, x)), ("zl", (every, zl, x)),
               ("x", (every, every, x)))

    def tail_of(piece):
        group, start, size = pieces[piece]
        if group in firsts and start == 2 * PIECE_COLS:
            return firsts.index(group)
        return None

    def source_of(piece, rows):
        group, start, size = pieces[piece]
        place = tail_of(piece)
        if place is not None:
            return tail.at[place, rows]
        return own_refs[group].at[rows, pl.ds(start, size)]

    def columns_of(piece, head):
        group, start, size = pieces[piece]
        if group in firsts:
            return pl.ds(pl.multiple_of(first_column(head // 2, head % 2, start), 128), size)
        return pl.ds(pl.multiple_of(head * own_refs[group].shape[1] + start, 128), size)

    def own_copy(piece):
        group = pieces[piece][0]
        return pltpu.make_async_copy(
            source_of(piece, pl.ds(0, own_refs[group].shape[0])),
            out_refs[group].at[zh, zl, x, :, columns_of(piece, h)],
            local_sem.at[piece],
        )

    def hop(piece, step, stream):
        group = pieces[piece][0]
        rows_all = own_refs[group].shape[0]
        rows = pl.ds(0, ROWS_A) if stream == 0 else pl.ds(ROWS_A, rows_all - ROWS_A)
        head = h if stream < 2 else h ^ 2
        peer, index = (order_a if stream == 0 else order_b)[step]
        view = out_refs[group].at[index + (rows, columns_of(piece, head))]
        return pltpu.make_async_remote_copy(
            src_ref=source_of(piece, rows) if step == 0 else view,
            dst_ref=view,
            send_sem=send_sem.at[piece, step, stream],
            recv_sem=recv_sem.at[piece, step, stream],
            device_id=peers[peer],
            device_id_type=MESH,
        )

    def streams(step):
        return range(2) if step == 0 else range(3)

    def across(piece, side):
        group = pieces[piece][0]
        view = out_refs[group].at[:, :, :, :, columns_of(piece, h ^ (2 * side))]
        return pltpu.make_async_remote_copy(
            src_ref=view,
            dst_ref=view,
            send_sem=core_send.at[piece, side],
            recv_sem=core_recv.at[piece, side],
            device_id=peers["core"],
            device_id_type=MESH,
        )

    def small(place, source, target, peer):
        return pltpu.make_async_remote_copy(
            src_ref=source,
            dst_ref=target,
            send_sem=small_send.at[place],
            recv_sem=small_recv.at[place],
            device_id=peer,
            device_id_type=MESH,
        )

    edge = small(0, edge_ref, edge_got, peers["core"])
    edge.start()
    tails = [
        pltpu.make_async_copy(
            own_refs[group].at[:, pl.ds(2 * PIECE_COLS, 128)], tail.at[place],
            tail_sem.at[place],
        )
        for place, group in enumerate(firsts)
    ]
    for copy in tails:
        copy.start()
    latents = [
        small(1 + place, latents_ref, latents_out.at[h], peer) for place, peer in enumerate(heads)
    ]
    for copy in latents:
        copy.start()
    latents_out[h] = latents_ref[...]
    bring_times = pltpu.make_async_copy(out_refs[0], times, tail_sem.at[len(firsts)])
    shares = [
        small(4 + place, mine, shared_out.at[d], peer) for place, peer in enumerate(datas)
    ]
    swaps = [
        small(11 + place, parts.at[d ^ (1 + place)], parts_got.at[d], peer)
        for place, peer in enumerate(datas)
    ]
    spreads = [
        small(18 + place, mods_out.at[h], mods_out.at[h], peer) for place, peer in enumerate(heads)
    ]

    def condition(turn):
        if turn == 2:
            edge.wait()
            for copy in tails:
                copy.wait()
            tail[...] = tail[...] + edge_got[...]
            for piece in range(len(pieces)):
                if tail_of(piece) is not None:
                    own_copy(piece).start()
        if turn == 6:
            for side in range(2):
                across(0, side).wait_recv()
            bring_times.start()
        if turn == 7:
            bring_times.wait()
            rows = times.shape[-2]
            mine[...] = shared_ref[...] + dot_nn(
                table_ref[...], times[...].reshape(8 * rows, times.shape[-1])
            )
            for copy in shares:
                copy.start()
            shared_out[d] = mine[...]
        if turn == 11:
            for copy in shares:
                copy.wait()
            count, lines, width = shared_out.shape
            signal = to_bf16(double_silu(shared_out[...])).reshape(count * lines, width)
            first = (d // 2) * WIDE + (d % 2) * ada_ref.shape[1]
            at = lax.broadcasted_iota(jnp.int32, (width, 128), 0)
            to = lax.broadcasted_iota(jnp.int32, (width, 128), 1)
            chosen = jnp.where((at == first + to) & (to < ada_ref.shape[1]), 1.0, 0.0)
            own = to_bf16(dot_nn(signal, to_bf16(chosen)))
            row = lax.broadcasted_iota(jnp.int32, (count * lines, count * lines), 0)
            source = lax.broadcasted_iota(jnp.int32, (count * lines, count * lines), 1)
            within = row % lines
            repeat = (source == row) & (within < 3) | (source == row - 3) & (within >= 3) & (within < 6)
            own = to_bf16(dot_nn(to_bf16(jnp.where(repeat, 1.0, 0.0)), own))[:, : ada_ref.shape[1]]
            within = lax.broadcasted_iota(jnp.int32, (count * lines, 1), 0) % lines
            part = jnp.where(within < 3, dot_nn(own, ada_ref[0]), dot_nn(own, ada_ref[1]))
            parts[...] = part.reshape(parts.shape)
            for copy in swaps:
                copy.start()
            parts_got[d] = parts[d]
        if turn == 15:
            for copy in swaps:
                copy.wait()
            total = parts_got[0]
            for place in range(1, 8):
                total = total + parts_got[place]
            mods_out[h] = total
            for copy in spreads:
                copy.start()
        if turn == 19:
            for copy in spreads + latents:
                copy.wait()

    for piece in range(len(pieces)):
        if tail_of(piece) is None:
            own_copy(piece).start()
    for turn in range(len(pieces) + 4):
        for step in range(5):
            piece = turn - step
            if not 0 <= piece < len(pieces):
                continue
            if step == 1:
                own_copy(piece).wait()
            if step >= 1:
                for stream in streams(step - 1):
                    hop(piece, step - 1, stream).wait_recv()
            if step < 4:
                for stream in streams(step):
                    hop(piece, step, stream).start()
            else:
                for side in range(2):
                    across(piece, side).start()
        condition(turn)
    for piece in range(len(pieces)):
        for step in range(4):
            for stream in streams(step):
                hop(piece, step, stream).wait_send()
        for side in range(2):
            if piece > 0:
                across(piece, side).wait_recv()
            across(piece, side).wait_send()


def gather_whole(owns, firsts, edge, latents, shared, table, ada, collective_id):
    groups = len(owns)
    pieces = len(gather_pieces([own.shape[1] for own in owns], firsts))
    rows = owns[0].shape[0]
    low = jnp.bfloat16
    mod_cols = ada.shape[2]
    *wholes, latents_all, shared_all, mods = pl.pallas_call(
        functools.partial(gather_kernel, groups, firsts),
        out_shape=[
            jax.ShapeDtypeStruct((2, 2, 2, own.shape[0], 4 * own.shape[1]), own.dtype)
            for own in owns
        ]
        + [
            jax.ShapeDtypeStruct((4,) + latents.shape, jnp.float32),
            jax.ShapeDtypeStruct((8,) + shared.shape, jnp.float32),
            jax.ShapeDtypeStruct((4, 8, mod_cols), jnp.float32),
        ],
        in_specs=[anywhere()] * groups + [vmem()] * 5,
        out_specs=[anywhere()] * groups + [vmem()] * 3,
        scratch_shapes=[
            pltpu.VMEM(edge.shape, low),
            pltpu.VMEM(edge.shape, low),
            pltpu.VMEM((2, 2, 2, rows, 4 * owns[0].shape[1]), low),
            pltpu.VMEM((8, 8, mod_cols), jnp.float32),
            pltpu.VMEM((8, 8, mod_cols), jnp.float32),
            pltpu.VMEM(shared.shape, jnp.float32),
            pltpu.SemaphoreType.DMA((pieces, 4, 3)),
            pltpu.SemaphoreType.DMA((pieces, 4, 3)),
            pltpu.SemaphoreType.DMA((pieces, 2)),
            pltpu.SemaphoreType.DMA((pieces, 2)),
            pltpu.SemaphoreType.DMA((pieces,)),
            pltpu.SemaphoreType.DMA((len(firsts) + 1,)),
            pltpu.SemaphoreType.DMA((21,)),
            pltpu.SemaphoreType.DMA((21,)),
        ],
        compiler_params=comm_params(collective_id),
        name="gather_weights",
    )(*owns, edge, latents, shared, table, ada)
    wholes = [whole.reshape(8 * own.shape[0], -1) for whole, own in zip(wholes, owns)]
    return wholes, latents_all, shared_all, mods


def gather_general(own):
    rows, columns = own.shape
    blocks = lax.all_gather(own, ("dp", "head"), axis=0, tiled=False)
    blocks = blocks.reshape(-1, lax.axis_size("head"), rows, columns)
    return blocks.transpose(0, 2, 1, 3).reshape(-1, lax.axis_size("head") * columns)


def reduce_kernel(plan, lefts, rights, *refs):
    left_refs, right_refs = refs[:lefts], refs[lefts : lefts + rights]
    (extra_ref, mod_ref, io_ref, signal_ref, slope_ref, table_ref, ada_ref, out_ref, total_ref,
     edge_ref, ada_out, time_out, io_out) = refs[lefts + rights : lefts + rights + 13]
    (made, near, left, left_t, right, send_a, send_b, got_a, got_b, keep_a, keep_b,
     mine, head_got, data_got, mod_got, io_got, mod_sum, io_sum, mod_all, io_all, part, part_got,
     inner, inner_all, near_send, near_recv, hop_send, hop_recv, left_sem,
     right_sem, edge_send, edge_recv, sum_send, sum_recv, small_send, small_recv) = refs[
        lefts + rights + 13 :
    ]
    layers = len(plan)
    per_group = D // PIECE_COLS
    pieces = 3 * layers * per_group
    d = lax.axis_index("dp")
    h = lax.axis_index("head")
    peers = link_peers(d, h)
    across = [(d, h ^ other) for other in (1, 2, 3)] + [(d ^ other, h) for other in range(1, 8)]
    greet(across)
    y, c = h // 2, h % 2
    zh, zl, x = d // 4, (d // 2) % 2, d % 2
    order = (("y", "x"), ("x", "zl"), ("zl", "zh"), ("zh", "y"))
    shape = made.shape[3:]
    rows_own = shape[-2]
    top, bottom = pl.ds(0, ROWS_A), pl.ds(ROWS_A, rows_own - ROWS_A)
    every = slice(None)

    def near_copy(piece, side):
        slot = piece % SLOTS
        return pltpu.make_async_remote_copy(
            src_ref=made.at[slot, side, 1 - c],
            dst_ref=near.at[slot, side],
            send_sem=near_send.at[slot, side],
            recv_sem=near_recv.at[slot, side],
            device_id=peers["core"],
            device_id_type=MESH,
        )

    def left_copy(place):
        rows = left_refs[place].shape[0]
        return pltpu.make_async_copy(
            left_refs[place], left.at[place, pl.ds(0, rows)], left_sem.at[place]
        )

    def turn_left(place, at):
        rows = left_refs[place].shape[0]
        left_copy(place).wait()
        left_t[at, :, :rows] = left[place, :rows].T

    def sources(layer, part, head, half):
        column = first_column(head // 2, head % 2, part * PIECE_COLS + (128 * half if part == 2 else 0))
        if part < 2:
            column += 128 * half
        for at, (left_place, right_place, start, stop) in enumerate(plan[layer][0]):
            if start <= column < stop:
                return left_place, right_place, column - start

    def right_copies(piece, layer, part):
        copies = []
        for head in range(4):
            for half in range(2):
                left_place, right_place, column = sources(layer, part, head, half)
                rows = right_refs[right_place].shape[0]
                copies.append(
                    pltpu.make_async_copy(
                        right_refs[right_place].at[:, pl.ds(column, 128)],
                        right.at[piece % 2, head, pl.ds(0, rows), pl.ds(128 * half, 128)],
                        right_sem.at[piece % 2, head, half],
                    )
                )
        return copies

    def right_copy(piece, right_place, head):
        start = head * D + (piece % per_group) * PIECE_COLS
        return pltpu.make_async_copy(
            right_refs[right_place].at[:, pl.ds(pl.multiple_of(start, PIECE_COLS), PIECE_COLS)],
            right.at[piece % 2, head],
            right_sem.at[piece % 2, head, 0],
        )

    def fetch(piece):
        for layer in range(layers):
            for part in range(per_group):

                @pl.when(piece == (3 * layer + 2) * per_group + part)
                def _():
                    for copy in right_copies(piece, layer, part):
                        copy.start()

            for member in range(2):

                @pl.when(piece // per_group == 3 * layer + member)
                def _():
                    for head in range(4):
                        right_copy(piece, plan[layer][1 + member][1], head).start()

    def bring(piece):
        slot = piece % SLOTS
        for layer in range(layers):
            used = []
            for left_place, _, _, _ in plan[layer][0]:
                if left_place not in used:
                    used.append(left_place)

            @pl.when(piece == (3 * layer + 2) * per_group)
            def _():
                for at, left_place in enumerate(used):
                    turn_left(left_place, at)

            for part in range(per_group):

                @pl.when(piece == (3 * layer + 2) * per_group + part)
                def _():
                    for copy in right_copies(piece, layer, part):
                        copy.wait()
                    for head in range(4):
                        pair = [sources(layer, part, head, half) for half in range(2)]
                        spans = [(0, 2)] if pair[0][0] == pair[1][0] else [(0, 1), (1, 2)]
                        for first, stop in spans:
                            left_place, right_place, _ = pair[first]
                            rows = right_refs[right_place].shape[0]
                            columns = slice(128 * first, 128 * stop)
                            made[slot, head // 2, head % 2, :, :, :, :, columns] = dot_nn(
                                left_t[used.index(left_place), :, :rows],
                                right[piece % 2, head, :rows, columns],
                            ).reshape(shape[:-1] + (128 * (stop - first),))

            for member in range(2):

                @pl.when(piece == (3 * layer + member) * per_group)
                def _():
                    turn_left(plan[layer][1 + member][0], 0)

        @pl.when((piece // per_group) % 3 != 2)
        def _():
            for head in range(4):
                right_copy(piece, plan[0][1][1], head).wait()
            for head in range(4):
                made[slot, head // 2, head % 2] = dot_nn(
                    left_t[0], right[piece % 2, head]
                ).reshape(shape)

        for side in range(2):
            near_copy(piece, side).start()

    def hop(piece, step, stream):
        slot = piece % SLOTS
        sent, got = (send_a, got_a) if stream == 0 else (send_b, got_b)
        return pltpu.make_async_remote_copy(
            src_ref=sent[step].at[slot],
            dst_ref=got[step].at[slot],
            send_sem=hop_send.at[step, stream, slot],
            recv_sem=hop_recv.at[step, stream, slot],
            device_id=peers[order[step][stream]],
            device_id_type=MESH,
        )

    def first(piece):
        slot = piece % SLOTS
        for side in range(2):
            near_copy(piece, side).wait()

        def total(side, *index):
            return made[(slot, side, c) + index] + near[(slot, side) + index]

        send_a[0][slot] = to_bf16(total(1 - y, every, every, every, top))
        hop(piece, 0, 0).start()
        send_b[0][slot] = to_bf16(total(every, every, every, 1 - x, bottom))
        hop(piece, 0, 1).start()
        keep_a[0][slot] = total(y, every, every, every, top)
        keep_b[0][slot] = total(every, every, every, x, bottom)

    cut_a = (None, (2, x), (1, zl), (0, zh))
    cut_b = (None, (2, zl), (1, zh), (0, y))

    def later(piece, step):
        slot = piece % SLOTS
        for stream in range(2):
            keep, got, sent = (keep_a, got_a, send_a) if stream == 0 else (keep_b, got_b, send_b)
            axis, mine = (cut_a if stream == 0 else cut_b)[step]
            hop(piece, step - 1, stream).wait()

            def total(which):
                index = (slot,) + (every,) * axis + (which,)
                return keep[step - 1][index] + got[step - 1][index].astype(jnp.float32)

            sent[step][slot] = to_bf16(total(1 - mine))
            hop(piece, step, stream).start()
            keep[step][slot] = total(mine)

    def last(piece):
        slot = piece % SLOTS
        for stream in range(2):
            keep, got = (keep_a, got_a) if stream == 0 else (keep_b, got_b)
            hop(piece, 3, stream).wait()
            out_ref[piece, top if stream == 0 else bottom, :] = keep[3][slot] + got[3][
                slot
            ].astype(jnp.float32)

    def small(place, source, target, peer):
        return pltpu.make_async_remote_copy(
            src_ref=source,
            dst_ref=target,
            send_sem=small_send.at[place],
            recv_sem=small_recv.at[place],
            device_id=peer,
            device_id_type=MESH,
        )

    heads = [(across[other - 1], h ^ other, other - 1) for other in (1, 2, 3)]
    datas = [(across[2 + other], d ^ other, other - 1) for other in range(1, 8)]
    mod_swaps = [small(at, mod_ref.at[place], mod_got.at[h], peer) for peer, place, at in heads]
    io_swaps = [small(3 + at, io_ref.at[place], io_got.at[h], peer) for peer, place, at in heads]
    mod_spreads = [small(6 + at, mod_sum, mod_all.at[d], peer) for peer, _, at in datas]
    io_moves = [small(13 + at, io_sum.at[place], io_all.at[d], peer) for peer, place, at in datas]
    part_spreads = [small(20 + at, part, part_got.at[h], peer) for peer, _, at in heads]
    inner_spreads = [small(23 + at, inner, inner_all.at[d], peer) for peer, _, at in datas]

    def total_of(ref):
        total = ref[0]
        for place in range(1, ref.shape[0]):
            total = total + ref[place]
        return total

    def exact(left, right, contract):
        return lax.dot_general(
            left, right, (contract, ((), ())), precision=HIGHEST_PRECISION,
            preferred_element_type=jnp.float32,
        )

    def condition(turn):
        @pl.when(turn == 2)
        def _():
            for copy in mod_swaps + io_swaps:
                copy.wait()
            mod_sum[...] = total_of(mod_got)
            io_sum[...] = total_of(io_got)
            for copy in mod_spreads + io_moves:
                copy.start()
            mod_all[d] = mod_sum[...]
            io_all[d] = io_sum[d]

        @pl.when(turn == 6)
        def _():
            for copy in mod_spreads + io_moves:
                copy.wait()
            io_out[...] = total_of(io_all)
            columns = ada_ref.shape[2]
            total = jnp.zeros(part.shape, jnp.float32)
            for layer in range(2):
                grads = mod_all[:, :, layer * columns : (layer + 1) * columns].reshape(
                    part.shape[0], columns
                )
                ada_out[layer] = exact(signal_ref[...], grads, ((0,), (0,)))
                total = total + exact(grads, ada_ref[layer].astype(jnp.float32), ((1,), (1,)))
            part[...] = total
            for copy in part_spreads:
                copy.start()
            part_got[h] = total

        @pl.when(turn == 10)
        def _():
            for copy in part_spreads:
                copy.wait()
            inner[...] = total_of(part_got) * slope_ref[...]
            for copy in inner_spreads:
                copy.start()
            inner_all[d] = inner[...]

        @pl.when(turn == 14)
        def _():
            for copy in inner_spreads:
                copy.wait()
            for place in range(2):
                time_out[place] = exact(table_ref[...], inner_all[2 * h + place], ((0,), (0,)))

    for copy in mod_swaps + io_swaps:
        copy.start()
    mod_got[h] = mod_ref[h]
    io_got[h] = io_ref[h]
    soonest = plan[0][1][0]
    left_copy(soonest).start()
    fetch(0)
    fetch(1)
    for place in range(lefts):
        if place != soonest:
            left_copy(place).start()
    bring(0)
    fetch(2)
    bring(1)

    @pl.loop(0, pieces + 4)
    def _(turn):
        @pl.when(turn + 3 < pieces)
        def _():
            fetch(turn + 3)

        @pl.when(turn < pieces)
        def _():
            first(turn)

        for step in (1, 2, 3):

            @pl.when((turn >= step) & (turn - step < pieces))
            def _():
                later(turn - step, step)

        @pl.when(turn >= 4)
        def _():
            last(turn - 4)

        @pl.when(turn + 2 < pieces)
        def _():
            bring(turn + 2)

        condition(turn)

    edges = []
    for layer in range(layers):
        piece = 3 * (layer + 1) * per_group - 1
        edges.append(
            pltpu.make_async_remote_copy(
                src_ref=out_ref.at[piece, :, pl.ds(0, 128)],
                dst_ref=edge_ref.at[layer],
                send_sem=edge_send.at[layer],
                recv_sem=edge_recv.at[layer],
                device_id=peers["core"],
                device_id_type=MESH,
            )
        )
        edges[-1].start()

    squares = jnp.zeros((rows_own, PIECE_COLS), jnp.float32)
    for piece in range(pieces):
        squares = squares + out_ref[piece] * out_ref[piece]
    row = lax.broadcasted_iota(jnp.int32, (8, 128), 0)
    column = lax.broadcasted_iota(jnp.int32, (8, 128), 1)
    square = jnp.sum(squares)
    for ref in (ada_out, time_out, io_out):
        square = square + jnp.sum(ref[...] * ref[...])
    mine[0] = extra_ref[...] + jnp.where((row == 0) & (column == 0), square, 0.0)
    for phase, (got, me, count) in enumerate(((head_got, h, 4), (data_got, d, 8))):
        copies = []
        for other in range(1, count):
            place = 3 * phase + other - 1
            copies.append(
                pltpu.make_async_remote_copy(
                    src_ref=mine.at[phase],
                    dst_ref=got.at[me],
                    send_sem=sum_send.at[place],
                    recv_sem=sum_recv.at[place],
                    device_id=across[place],
                    device_id_type=MESH,
                )
            )
            copies[-1].start()
        got[me] = mine[phase]
        for copy in copies:
            copy.wait()
        total = got[0]
        for other in range(1, count):
            total = total + got[other]
        if phase == 0:
            mine[1] = total
        else:
            total_ref[...] = total
    for copy in edges:
        copy.wait()


def reduce_whole(plan, lefts, rights, smalls, collective_id):
    layers = len(plan)
    frames = lefts[0].shape[0]
    rows = D // 8
    per_group = D // PIECE_COLS
    pieces = 3 * layers * per_group
    leads = ((2, 2, 2), (2, 2), (2,), ())

    def buffers(count, dtype):
        return [pltpu.VMEM((SLOTS,) + lead + (count, PIECE_COLS), dtype) for lead in leads]

    bottom_rows = rows - ROWS_A
    blocks = (2, 2, 2, rows, PIECE_COLS)
    low = jnp.bfloat16
    mod, io, signal, ada = smalls[1], smalls[2], smalls[3], smalls[6]
    summed, *others = pl.pallas_call(
        functools.partial(reduce_kernel, plan, len(lefts), len(rights)),
        out_shape=[
            jax.ShapeDtypeStruct((pieces, rows, PIECE_COLS), jnp.float32),
            jax.ShapeDtypeStruct((8, 128), jnp.float32),
            jax.ShapeDtypeStruct((layers, rows, 128), jnp.float32),
            jax.ShapeDtypeStruct(ada.shape, jnp.float32),
            jax.ShapeDtypeStruct((2, rows, rows), jnp.float32),
            jax.ShapeDtypeStruct(io.shape[2:], jnp.float32),
        ],
        in_specs=[anywhere()] * (len(lefts) + len(rights)) + [vmem()] * 7,
        out_specs=[vmem()] * 6,
        scratch_shapes=[
            pltpu.VMEM((SLOTS, 2, 2) + blocks, jnp.float32),
            pltpu.VMEM((SLOTS, 2) + blocks, jnp.float32),
            pltpu.VMEM((len(lefts), frames, D), low),
            pltpu.VMEM((3, D, frames), low),
            pltpu.VMEM((2, 4, frames, PIECE_COLS), low),
            buffers(ROWS_A, low),
            buffers(bottom_rows, low),
            buffers(ROWS_A, low),
            buffers(bottom_rows, low),
            buffers(ROWS_A, jnp.float32),
            buffers(bottom_rows, jnp.float32),
            pltpu.VMEM((2, 8, 128), jnp.float32),
            pltpu.VMEM((4, 8, 128), jnp.float32),
            pltpu.VMEM((8, 8, 128), jnp.float32),
            pltpu.VMEM(mod.shape, jnp.float32),
            pltpu.VMEM(io.shape, jnp.float32),
            pltpu.VMEM(mod.shape[1:], jnp.float32),
            pltpu.VMEM(io.shape[1:], jnp.float32),
            pltpu.VMEM((8,) + mod.shape[1:], jnp.float32),
            pltpu.VMEM(io.shape[1:], jnp.float32),
            pltpu.VMEM(signal.shape, jnp.float32),
            pltpu.VMEM((4,) + signal.shape, jnp.float32),
            pltpu.VMEM(signal.shape, jnp.float32),
            pltpu.VMEM((8,) + signal.shape, jnp.float32),
            pltpu.SemaphoreType.DMA((SLOTS, 2)),
            pltpu.SemaphoreType.DMA((SLOTS, 2)),
            pltpu.SemaphoreType.DMA((4, 2, SLOTS)),
            pltpu.SemaphoreType.DMA((4, 2, SLOTS)),
            pltpu.SemaphoreType.DMA((len(lefts),)),
            pltpu.SemaphoreType.DMA((2, 4, 2)),
            pltpu.SemaphoreType.DMA((layers,)),
            pltpu.SemaphoreType.DMA((layers,)),
            pltpu.SemaphoreType.DMA((10,)),
            pltpu.SemaphoreType.DMA((10,)),
            pltpu.SemaphoreType.DMA((30,)),
            pltpu.SemaphoreType.DMA((30,)),
        ],
        compiler_params=comm_params(collective_id),
        name="reduce_grads",
    )(*lefts, *rights, *smalls)
    summed = summed.reshape(3 * layers, per_group, rows, PIECE_COLS).transpose(0, 2, 1, 3)
    return list(summed.reshape(3 * layers, rows, D)), *others


def reduce_general(part):
    data_count, head_count = lax.axis_size("dp"), lax.axis_size("head")
    blocks = part.reshape(
        data_count, part.shape[0] // data_count, head_count, part.shape[1] // head_count
    ).transpose(0, 2, 1, 3)
    blocks = blocks.reshape((-1,) + blocks.shape[2:])
    return lax.psum_scatter(blocks, ("dp", "head"), scatter_dimension=0, tiled=True)[0]


KIND_AT = (1, 2, 3, 0)


def owner_of(kind, layer):
    return 4 * layer + KIND_AT.index(kind)


def is_owner_of(me, kind):
    return (me % 4 == KIND_AT.index(kind)) & (me < 8)


def to_owner_kernel(count, *refs):
    block_refs, out_ref, send_sem, recv_sem = refs[:4], refs[4], refs[5], refs[6]
    me = lax.axis_index("dp")
    out_ref[...] = jnp.zeros_like(out_ref)
    greet([{"dp": lax.rem(me + shift, count)} for shift in range(1, count)])

    def copy(kind, layer, source):
        width = block_refs[kind].shape[-1]
        return pltpu.make_async_remote_copy(
            src_ref=block_refs[kind].at[layer],
            dst_ref=out_ref.at[source, :, pl.ds(0, width)],
            send_sem=send_sem.at[2 * kind + layer],
            recv_sem=recv_sem.at[source],
            device_id={"dp": owner_of(kind, layer)},
            device_id_type=MESH,
        )

    for kind in range(4):
        for layer in range(2):

            @pl.when(me != owner_of(kind, layer))
            def _():
                copy(kind, layer, me).start()

            @pl.when(me == owner_of(kind, layer))
            def _():
                out_ref[me, :, : block_refs[kind].shape[-1]] = block_refs[kind][layer]

    for kind in range(4):

        @pl.when(is_owner_of(me, kind))
        def _():
            @pl.loop(0, count)
            def _(source):
                @pl.when(source != me)
                def _():
                    copy(kind, 0, source).wait_recv()

        for layer in range(2):

            @pl.when(me != owner_of(kind, layer))
            def _():
                copy(kind, layer, me).wait_send()


def to_owner(blocks, collective_id):
    count = lax.axis_size("dp")
    rows = blocks[0].shape[1]
    wide = max(block.shape[2] for block in blocks)
    return pl.pallas_call(
        functools.partial(to_owner_kernel, count),
        out_shape=jax.ShapeDtypeStruct((count, rows, wide), jnp.float32),
        in_specs=[vmem()] * 4,
        out_specs=vmem(),
        scratch_shapes=[pltpu.SemaphoreType.DMA((8,)), pltpu.SemaphoreType.DMA((count,))],
        compiler_params=comm_params(collective_id),
        name="to_owner",
    )(*blocks)


def from_owner_kernel(count, widths, x_ref, out_ref, send_sem, recv_sem):
    me = lax.axis_index("dp")
    greet([{"dp": lax.rem(me + shift, count)} for shift in range(1, count)])

    def copy(kind, matrix, target):
        columns = pl.ds(0, widths[kind])
        return pltpu.make_async_remote_copy(
            src_ref=x_ref.at[target, :, columns],
            dst_ref=out_ref.at[matrix, :, columns],
            send_sem=send_sem.at[target],
            recv_sem=recv_sem.at[matrix],
            device_id={"dp": target},
            device_id_type=MESH,
        )

    for kind in range(4):

        @pl.when(is_owner_of(me, kind))
        def _():
            @pl.loop(0, count)
            def _(target):
                @pl.when(target != me)
                def _():
                    copy(kind, me, target).start()

            out_ref[me] = x_ref[me]

    for kind in range(4):
        for layer in range(2):
            matrix = owner_of(kind, layer)

            @pl.when(me != matrix)
            def _():
                copy(kind, matrix, me).wait_recv()

        @pl.when(is_owner_of(me, kind))
        def _():
            @pl.loop(0, count)
            def _(target):
                @pl.when(target != me)
                def _():
                    copy(kind, me, target).wait_send()


def from_owner(x, widths, collective_id):
    count = lax.axis_size("dp")
    return pl.pallas_call(
        functools.partial(from_owner_kernel, count, widths),
        out_shape=jax.ShapeDtypeStruct((8,) + x.shape[1:], x.dtype),
        in_specs=[vmem()],
        out_specs=vmem(),
        scratch_shapes=[pltpu.SemaphoreType.DMA((count,)), pltpu.SemaphoreType.DMA((8,))],
        compiler_params=comm_params(collective_id),
        name="from_owner",
    )(x)


def gram_kernel(x_ref, out_ref, high, rest, upper, chip, got, whole, send_sem, recv_sem):
    h = lax.axis_index("head")
    c = h % 2
    greet([{"head": h ^ other} for other in (1, 2)])
    third = PIECE_COLS
    values = x_ref[...]
    high[...] = to_bf16(values)
    rest[...] = to_bf16(values - high[...].astype(jnp.float32))

    def dots(first, second):
        return (
            dot_nt(high[first], high[second])
            + dot_nt(high[first], rest[second])
            + dot_nt(rest[first], high[second])
        )

    r0, r1, r2 = (pl.ds(third * place, third) for place in range(3))

    def blocks(core):
        @pl.when(core == 0)
        def _():
            upper[0] = dots(r0, pl.ds(0, 3 * third))

        @pl.when(core == 1)
        def _():
            upper[1, :, : 2 * third] = dots(r1, pl.ds(third, 2 * third))
            upper[1, :, 2 * third :] = dots(r2, r2)

    near = send_to(upper.at[1 - c], got.at[0], (send_sem, recv_sem), 0, h ^ 1)
    blocks(1 - c)
    near.start()
    blocks(c)
    near.wait()

    def step(place, source, target, peer):
        copy = send_to(source, target, (send_sem, recv_sem), place, peer)
        copy.start()
        copy.wait()

    chip[...] = upper[c] + got[0]
    step(1, chip, got.at[1], h ^ 2)
    whole[c] = chip[...] + got[1]
    step(2, whole.at[c], whole.at[c], h ^ 1)
    out_ref[r0, :] = whole[0]
    out_ref[r1, pl.ds(third, 2 * third)] = whole[1, :, : 2 * third]
    out_ref[r2, r2] = whole[1, :, 2 * third :]
    out_ref[r1, r0] = whole[0, :, third : 2 * third].T
    out_ref[r2, r0] = whole[0, :, 2 * third :].T
    out_ref[r2, r1] = whole[1, :, third : 2 * third].T


def gram_sum(x, collective_id):
    rows, columns = x.shape
    third = PIECE_COLS
    return pl.pallas_call(
        gram_kernel,
        out_shape=jax.ShapeDtypeStruct((rows, rows), jnp.float32),
        in_specs=[vmem()],
        out_specs=vmem(),
        scratch_shapes=[
            pltpu.VMEM((rows, columns), jnp.bfloat16),
            pltpu.VMEM((rows, columns), jnp.bfloat16),
            pltpu.VMEM((2, third, rows), jnp.float32),
            pltpu.VMEM((third, rows), jnp.float32),
            pltpu.VMEM((2, third, rows), jnp.float32),
            pltpu.VMEM((2, third, rows), jnp.float32),
            pltpu.SemaphoreType.DMA((3,)),
            pltpu.SemaphoreType.DMA((3,)),
        ],
        compiler_params=comm_params(collective_id),
        name="gram_sum",
    )(x)


def send_to(source, target, sems, place, peer):
    return pltpu.make_async_remote_copy(
        src_ref=source,
        dst_ref=target,
        send_sem=sems[0].at[place],
        recv_sem=sems[1].at[place],
        device_id={"head": peer},
        device_id_type=MESH,
    )


def half_mask(half):
    lane = lax.broadcasted_iota(jnp.int32, (1, 128), 1)
    return (lane // 64) == half


def dot_nt(left, right):
    return lax.dot_general(
        left, right, (((1,), (1,)), ((), ())), preferred_element_type=jnp.float32
    )


def dot_nn(left, right):
    return lax.dot_general(
        left, right, (((1,), (0,)), ((), ())), preferred_element_type=jnp.float32
    )


def dot_tn(left, right):
    return lax.dot_general(
        left, right, (((0,), (0,)), ((), ())), preferred_element_type=jnp.float32
    )


def lanes(start, size):
    return pl.ds(pl.multiple_of(start, 128), size)


def window(head):
    return 128 * ((3 * head) // 2)


def bring_heads(h, rows_ref, pair_all, quad_all, parts, sems):
    c = h % 2
    tile = quad_all.shape[1]
    own, shared = pl.ds(0, 2 * tile), pl.ds(2 * tile, tile)
    pair, quad = [], []
    for part in range(parts):
        pair.append(
            send_to(
                rows_ref.at[own, lanes(part * D + (1 - c) * HALF, HALF)],
                pair_all.at[c, :, pl.ds(part * HALF, HALF)],
                sems, part, h ^ 1,
            )
        )
        for other in (1, 2, 3):
            quad.append(
                send_to(
                    rows_ref.at[shared, lanes(part * D + window(h ^ other), WIDE)],
                    quad_all.at[h, :, pl.ds(part * WIDE, WIDE)],
                    sems, 3 * other + part, h ^ other,
                )
            )
    for copy in pair + quad:
        copy.start()
    for part in range(parts):
        pair_all[c, :, part * HALF : (part + 1) * HALF] = rows_ref[
            own, lanes(part * D + c * HALF, HALF)
        ]
        quad_all[h, :, part * WIDE : (part + 1) * WIDE] = rows_ref[
            shared, lanes(part * D + window(h), WIDE)
        ]
    return pair, quad


def return_pair(h, pair_out, rows_ref, parts, sems):
    c = h % 2
    own = pl.ds(0, pair_out.shape[1])
    copies = []
    for part in range(parts):
        columns = lanes(part * D + c * HALF, HALF)
        copies.append(
            send_to(
                pair_out.at[1 - c, :, pl.ds(part * HALF, HALF)], rows_ref.at[own, columns],
                sems, 12 + part, h ^ 1,
            )
        )
        copies[-1].start()
        rows_ref[own, columns] = pair_out[c, :, part * HALF : (part + 1) * HALF]
    return copies


def return_quad(h, quad_out, quad_got, sems):
    copies = []
    for other in (1, 2, 3):
        copies.append(
            send_to(quad_out.at[h ^ other], quad_got.at[h], sems, 14 + other, h ^ other)
        )
        copies[-1].start()
    quad_got[h] = quad_out[h]
    return copies


def merge_quad(quad_got, rows_ref, parts):
    tile = quad_got.shape[1]
    shared = slice(2 * tile, 3 * tile)
    for part in range(parts):
        base, start = part * WIDE, part * D
        for side in range(2):
            left, right = quad_got.at[2 * side], quad_got.at[2 * side + 1]
            at = start + side * HALF
            rows_ref[shared, at : at + 128] = left[:, base : base + 128]
            rows_ref[shared, at + 128 : at + 256] = (
                left[:, base + 128 : base + 256] + right[:, base : base + 128]
            )
            rows_ref[shared, at + 256 : at + 384] = right[:, base + 128 : base + 256]


def row_half(half):
    row = lax.broadcasted_iota(jnp.int32, (128, 1), 0)
    return (row // 64) == half


CHUNKS = ((0, 384), (384, 832))


def probabilities(scores):
    top = jnp.max(scores, 0, keepdims=True)
    exponent = jnp.exp(scores - top)
    total = jnp.sum(exponent, 0, keepdims=True)
    return exponent * (1.0 / total), top + jnp.log(total)


def attend_kernel(rows_ref, mixed_ref, pair_all, quad_all, log_ref, pair_out, quad_out, quad_got,
                  joined, send_sem, recv_sem):
    h = lax.axis_index("head")
    sems = (send_sem, recv_sem)
    greet([{"head": h ^ other} for other in (1, 2, 3)])
    pair_copies, quad_copies = bring_heads(h, rows_ref, pair_all, quad_all, 3, sems)
    tile = quad_all.shape[1]
    length = 4 * tile

    def heads(query, keys, values, members):
        values_t = values.T
        for start, stop in CHUNKS:
            mixed = jnp.zeros((128, stop - start), jnp.float32)
            for half, log_row in members:
                chunk = jnp.where(half_mask(half), query[start:stop], 0) * 0.125
                probability, logs = probabilities(dot_nt(keys, chunk))
                mixed = mixed + dot_nn(
                    jnp.where(row_half(half), values_t, 0), to_bf16(probability)
                )
                log_ref[log_row : log_row + 1, start:stop] = logs
            joined[start:stop, :] = to_bf16(mixed.T)

    log_ref[...] = jnp.zeros_like(log_ref)
    quad_out[...] = jnp.zeros_like(quad_out)
    def pair_heads(pair):
        query, keys, values = (
            pair_all[:, :, part * HALF + pair * 128 : part * HALF + pair * 128 + 128].reshape(
                length, 128
            )
            for part in range(3)
        )
        heads(query, keys, values, ((0, 2 * pair), (1, 2 * pair + 1)))
        pair_out[:, :, pair * 128 : pair * 128 + 128] = joined[...].reshape(2, 2 * tile, 128)

    for copy in pair_copies:
        copy.wait()
    pair_heads(0)
    pair_heads(1)
    for copy in quad_copies:
        copy.wait()
    for member in range(3):
        place = h % 2 + member
        at = (place // 2) * 128
        query, keys, values = (
            quad_all[:, :, lanes(part * WIDE + at, 128)].reshape(length, 128) for part in range(3)
        )
        heads(query, keys, values, ((place % 2, 6 + member),))
        quad_out[:, :, lanes(at, 128)] += joined[...].reshape(4, tile, 128)
    back_quad = return_quad(h, quad_out, quad_got, sems)
    pair_heads(2)
    back = return_pair(h, pair_out, mixed_ref, 1, sems)
    for copy in back + back_quad:
        copy.wait()
    merge_quad(quad_got, mixed_ref, 1)


def attend(rows, collective_id):
    frames = rows.shape[0]
    tile = frames // 3
    low = jnp.bfloat16
    return pl.pallas_call(
        attend_kernel,
        out_shape=[
            jax.ShapeDtypeStruct((frames, D), low),
            jax.ShapeDtypeStruct((2, 2 * tile, 3 * HALF), low),
            jax.ShapeDtypeStruct((4, tile, 3 * WIDE), low),
            jax.ShapeDtypeStruct((16, 4 * tile), jnp.float32),
        ],
        in_specs=[vmem()],
        out_specs=[vmem()] * 4,
        scratch_shapes=[
            pltpu.VMEM((2, 2 * tile, HALF), low),
            pltpu.VMEM((4, tile, WIDE), low),
            pltpu.VMEM((4, tile, WIDE), low),
            pltpu.VMEM((4 * tile, 128), low),
            pltpu.SemaphoreType.DMA((18,)),
            pltpu.SemaphoreType.DMA((18,)),
        ],
        compiler_params=comm_params(collective_id),
        name="attend",
    )(rows)


def attend_back_kernel(pair_all, quad_all, log_ref, grad_ref, rows_ref, pair_mixed, quad_mixed,
                       pair_out, quad_out, quad_got, grad_keys, grad_values, grads, send_sem,
                       recv_sem):
    h = lax.axis_index("head")
    sems = (send_sem, recv_sem)
    greet([{"head": h ^ other} for other in (1, 2, 3)])
    pair_copies, quad_copies = bring_heads(h, grad_ref, pair_mixed, quad_mixed, 1, sems)
    tile = quad_all.shape[1]
    length = 4 * tile

    def heads(query, keys, values, grad_out, members):
        keys_t = keys.T
        grad_keys[...] = jnp.zeros_like(grad_keys)
        grad_values[...] = jnp.zeros_like(grad_values)
        for start, stop in CHUNKS:
            grad_query = jnp.zeros((128, stop - start), jnp.float32)
            for half, log_row in members:
                mask = half_mask(half)
                chunk = jnp.where(mask, query[start:stop], 0) * 0.125
                grad_chunk = jnp.where(mask, grad_out[start:stop], 0)
                probability = jnp.exp(
                    dot_nt(keys, chunk) - log_ref[log_row : log_row + 1, start:stop]
                )
                grad_prob = dot_nt(values, grad_chunk)
                mean = jnp.sum(probability * grad_prob, 0, keepdims=True)
                grad_scores = to_bf16(probability * (grad_prob - mean))
                grad_keys[...] += dot_nn(grad_scores, chunk)
                grad_values[...] += dot_nn(to_bf16(probability), grad_chunk)
                grad_query = grad_query + dot_nn(
                    jnp.where(row_half(half), keys_t, 0), grad_scores
                )
            grads[0, start:stop, :] = to_bf16(grad_query.T * 0.125)
        grads[1] = to_bf16(grad_keys[...])
        grads[2] = to_bf16(grad_values[...])

    quad_out[...] = jnp.zeros_like(quad_out)
    def pair_heads(pair):
        at = [part * HALF + pair * 128 for part in range(3)]
        query, keys, values = (
            pair_all[:, :, start : start + 128].reshape(length, 128) for start in at
        )
        grad_out = pair_mixed[:, :, at[0] : at[0] + 128].reshape(length, 128)
        heads(query, keys, values, grad_out, ((0, 2 * pair), (1, 2 * pair + 1)))
        for part in range(3):
            pair_out[:, :, at[part] : at[part] + 128] = grads[part].reshape(2, 2 * tile, 128)

    for copy in pair_copies:
        copy.wait()
    pair_heads(0)
    for copy in quad_copies:
        copy.wait()
    for member in range(3):
        place = h % 2 + member
        at = (place // 2) * 128
        query, keys, values = (
            quad_all[:, :, lanes(part * WIDE + at, 128)].reshape(length, 128) for part in range(3)
        )
        grad_out = quad_mixed[:, :, lanes(at, 128)].reshape(length, 128)
        heads(query, keys, values, grad_out, ((place % 2, 6 + member),))
        for part in range(3):
            quad_out[:, :, lanes(part * WIDE + at, 128)] += grads[part].reshape(4, tile, 128)
    back_quad = return_quad(h, quad_out, quad_got, sems)
    pair_heads(1)
    pair_heads(2)
    back = return_pair(h, pair_out, rows_ref, 3, sems)
    for copy in back + back_quad:
        copy.wait()
    merge_quad(quad_got, rows_ref, 3)


def attend_back(pair_all, quad_all, logs, grad_mixed, collective_id):
    rows, tile = pair_all.shape[1], quad_all.shape[1]
    low = jnp.bfloat16
    return pl.pallas_call(
        attend_back_kernel,
        out_shape=jax.ShapeDtypeStruct((3 * tile, 3 * D), low),
        in_specs=[vmem()] * 4,
        out_specs=vmem(),
        scratch_shapes=[
            pltpu.VMEM((2, rows, HALF), low),
            pltpu.VMEM((4, tile, WIDE), low),
            pltpu.VMEM(pair_all.shape, low),
            pltpu.VMEM(quad_all.shape, low),
            pltpu.VMEM(quad_all.shape, low),
            pltpu.VMEM((4 * tile, 128), jnp.float32),
            pltpu.VMEM((4 * tile, 128), jnp.float32),
            pltpu.VMEM((3, 4 * tile, 128), low),
            pltpu.SemaphoreType.DMA((18,)),
            pltpu.SemaphoreType.DMA((18,)),
        ],
        compiler_params=comm_params(collective_id),
        name="attend_back",
    )(pair_all, quad_all, logs, grad_mixed)


def cross_frames(clip, tile):
    return slice(2 * clip, 2 + clip), (2 - clip) * tile


def masked_scores(keys, query_half, length):
    token = lax.broadcasted_iota(jnp.int32, (keys.shape[0], 1), 0)
    return jnp.where(token < length, dot_nt(keys, query_half), -1e30)


def cross_kernel(query_ref, keys_ref, values_ref, len_ref, out_ref):
    tile = query_ref.shape[1]
    for clip in range(2):
        tiles, count = cross_frames(clip, tile)
        query = query_ref[tiles].reshape(count, 128)
        values_t = values_ref[clip].T
        mixed = jnp.zeros((128, count), jnp.float32)
        for half in range(2):
            chunk = jnp.where(half_mask(half), query, 0) * 0.125
            probability, _ = probabilities(masked_scores(keys_ref[clip], chunk, len_ref[clip]))
            mixed = mixed + dot_nn(jnp.where(row_half(half), values_t, 0), to_bf16(probability))
        out_ref[tiles] = to_bf16(mixed.T).reshape(2 - clip, tile, 128)


def cross(query, pair_kv, lengths):
    _, tile, width = query.shape
    blocks = width // 128
    tokens = pair_kv.shape[1]
    return pl.pallas_call(
        cross_kernel,
        grid=(blocks,),
        out_shape=jax.ShapeDtypeStruct(query.shape, jnp.bfloat16),
        in_specs=[
            pl.BlockSpec((3, tile, 128), lambda i: (0, 0, i)),
            pl.BlockSpec((2, tokens, 128), lambda i: (0, 0, i)),
            pl.BlockSpec((2, tokens, 128), lambda i: (0, 0, blocks + i)),
            pl.BlockSpec(memory_space=pltpu.SMEM),
        ],
        out_specs=pl.BlockSpec((3, tile, 128), lambda i: (0, 0, i)),
        compiler_params=pltpu.CompilerParams(vmem_limit_bytes=VMEM_BYTES),
        name="cross",
    )(query, pair_kv, pair_kv, lengths)


def cross_back_kernel(query_ref, keys_ref, values_ref, grad_ref, len_ref, grad_query_ref,
                      grad_keys_ref, grad_values_ref):
    tile = query_ref.shape[1]
    tokens = keys_ref.shape[1]
    for clip in range(2):
        tiles, count = cross_frames(clip, tile)
        keys, values = keys_ref[clip], values_ref[clip]
        query = query_ref[tiles].reshape(count, 128)
        grad = grad_ref[tiles].reshape(count, 128)
        keys_t = keys.T
        grad_keys = jnp.zeros((tokens, 128), jnp.float32)
        grad_values = jnp.zeros((tokens, 128), jnp.float32)
        grad_query = jnp.zeros((128, count), jnp.float32)
        for half in range(2):
            mask = half_mask(half)
            chunk = jnp.where(mask, query, 0) * 0.125
            grad_half = jnp.where(mask, grad, 0)
            probability, _ = probabilities(masked_scores(keys, chunk, len_ref[clip]))
            grad_prob = dot_nt(values, grad_half)
            mean = jnp.sum(probability * grad_prob, 0, keepdims=True)
            grad_scores = to_bf16(probability * (grad_prob - mean))
            grad_keys = grad_keys + dot_nn(grad_scores, chunk)
            grad_values = grad_values + dot_nn(to_bf16(probability), grad_half)
            grad_query = grad_query + dot_nn(jnp.where(row_half(half), keys_t, 0), grad_scores)
        grad_query_ref[tiles] = to_bf16(grad_query.T * 0.125).reshape(2 - clip, tile, 128)
        grad_keys_ref[clip] = to_bf16(grad_keys)
        grad_values_ref[clip] = to_bf16(grad_values)


def cross_back(query, pair_kv, lengths, grad):
    _, tile, width = query.shape
    blocks = width // 128
    tokens = pair_kv.shape[1]
    rows_spec = pl.BlockSpec((3, tile, 128), lambda i: (0, 0, i))
    keys_spec = pl.BlockSpec((2, tokens, 128), lambda i: (0, 0, i))
    return pl.pallas_call(
        cross_back_kernel,
        grid=(blocks,),
        out_shape=[
            jax.ShapeDtypeStruct(query.shape, jnp.bfloat16),
            jax.ShapeDtypeStruct((2, tokens, width), jnp.bfloat16),
            jax.ShapeDtypeStruct((2, tokens, width), jnp.bfloat16),
        ],
        in_specs=[
            rows_spec,
            keys_spec,
            pl.BlockSpec((2, tokens, 128), lambda i: (0, 0, blocks + i)),
            rows_spec,
            pl.BlockSpec(memory_space=pltpu.SMEM),
        ],
        out_specs=[rows_spec, keys_spec, keys_spec],
        compiler_params=pltpu.CompilerParams(vmem_limit_bytes=VMEM_BYTES),
        name="cross_back",
    )(query, pair_kv, pair_kv, grad, lengths)


def body(
    clean_latents,
    noise_draw,
    timesteps,
    captions,
    cap_len,
    pairing,
    adam_step,
    qkv_weight,
    out_weight,
    up_weight,
    down_weight,
    ada_weight,
    time_weight,
    io_weight,
    qkv_moment,
    out_moment,
    up_moment,
    down_moment,
    ada_first,
    ada_second,
    time_first,
    time_second,
    io_first,
    io_second,
):
    data_count = lax.axis_size("dp")
    head_count = lax.axis_size("head")
    clip_count, tile, channels = clean_latents.shape
    length = tile * head_count
    rows_own = qkv_weight.shape[1]
    d, h = lax.axis_index("dp"), lax.axis_index("head")
    own_clip, core = h // 2, h % 2
    own_row = d * rows_own
    linked = data_count == 8 and rows_own == 96
    ids = iter(range(64))

    def swap(x, axis):
        return exchange(x, axis, True, next(ids))

    def spread(x, axis):
        return exchange(x, axis, False, next(ids))

    def by_tile(values):
        own = lax.dynamic_slice_in_dim(values, own_clip, 1, 0)
        return jnp.concatenate([own, own, values[2:3]])

    def by_clip(tiles):
        own = tiles[0:1] + tiles[1:2]
        none = jnp.zeros_like(own)
        return jnp.concatenate(
            [jnp.where(own_clip == 0, own, none), jnp.where(own_clip == 1, own, none), tiles[2:3]]
        )

    block = 3 * D // head_count
    share = D // head_count
    is_first = core == 0
    latents = jnp.concatenate([clean_latents, noise_draw], -1).transpose(0, 2, 1)
    latents = latents.reshape(-1, tile)

    def with_edge(qkv, out, edge):
        return jnp.where(
            is_first,
            jnp.concatenate([qkv, edge, out[..., :128]], -1),
            jnp.concatenate([qkv[..., 64:], edge, out], -1),
        )

    def without_edge(own, edge):
        qkv = jnp.where(
            is_first, own[..., :block], jnp.concatenate([edge, own[..., : block - 64]], -1)
        )
        out = jnp.where(
            is_first, jnp.concatenate([own[..., block + 64 :], edge], -1), own[..., block:]
        )
        return qkv, out

    keep_mask = jnp.arange(CAP)[None, :] < cap_len[:, None]
    cap_mean = product("ft,ftd->fd", keep_mask.astype(jnp.bfloat16), captions) / cap_len[
        :, None
    ].astype(jnp.float32)
    cap_unit = cap_mean * lax.rsqrt(jnp.mean(cap_mean * cap_mean, -1, keepdims=True) + 1e-06)
    own_captions = jnp.concatenate([lax.dynamic_slice_in_dim(captions, own_clip, 1, 0), captions[2:3]])
    own_lengths = jnp.concatenate([lax.dynamic_slice_in_dim(cap_len, own_clip, 1, 0), cap_len[2:3]])

    qkv_low, out_low = to_bf16(qkv_weight), to_bf16(out_weight)
    edge = jnp.where(is_first, out_low[..., 128:], qkv_low[..., :64])
    time_cols = time_weight.shape[1]
    io_cols = io_weight.shape[2]
    ada_cols = ada_weight.shape[2]
    ada_bf = to_bf16(ada_weight)
    io_flat = io_weight.transpose(1, 0, 2).reshape(rows_own, 2 * io_cols)
    small_own = jnp.pad(
        to_bf16(jnp.concatenate([time_weight, io_flat], 1)),
        ((0, 0), (0, WIDE - time_cols - 2 * io_cols)),
    )
    table_bf = to_bf16(time_table(timesteps, D))

    def listed(first_groups):
        listed_groups = [small_own]
        for layer in range(2):
            listed_groups.append(first_groups[layer])
            listed_groups.append(to_bf16(up_weight[layer]))
            listed_groups.append(to_bf16(down_weight[layer]))
        return listed_groups

    if linked:
        none = jnp.zeros_like(edge)
        edge = jnp.where(
            is_first, jnp.concatenate([edge, none], -1), jnp.concatenate([none, edge], -1)
        )
        shared = jnp.concatenate(
            [
                jnp.zeros((clip_count, D)),
                cap_unit,
                jnp.pad(timesteps[None], ((0, 7 - 2 * clip_count), (0, D - clip_count))),
            ]
        )
        shared = jnp.pad(shared, ((0, 8 - shared.shape[0]), (0, head_count * WIDE - D)))
        gathered, latents_all, shared_all, mods = gather_whole(
            listed(with_edge(qkv_low, out_low, none)),
            (1, 4),
            edge,
            latents,
            shared,
            jnp.pad(table_bf, ((0, 8 - clip_count), (0, 0))),
            ada_bf,
            next(ids),
        )
        start = (d // 2) * WIDE + (d % 2) * rows_own
        hidden_own = lax.dynamic_slice(
            shared_all, (0, 0, start), (data_count, clip_count, rows_own)
        ).reshape(-1, rows_own)
        times_all = shared_all[:, 2 * clip_count, :clip_count].reshape(-1)
        table_own = to_bf16(time_table(times_all, D)).astype(jnp.float32)
        table_own = lax.dynamic_slice_in_dim(table_own, own_row, rows_own, 1)
        cap_all = shared_all[:, clip_count : 2 * clip_count, :D].reshape(-1, D)
        signal_own = to_bf16(double_silu(hidden_own))
        mods = mods[:, : 2 * clip_count].reshape(head_count, 2, clip_count, ada_cols)
        mods = mods.transpose(0, 2, 1, 3)
    else:
        edge = lax.ppermute(edge, "head", [(place, place ^ 1) for place in range(head_count)])
        gathered = [gather_general(own) for own in listed(with_edge(qkv_low, out_low, edge))]
        latents_all = spread(latents, "head")
        time_full = gathered[0].reshape(D, head_count, WIDE)[:, :, :time_cols].reshape(D, D)
        time_hidden = jnp.dot(table_bf, time_full, preferred_element_type=jnp.float32)
        shared = jnp.concatenate([time_hidden, table_bf.astype(jnp.float32), cap_unit], 1)
        shared_all = spread(shared, "dp").reshape(-1, 3 * D)
        hidden_own = lax.dynamic_slice_in_dim(shared_all, own_row, rows_own, 1)
        table_own = lax.dynamic_slice_in_dim(shared_all, D + own_row, rows_own, 1)
        cap_all = shared_all[:, 2 * D :]
        signal_own = to_bf16(double_silu(hidden_own))
        mod_part = product("fd,ldn->fln", signal_own, ada_bf)
        mod_part = mod_part.reshape(data_count, clip_count, 2 * ada_cols)
        mods = spread(jnp.sum(swap(mod_part, "dp"), 0), "head")
    up_full = [gathered[2], gathered[5]]
    down_full = [gathered[3], gathered[6]]
    io_full = (
        gathered[0]
        .reshape(D, head_count, WIDE)[:, :, time_cols : time_cols + 2 * io_cols]
        .reshape(D, head_count, 2, io_cols)
        .transpose(2, 0, 1, 3)
        .reshape(2, D, channels)
    )
    mod_all = (
        mods.reshape(head_count, clip_count, 2, ada_cols)
        .transpose(1, 2, 0, 3)
        .reshape(clip_count, 2, 6 * D)
    )
    tile_mods = by_tile(mod_all)

    def split_first(whole):
        qkv, out = [], []
        for side in range(2):
            at = 2 * side * D
            qkv += [whole[:, at : at + 640], whole[:, at + D : at + D + 512]]
            out += [whole[:, at + 640 : at + D], whole[:, at + D + 512 : at + 2 * D]]
        return jnp.concatenate(qkv, 1), jnp.concatenate(out, 1)

    def join_first(qkv, out):
        columns = []
        for side in range(2):
            q, o = side * 2 * block, side * 2 * share
            columns += [qkv[:, q : q + 640], out[:, o : o + 128]]
            columns += [qkv[:, q + 640 : q + 1152], out[:, o + 128 : o + 384]]
        return jnp.concatenate(columns, 1)

    if linked:
        qkv_full = [gathered[1 + 3 * layer][:, : 3 * D] for layer in range(2)]
        out_full = [gathered[1 + 3 * layer][:, 3 * D :] for layer in range(2)]
    else:
        qkv_full, out_full = zip(*[split_first(gathered[1 + 3 * layer]) for layer in range(2)])

    latents_all = latents_all.reshape(head_count, clip_count, 2 * channels, tile)
    own_latents = lax.dynamic_slice(
        latents_all, (2 * core, own_clip, 0, 0), (2, 1, 2 * channels, tile)
    )[:, 0]
    latents = jnp.concatenate(
        [own_latents, lax.dynamic_slice_in_dim(latents_all, h, 1, 0)[0, 2:3]]
    )
    clean_rows, noise_rows = latents[:, :channels], latents[:, channels:]
    tile_times = by_tile(timesteps)[:, None, None]
    input_bf = to_bf16((1.0 - tile_times) * clean_rows + tile_times * noise_rows)
    target = noise_rows - clean_rows
    hidden = product("fcl,dc->fld", input_bf, io_full[0])

    frames = clip_count * tile

    def layer_forward(layer_index, hidden):
        modulation = tile_mods[:, layer_index].reshape(clip_count, 1, 6, D)
        mod_parts = [modulation[:, :, member] for member in range(6)]
        normed = to_bf16(modulate(hidden, mod_parts[0], mod_parts[1]))
        weight = qkv_full[layer_index]
        if layer_index == 0:
            projected = to_bf16(product("fld,dn->fln", normed, weight))
            mixed, *attended = attend(projected.reshape(frames, 3 * D), next(ids))
            mixed = mixed.reshape(clip_count, tile, D)
        else:
            query = to_bf16(product("fld,dn->fln", normed, weight[:, :D]))
            pair_kv = to_bf16(product("ftd,dn->ftn", own_captions, weight[:, D:]))
            attended = (query, pair_kv)
            mixed = cross(query, pair_kv, own_lengths)
        branch = product("fle,de->fld", mixed, out_full[layer_index])
        middle = hidden + mod_parts[2] * branch
        normed2 = to_bf16(modulate(middle, mod_parts[3], mod_parts[4]))
        upper = product("fld,dn->fln", normed2, up_full[layer_index])
        active = to_bf16(soft_gelu(upper))
        down_out = product("fln,dn->fld", active, down_full[layer_index])
        kept = (hidden, mod_parts, normed, attended, mixed, branch, middle, normed2, upper,
                active, down_out)
        return (middle + mod_parts[5] * down_out, kept)

    saved_layers = []
    for layer_index in range(2):
        hidden, kept = layer_forward(layer_index, hidden)
        saved_layers.append(kept)
    final = norm_rows(hidden)
    final_bf = to_bf16(final)
    predicted = product("fld,dc->fcl", final_bf, io_full[1])
    errors = predicted - target
    flow_part = jnp.sum(jnp.mean(errors * errors, 1))
    grad_pred = to_bf16(2.0 * errors / channels)
    pool_sum = jnp.sum(spread(by_clip(jnp.sum(final, 1)), "head"), 0)
    pooled_out = pool_sum / length

    def contrast_of(pool_total):
        pooled = pool_total / length
        unit_rows = pooled * lax.rsqrt(jnp.mean(pooled * pooled, -1, keepdims=True) + 1e-06)
        logits = exact_product("id,jd->ij", unit_rows, cap_all) * (2.0 / math.sqrt(D))
        row_top = jnp.max(logits, -1, keepdims=True)
        log_total = row_top[:, 0] + jnp.log(jnp.sum(jnp.exp(logits - row_top), -1))
        picked = jnp.sum(
            jnp.where(jnp.arange(logits.shape[1])[None, :] == pairing[:, None], logits, 0.0), -1
        )
        return length * jnp.sum(log_total - picked)

    contrast_value, contrast_back = jax.vjp(contrast_of, pool_sum)
    grad_pool = by_tile(contrast_back(jnp.ones_like(contrast_value))[0])
    loss_part = flow_part + contrast_value / head_count
    grad_final = product("fcl,dc->fld", grad_pred, io_full[1]) + grad_pool[:, None, :]
    final_value, final_back = jax.vjp(norm_rows, hidden)
    grad_hidden = final_back(grad_final)[0]
    fin_grad = product("fcl,fld->dc", grad_pred, final_bf)
    plan, lefts, rights = [], [], []

    def listed_factors(factors, factor):
        factors.append(factor.reshape(-1, factor.shape[-1]))
        return len(factors) - 1

    mod_grads = [None, None]
    for layer_index in (1, 0):
        (
            layer_hidden,
            mod_parts,
            layer_normed,
            attended,
            layer_mixed,
            layer_branch,
            layer_middle,
            layer_normed2,
            layer_upper,
            layer_active,
            layer_down_out,
        ) = saved_layers[layer_index]
        weight = qkv_full[layer_index]
        d_gate2 = jnp.sum(layer_down_out * grad_hidden, axis=1, keepdims=True)
        grad_down = to_bf16(mod_parts[5] * grad_hidden)
        grad_active = product("fld,dn->fln", grad_down, down_full[layer_index])
        grad_upper = to_bf16(grad_active * soft_gelu_slope(layer_upper))
        grad_normed2 = product("fln,dn->fld", grad_upper, up_full[layer_index])
        mod_value, mod_back = jax.vjp(modulate, layer_middle, mod_parts[3], mod_parts[4])
        grad_middle, d_shift2, d_scale2 = mod_back(grad_normed2)
        grad_middle = grad_middle + grad_hidden
        d_gate1 = jnp.sum(layer_branch * grad_middle, axis=1, keepdims=True)
        grad_branch = to_bf16(mod_parts[2] * grad_middle)
        grad_mixed = to_bf16(product("fld,de->fle", grad_branch, out_full[layer_index]))
        branch_place, branch_right = listed_factors(lefts, grad_branch), listed_factors(rights, layer_mixed)
        normed_place = listed_factors(lefts, layer_normed)
        if layer_index == 0:
            grad_proj = attend_back(*attended, grad_mixed.reshape(frames, D), next(ids))
            grad_normed = product("fn,dn->fd", grad_proj, weight)
            first = [(normed_place, listed_factors(rights, grad_proj), 0, 3 * D)]
        else:
            query, pair_kv = attended
            grad_query, grad_keys, grad_values = cross_back(query, pair_kv, own_lengths, grad_mixed)
            grad_normed = product("fln,dn->fld", grad_query, weight[:, :D])
            caption_place = listed_factors(lefts, own_captions)
            first = [
                (normed_place, listed_factors(rights, grad_query), 0, D),
                (caption_place, listed_factors(rights, grad_keys), D, 2 * D),
                (caption_place, listed_factors(rights, grad_values), 2 * D, 3 * D),
            ]
        first.append((branch_place, branch_right, 3 * D, 4 * D))
        plan.append(
            (
                tuple(first),
                (listed_factors(lefts, layer_normed2), listed_factors(rights, grad_upper)),
                (listed_factors(lefts, grad_down), listed_factors(rights, layer_active)),
            )
        )
        first_value, first_back = jax.vjp(modulate, layer_hidden, mod_parts[0], mod_parts[1])
        grad_in, d_shift1, d_scale1 = first_back(grad_normed.reshape(clip_count, tile, D))
        mod_grads[layer_index] = jnp.concatenate(
            [d_shift1, d_scale1, d_gate1, d_shift2, d_scale2, d_gate2], -1
        )[:, 0]
        grad_hidden = grad_in + grad_middle
    in_grad = product("fld,fcl->dc", to_bf16(grad_hidden), input_bf)

    mod_size = clip_count * 2 * ada_cols
    io_size = rows_own * 2 * io_cols
    mod_grad = by_clip(jnp.stack(mod_grads, 1)).reshape(clip_count, 2, head_count, ada_cols)
    mod_grad = mod_grad.transpose(2, 0, 1, 3).reshape(head_count, clip_count, 2 * ada_cols)
    io_part = (
        jnp.stack([in_grad, fin_grad])
        .reshape(2, data_count, rows_own, head_count, io_cols)
        .transpose(3, 1, 0, 2, 4)
        .reshape(head_count, data_count, io_size)
    )
    signal_own_value, signal_back = jax.vjp(double_silu, hidden_own)
    if linked:

        def padded_clips(values):
            values = values.reshape(data_count, clip_count, rows_own)
            values = jnp.pad(values, ((0, 0), (0, 8 - clip_count), (0, 0)))
            return values.reshape(-1, rows_own)

        io_lines = -(-io_size // 1024) * 8
        io_part = jnp.pad(io_part, ((0, 0), (0, 0), (0, io_lines * 128 - io_size)))
        smalls = (
            jnp.pad(loss_part.reshape(1, 1), ((0, 7), (1, 126))),
            jnp.pad(mod_grad, ((0, 0), (0, 8 - clip_count), (0, 0))),
            io_part.reshape(head_count, data_count, io_lines, 128),
            padded_clips(signal_own.astype(jnp.float32)),
            padded_clips(signal_back(jnp.ones_like(hidden_own))[0]),
            padded_clips(table_own),
            ada_bf,
        )
        owned, totals, edge, ada_grad, time_grad, io_grad = reduce_whole(
            tuple(plan), lefts, rights, smalls, next(ids)
        )
        totals = totals[0, :2]
        edge = edge[::-1]
        edge = jnp.where(is_first, edge[..., :64], edge[..., 64:])
        time_grad = jnp.concatenate([time_grad[0], time_grad[1]], 1)
        io_grad = io_grad.reshape(-1)[:io_size].reshape(2, rows_own, io_cols)
    else:
        io_grad = lax.psum(io_part, ("dp", "head"))
        io_grad = lax.dynamic_slice(io_grad, (h, d, 0), (1, 1, io_size))
        io_grad = io_grad.reshape(2, rows_own, io_cols)
        mod_grad = jnp.sum(swap(mod_grad, "head"), 0)
        mod_grad = spread(mod_grad, "dp").reshape(-1, 2, ada_cols)
        ada_grad = exact_product("fd,fln->ldn", signal_own.astype(jnp.float32), mod_grad)
        grad_signal = exact_product("fln,ldn->fd", mod_grad, ada_bf.astype(jnp.float32))
        grad_signal = jnp.sum(spread(grad_signal, "head"), 0)
        grad_cond = spread(signal_back(grad_signal)[0], "dp").transpose(1, 0, 2).reshape(-1, D)
        time_grad = exact_product(
            "fd,fn->dn",
            table_own,
            lax.dynamic_slice_in_dim(grad_cond, h * time_cols, time_cols, 1),
        )

        def made(left_place, right_place):
            return product("fd,fn->dn", lefts[left_place], rights[right_place])

        owned = []
        for first, *pairs in plan:
            columns = jnp.concatenate([made(*source[:2]) for source in first], 1)
            owned += [made(*pair) for pair in pairs]
            owned.append(join_first(columns[:, : 3 * D], columns[:, 3 * D :]))
        owned = [reduce_general(part) for part in owned]
        square = sum((jnp.sum(part * part) for part in owned + [ada_grad, time_grad, io_grad]))
        totals = lax.psum(jnp.stack([square, loss_part]), ("dp", "head"))
        edge = jnp.stack([owned[5], owned[2]])
        edge = jnp.where(is_first, edge[..., block : block + 64], edge[..., block - 64 : block])
        edge = spread(edge.reshape(-1, 128), "head")
        edge = lax.dynamic_slice_in_dim(edge, h ^ 1, 1, 0).reshape(2, rows_own, 64)
    first_own = jnp.stack([owned[5], owned[2]])
    total_square, total_loss = totals[0], totals[1]
    qkv_shard, out_shard = without_edge(first_own, edge)
    shards = (
        qkv_shard,
        out_shard,
        jnp.stack([owned[3], owned[0]]),
        jnp.stack([owned[4], owned[1]]),
        ada_grad,
        time_grad[None],
        io_grad,
    )
    old_moments = (qkv_moment, out_moment, up_moment, down_moment)
    grad_norm = jnp.sqrt(total_square)
    clip_scale = jnp.minimum(1.0, CLIP_NORM / (grad_norm + 1e-06))
    moments = tuple(
        (MUON_BETA * old_moments[member] + clip_scale * shards[member] for member in range(4))
    )
    coeff_a, coeff_b, coeff_c = NEWTON_COEFFS
    widths = [-(-moment.shape[2] // 128) * 128 for moment in moments]
    padded = [
        jnp.pad(moment, ((0, 0), (0, 0), (0, width - moment.shape[2])))
        for moment, width in zip(moments, widths)
    ]
    own_matrix = to_owner(padded, next(ids)).reshape(D, -1)

    def near_product(form, left, right):
        return jnp.einsum(form, left, right, precision=lax.Precision.HIGH)

    gram = gram_sum(own_matrix, next(ids))
    unit = jnp.eye(D, dtype=jnp.float32)
    size_frob = jnp.sqrt(jnp.sum(gram * unit)) + 1e-07
    gram = gram / (size_frob * size_frob)
    factor = None
    for ns_step in range(NS_STEPS):
        poly = coeff_a * unit + coeff_b * gram + coeff_c * near_product("rk,kj->rj", gram, gram)
        factor = poly if factor is None else near_product("rk,kj->rj", poly, factor)
        if ns_step < NS_STEPS - 1:
            gram = near_product("rk,kj->rj", near_product("rk,kj->rj", poly, gram), poly)
    ortho_matrix = near_product("rk,kc->rc", factor, own_matrix) / size_frob
    ortho_back = to_bf16(ortho_matrix).reshape(data_count, rows_own, -1)
    ortho_back = from_owner(ortho_back, tuple(widths), next(ids)).astype(jnp.float32)
    ortho_rows = tuple(
        (
            jnp.stack(
                [
                    ortho_back[owner_of(member, layer), :, : moments[member].shape[2]]
                    for layer in range(2)
                ]
            )
            for member in range(4)
        )
    )
    muon_weights = (qkv_weight, out_weight, up_weight, down_weight)
    muon_new = tuple(
        (
            muon_weights[member] * (1.0 - MUON_RATE * MUON_DECAY)
            - MUON_RATE
            * 0.2
            * math.sqrt(max(D, muon_weights[member].shape[2] * head_count))
            * ortho_rows[member]
            for member in range(4)
        )
    )
    step_count = adam_step[0].astype(jnp.float32)
    ada_new, ada_first_new, ada_second_new = adam_update(
        ada_weight, clip_scale * shards[4], ada_first, ada_second, step_count
    )
    time_new, time_first_new, time_second_new = adam_update(
        time_weight, clip_scale * shards[5][0], time_first, time_second, step_count
    )
    io_new, io_first_new, io_second_new = adam_update(
        io_weight, clip_scale * shards[6], io_first, io_second, step_count
    )
    return (
        total_loss,
        grad_norm,
        pooled_out,
        muon_new[0],
        moments[0],
        muon_new[1],
        moments[1],
        muon_new[2],
        moments[2],
        muon_new[3],
        moments[3],
        ada_new,
        ada_first_new,
        ada_second_new,
        time_new,
        time_first_new,
        time_second_new,
        io_new,
        io_first_new,
        io_second_new,
    )


def solution(mesh):
    placed = (
        P("dp", "head", None),
        P("dp", "head", None),
        P("dp"),
        P("dp", None, None),
        P("dp"),
        P("dp"),
        P(),
        P(None, "dp", "head"),
        P(None, "dp", "head"),
        P(None, "dp", "head"),
        P(None, "dp", "head"),
        P(None, "dp", "head"),
        P("dp", "head"),
        P(None, "dp", "head"),
        P(None, "dp", "head"),
        P(None, "dp", "head"),
        P(None, "dp", "head"),
        P(None, "dp", "head"),
        P(None, "dp", "head"),
        P(None, "dp", "head"),
        P("dp", "head"),
        P("dp", "head"),
        P(None, "dp", "head"),
        P(None, "dp", "head"),
    )
    return jax.shard_map(
        body,
        mesh=mesh,
        in_specs=placed,
        out_specs=(
            P(),
            P(),
            P("dp", None),
            P(None, "dp", "head"),
            P(None, "dp", "head"),
            P(None, "dp", "head"),
            P(None, "dp", "head"),
            P(None, "dp", "head"),
            P(None, "dp", "head"),
            P(None, "dp", "head"),
            P(None, "dp", "head"),
            P(None, "dp", "head"),
            P(None, "dp", "head"),
            P(None, "dp", "head"),
            P("dp", "head"),
            P("dp", "head"),
            P("dp", "head"),
            P(None, "dp", "head"),
            P(None, "dp", "head"),
            P(None, "dp", "head"),
        ),
        check_vma=False,
    )
```
